32 devices in a mesh: section: 2 (over x), dp: 16 (over z, y, core).
Axes of the slice: x: 2, y: 2, z: 4, core: 2. Of those that a mesh axis runs over, the one named last changes fastest.
Arguments:
- chars: bfloat16 [2, 16, 64, 16, 256], P(None, 'dp'), may hold values from -6 to 6
- counts: int32 [2, 16, 64], P(None, 'dp'), may hold values from 1 to 16
- languages: int32 [2, 16], P(None, 'dp'), may hold values from 0 to 7
- language_table: bfloat16 [8, 256], replicated, may hold values from -6 to 6
- char_gain_attn: float32 [256], replicated, may hold values from 0.5 to 1.5
- char_project: bfloat16 [256, 768], replicated, may hold values from -0.375 to 0.375
- char_output: bfloat16 [256, 256], replicated, may hold values from -0.75 to 0.75
- char_gain_mlp: float32 [256], replicated, may hold values from 0.5 to 1.5
- char_expand: bfloat16 [256, 1024], replicated, may hold values from -0.375 to 0.375
- char_shrink: bfloat16 [1024, 256], replicated, may hold values from -0.1875 to 0.1875
- word_input: bfloat16 [256, 512], replicated, may hold values from -0.375 to 0.375
- word_gain_attn: float32 [512], replicated, may hold values from 0.5 to 1.5
- word_project: bfloat16 [512, 1536], replicated, may hold values from -0.25 to 0.25
- word_output: bfloat16 [512, 512], replicated, may hold values from -1 to 1
- word_gain_mlp: float32 [512], replicated, may hold values from 0.5 to 1.5
- word_expand: bfloat16 [512, 2048], replicated, may hold values from -0.25 to 0.25
- word_shrink: bfloat16 [2048, 512], replicated, may hold values from -0.125 to 0.125
- cotangent: bfloat16 [2, 16, 64, 512], P(None, 'dp'), may hold values from -6 to 6
Outputs:
- output: float32 [2, 16, 64, 512], P('section', 'dp')
- chars_grad: float32 [2, 16, 64, 16, 256], P('section', 'dp')
- language_table_grad: float32 [8, 256], P(None, 'dp')
- char_gain_attn_grad: float32 [256], P('dp')
- char_project_grad: float32 [256, 768], P('dp')
- char_output_grad: float32 [256, 256], P('dp')
- char_gain_mlp_grad: float32 [256], P('dp')
- char_expand_grad: float32 [256, 1024], P('dp')
- char_shrink_grad: float32 [1024, 256], P('dp')
- word_input_grad: float32 [256, 512], P('dp')
- word_gain_attn_grad: float32 [512], P('dp')
- word_project_grad: float32 [512, 1536], P('dp')
- word_output_grad: float32 [512, 512], P('dp')
- word_gain_mlp_grad: float32 [512], P('dp')
- word_expand_grad: float32 [512, 2048], P('dp')
- word_shrink_grad: float32 [2048, 512], P('dp')
The draws below stay inside these ranges and needn't reach their ends.
Inputs may be any that keep to these rules, and one draw needn't show every extreme that they name: `counts`: characters of each word; slots from the count on are padding.
All inputs are finite; a program needn't handle non-finite values.
Results may differ from the reference program's by a relative error of at most 0.015.
Values may be sent and summed in bfloat16 or wider, within the bound.
No kernel may reach another device: no remote copies, remote signals or barrier semaphores. Data moves between devices by JAX's collectives and lax.ppermute only.
A program may use at most 192 MiB of HBM per device.

```python
import jax
import jax.numpy as jnp
from jax import lax

CD = 256
CH = 4
CF = 1024
CL = 16
D = 512
H = 8
FF = 2048
LANGS = 8
WORDS = 64
MICRO = 2
BATCH = 16


def plant(values, key, least, high):
    longest = values.shape.index(max(values.shape))
    spots = []
    for shift in (0, 1):
        where = [jax.random.randint(jax.random.fold_in(key, axis), (), 0, length) for axis, length in enumerate(values.shape)]
        where[longest] = (where[longest] + shift) % values.shape[longest]
        spots.append(tuple(where))
    return values.at[spots[0]].set(least).at[spots[1]].set(high)


def block_scale(own_key, extent, cuts, low, largest):
    level, own = 1.0, jax.random.fold_in(own_key, 6)
    for axis_at, blocks in cuts:
        steps = jnp.exp(jax.random.uniform(jax.random.fold_in(own, axis_at), (blocks,), jnp.float32, low / len(cuts), largest / len(cuts)))
        level = level * jnp.repeat(steps, extent[axis_at] // blocks).reshape([-1 if axis == axis_at else 1 for axis in range(len(extent))])
    return level


def centred(rng, extent, width, limit, shards=(), kind=jnp.bfloat16):
    values = width * jax.random.normal(rng, extent, jnp.float32)
    if shards:
        values = values * block_scale(rng, extent, shards, -0.22, 0.18)
    return jnp.clip(values, -limit, limit).astype(kind)


def setup_inputs(seed: int = 0) -> dict:
    keys = jax.random.split(jax.random.key(seed), 19)
    chars = centred(keys[0], (MICRO, BATCH, WORDS, CL, CD), 1.0, 6.0, ((1, 16),))
    counts = plant(jax.random.randint(keys[1], (MICRO, BATCH, WORDS), 1, CL + 1), jax.random.fold_in(keys[1], 1), 1, CL).astype(jnp.int32)
    languages = plant(jax.random.randint(keys[2], (MICRO, BATCH), 0, LANGS), jax.random.fold_in(keys[2], 1), 0, LANGS - 1).astype(jnp.int32)
    language_table = centred(keys[3], (LANGS, CD), 1.0, 6.0)
    char_gain_attn = jnp.clip(1.0 + 0.1 * jax.random.normal(keys[4], (CD,), jnp.float32), 0.5, 1.5)
    char_project = centred(keys[5], (CD, 3 * CD), CD ** -0.5, 0.375)
    char_output = centred(keys[6], (CD, CD), (CD // 4) ** -0.5, 0.75)
    char_gain_mlp = jnp.clip(1.0 + 0.1 * jax.random.normal(keys[7], (CD,), jnp.float32), 0.5, 1.5)
    char_expand = centred(keys[8], (CD, CF), CD ** -0.5, 0.375)
    char_shrink = centred(keys[9], (CF, CD), CF ** -0.5, 0.1875)
    word_input = centred(keys[10], (CD, D), CD ** -0.5, 0.375)
    word_gain_attn = jnp.clip(1.0 + 0.1 * jax.random.normal(keys[11], (D,), jnp.float32), 0.5, 1.5)
    word_project = centred(keys[12], (D, 3 * D), D ** -0.5, 0.25)
    word_output = centred(keys[13], (D, D), (D // 16) ** -0.5, 1.0)
    word_gain_mlp = jnp.clip(1.0 + 0.1 * jax.random.normal(keys[14], (D,), jnp.float32), 0.5, 1.5)
    word_expand = centred(keys[15], (D, FF), D ** -0.5, 0.25)
    word_shrink = centred(keys[16], (FF, D), FF ** -0.5, 0.125)
    cotangent = centred(keys[17], (MICRO, BATCH, WORDS, D), 1.0, 6.0, ((1, 16),))
    return dict(chars=chars, counts=counts, languages=languages, language_table=language_table, char_gain_attn=char_gain_attn, char_project=char_project, char_output=char_output, char_gain_mlp=char_gain_mlp, char_expand=char_expand, char_shrink=char_shrink, word_input=word_input, word_gain_attn=word_gain_attn, word_project=word_project, word_output=word_output, word_gain_mlp=word_gain_mlp, word_expand=word_expand, word_shrink=word_shrink, cotangent=cotangent)


eps = 1e-05
highest = lax.Precision.HIGHEST

@jax.custom_vjp
def low(v):
    return lax.optimization_barrier(v.astype(jnp.bfloat16)).astype(jnp.float32)

@jax.custom_vjp
def low_back(v):
    return v

def low_keep(v):
    return (low(v), None)

def low_pass(kept, grad):
    return (grad,)

def back_keep(v):
    return (v, None)

def back_low(kept, grad):
    return (low(grad),)
low.defvjp(low_keep, low_pass)
low_back.defvjp(back_keep, back_low)

def rounded_both(value):
    return low_back(low(value))

def rms_norm(inputs, gain):
    return inputs * lax.rsqrt(lax.optimization_barrier(jnp.mean(inputs * inputs, axis=-1, keepdims=True)) + eps) * gain

def block(inputs, weights, head_count, key_mask):
    gain_attn, project, output, gain_mlp, expand, shrink = weights
    row_count, length, channels = inputs.shape
    head_size = channels // head_count
    normed = low(rms_norm(inputs, gain_attn))
    qkv = rounded_both(jnp.einsum('blc,cf->blf', normed, project, precision=highest))
    pieces = qkv.reshape(row_count, length, 3, head_count, head_size)
    scores = low_back(jnp.einsum('bqhd,bkhd->bhqk', pieces[:, :, 0], pieces[:, :, 1], precision=highest) * head_size ** (-0.5))
    scores = jnp.where(key_mask, scores, -1e+30)
    attn_probs = low(jax.nn.softmax(scores, axis=-1))
    mixed_heads = jnp.einsum('bhqk,bkhd->bqhd', attn_probs, pieces[:, :, 2], precision=highest)
    mixed_heads = rounded_both(mixed_heads.reshape(row_count, length, channels))
    middle = inputs + low_back(jnp.einsum('blc,cd->bld', mixed_heads, output, precision=highest))
    normed_mlp = low(rms_norm(middle, gain_mlp))
    before = low_back(jnp.einsum('blc,cf->blf', normed_mlp, expand, precision=highest))
    hidden = rounded_both(jax.nn.gelu(before))
    return middle + low_back(jnp.einsum('blf,fc->blc', hidden, shrink, precision=highest))

def forward(char_text, char_count, language, weights):
    lang_table = weights[0]
    char_weights = weights[1:7]
    word_input = weights[7]
    word_weights = weights[8:]
    onehot = (jnp.arange(LANGS) == language).astype(jnp.float32)
    inputs = char_text + jnp.dot(onehot, lang_table, precision=highest)[None, None, :]
    present = jnp.arange(CL)[None, :] < char_count[:, None]
    char_result = block(inputs, char_weights, CH, present[:, None, None, :])
    summed = lax.optimization_barrier(jnp.sum(jnp.where(present[:, :, None], char_result, 0.0), axis=1))
    pooled = rounded_both(summed / char_count[:, None].astype(jnp.float32))
    word_start = low_back(jnp.dot(pooled, word_input, precision=highest))
    causal = (jnp.arange(WORDS)[:, None] >= jnp.arange(WORDS)[None, :])[None, None]
    return block(word_start[None], word_weights, H, causal)[0]

def reference(chars, counts, languages, language_table, char_gain_attn, char_project, char_output, char_gain_mlp, char_expand, char_shrink, word_input, word_gain_attn, word_project, word_output, word_gain_mlp, word_expand, word_shrink, cotangent):
    weights = tuple((entry.astype(jnp.float32) for entry in (language_table, char_gain_attn, char_project, char_output, char_gain_mlp, char_expand, char_shrink, word_input, word_gain_attn, word_project, word_output, word_gain_mlp, word_expand, word_shrink)))
    seq_total = MICRO * BATCH
    texts = chars.reshape(seq_total, WORDS, CL, CD).astype(jnp.float32)
    count_rows = counts.reshape(seq_total, WORDS)
    lang_rows = languages.reshape(seq_total)
    cot_rows = cotangent.reshape(seq_total, WORDS, D).astype(jnp.float32)

    def one_sequence(totals, sample):
        char_text, char_count, language, cot_seq = sample

        def local_forward(text_value, weight_values):
            return forward(text_value, char_count, language, weight_values)
        result, pullback = jax.vjp(local_forward, char_text, weights)
        dtext, dweights = pullback(cot_seq)
        return (tuple((first + second for first, second in zip(totals, dweights))), (result, dtext))
    zero_grads = tuple((jnp.zeros_like(entry) for entry in weights))
    totals, (results, dtexts) = lax.scan(one_sequence, zero_grads, (texts, count_rows, lang_rows, cot_rows))
    return (results.reshape(MICRO, BATCH, WORDS, D), dtexts.reshape(MICRO, BATCH, WORDS, CL, CD), totals[0], totals[1], totals[2], totals[3], totals[4], totals[5], totals[6], totals[7], totals[8], totals[9], totals[10], totals[11], totals[12], totals[13])
```

```python
import jax
import jax.numpy as jnp
from jax import lax
from jax.sharding import PartitionSpec as P

CH = 4
H = 8


eps = 1e-05


def norm_forward(inputs, gain):
    return inputs * lax.rsqrt(jnp.mean(inputs * inputs, axis=-1, keepdims=True) + eps) * gain


def attend_forward(normed, project, head_count, key_mask):
    row_count, length, channels = normed.shape
    head_size = channels // head_count
    qkv = jnp.einsum("blc,cf->blf", normed, project, preferred_element_type=jnp.float32).astype(
        jnp.bfloat16
    )
    pieces = qkv.reshape(row_count, length, 3, head_count, head_size)
    scores = jnp.einsum(
        "bqhd,bkhd->bhqk", pieces[:, :, 0], pieces[:, :, 1], preferred_element_type=jnp.float32
    ) * head_size ** (-0.5)
    scores = jnp.where(key_mask, scores, -1e30)
    row_max = jnp.max(scores, axis=-1, keepdims=True)
    weights_exp = jnp.exp(scores - row_max)
    row_total = jnp.sum(weights_exp, axis=-1, keepdims=True)
    attn_probs = (weights_exp / row_total).astype(jnp.bfloat16)
    mixed_heads = jnp.einsum(
        "bhqk,bkhd->bqhd", attn_probs, pieces[:, :, 2], preferred_element_type=jnp.float32
    )
    mixed_heads = mixed_heads.reshape(row_count, length, channels).astype(jnp.bfloat16)
    return (qkv, row_max + jnp.log(row_total), mixed_heads)


def attend_backward(
    normed, project, output, qkv, logsum, mixed_heads, dmiddle_low, head_count, key_mask
):
    row_count, length, channels = normed.shape
    head_size = channels // head_count
    scaling = head_size ** (-0.5)
    output_grad = jnp.einsum(
        "blc,bld->cd", mixed_heads, dmiddle_low, preferred_element_type=jnp.float32
    )
    dmixed = jnp.einsum(
        "bld,cd->blc", dmiddle_low, output, preferred_element_type=jnp.float32
    ).astype(jnp.bfloat16)
    dmixed = dmixed.reshape(row_count, length, head_count, head_size)
    pieces = qkv.reshape(row_count, length, 3, head_count, head_size)
    scores = (
        jnp.einsum(
            "bqhd,bkhd->bhqk", pieces[:, :, 0], pieces[:, :, 1], preferred_element_type=jnp.float32
        )
        * scaling
    )
    scores = jnp.where(key_mask, scores, -1e30)
    attn_probs = jnp.exp(scores - logsum)
    dprobs = jnp.einsum(
        "bqhd,bkhd->bhqk", dmixed, pieces[:, :, 2], preferred_element_type=jnp.float32
    )
    row_delta = jnp.sum(attn_probs * dprobs, axis=-1, keepdims=True)
    dscores = (attn_probs * (dprobs - row_delta)).astype(jnp.bfloat16)
    dquery = (
        jnp.einsum("bhqk,bkhd->bqhd", dscores, pieces[:, :, 1], preferred_element_type=jnp.float32)
        * scaling
    )
    dkeys = (
        jnp.einsum("bhqk,bqhd->bkhd", dscores, pieces[:, :, 0], preferred_element_type=jnp.float32)
        * scaling
    )
    dvalues = jnp.einsum(
        "bhqk,bqhd->bkhd",
        attn_probs.astype(jnp.bfloat16),
        dmixed,
        preferred_element_type=jnp.float32,
    )
    dqkv = (
        jnp.stack([dquery, dkeys, dvalues], axis=2)
        .reshape(row_count, length, 3 * channels)
        .astype(jnp.bfloat16)
    )
    project_grad = jnp.einsum("blc,blf->cf", normed, dqkv, preferred_element_type=jnp.float32)
    dnormed = jnp.einsum("blf,cf->blc", dqkv, project, preferred_element_type=jnp.float32)
    return (dnormed, project_grad, output_grad)


def block_forward(inputs, weights, head_count, key_mask):
    gain_attn, project, output, gain_mlp, expand, shrink = weights
    normed = norm_forward(inputs, gain_attn).astype(jnp.bfloat16)
    qkv, logsum, mixed_heads = attend_forward(normed, project, head_count, key_mask)
    middle = inputs + jnp.einsum(
        "blc,cd->bld", mixed_heads, output, preferred_element_type=jnp.float32
    )
    normed_mlp = norm_forward(middle, gain_mlp).astype(jnp.bfloat16)
    before = jnp.einsum("blc,cf->blf", normed_mlp, expand, preferred_element_type=jnp.float32)
    hidden = jax.nn.gelu(before).astype(jnp.bfloat16)
    result = middle + jnp.einsum("blf,fc->blc", hidden, shrink, preferred_element_type=jnp.float32)
    return (result, (inputs, normed, qkv, logsum, mixed_heads, middle, normed_mlp, before, hidden))


def block_backward(dresult, stored, weights, head_count, key_mask):
    gain_attn, project, output, gain_mlp, expand, shrink = weights
    inputs, normed, qkv, logsum, mixed_heads, middle, normed_mlp, before, hidden = stored
    grad_low = dresult.astype(jnp.bfloat16)
    shrink_grad = jnp.einsum("blf,blc->fc", hidden, grad_low, preferred_element_type=jnp.float32)
    dhidden = jnp.einsum(
        "blc,fc->blf", grad_low, shrink, preferred_element_type=jnp.float32
    ).astype(jnp.bfloat16)
    gelu_pull = jax.vjp(jax.nn.gelu, before)[1]
    dbefore = gelu_pull(dhidden.astype(jnp.float32))[0].astype(jnp.bfloat16)
    expand_grad = jnp.einsum("blc,blf->cf", normed_mlp, dbefore, preferred_element_type=jnp.float32)
    dnormed_mlp = jnp.einsum("blf,cf->blc", dbefore, expand, preferred_element_type=jnp.float32)
    norm_pull = jax.vjp(norm_forward, middle, gain_mlp)[1]
    dmiddle_norm, gain_mlp_grad = norm_pull(dnormed_mlp)
    dmiddle = dresult + dmiddle_norm
    dnormed, project_grad, output_grad = attend_backward(
        normed,
        project,
        output,
        qkv,
        logsum,
        mixed_heads,
        dmiddle.astype(jnp.bfloat16),
        head_count,
        key_mask,
    )
    first_pull = jax.vjp(norm_forward, inputs, gain_attn)[1]
    dinputs_norm, gain_attn_grad = first_pull(dnormed)
    return (
        dmiddle + dinputs_norm,
        (gain_attn_grad, project_grad, output_grad, gain_mlp_grad, expand_grad, shrink_grad),
    )


def char_front(char_text, char_count, language, lang_table, weights):
    present = lax.broadcasted_iota(jnp.int32, char_text.shape[:2], 1) < char_count[:, None]
    onehot = (lax.broadcasted_iota(jnp.int32, (lang_table.shape[0],), 0) == language).astype(
        jnp.bfloat16
    )
    lang_row = jnp.dot(onehot, lang_table, preferred_element_type=jnp.float32)
    inputs = char_text.astype(jnp.float32) + lang_row
    result, stored = block_forward(inputs, weights, CH, present[:, None, None, :])
    summed = jnp.sum(jnp.where(present[:, :, None], result, 0.0), axis=1)
    pooled = (summed / char_count[:, None].astype(jnp.float32)).astype(jnp.bfloat16)
    return (pooled, stored, present, onehot)


def char_back(stored, present, onehot, char_count, dpooled, weights):
    spread = dpooled.astype(jnp.float32) / char_count[:, None].astype(jnp.float32)
    dresult = jnp.where(present[:, :, None], spread[:, None, :], 0.0)
    dinputs, gradients = block_backward(dresult, stored, weights, CH, present[:, None, None, :])
    table_grad = onehot.astype(jnp.float32)[:, None] * jnp.sum(dinputs, axis=(0, 1))[None, :]
    return (dinputs, (table_grad,) + gradients)


def word_full(pooled, cot_rows, word_input, weights):
    length = pooled.shape[0]
    word_start = jnp.dot(pooled, word_input, preferred_element_type=jnp.float32)[None]
    causal = (
        lax.broadcasted_iota(jnp.int32, (length, length), 0)
        >= lax.broadcasted_iota(jnp.int32, (length, length), 1)
    )[None, None]
    result, stored = block_forward(word_start, weights, H, causal)
    dstart, gradients = block_backward(
        cot_rows.astype(jnp.float32)[None], stored, weights, H, causal
    )
    grad_low = dstart[0].astype(jnp.bfloat16)
    input_grad = jnp.einsum("wc,wd->cd", pooled, grad_low, preferred_element_type=jnp.float32)
    dpooled = jnp.einsum(
        "wd,cd->wc", grad_low, word_input, preferred_element_type=jnp.float32
    ).astype(jnp.bfloat16)
    return (result[0], dpooled, (input_grad,) + gradients)


def reduce_rows(gradients):
    shards = lax.axis_size("dp")
    flat = []
    for place, gradient in enumerate(gradients):
        if place == 0:
            gradient = gradient.T
        flat.append(gradient.astype(jnp.bfloat16).reshape(shards, -1))
    packed = jnp.concatenate(flat, axis=1)
    me = lax.axis_index("dp")
    packed = jnp.take(packed, jnp.arange(shards) ^ me, axis=0)
    bit = 1
    while packed.shape[0] > 1:
        pairs = packed.reshape(packed.shape[0] // 2, 2, packed.shape[1])
        arrived = lax.ppermute(pairs[:, 1], "dp", [(i, i ^ bit) for i in range(shards)])
        packed = (pairs[:, 0].astype(jnp.float32) + arrived.astype(jnp.float32)).astype(
            jnp.bfloat16
        )
        bit *= 2
    arrived = lax.ppermute(packed, "section", [(0, 1), (1, 0)])
    total = (packed.astype(jnp.float32) + arrived.astype(jnp.float32))[0]
    outs = []
    at = 0
    for place, gradient in enumerate(gradients):
        size = gradient.size // shards
        piece = total[at : at + size]
        at += size
        if place == 0:
            outs.append(piece.reshape(-1, gradient.shape[0]).T)
        else:
            outs.append(piece.reshape((gradient.shape[0] // shards,) + gradient.shape[1:]))
    return tuple(outs)


def local(
    chars,
    counts,
    languages,
    language_table,
    char_gain_attn,
    char_project,
    char_output,
    char_gain_mlp,
    char_expand,
    char_shrink,
    word_input,
    word_gain_attn,
    word_project,
    word_output,
    word_gain_mlp,
    word_expand,
    word_shrink,
    cotangent,
):
    char_weights = (
        char_gain_attn,
        char_project,
        char_output,
        char_gain_mlp,
        char_expand,
        char_shrink,
    )
    word_weights = (
        word_gain_attn,
        word_project,
        word_output,
        word_gain_mlp,
        word_expand,
        word_shrink,
    )
    section_index = lax.axis_index("section")
    char_text = chars[section_index, 0]
    char_count = counts[section_index, 0]
    language = languages[section_index, 0]
    cot_rows = cotangent[section_index, 0]
    pooled, stored, present, onehot = char_front(
        char_text, char_count, language, language_table, char_weights
    )
    result, dpooled, word_grads = word_full(pooled, cot_rows, word_input, word_weights)
    text_grad, char_grads = char_back(stored, present, onehot, char_count, dpooled, char_weights)
    totals = reduce_rows(char_grads + word_grads)
    return (result[None, None], text_grad[None, None]) + totals


def solution(mesh):
    placed = (
        P(None, "dp", None, None, None),
        P(None, "dp", None),
        P(None, "dp"),
        P(),
        P(),
        P(),
        P(),
        P(),
        P(),
        P(),
        P(),
        P(),
        P(),
        P(),
        P(),
        P(),
        P(),
        P(None, "dp", None, None),
    )
    return jax.shard_map(
        local,
        mesh=mesh,
        in_specs=placed,
        out_specs=(
            P("section", "dp", None, None),
            P("section", "dp", None, None, None),
            P(None, "dp"),
            P("dp"),
            P("dp", None),
            P("dp", None),
            P("dp"),
            P("dp", None),
            P("dp", None),
            P("dp", None),
            P("dp"),
            P("dp", None),
            P("dp", None),
            P("dp"),
            P("dp", None),
            P("dp", None),
        ),
        check_vma=False,
    )
```

```python
import functools

import jax
import jax.numpy as jnp
from jax import lax
from jax.experimental import pallas as pl
from jax.experimental.pallas import tpu as pltpu
from jax.sharding import PartitionSpec as P

CH = 4
H = 8
HEAD = 64
SLAB = 256
BLOCK = 128
STEP = 256
VMEM_LIMIT = 60 * 1024 * 1024

eps = 1e-05

f32 = jnp.float32
bf16 = jnp.bfloat16


def dot(a, b):
    return jnp.dot(a, b, preferred_element_type=f32)


def dot_nt(a, b):
    return lax.dot_general(a, b, (((1,), (1,)), ((), ())), preferred_element_type=f32)


def lanes(shape):
    return lax.broadcasted_iota(jnp.int32, shape, 1)


def rows_of(shape):
    return lax.broadcasted_iota(jnp.int32, shape, 0)


def flip(a):
    size = a.shape[1]
    width = min(size, 256)
    eye = jnp.where(rows_of((width, width)) == lanes((width, width)), 1.0, 0.0).astype(bf16)
    return jnp.concatenate(
        [dot_nt(eye, a[:, at : at + width]).astype(bf16) for at in range(0, size, width)], axis=0
    )


def head_mask(head):
    return jnp.where(lanes((1, SLAB)) // HEAD == head, 1.0, 0.0).astype(bf16)


def stack_heads(a):
    return jnp.concatenate([a * head_mask(head) for head in range(SLAB // HEAD)], axis=0)


def merge_heads(a):
    rows = a.shape[0] // (SLAB // HEAD)
    head = lanes((rows, SLAB)) // HEAD
    total = a[:rows]
    for place in range(1, SLAB // HEAD):
        total = jnp.where(head == place, a[place * rows : (place + 1) * rows], total)
    return total


def compact(scores, length):
    group = lanes((length, BLOCK)) // length
    total = scores[:length]
    for place in range(1, BLOCK // length):
        total = jnp.where(group == place, scores[place * length : (place + 1) * length], total)
    return total


def expand(values, length):
    group = lanes((length, BLOCK)) // length
    return jnp.concatenate(
        [jnp.where(group == place, values, 0.0) for place in range(BLOCK // length)], axis=0
    ).astype(bf16)


def attend(q, k, v, key_mask, length):
    heads = SLAB // HEAD
    scores = dot_nt(stack_heads(k), q)
    v_flipped = flip(v)
    kept = []
    mixed = []
    for head in range(heads):
        piece = compact(scores[head * BLOCK : (head + 1) * BLOCK], length) * HEAD**-0.5
        piece = jnp.where(key_mask, piece, -1e30)
        weights = jnp.exp(piece - jnp.max(piece, axis=0, keepdims=True))
        probs = weights / jnp.sum(weights, axis=0, keepdims=True)
        kept.append(probs)
        mixed.append(dot(v_flipped[head * HEAD : (head + 1) * HEAD], expand(probs, length)))
    return (kept, jnp.concatenate(mixed, axis=0).astype(bf16))


def attend_back(q, k, v, probs, dmixed, length):
    heads = SLAB // HEAD
    dprobs = dot_nt(stack_heads(v), dmixed)
    k_flipped = flip(k)
    dq = []
    dk = []
    dv = []
    for head in range(heads):
        own = probs[head]
        piece = compact(dprobs[head * BLOCK : (head + 1) * BLOCK], length)
        delta = jnp.sum(own * piece, axis=0, keepdims=True)
        dscores = expand(own * (piece - delta), length)
        dq.append(dot(k_flipped[head * HEAD : (head + 1) * HEAD], dscores))
        dk.append(dot(dscores, q))
        dv.append(dot(expand(own, length), dmixed))
    scaling = HEAD**-0.5
    dq = flip((jnp.concatenate(dq, axis=0) * scaling).astype(bf16))
    dk = (merge_heads(jnp.concatenate(dk, axis=0)) * scaling).astype(bf16)
    dv = merge_heads(jnp.concatenate(dv, axis=0)).astype(bf16)
    return (dq, dk, dv)


def unit(x):
    scale = lax.rsqrt(jnp.mean(x * x, axis=-1, keepdims=True) + eps)
    return (x * scale, scale)


def unit_back(dnormed, gain, normal, scale):
    weighted = dnormed * gain
    return scale * (weighted - normal * jnp.mean(normal * weighted, axis=-1, keepdims=True))


def gelu_parts(before):
    c = 0.7978845608028654
    square = before * before
    half = 0.5 * jnp.tanh(before * (c + (c * 0.044715) * square)) + 0.5
    value = before * half
    slope = half + value * (1.0 - half) * (2.0 * c + (6.0 * c * 0.044715) * square)
    return (value, slope)


def char_rows(chars_ref, table_ref, language):
    table = table_ref[...].astype(f32)
    row = jnp.sum(jnp.where(rows_of(table.shape) == language, table, 0.0), axis=0, keepdims=True)
    return chars_ref[0].astype(f32) + row


def counts_by_row(counts_ref, step, slots):
    words = counts_ref.shape[-1]
    counts = jnp.broadcast_to(counts_ref[0].astype(f32), (8, words)).astype(bf16)
    shape = (words, STEP)
    member = (lanes(shape) + step * STEP) // slots == rows_of(shape)
    return dot(counts, jnp.where(member, 1.0, 0.0).astype(bf16))[:1]


def char_forward_kernel(
    slots,
    where_ref,
    chars_ref,
    counts_ref,
    table_ref,
    gain_attn_ref,
    project_ref,
    output_ref,
    gain_mlp_ref,
    expand_ref,
    shrink_ref,
    pooled_ref,
    hidden_sum_ref,
    qkv_ref,
    probs_ref,
    mixed_ref,
    middle_ref,
    slope_ref,
    sums,
):
    step = pl.program_id(0)
    x = char_rows(chars_ref, table_ref, where_ref[1])
    normal, _ = unit(x)
    normed = (normal * gain_attn_ref[...]).astype(bf16)
    qkv = dot(normed, project_ref[...]).astype(bf16)
    qkv_ref[...] = qkv
    row_counts = counts_by_row(counts_ref, step, slots)
    mixed = []
    for block in range(STEP // BLOCK):
        part = slice(block * BLOCK, (block + 1) * BLOCK)
        key_mask = rows_of((slots, BLOCK)).astype(f32) < row_counts[:, part]
        probs, piece = attend(
            qkv[part, :SLAB], qkv[part, SLAB : 2 * SLAB], qkv[part, 2 * SLAB :], key_mask, slots
        )
        for head in range(CH):
            probs_ref[head * slots : (head + 1) * slots, part] = probs[head]
        mixed_ref[:, part] = piece
        mixed.append(flip(piece))
    mixed = jnp.concatenate(mixed, axis=0)
    middle = x + dot(mixed, output_ref[...])
    middle_ref[...] = middle
    normal, _ = unit(middle)
    normed = (normal * gain_mlp_ref[...]).astype(bf16)
    word_shape = (STEP // slots, STEP)
    lane = lanes(word_shape)
    member = (lane // slots == rows_of(word_shape)) & ((lane % slots).astype(f32) < row_counts)
    member = jnp.where(member, 1.0, 0.0).astype(bf16)
    words = pl.ds(pl.multiple_of(step * (STEP // slots), STEP // slots), STEP // slots)
    for at in range(0, expand_ref.shape[1], 256):
        part = slice(at, at + 256)
        value, slope = gelu_parts(dot(normed, expand_ref[:, part]))
        slope_ref[:, part] = slope.astype(bf16)
        hidden_sum_ref[words, part] = dot(member, value.astype(bf16)).astype(bf16)
    high = middle.astype(bf16)
    low = (middle - high.astype(f32)).astype(bf16)
    sums[words, :] = dot(member, high) + dot(member, low)

    @pl.when(step == pl.num_programs(0) - 1)
    def _():
        words = counts_ref.shape[-1]
        shape = (words, words)
        column = jnp.sum(
            jnp.where(
                rows_of(shape) == lanes(shape),
                jnp.broadcast_to(counts_ref[0].astype(f32), shape),
                0.0,
            ),
            axis=1,
            keepdims=True,
        )
        total = sums[...] + dot(hidden_sum_ref[...], shrink_ref[...])
        pooled_ref[...] = (total / column).astype(bf16)


def char_forward(where, chars, counts, table, weights, slots):
    gain_attn, project, output, gain_mlp, expand_w, shrink = weights
    rows, width = chars.shape[1:]
    words = rows // slots
    hidden = expand_w.shape[1]

    def whole(array):
        return pl.BlockSpec(array.shape, lambda i, w: (0,) * array.ndim)

    return pl.pallas_call(
        functools.partial(char_forward_kernel, slots),
        grid_spec=pltpu.PrefetchScalarGridSpec(
            num_scalar_prefetch=1,
            grid=(rows // STEP,),
            in_specs=[
                pl.BlockSpec((1, STEP, width), lambda i, w: (w[0], i, 0)),
                pl.BlockSpec((1, 1, words), lambda i, w: (w[0], 0, 0)),
                whole(table),
                whole(gain_attn),
                whole(project),
                whole(output),
                whole(gain_mlp),
                whole(expand_w),
                whole(shrink),
            ],
            out_specs=[
                pl.BlockSpec((words, width), lambda i, w: (0, 0)),
                pl.BlockSpec((words, hidden), lambda i, w: (0, 0)),
                pl.BlockSpec((STEP, 3 * width), lambda i, w: (i, 0)),
                pl.BlockSpec((CH * slots, STEP), lambda i, w: (0, i)),
                pl.BlockSpec((width, STEP), lambda i, w: (0, i)),
                pl.BlockSpec((STEP, width), lambda i, w: (i, 0)),
                pl.BlockSpec((STEP, hidden), lambda i, w: (i, 0)),
            ],
            scratch_shapes=[pltpu.VMEM((words, width), f32)],
        ),
        out_shape=[
            jax.ShapeDtypeStruct((words, width), bf16),
            jax.ShapeDtypeStruct((words, hidden), bf16),
            jax.ShapeDtypeStruct((rows, 3 * width), bf16),
            jax.ShapeDtypeStruct((CH * slots, rows), f32),
            jax.ShapeDtypeStruct((width, rows), bf16),
            jax.ShapeDtypeStruct((rows, width), f32),
            jax.ShapeDtypeStruct((rows, hidden), bf16),
        ],
        compiler_params=pltpu.CompilerParams(vmem_limit_bytes=VMEM_LIMIT),
        name="char_forward",
    )(where, chars, counts, table, gain_attn, project, output, gain_mlp, expand_w, shrink)


CHAR_SLOT = 208


def char_backward_kernel(
    slots,
    shards,
    where_ref,
    chars_ref,
    counts_ref,
    table_ref,
    gain_attn_ref,
    project_ref,
    output_ref,
    gain_mlp_ref,
    expand_ref,
    shrink_ref,
    dpooled_ref,
    hidden_sum_ref,
    qkv_ref,
    probs_ref,
    mixed_ref,
    middle_ref,
    slope_ref,
    grad_ref,
    keep_ref,
    send_ref,
    spread_high,
    spread_low,
    dhidden_words,
    dbefore,
    dqkv,
    dy,
    normed_t,
    normed_mlp_t,
    gains,
    packed,
    sems,
):
    step = pl.program_id(0)
    words = counts_ref.shape[-1]

    @pl.when(step == 0)
    def _():
        shape = (words, words)
        column = jnp.sum(
            jnp.where(
                rows_of(shape) == lanes(shape),
                jnp.broadcast_to(counts_ref[0].astype(f32), shape),
                0.0,
            ),
            axis=1,
            keepdims=True,
        )
        spread = dpooled_ref[...].astype(f32) / column
        high = spread.astype(bf16)
        spread_high[...] = high
        spread_low[...] = (spread - high.astype(f32)).astype(bf16)
        dhidden_words[...] = dot_nt(high, shrink_ref[...]).astype(bf16)
        gains[...] = jnp.zeros_like(gains)

    at_step = pl.ds(pl.multiple_of(step * STEP, STEP), STEP)
    shape = (STEP, words)
    row = rows_of(shape) + step * STEP
    member = (row // slots == lanes(shape)) & (row % slots < counts_ref[0])
    member = jnp.where(member, 1.0, 0.0).astype(bf16)
    dnormed = jnp.zeros((STEP, gain_mlp_ref.shape[1]), f32)
    for at in range(0, expand_ref.shape[1], 256):
        part = slice(at, at + 256)
        piece = dot(member, dhidden_words[:, part]).astype(bf16) * slope_ref[:, part]
        dbefore[at_step, part] = piece
    dnormed = dot_nt(dbefore[at_step, :], expand_ref[...])
    normal, scale = unit(middle_ref[...])
    normed_mlp_t[:, at_step] = flip((normal * gain_mlp_ref[...]).astype(bf16))
    gains[1:2] += jnp.sum(dnormed * normal, axis=0, keepdims=True)
    dmiddle = (
        dot(member, spread_high[...])
        + dot(member, spread_low[...])
        + unit_back(dnormed, gain_mlp_ref[...], normal, scale)
    )
    dy_low = dmiddle.astype(bf16)
    dy[at_step, :] = dy_low
    dmixed = dot_nt(dy_low, output_ref[...]).astype(bf16)
    for block in range(STEP // BLOCK):
        part = slice(block * BLOCK, (block + 1) * BLOCK)
        probs = [probs_ref[head * slots : (head + 1) * slots, part] for head in range(CH)]
        pieces = attend_back(
            qkv_ref[part, :SLAB],
            qkv_ref[part, SLAB : 2 * SLAB],
            qkv_ref[part, 2 * SLAB :],
            probs,
            dmixed[part],
            slots,
        )
        at_block = pl.ds(pl.multiple_of(step * STEP + block * BLOCK, BLOCK), BLOCK)
        for place in range(3):
            dqkv[at_block, place * SLAB : (place + 1) * SLAB] = pieces[place]
    dnormed = dot_nt(dqkv[at_step, :], project_ref[...])
    normal, scale = unit(char_rows(chars_ref, table_ref, where_ref[1]))
    normed_t[:, at_step] = flip((normal * gain_attn_ref[...]).astype(bf16))
    gains[0:1] += jnp.sum(dnormed * normal, axis=0, keepdims=True)
    dx = dmiddle + unit_back(dnormed, gain_attn_ref[...], normal, scale)
    grad_ref[...] = dx
    row_sum = jnp.sum(dx, axis=0, keepdims=True)
    gains[8:16] += jnp.where(rows_of((8, 1)) == where_ref[1], row_sum, 0.0)

    @pl.when(step == pl.num_programs(0) - 1)
    def _():
        me = where_ref[2]
        width = gains.shape[1]

        def place(shard):
            other = shard ^ me
            return (other & 1) * 8 + ((other >> 1) & 3) * 2 + (other >> 3)

        def put(gradient, at):
            size = gradient.shape[0] // shards
            for shard in range(shards):
                piece = gradient[shard * size : (shard + 1) * size].astype(bf16)
                for column in range(gradient.shape[1] // width):
                    start = at + column * size
                    packed[place(shard), start : start + size] = piece[
                        :, column * width : (column + 1) * width
                    ]
            return at + size * (gradient.shape[1] // width)

        at = put(dot(normed_t[...], dqkv[...]), 0)
        at = put(dot(mixed_ref[...], dy[...]), at)
        at = put(dot(normed_mlp_t[...], dbefore[...]), at)
        at = put(dot(flip(hidden_sum_ref[...]), spread_high[...]), at)
        extra = gains[...].astype(bf16)
        for shard in range(shards):
            packed[shard, at : at + 16] = extra
        half = shards // 2
        copies = [
            pltpu.make_async_copy(packed.at[pl.ds(half, half)], send_ref, sems.at[0]),
            pltpu.make_async_copy(packed.at[pl.ds(0, half)], keep_ref, sems.at[1]),
        ]
        for copy in copies:
            copy.start()
        for copy in copies:
            copy.wait()


def char_backward(where, chars, counts, table, weights, dpooled, stored, slots, shards):
    gain_attn, project, output, gain_mlp, expand_w, shrink = weights
    hidden_sum, qkv, probs, mixed, middle, slope = stored
    rows, width = chars.shape[1:]
    words = rows // slots
    hidden = expand_w.shape[1]

    def whole(array):
        return pl.BlockSpec(array.shape, lambda i, w: (0,) * array.ndim)

    half = (shards // 2, CHAR_SLOT, width)
    return pl.pallas_call(
        functools.partial(char_backward_kernel, slots, shards),
        grid_spec=pltpu.PrefetchScalarGridSpec(
            num_scalar_prefetch=1,
            grid=(rows // STEP,),
            in_specs=[
                pl.BlockSpec((1, STEP, width), lambda i, w: (w[0], i, 0)),
                pl.BlockSpec((1, 1, words), lambda i, w: (w[0], 0, 0)),
                whole(table),
                whole(gain_attn),
                whole(project),
                whole(output),
                whole(gain_mlp),
                whole(expand_w),
                whole(shrink),
                whole(dpooled),
                whole(hidden_sum),
                pl.BlockSpec((STEP, 3 * width), lambda i, w: (i, 0)),
                pl.BlockSpec((CH * slots, STEP), lambda i, w: (0, i)),
                whole(mixed),
                pl.BlockSpec((STEP, width), lambda i, w: (i, 0)),
                pl.BlockSpec((STEP, hidden), lambda i, w: (i, 0)),
            ],
            out_specs=[
                pl.BlockSpec((STEP, width), lambda i, w: (i, 0)),
                pl.BlockSpec(memory_space=pl.ANY),
                pl.BlockSpec(memory_space=pl.ANY),
            ],
            scratch_shapes=[
                pltpu.VMEM((words, width), bf16),
                pltpu.VMEM((words, width), bf16),
                pltpu.VMEM((words, hidden), bf16),
                pltpu.VMEM((rows, hidden), bf16),
                pltpu.VMEM((rows, 3 * width), bf16),
                pltpu.VMEM((rows, width), bf16),
                pltpu.VMEM((width, rows), bf16),
                pltpu.VMEM((width, rows), bf16),
                pltpu.VMEM((16, width), f32),
                pltpu.VMEM((shards, CHAR_SLOT, width), bf16),
                pltpu.SemaphoreType.DMA((2,)),
            ],
        ),
        out_shape=[
            jax.ShapeDtypeStruct((rows, width), f32),
            jax.ShapeDtypeStruct(half, bf16),
            jax.ShapeDtypeStruct(half, bf16),
        ],
        compiler_params=pltpu.CompilerParams(vmem_limit_bytes=VMEM_LIMIT),
        name="char_backward",
    )(
        where,
        chars,
        counts,
        table,
        gain_attn,
        project,
        output,
        gain_mlp,
        expand_w,
        shrink,
        dpooled,
        hidden_sum,
        qkv,
        probs,
        mixed,
        middle,
        slope,
    )


WORD_SLOT = 416


def word_kernel(
    length,
    shards,
    where_ref,
    own_ref,
    core_ref,
    high_ref,
    section_ref,
    both_ref,
    cot_ref,
    cot_core_ref,
    cot_high_ref,
    input_ref,
    gain_attn_ref,
    project_ref,
    output_ref,
    gain_mlp_ref,
    expand_ref,
    shrink_ref,
    result_ref,
    dpooled_ref,
    keep_ref,
    send0_ref,
    send1_ref,
    send2_ref,
    pooled,
    dz,
    start,
    normed,
    normed_t,
    qkv,
    kept,
    mixed_t,
    middle,
    normed_mlp_t,
    hidden,
    slope,
    dbefore,
    dmixed,
    dqkv,
    dy,
    packed,
    sems,
):
    total = pooled.shape[0]
    width = output_ref.shape[0]
    section = where_ref[0]
    me = where_ref[2]
    slabs = width // SLAB
    pooled[0:length] = own_ref[...]
    pooled[length : 2 * length] = core_ref[...]
    for place, ref in enumerate((high_ref, section_ref, both_ref)):
        pooled[(2 + 2 * place) * length : (4 + 2 * place) * length] = ref[...]
    at = 0
    for other in (section, 1 - section):
        dz[at : at + length] = cot_ref[other]
        dz[at + length : at + 2 * length] = cot_core_ref[other]
        dz[at + 2 * length : at + 3 * length] = cot_high_ref[0, other]
        dz[at + 3 * length : at + 4 * length] = cot_high_ref[1, other]
        at += 4 * length

    x = dot(pooled[...], input_ref[...])
    start[...] = x
    normal, _ = unit(x)
    low = (normal * gain_attn_ref[...]).astype(bf16)
    normed[...] = low
    normed_t[...] = flip(low)
    qkv[...] = dot(low, project_ref[...]).astype(bf16)
    causal = rows_of((length, BLOCK)) <= lanes((length, BLOCK)) % length
    for block in range(total // BLOCK):
        part = slice(block * BLOCK, (block + 1) * BLOCK)
        for slab in range(slabs):
            at = slab * SLAB
            probs, piece = attend(
                qkv[part, at : at + SLAB],
                qkv[part, width + at : width + at + SLAB],
                qkv[part, 2 * width + at : 2 * width + at + SLAB],
                causal,
                length,
            )
            for head in range(SLAB // HEAD):
                kept[block * slabs + slab, head] = probs[head]
            mixed_t[at : at + SLAB, part] = piece
            dmixed[part, at : at + SLAB] = flip(piece)
    x = x + dot(dmixed[...], output_ref[...])
    middle[...] = x
    normal, _ = unit(x)
    low = (normal * gain_mlp_ref[...]).astype(bf16)
    normed_mlp_t[...] = flip(low)
    dz_all = dz[...]
    for at in range(0, expand_ref.shape[1], 256):
        part = slice(at, at + 256)
        value, bend = gelu_parts(dot(low, expand_ref[:, part]))
        hidden[:, part] = value.astype(bf16)
        dhidden = dot_nt(dz_all, shrink_ref[part, :]).astype(bf16)
        dbefore[:, part] = dhidden * bend.astype(bf16)
    result_ref[...] = middle[:length] + dot(hidden[:length], shrink_ref[...])

    dnormed = dot_nt(dbefore[...], expand_ref[...])
    normal, scale = unit(middle[...])
    gain_mlp_grad = jnp.sum(dnormed * normal, axis=0, keepdims=True)
    dmiddle = dz_all.astype(f32) + unit_back(dnormed, gain_mlp_ref[...], normal, scale)
    dy_low = dmiddle.astype(bf16)
    dy[...] = dy_low
    dmixed[...] = dot_nt(dy_low, output_ref[...]).astype(bf16)
    for block in range(total // BLOCK):
        part = slice(block * BLOCK, (block + 1) * BLOCK)
        for slab in range(slabs):
            at = slab * SLAB
            pieces = attend_back(
                qkv[part, at : at + SLAB],
                qkv[part, width + at : width + at + SLAB],
                qkv[part, 2 * width + at : 2 * width + at + SLAB],
                [kept[block * slabs + slab, head] for head in range(SLAB // HEAD)],
                dmixed[part, at : at + SLAB],
                length,
            )
            for place in range(3):
                dqkv[part, place * width + at : place * width + at + SLAB] = pieces[place]
    dnormed = dot_nt(dqkv[...], project_ref[...])
    normal, scale = unit(start[...])
    gain_attn_grad = jnp.sum(dnormed * normal, axis=0, keepdims=True)
    dword = (dmiddle + unit_back(dnormed, gain_attn_ref[...], normal, scale)).astype(bf16)
    dpooled_ref[...] = dot_nt(dword[:length], input_ref[...]).astype(bf16)
    normed[...] = dword

    low_shards = [0, 1, 2, 3]

    def shard_of(place):
        return (me & 9) | (place << 1)

    def slot_of(place):
        return place ^ ((me >> 1) & 3)

    def own_rows(flipped, size):
        return jnp.concatenate(
            [
                flipped[pl.ds(pl.multiple_of(shard_of(place) * size, size), size), :]
                for place in low_shards
            ],
            axis=0,
        )

    def own_columns(ref, size):
        return ref[:, pl.ds(pl.multiple_of(section * size, size), size)]

    def put(gradient, at):
        size = gradient.shape[0] // len(low_shards)
        for place in low_shards:
            piece = gradient[place * size : (place + 1) * size].astype(bf16)
            for column in range(gradient.shape[1] // SLAB):
                first = at + column * size
                packed[slot_of(place), first : first + size] = piece[
                    :, column * SLAB : (column + 1) * SLAB
                ]
        return at + size * (gradient.shape[1] // SLAB)

    dmixed[:, :SLAB] = pooled[...]
    pooled_t = flip(dmixed[:, :SLAB])
    mixed_holder = normed_t
    size = normed_t.shape[0] // shards
    lhs = own_rows(normed_t, size)
    mixed_holder[0 : pooled_t.shape[0]] = pooled_t
    at = put(
        dot(
            own_rows(mixed_holder, pooled_t.shape[0] // shards),
            own_columns(normed, width // 2),
        ),
        0,
    )
    at = put(dot(lhs, own_columns(dqkv, 3 * width // 2)), at)
    at = put(dot(own_rows(mixed_t, size), own_columns(dy, width // 2)), at)
    at = put(dot(own_rows(normed_mlp_t, size), own_columns(dbefore, expand_ref.shape[1] // 2)), at)
    size = hidden.shape[1] // shards
    lhs = jnp.concatenate(
        [
            flip(hidden[:, pl.ds(pl.multiple_of(shard_of(place) * size, size), size)])
            for place in low_shards
        ],
        axis=0,
    )
    at = put(dot(lhs, own_columns(dz, width // 2)), at)
    extra = jnp.concatenate(
        [gain_attn_grad[:, :SLAB], gain_attn_grad[:, SLAB:]]
        + [gain_mlp_grad[:, :SLAB], gain_mlp_grad[:, SLAB:]]
        + [jnp.zeros((12, SLAB), f32)],
        axis=0,
    ).astype(bf16)
    for place in low_shards:
        packed[place, at : at + 16] = extra
    copies = [
        pltpu.make_async_copy(packed.at[place], ref, sems.at[place])
        for place, ref in enumerate((keep_ref, send0_ref, send1_ref, send2_ref))
    ]
    for copy in copies:
        copy.start()
    for copy in copies:
        copy.wait()


def word_group(where, pooled, cotangents, word_input, weights, shards):
    gain_attn, project, output, gain_mlp, expand_w, shrink = weights
    length, channels = pooled[0].shape
    width = output.shape[0]
    hidden = expand_w.shape[1]
    total = 8 * length
    slot = (WORD_SLOT, SLAB)
    vmem = pl.BlockSpec(memory_space=pltpu.VMEM)
    hbm = pl.BlockSpec(memory_space=pl.ANY)
    return pl.pallas_call(
        functools.partial(word_kernel, length, shards),
        in_specs=[pl.BlockSpec(memory_space=pltpu.SMEM)] + [vmem] * 15,
        out_specs=[vmem, vmem, hbm, hbm, hbm, hbm],
        out_shape=[
            jax.ShapeDtypeStruct((length, width), f32),
            jax.ShapeDtypeStruct((length, channels), bf16),
        ]
        + [jax.ShapeDtypeStruct(slot, bf16)] * 4,
        scratch_shapes=[
            pltpu.VMEM((total, channels), bf16),
            pltpu.VMEM((total, width), bf16),
            pltpu.VMEM((total, width), f32),
            pltpu.VMEM((total, width), bf16),
            pltpu.VMEM((width, total), bf16),
            pltpu.VMEM((total, 3 * width), bf16),
            pltpu.VMEM((total // BLOCK * (width // SLAB), SLAB // HEAD, length, BLOCK), f32),
            pltpu.VMEM((width, total), bf16),
            pltpu.VMEM((total, width), f32),
            pltpu.VMEM((width, total), bf16),
            pltpu.VMEM((total, hidden), bf16),
            pltpu.VMEM((8, 128), bf16),
            pltpu.VMEM((total, hidden), bf16),
            pltpu.VMEM((total, width), bf16),
            pltpu.VMEM((total, 3 * width), bf16),
            pltpu.VMEM((total, width), bf16),
            pltpu.VMEM((4,) + slot, bf16),
            pltpu.SemaphoreType.DMA((4,)),
        ],
        compiler_params=pltpu.CompilerParams(vmem_limit_bytes=VMEM_LIMIT),
        name="word_group",
    )(where, *pooled, *cotangents, word_input, gain_attn, project, output, gain_mlp, expand_w, shrink)


def core_sum_kernel(keep_ref, arrived_ref, *out_refs):
    for place, ref in enumerate(out_refs):
        part = slice(2 * place, 2 * place + 2)
        ref[...] = (keep_ref[part].astype(f32) + arrived_ref[part].astype(f32)).astype(bf16)


def core_sum(keep, arrived):
    piece = jax.ShapeDtypeStruct((2,) + keep.shape[1:], bf16)
    return pl.pallas_call(
        core_sum_kernel,
        out_shape=[piece] * (keep.shape[0] // 2),
        compiler_params=pltpu.CompilerParams(vmem_limit_bytes=VMEM_LIMIT),
        name="core_sum",
    )(keep, arrived)


def plane_sum_kernel(*refs):
    word, char, near_ref, far_ref = (refs[:4], refs[4:8], refs[8], refs[9])
    rows = word[0].shape[0]

    def total(parts, pick):
        return functools.reduce(lambda a, b: a + b, [pick(part).astype(f32) for part in parts])

    near_ref[:rows] = total(word, lambda r: r[...]).astype(bf16)
    near_ref[rows:] = total(char, lambda r: r[0]).astype(bf16)
    far_ref[...] = total(char, lambda r: r[1]).astype(bf16)


def plane_sum(word, char):
    rows = word[0].shape[0] + char[0].shape[1]
    return pl.pallas_call(
        plane_sum_kernel,
        out_shape=[
            jax.ShapeDtypeStruct((rows, SLAB), bf16),
            jax.ShapeDtypeStruct(char[0].shape[1:], bf16),
        ],
        compiler_params=pltpu.CompilerParams(vmem_limit_bytes=VMEM_LIMIT),
        name="plane_sum",
    )(*word, *char)


def last_sum_kernel(shapes, where_ref, near_ref, section_ref, high_ref, both_ref, *outs):
    word_rows = WORD_SLOT
    section = where_ref[0]
    me = where_ref[2]
    own = near_ref[:word_rows].astype(f32)
    other = section_ref[:word_rows].astype(f32)
    halves = (jnp.where(section == 0, own, other), jnp.where(section == 0, other, own))
    char = (
        near_ref[word_rows:].astype(f32)
        + section_ref[word_rows:].astype(f32)
        + high_ref[...].astype(f32)
        + both_ref[...].astype(f32)
    )

    def mine(vector, size):
        turned = pltpu.roll(vector, lax.rem(SLAB - lax.rem(me * size, SLAB), SLAB), 1)
        return turned[:, :size]

    (
        table_ref,
        gain_attn_ref,
        project_ref,
        output_ref,
        gain_mlp_ref,
        expand_ref,
        shrink_ref,
        w_input_ref,
        w_gain_attn_ref,
        w_project_ref,
        w_output_ref,
        w_gain_mlp_ref,
        w_expand_ref,
        w_shrink_ref,
    ) = outs
    at = 0
    for ref in (project_ref, output_ref, expand_ref, shrink_ref):
        size = ref.shape[0]
        for column in range(ref.shape[1] // SLAB):
            ref[:, column * SLAB : (column + 1) * SLAB] = char[at : at + size]
            at += size
    size = gain_attn_ref.shape[1]
    extra = char[at : at + 16]
    turned = mine(extra, size)
    gain_attn_ref[...] = turned[0:1]
    gain_mlp_ref[...] = turned[1:2]
    table_ref[...] = turned[8:16]
    at = 0
    for ref in (w_input_ref, w_project_ref, w_output_ref, w_expand_ref, w_shrink_ref):
        size = ref.shape[0]
        columns = ref.shape[1] // (2 * SLAB)
        for column in range(columns):
            for half in range(2):
                first = (half * columns + column) * SLAB
                ref[:, first : first + SLAB] = halves[half][at : at + size]
            at += size
    size = w_gain_attn_ref.shape[1]
    extra = own[at : at + 8]
    turned = mine(extra, size)
    upper = me * size >= SLAB
    w_gain_attn_ref[...] = jnp.where(upper, turned[1:2], turned[0:1])
    w_gain_mlp_ref[...] = jnp.where(upper, turned[3:4], turned[2:3])


def last_sum(where, near, arrived, shapes):
    vmem = pl.BlockSpec(memory_space=pltpu.VMEM)
    return pl.pallas_call(
        functools.partial(last_sum_kernel, shapes),
        in_specs=[pl.BlockSpec(memory_space=pltpu.SMEM)] + [vmem] * 4,
        out_specs=[vmem] * len(shapes),
        out_shape=[jax.ShapeDtypeStruct(shape, f32) for shape in shapes],
        compiler_params=pltpu.CompilerParams(vmem_limit_bytes=VMEM_LIMIT),
        name="last_sum",
    )(where, near, *arrived)


def exchange(value, section_bit, dp_bits):
    shards = lax.axis_size("dp")
    pairs = [
        (s * shards + d, (s ^ section_bit) * shards + (d ^ dp_bits))
        for s in range(lax.axis_size("section"))
        for d in range(shards)
    ]
    return lax.ppermute(value, ("section", "dp"), pairs)


CORE, SIDE, NEAR, FAR = (1, 2, 4, 8)


def local_grouped(
    chars, counts, languages, language_table, char_weights, word_input, word_weights, cotangent
):
    section = lax.axis_index("section")
    me = lax.axis_index("dp")
    shards = lax.axis_size("dp")
    micros, _, words, slots, width = chars.shape
    rows = words * slots
    where = jnp.stack([section, languages[section, 0], me]).astype(jnp.int32)
    cot = cotangent[:, 0]
    cot_core = exchange(cot, 0, CORE)
    cot_high = exchange(jnp.stack([cot, cot_core]), 0, FAR)
    char_weights = tuple(w[None] if w.ndim == 1 else w for w in char_weights)
    word_weights = tuple(w[None] if w.ndim == 1 else w for w in word_weights)
    chars = chars.reshape(micros, rows, width)
    counts = counts.reshape(micros, 1, words)
    pooled, *stored = char_forward(where, chars, counts, language_table, char_weights, slots)
    pooled_core = exchange(pooled, 0, CORE)
    pair = jnp.concatenate([pooled, pooled_core])
    others = (exchange(pair, 0, FAR), exchange(pair, 1, 0), exchange(pair, 1, FAR))
    result, dpooled, *pieces = word_group(
        where,
        (pooled, pooled_core) + others,
        (cot, cot_core, cot_high),
        word_input,
        word_weights,
        shards,
    )
    word = (pieces[0],) + tuple(
        exchange(piece, 0, bits) for piece, bits in zip(pieces[1:], (SIDE, NEAR, SIDE | NEAR))
    )
    chars_grad, keep, send = char_backward(
        where, chars, counts, language_table, char_weights, dpooled, stored, slots, shards
    )
    pieces = core_sum(keep, exchange(send, 0, CORE))
    char = (pieces[0],) + tuple(
        exchange(piece, 0, bits) for piece, bits in zip(pieces[1:], (SIDE, NEAR, SIDE | NEAR))
    )
    near, far = plane_sum(word, char)
    arrived = (exchange(near, 1, 0), exchange(far, 0, FAR), exchange(far, 1, FAR))
    shapes = [(language_table.shape[0], language_table.shape[1] // shards)]
    for weight in char_weights + (word_input,) + word_weights:
        if weight.shape[0] == 1:
            shapes.append((1, weight.shape[1] // shards))
        else:
            shapes.append((weight.shape[0] // shards, weight.shape[1]))
    totals = last_sum(where, near, arrived, shapes)
    totals = [total[0] if total.shape[0] == 1 else total for total in totals]
    return (result[None, None], chars_grad.reshape((1, 1, words, slots, width))) + tuple(totals)


def norm_forward(inputs, gain):
    return inputs * lax.rsqrt(jnp.mean(inputs * inputs, axis=-1, keepdims=True) + eps) * gain


def attend_forward(normed, project, head_count, key_mask):
    row_count, length, channels = normed.shape
    head_size = channels // head_count
    qkv = jnp.einsum("blc,cf->blf", normed, project, preferred_element_type=jnp.float32).astype(
        jnp.bfloat16
    )
    pieces = qkv.reshape(row_count, length, 3, head_count, head_size)
    scores = jnp.einsum(
        "bqhd,bkhd->bhqk", pieces[:, :, 0], pieces[:, :, 1], preferred_element_type=jnp.float32
    ) * head_size ** (-0.5)
    scores = jnp.where(key_mask, scores, -1e30)
    row_max = jnp.max(scores, axis=-1, keepdims=True)
    weights_exp = jnp.exp(scores - row_max)
    row_total = jnp.sum(weights_exp, axis=-1, keepdims=True)
    attn_probs = (weights_exp / row_total).astype(jnp.bfloat16)
    mixed_heads = jnp.einsum(
        "bhqk,bkhd->bqhd", attn_probs, pieces[:, :, 2], preferred_element_type=jnp.float32
    )
    mixed_heads = mixed_heads.reshape(row_count, length, channels).astype(jnp.bfloat16)
    return (qkv, row_max + jnp.log(row_total), mixed_heads)


def attend_backward(
    normed, project, output, qkv, logsum, mixed_heads, dmiddle_low, head_count, key_mask
):
    row_count, length, channels = normed.shape
    head_size = channels // head_count
    scaling = head_size ** (-0.5)
    output_grad = jnp.einsum(
        "blc,bld->cd", mixed_heads, dmiddle_low, preferred_element_type=jnp.float32
    )
    dmixed = jnp.einsum(
        "bld,cd->blc", dmiddle_low, output, preferred_element_type=jnp.float32
    ).astype(jnp.bfloat16)
    dmixed = dmixed.reshape(row_count, length, head_count, head_size)
    pieces = qkv.reshape(row_count, length, 3, head_count, head_size)
    scores = (
        jnp.einsum(
            "bqhd,bkhd->bhqk", pieces[:, :, 0], pieces[:, :, 1], preferred_element_type=jnp.float32
        )
        * scaling
    )
    scores = jnp.where(key_mask, scores, -1e30)
    attn_probs = jnp.exp(scores - logsum)
    dprobs = jnp.einsum(
        "bqhd,bkhd->bhqk", dmixed, pieces[:, :, 2], preferred_element_type=jnp.float32
    )
    row_delta = jnp.sum(attn_probs * dprobs, axis=-1, keepdims=True)
    dscores = (attn_probs * (dprobs - row_delta)).astype(jnp.bfloat16)
    dquery = (
        jnp.einsum("bhqk,bkhd->bqhd", dscores, pieces[:, :, 1], preferred_element_type=jnp.float32)
        * scaling
    )
    dkeys = (
        jnp.einsum("bhqk,bqhd->bkhd", dscores, pieces[:, :, 0], preferred_element_type=jnp.float32)
        * scaling
    )
    dvalues = jnp.einsum(
        "bhqk,bqhd->bkhd",
        attn_probs.astype(jnp.bfloat16),
        dmixed,
        preferred_element_type=jnp.float32,
    )
    dqkv = (
        jnp.stack([dquery, dkeys, dvalues], axis=2)
        .reshape(row_count, length, 3 * channels)
        .astype(jnp.bfloat16)
    )
    project_grad = jnp.einsum("blc,blf->cf", normed, dqkv, preferred_element_type=jnp.float32)
    dnormed = jnp.einsum("blf,cf->blc", dqkv, project, preferred_element_type=jnp.float32)
    return (dnormed, project_grad, output_grad)


def block_forward(inputs, weights, head_count, key_mask):
    gain_attn, project, output, gain_mlp, expand, shrink = weights
    normed = norm_forward(inputs, gain_attn).astype(jnp.bfloat16)
    qkv, logsum, mixed_heads = attend_forward(normed, project, head_count, key_mask)
    middle = inputs + jnp.einsum(
        "blc,cd->bld", mixed_heads, output, preferred_element_type=jnp.float32
    )
    normed_mlp = norm_forward(middle, gain_mlp).astype(jnp.bfloat16)
    before = jnp.einsum("blc,cf->blf", normed_mlp, expand, preferred_element_type=jnp.float32)
    hidden = jax.nn.gelu(before).astype(jnp.bfloat16)
    result = middle + jnp.einsum("blf,fc->blc", hidden, shrink, preferred_element_type=jnp.float32)
    return (result, (inputs, normed, qkv, logsum, mixed_heads, middle, normed_mlp, before, hidden))


def block_backward(dresult, stored, weights, head_count, key_mask):
    gain_attn, project, output, gain_mlp, expand, shrink = weights
    inputs, normed, qkv, logsum, mixed_heads, middle, normed_mlp, before, hidden = stored
    grad_low = dresult.astype(jnp.bfloat16)
    shrink_grad = jnp.einsum("blf,blc->fc", hidden, grad_low, preferred_element_type=jnp.float32)
    dhidden = jnp.einsum(
        "blc,fc->blf", grad_low, shrink, preferred_element_type=jnp.float32
    ).astype(jnp.bfloat16)
    gelu_pull = jax.vjp(jax.nn.gelu, before)[1]
    dbefore = gelu_pull(dhidden.astype(jnp.float32))[0].astype(jnp.bfloat16)
    expand_grad = jnp.einsum("blc,blf->cf", normed_mlp, dbefore, preferred_element_type=jnp.float32)
    dnormed_mlp = jnp.einsum("blf,cf->blc", dbefore, expand, preferred_element_type=jnp.float32)
    norm_pull = jax.vjp(norm_forward, middle, gain_mlp)[1]
    dmiddle_norm, gain_mlp_grad = norm_pull(dnormed_mlp)
    dmiddle = dresult + dmiddle_norm
    dnormed, project_grad, output_grad = attend_backward(
        normed,
        project,
        output,
        qkv,
        logsum,
        mixed_heads,
        dmiddle.astype(jnp.bfloat16),
        head_count,
        key_mask,
    )
    first_pull = jax.vjp(norm_forward, inputs, gain_attn)[1]
    dinputs_norm, gain_attn_grad = first_pull(dnormed)
    return (
        dmiddle + dinputs_norm,
        (gain_attn_grad, project_grad, output_grad, gain_mlp_grad, expand_grad, shrink_grad),
    )


def char_front(char_text, char_count, language, lang_table, weights):
    present = lax.broadcasted_iota(jnp.int32, char_text.shape[:2], 1) < char_count[:, None]
    onehot = (lax.broadcasted_iota(jnp.int32, (lang_table.shape[0],), 0) == language).astype(
        jnp.bfloat16
    )
    lang_row = jnp.dot(onehot, lang_table, preferred_element_type=jnp.float32)
    inputs = char_text.astype(jnp.float32) + lang_row
    result, stored = block_forward(inputs, weights, CH, present[:, None, None, :])
    summed = jnp.sum(jnp.where(present[:, :, None], result, 0.0), axis=1)
    pooled = (summed / char_count[:, None].astype(jnp.float32)).astype(jnp.bfloat16)
    return (pooled, stored, present, onehot)


def char_back(stored, present, onehot, char_count, dpooled, weights):
    spread = dpooled.astype(jnp.float32) / char_count[:, None].astype(jnp.float32)
    dresult = jnp.where(present[:, :, None], spread[:, None, :], 0.0)
    dinputs, gradients = block_backward(dresult, stored, weights, CH, present[:, None, None, :])
    table_grad = onehot.astype(jnp.float32)[:, None] * jnp.sum(dinputs, axis=(0, 1))[None, :]
    return (dinputs, (table_grad,) + gradients)


def word_full(pooled, cot_rows, word_input, weights):
    length = pooled.shape[0]
    word_start = jnp.dot(pooled, word_input, preferred_element_type=jnp.float32)[None]
    causal = (
        lax.broadcasted_iota(jnp.int32, (length, length), 0)
        >= lax.broadcasted_iota(jnp.int32, (length, length), 1)
    )[None, None]
    result, stored = block_forward(word_start, weights, H, causal)
    dstart, gradients = block_backward(
        cot_rows.astype(jnp.float32)[None], stored, weights, H, causal
    )
    grad_low = dstart[0].astype(jnp.bfloat16)
    input_grad = jnp.einsum("wc,wd->cd", pooled, grad_low, preferred_element_type=jnp.float32)
    dpooled = jnp.einsum(
        "wd,cd->wc", grad_low, word_input, preferred_element_type=jnp.float32
    ).astype(jnp.bfloat16)
    return (result[0], dpooled, (input_grad,) + gradients)


def reduce_rows(gradients):
    shards = lax.axis_size("dp")
    flat = []
    for place, gradient in enumerate(gradients):
        if place == 0:
            gradient = gradient.T
        flat.append(gradient.astype(jnp.bfloat16).reshape(shards, -1))
    packed = jnp.concatenate(flat, axis=1)
    me = lax.axis_index("dp")
    packed = jnp.take(packed, jnp.arange(shards) ^ me, axis=0)
    bit = 1
    while packed.shape[0] > 1:
        pairs = packed.reshape(packed.shape[0] // 2, 2, packed.shape[1])
        arrived = lax.ppermute(pairs[:, 1], "dp", [(i, i ^ bit) for i in range(shards)])
        packed = (pairs[:, 0].astype(jnp.float32) + arrived.astype(jnp.float32)).astype(
            jnp.bfloat16
        )
        bit *= 2
    arrived = lax.ppermute(packed, "section", [(0, 1), (1, 0)])
    total = (packed.astype(jnp.float32) + arrived.astype(jnp.float32))[0]
    outs = []
    at = 0
    for place, gradient in enumerate(gradients):
        size = gradient.size // shards
        piece = total[at : at + size]
        at += size
        if place == 0:
            outs.append(piece.reshape(-1, gradient.shape[0]).T)
        else:
            outs.append(piece.reshape((gradient.shape[0] // shards,) + gradient.shape[1:]))
    return tuple(outs)


def local(
    chars,
    counts,
    languages,
    language_table,
    char_gain_attn,
    char_project,
    char_output,
    char_gain_mlp,
    char_expand,
    char_shrink,
    word_input,
    word_gain_attn,
    word_project,
    word_output,
    word_gain_mlp,
    word_expand,
    word_shrink,
    cotangent,
):
    char_weights = (
        char_gain_attn,
        char_project,
        char_output,
        char_gain_mlp,
        char_expand,
        char_shrink,
    )
    word_weights = (
        word_gain_attn,
        word_project,
        word_output,
        word_gain_mlp,
        word_expand,
        word_shrink,
    )
    if lax.axis_size("dp") == 16:
        return local_grouped(
            chars,
            counts,
            languages,
            language_table,
            char_weights,
            word_input,
            word_weights,
            cotangent,
        )
    section_index = lax.axis_index("section")
    char_text = chars[section_index, 0]
    char_count = counts[section_index, 0]
    language = languages[section_index, 0]
    cot_rows = cotangent[section_index, 0]
    pooled, stored, present, onehot = char_front(
        char_text, char_count, language, language_table, char_weights
    )
    result, dpooled, word_grads = word_full(pooled, cot_rows, word_input, word_weights)
    text_grad, char_grads = char_back(stored, present, onehot, char_count, dpooled, char_weights)
    totals = reduce_rows(char_grads + word_grads)
    return (result[None, None], text_grad[None, None]) + totals


def solution(mesh):
    placed = (
        P(None, "dp", None, None, None),
        P(None, "dp", None),
        P(None, "dp"),
        P(),
        P(),
        P(),
        P(),
        P(),
        P(),
        P(),
        P(),
        P(),
        P(),
        P(),
        P(),
        P(),
        P(),
        P(None, "dp", None, None),
    )
    return jax.shard_map(
        local,
        mesh=mesh,
        in_specs=placed,
        out_specs=(
            P("section", "dp", None, None),
            P("section", "dp", None, None, None),
            P(None, "dp"),
            P("dp"),
            P("dp", None),
            P("dp", None),
            P("dp"),
            P("dp", None),
            P("dp", None),
            P("dp", None),
            P("dp"),
            P("dp", None),
            P("dp", None),
            P("dp"),
            P("dp", None),
            P("dp", None),
        ),
        check_vma=False,
    )
```

```python
import functools

import jax
import jax.numpy as jnp
from jax import lax
from jax.experimental import pallas as pl
from jax.experimental.pallas import tpu as pltpu
from jax.sharding import PartitionSpec as P

CH = 4
H = 8
HEAD = 64
SLAB = 256
BLOCK = 128
MIB = 1024 * 1024

eps = 1e-05

f32 = jnp.float32
bf16 = jnp.bfloat16


def dot(a, b):
    return jnp.dot(a, b, preferred_element_type=f32)


def dot_nt(a, b):
    return lax.dot_general(a, b, (((1,), (1,)), ((), ())), preferred_element_type=f32)


def position():
    return (lax.axis_index("section"), lax.axis_index("dp"))


def lanes(shape):
    return lax.broadcasted_iota(jnp.int32, shape, 1)


def rows_of(shape):
    return lax.broadcasted_iota(jnp.int32, shape, 0)


def flip(a):
    size = a.shape[1]
    width = min(size, 256)
    eye = jnp.where(rows_of((width, width)) == lanes((width, width)), 1.0, 0.0).astype(bf16)
    return jnp.concatenate(
        [dot_nt(eye, a[:, at : at + width]).astype(bf16) for at in range(0, size, width)], axis=0
    )


def head_mask(head):
    return jnp.where(lanes((1, SLAB)) // HEAD == head, 1.0, 0.0).astype(bf16)


def stack_heads(a):
    return jnp.concatenate([a * head_mask(head) for head in range(SLAB // HEAD)], axis=0)


def merge_heads(a):
    rows = a.shape[0] // (SLAB // HEAD)
    head = lanes((rows, SLAB)) // HEAD
    total = a[:rows]
    for place in range(1, SLAB // HEAD):
        total = jnp.where(head == place, a[place * rows : (place + 1) * rows], total)
    return total


def compact(scores, length):
    group = lanes((length, BLOCK)) // length
    total = scores[:length]
    for place in range(1, BLOCK // length):
        total = jnp.where(group == place, scores[place * length : (place + 1) * length], total)
    return total


def expand(values, length):
    group = lanes((length, BLOCK)) // length
    return jnp.concatenate(
        [jnp.where(group == place, values, 0.0) for place in range(BLOCK // length)], axis=0
    ).astype(bf16)


def attend(q, k, v, key_mask, length):
    heads = SLAB // HEAD
    scores = dot_nt(stack_heads(k), q)
    v_flipped = flip(v)
    kept = []
    mixed = []
    for head in range(heads):
        piece = compact(scores[head * BLOCK : (head + 1) * BLOCK], length) * HEAD**-0.5
        piece = jnp.where(key_mask, piece, -1e30)
        weights = jnp.exp(piece - jnp.max(piece, axis=0, keepdims=True))
        probs = weights / jnp.sum(weights, axis=0, keepdims=True)
        kept.append(probs)
        mixed.append(dot(v_flipped[head * HEAD : (head + 1) * HEAD], expand(probs, length)))
    return (kept, jnp.concatenate(mixed, axis=0).astype(bf16))


def attend_back(q, k, v, probs, dmixed, length):
    heads = SLAB // HEAD
    dprobs = dot_nt(stack_heads(v), dmixed)
    k_flipped = flip(k)
    dq = []
    dk = []
    dv = []
    for head in range(heads):
        own = probs[head]
        piece = compact(dprobs[head * BLOCK : (head + 1) * BLOCK], length)
        delta = jnp.sum(own * piece, axis=0, keepdims=True)
        dscores = expand(own * (piece - delta), length)
        dq.append(dot(k_flipped[head * HEAD : (head + 1) * HEAD], dscores))
        dk.append(dot(dscores, q))
        dv.append(dot(expand(own, length), dmixed))
    scaling = HEAD**-0.5
    dq = flip((jnp.concatenate(dq, axis=0) * scaling).astype(bf16))
    dk = (merge_heads(jnp.concatenate(dk, axis=0)) * scaling).astype(bf16)
    dv = merge_heads(jnp.concatenate(dv, axis=0)).astype(bf16)
    return (dq, dk, dv)


def unit(x):
    scale = lax.rsqrt(jnp.mean(x * x, axis=-1, keepdims=True) + eps)
    return (x * scale, scale)


def unit_back(dnormed, gain, normal, scale):
    weighted = dnormed * gain
    return scale * (weighted - normal * jnp.mean(normal * weighted, axis=-1, keepdims=True))


def gelu_parts(before):
    c = 0.7978845608028654
    square = before * before
    half = 0.5 * jnp.tanh(before * (c + (c * 0.044715) * square)) + 0.5
    value = before * half
    slope = half + value * (1.0 - half) * (2.0 * c + (6.0 * c * 0.044715) * square)
    return (value, slope)


def char_rows(chars, table_ref, language):
    table = table_ref[...].astype(f32)
    row = jnp.sum(jnp.where(rows_of(table.shape) == language, table, 0.0), axis=0, keepdims=True)
    return chars.astype(f32) + row


def counts_by_row(counts, rows, slots):
    words = counts.shape[-1]
    counts = jnp.broadcast_to(counts.astype(f32), (8, words)).astype(bf16)
    shape = (words, rows)
    member = lanes(shape) // slots == rows_of(shape)
    return dot(counts, jnp.where(member, 1.0, 0.0).astype(bf16))[:1]


def counts_column(counts):
    words = counts.shape[-1]
    shape = (words, words)
    spread = jnp.broadcast_to(counts.astype(f32), shape)
    return jnp.sum(
        jnp.where(rows_of(shape) == lanes(shape), spread, 0.0), axis=1, keepdims=True
    )


def fetch_all(sources, targets, sems):
    fetches = [
        pltpu.make_async_copy(source, target, sems.at[place])
        for place, (source, target) in enumerate(zip(sources, targets))
    ]
    for fetch in fetches:
        fetch.start()
    return fetches


def in_hbm(array):
    return pltpu.with_memory_space_constraint(array, pltpu.HBM)


def char_forward_kernel(
    slots,
    languages_ref,
    chars_hbm,
    counts_hbm,
    table_hbm,
    gain_attn_hbm,
    project_hbm,
    output_hbm,
    gain_mlp_hbm,
    expand_hbm,
    shrink_hbm,
    pooled_ref,
    hidden_sum_ref,
    qkv_ref,
    probs_ref,
    mixed_ref,
    middle_ref,
    slope_ref,
    chars_ref,
    counts_ref,
    table_ref,
    gain_attn_ref,
    project_ref,
    output_ref,
    gain_mlp_ref,
    expand_ref,
    shrink_ref,
    sems,
):
    section, _ = position()
    fetches = fetch_all(
        (
            counts_hbm,
            table_hbm,
            gain_attn_hbm,
            chars_hbm.at[section],
            project_hbm,
            output_hbm,
            gain_mlp_hbm,
            expand_hbm,
            shrink_hbm,
        ),
        (
            counts_ref,
            table_ref,
            gain_attn_ref,
            chars_ref,
            project_ref,
            output_ref,
            gain_mlp_ref,
            expand_ref,
            shrink_ref,
        ),
        sems,
    )
    fetches[0].wait()
    counts = counts_ref[section]
    rows = chars_ref.shape[0]
    words = counts.shape[-1]
    row_counts = counts_by_row(counts, rows, slots)
    for fetch in fetches[1:4]:
        fetch.wait()
    x = char_rows(chars_ref[...], table_ref, languages_ref[section, 0])
    normal, _ = unit(x)
    normed = (normal * gain_attn_ref[...]).astype(bf16)
    fetches[4].wait()
    qkv_ref[...] = dot(normed, project_ref[...]).astype(bf16)
    mixed = []
    for block in range(rows // BLOCK):
        part = slice(block * BLOCK, (block + 1) * BLOCK)
        key_mask = rows_of((slots, BLOCK)).astype(f32) < row_counts[:, part]
        probs, piece = attend(
            qkv_ref[part, :SLAB],
            qkv_ref[part, SLAB : 2 * SLAB],
            qkv_ref[part, 2 * SLAB :],
            key_mask,
            slots,
        )
        for head in range(CH):
            probs_ref[head * slots : (head + 1) * slots, part] = probs[head]
        mixed_ref[:, part] = piece
        mixed.append(flip(piece))
    mixed = jnp.concatenate(mixed, axis=0)
    fetches[5].wait()
    middle = x + dot(mixed, output_ref[...])
    middle_ref[...] = middle
    normal, _ = unit(middle)
    fetches[6].wait()
    normed = (normal * gain_mlp_ref[...]).astype(bf16)
    word_shape = (words, rows)
    lane = lanes(word_shape)
    member = (lane // slots == rows_of(word_shape)) & ((lane % slots).astype(f32) < row_counts)
    member = jnp.where(member, 1.0, 0.0).astype(bf16)
    fetches[7].wait()
    for at in range(0, expand_ref.shape[1], 256):
        part = slice(at, at + 256)
        value, slope = gelu_parts(dot(normed, expand_ref[:, part]))
        slope_ref[:, part] = slope.astype(bf16)
        hidden_sum_ref[:, part] = dot(member, value.astype(bf16)).astype(bf16)
    high = middle.astype(bf16)
    low = (middle - high.astype(f32)).astype(bf16)
    fetches[8].wait()
    total = dot(member, high) + dot(member, low) + dot(hidden_sum_ref[...], shrink_ref[...])
    pooled_ref[...] = (total / counts_column(counts)).astype(bf16)


def char_forward(languages, chars, counts, table, weights, slots):
    rows, width = chars.shape[1:]
    words = rows // slots
    hidden = weights[4].shape[1]
    vmem = pl.BlockSpec(memory_space=pltpu.VMEM)
    hbm = pl.BlockSpec(memory_space=pltpu.HBM)
    fetched = (counts, table) + tuple(weights)
    return pl.pallas_call(
        functools.partial(char_forward_kernel, slots),
        in_specs=[pl.BlockSpec(memory_space=pltpu.SMEM)] + [hbm] * 9,
        out_specs=[vmem] * 7,
        out_shape=[
            jax.ShapeDtypeStruct((words, width), bf16),
            jax.ShapeDtypeStruct((words, hidden), bf16),
            jax.ShapeDtypeStruct((rows, 3 * width), bf16),
            jax.ShapeDtypeStruct((CH * slots, rows), f32),
            jax.ShapeDtypeStruct((width, rows), bf16),
            jax.ShapeDtypeStruct((rows, width), f32),
            jax.ShapeDtypeStruct((rows, hidden), bf16),
        ],
        scratch_shapes=[pltpu.VMEM(chars.shape[1:], bf16)]
        + [pltpu.VMEM(array.shape, array.dtype) for array in fetched]
        + [pltpu.SemaphoreType.DMA((9,))],
        compiler_params=pltpu.CompilerParams(vmem_limit_bytes=16 * MIB),
        cost_estimate=pl.CostEstimate(
            flops=64 * rows * width * width, bytes_accessed=8 * MIB, transcendentals=0
        ),
        name="char_forward",
    )(languages, *[in_hbm(array) for array in (chars,) + fetched])


CHAR_MLP_SLOT = 128
CHAR_ATTN_SLOT = 80


def char_slot(shard, me):
    other = shard ^ me
    return (other & 1) * 8 + ((other >> 1) & 3) * 2 + (other >> 3)


def put_char(packed, me, shards, gradient, at):
    size = gradient.shape[0] // shards
    for shard in range(shards):
        piece = gradient[shard * size : (shard + 1) * size].astype(bf16)
        for column in range(gradient.shape[1] // SLAB):
            start = at + column * size
            packed[char_slot(shard, me), start : start + size] = piece[
                :, column * SLAB : (column + 1) * SLAB
            ]
    return at + size * (gradient.shape[1] // SLAB)


def hand_out(packed, keep_ref, send_ref, sems):
    half = packed.shape[0] // 2
    copies = [
        pltpu.make_async_copy(packed.at[pl.ds(half, half)], send_ref, sems.at[0]),
        pltpu.make_async_copy(packed.at[pl.ds(0, half)], keep_ref, sems.at[1]),
    ]
    for copy in copies:
        copy.start()
    for copy in copies:
        copy.wait()


def char_mlp_back_kernel(
    slots,
    shards,
    counts_hbm,
    gain_mlp_ref,
    expand_ref,
    shrink_ref,
    dpooled_ref,
    hidden_sum_ref,
    middle_ref,
    slope_ref,
    dmiddle_ref,
    gain_ref,
    keep_ref,
    send_ref,
    counts_ref,
    dhidden_words,
    dbefore,
    packed,
    sems,
):
    section, me = position()
    fetch = pltpu.make_async_copy(counts_hbm, counts_ref, sems.at[2])
    fetch.start()
    fetch.wait()
    counts = counts_ref[section]
    rows, width = middle_ref.shape
    words = counts.shape[-1]
    spread = dpooled_ref[...].astype(f32) / counts_column(counts)
    spread_high = spread.astype(bf16)
    spread_low = (spread - spread_high.astype(f32)).astype(bf16)
    dhidden_words[...] = dot_nt(spread_high, shrink_ref[...]).astype(bf16)
    shape = (rows, words)
    row = rows_of(shape)
    member = (row // slots == lanes(shape)) & (row % slots < counts)
    member = jnp.where(member, 1.0, 0.0).astype(bf16)
    for at in range(0, expand_ref.shape[1], 256):
        part = slice(at, at + 256)
        dbefore[:, part] = dot(member, dhidden_words[:, part]).astype(bf16) * slope_ref[:, part]
    dnormed = dot_nt(dbefore[...], expand_ref[...])
    normal, scale = unit(middle_ref[...])
    normed_mlp_t = flip((normal * gain_mlp_ref[...]).astype(bf16))
    gain_ref[...] = jnp.broadcast_to(
        jnp.sum(dnormed * normal, axis=0, keepdims=True), gain_ref.shape
    )
    dmiddle_ref[...] = (
        dot(member, spread_high)
        + dot(member, spread_low)
        + unit_back(dnormed, gain_mlp_ref[...], normal, scale)
    )
    at = put_char(packed, me, shards, dot(normed_mlp_t, dbefore[...]), 0)
    put_char(packed, me, shards, dot(flip(hidden_sum_ref[...]), spread_high), at)
    hand_out(packed, keep_ref, send_ref, sems)


def char_mlp_back(counts, weights, dpooled, stored, slots, shards):
    _, _, _, gain_mlp, expand_w, shrink = weights
    hidden_sum, _, _, _, middle, slope = stored
    rows, width = middle.shape
    words = rows // slots
    hidden = expand_w.shape[1]
    half = (shards // 2, CHAR_MLP_SLOT, width)
    vmem = pl.BlockSpec(memory_space=pltpu.VMEM)
    hbm = pl.BlockSpec(memory_space=pltpu.HBM)
    return pl.pallas_call(
        functools.partial(char_mlp_back_kernel, slots, shards),
        in_specs=[hbm] + [vmem] * 7,
        out_specs=[vmem, vmem, hbm, hbm],
        out_shape=[
            jax.ShapeDtypeStruct((rows, width), f32),
            jax.ShapeDtypeStruct((8, width), f32),
            jax.ShapeDtypeStruct(half, bf16),
            jax.ShapeDtypeStruct(half, bf16),
        ],
        scratch_shapes=[
            pltpu.VMEM(counts.shape, counts.dtype),
            pltpu.VMEM((words, hidden), bf16),
            pltpu.VMEM((rows, hidden), bf16),
            pltpu.VMEM((shards, CHAR_MLP_SLOT, width), bf16),
            pltpu.SemaphoreType.DMA((3,)),
        ],
        compiler_params=pltpu.CompilerParams(vmem_limit_bytes=16 * MIB),
        cost_estimate=pl.CostEstimate(
            flops=64 * rows * width * width, bytes_accessed=8 * MIB, transcendentals=0
        ),
        name="char_mlp_back",
    )(in_hbm(counts), gain_mlp, expand_w, shrink, dpooled, hidden_sum, middle, slope)


def char_attn_back_kernel(
    slots,
    shards,
    languages_ref,
    _,
    chars_hbm,
    table_ref,
    gain_attn_ref,
    project_ref,
    output_ref,
    dmiddle_ref,
    gain_mlp_grad_ref,
    qkv_ref,
    probs_ref,
    mixed_ref,
    grad_ref,
    keep_ref,
    send_ref,
    chars_ref,
    dqkv,
    packed,
    sems,
):
    section, me = position()
    fetch = pltpu.make_async_copy(chars_hbm.at[section], chars_ref, sems.at[2])
    fetch.start()
    rows, width = dmiddle_ref.shape
    language = languages_ref[section, 0]
    dy = dmiddle_ref[...].astype(bf16)
    dmixed = dot_nt(dy, output_ref[...]).astype(bf16)
    for block in range(rows // BLOCK):
        part = slice(block * BLOCK, (block + 1) * BLOCK)
        probs = [probs_ref[head * slots : (head + 1) * slots, part] for head in range(CH)]
        pieces = attend_back(
            qkv_ref[part, :SLAB],
            qkv_ref[part, SLAB : 2 * SLAB],
            qkv_ref[part, 2 * SLAB :],
            probs,
            dmixed[part],
            slots,
        )
        for number in range(3):
            dqkv[part, number * SLAB : (number + 1) * SLAB] = pieces[number]
    dnormed = dot_nt(dqkv[...], project_ref[...])
    fetch.wait()
    normal, scale = unit(char_rows(chars_ref[...], table_ref, language))
    normed_t = flip((normal * gain_attn_ref[...]).astype(bf16))
    gain_attn_grad = jnp.sum(dnormed * normal, axis=0, keepdims=True)
    dx = dmiddle_ref[...] + unit_back(dnormed, gain_attn_ref[...], normal, scale)
    grad_ref[...] = dx
    row_sum = jnp.sum(dx, axis=0, keepdims=True)
    at = put_char(packed, me, shards, dot(normed_t, dqkv[...]), 0)
    at = put_char(packed, me, shards, dot(mixed_ref[...], dy), at)
    extra = jnp.concatenate(
        [
            gain_attn_grad,
            gain_mlp_grad_ref[:7],
            jnp.where(rows_of((8, 1)) == language, row_sum, 0.0),
        ],
        axis=0,
    ).astype(bf16)
    for shard in range(shards):
        packed[shard, at : at + 16] = extra
    hand_out(packed, keep_ref, send_ref, sems)


def char_attn_back(
    languages, chars, table, weights, dmiddle, gain_mlp_grad, stored, slots, shards, after
):
    gain_attn, project, output, _, _, _ = weights
    _, qkv, probs, mixed, _, _ = stored
    rows, width = dmiddle.shape
    half = (shards // 2, CHAR_ATTN_SLOT, width)
    vmem = pl.BlockSpec(memory_space=pltpu.VMEM)
    hbm = pl.BlockSpec(memory_space=pltpu.HBM)
    return pl.pallas_call(
        functools.partial(char_attn_back_kernel, slots, shards),
        in_specs=[pl.BlockSpec(memory_space=pltpu.SMEM), pl.BlockSpec(memory_space=pl.ANY), hbm]
        + [vmem] * 9,
        out_specs=[vmem, hbm, hbm],
        out_shape=[
            jax.ShapeDtypeStruct((rows, width), f32),
            jax.ShapeDtypeStruct(half, bf16),
            jax.ShapeDtypeStruct(half, bf16),
        ],
        scratch_shapes=[
            pltpu.VMEM((rows, width), bf16),
            pltpu.VMEM((rows, 3 * width), bf16),
            pltpu.VMEM((shards, CHAR_ATTN_SLOT, width), bf16),
            pltpu.SemaphoreType.DMA((3,)),
        ],
        compiler_params=pltpu.CompilerParams(vmem_limit_bytes=16 * MIB),
        cost_estimate=pl.CostEstimate(
            flops=64 * rows * width * width, bytes_accessed=8 * MIB, transcendentals=0
        ),
        name="char_attn_back",
    )(
        languages,
        after,
        in_hbm(chars),
        table,
        gain_attn,
        project,
        output,
        dmiddle,
        gain_mlp_grad,
        qkv,
        probs,
        mixed,
    )


WORD_SLOT = 416


def word_kernel(
    length,
    shards,
    own_ref,
    far_ref,
    section_ref,
    both_ref,
    cot_ref,
    cot_far_ref,
    input_ref,
    gain_attn_ref,
    project_ref,
    output_ref,
    gain_mlp_ref,
    expand_ref,
    shrink_ref,
    result_ref,
    dpooled_ref,
    keep_ref,
    send_ref,
    pooled,
    dz,
    start,
    normed,
    normed_t,
    qkv,
    kept,
    mixed_t,
    middle,
    normed_mlp_t,
    hidden,
    pooled_t,
    dbefore,
    dmixed,
    dqkv,
    dy,
    packed,
    sems,
):
    total = pooled.shape[0]
    width = output_ref.shape[0]
    section, me = position()
    slabs = width // SLAB
    for place, ref in enumerate((own_ref, far_ref, section_ref, both_ref)):
        pooled[place * length : (place + 1) * length] = ref[...]
    for place, (ref, other) in enumerate(
        ((cot_ref, section), (cot_far_ref, section), (cot_ref, 1 - section), (cot_far_ref, 1 - section))
    ):
        dz[place * length : (place + 1) * length] = ref[other]

    x = dot(pooled[...], input_ref[...])
    start[...] = x
    normal, _ = unit(x)
    low = (normal * gain_attn_ref[...]).astype(bf16)
    normed[...] = low
    normed_t[...] = flip(low)
    qkv[...] = dot(low, project_ref[...]).astype(bf16)
    causal = rows_of((length, BLOCK)) <= lanes((length, BLOCK)) % length
    for block in range(total // BLOCK):
        part = slice(block * BLOCK, (block + 1) * BLOCK)
        for slab in range(slabs):
            at = slab * SLAB
            probs, piece = attend(
                qkv[part, at : at + SLAB],
                qkv[part, width + at : width + at + SLAB],
                qkv[part, 2 * width + at : 2 * width + at + SLAB],
                causal,
                length,
            )
            for head in range(SLAB // HEAD):
                kept[block * slabs + slab, head] = probs[head]
            mixed_t[at : at + SLAB, part] = piece
            dmixed[part, at : at + SLAB] = flip(piece)
    x = x + dot(dmixed[...], output_ref[...])
    middle[...] = x
    normal, _ = unit(x)
    low = (normal * gain_mlp_ref[...]).astype(bf16)
    normed_mlp_t[...] = flip(low)
    dz_all = dz[...]
    for at in range(0, expand_ref.shape[1], 256):
        part = slice(at, at + 256)
        value, bend = gelu_parts(dot(low, expand_ref[:, part]))
        hidden[:, part] = value.astype(bf16)
        dhidden = dot_nt(dz_all, shrink_ref[part, :]).astype(bf16)
        dbefore[:, part] = dhidden * bend.astype(bf16)
    result_ref[...] = middle[:length] + dot(hidden[:length], shrink_ref[...])

    dnormed = dot_nt(dbefore[...], expand_ref[...])
    normal, scale = unit(middle[...])
    gain_mlp_grad = jnp.sum(dnormed * normal, axis=0, keepdims=True)
    dmiddle = dz_all.astype(f32) + unit_back(dnormed, gain_mlp_ref[...], normal, scale)
    dy_low = dmiddle.astype(bf16)
    dy[...] = dy_low
    dmixed[...] = dot_nt(dy_low, output_ref[...]).astype(bf16)
    for block in range(total // BLOCK):
        part = slice(block * BLOCK, (block + 1) * BLOCK)
        for slab in range(slabs):
            at = slab * SLAB
            pieces = attend_back(
                qkv[part, at : at + SLAB],
                qkv[part, width + at : width + at + SLAB],
                qkv[part, 2 * width + at : 2 * width + at + SLAB],
                [kept[block * slabs + slab, head] for head in range(SLAB // HEAD)],
                dmixed[part, at : at + SLAB],
                length,
            )
            for place in range(3):
                dqkv[part, place * width + at : place * width + at + SLAB] = pieces[place]
    dnormed = dot_nt(dqkv[...], project_ref[...])
    normal, scale = unit(start[...])
    gain_attn_grad = jnp.sum(dnormed * normal, axis=0, keepdims=True)
    dword = (dmiddle + unit_back(dnormed, gain_attn_ref[...], normal, scale)).astype(bf16)
    dpooled_ref[...] = dot_nt(dword[:length], input_ref[...]).astype(bf16)
    normed[...] = dword

    low_shards = range(shards // 2)

    def shard_of(place):
        return (me & 8) | place

    def slot_of(place):
        other = place ^ (me & 7)
        return (other & 1) * 4 + (other >> 1)

    def own_rows(flipped, size):
        first = pl.multiple_of(shard_of(0) * size, 8 * size)
        return flipped[pl.ds(first, 8 * size), :]

    def own_columns(ref, size):
        return ref[:, pl.ds(pl.multiple_of(section * size, size), size)]

    def put(gradient, at):
        size = gradient.shape[0] // len(low_shards)
        for place in low_shards:
            piece = gradient[place * size : (place + 1) * size].astype(bf16)
            for column in range(gradient.shape[1] // SLAB):
                first = at + column * size
                packed[slot_of(place), first : first + size] = piece[
                    :, column * SLAB : (column + 1) * SLAB
                ]
        return at + size * (gradient.shape[1] // SLAB)

    size = normed_t.shape[0] // shards
    lhs = own_rows(normed_t, size)
    pooled_t[...] = flip(pooled[...])
    at = put(
        dot(
            own_rows(pooled_t, pooled_t.shape[0] // shards),
            own_columns(normed, width // 2),
        ),
        0,
    )
    at = put(dot(lhs, own_columns(dqkv, 3 * width // 2)), at)
    at = put(dot(own_rows(mixed_t, size), own_columns(dy, width // 2)), at)
    at = put(dot(own_rows(normed_mlp_t, size), own_columns(dbefore, expand_ref.shape[1] // 2)), at)
    size = hidden.shape[1] // 2
    lhs = flip(hidden[:, pl.ds(pl.multiple_of((me >> 3) * size, size), size)])
    at = put(dot(lhs, own_columns(dz, width // 2)), at)
    extra = jnp.concatenate(
        [gain_attn_grad[:, :SLAB], gain_attn_grad[:, SLAB:]]
        + [gain_mlp_grad[:, :SLAB], gain_mlp_grad[:, SLAB:]]
        + [jnp.zeros((12, SLAB), f32)],
        axis=0,
    ).astype(bf16)
    for place in low_shards:
        packed[place, at : at + 16] = extra
    hand_out(packed, keep_ref, send_ref, sems)


def word_group(pooled, cotangents, word_input, weights, shards):
    gain_attn, project, output, gain_mlp, expand_w, shrink = weights
    length, channels = pooled[0].shape
    width = output.shape[0]
    hidden = expand_w.shape[1]
    total = 4 * length
    half = (4, WORD_SLOT, SLAB)
    vmem = pl.BlockSpec(memory_space=pltpu.VMEM)
    hbm = pl.BlockSpec(memory_space=pltpu.HBM)
    return pl.pallas_call(
        functools.partial(word_kernel, length, shards),
        in_specs=[vmem] * 13,
        out_specs=[vmem, vmem, hbm, hbm],
        out_shape=[
            jax.ShapeDtypeStruct((length, width), f32),
            jax.ShapeDtypeStruct((length, channels), bf16),
            jax.ShapeDtypeStruct(half, bf16),
            jax.ShapeDtypeStruct(half, bf16),
        ],
        scratch_shapes=[
            pltpu.VMEM((total, channels), bf16),
            pltpu.VMEM((total, width), bf16),
            pltpu.VMEM((total, width), f32),
            pltpu.VMEM((total, width), bf16),
            pltpu.VMEM((width, total), bf16),
            pltpu.VMEM((total, 3 * width), bf16),
            pltpu.VMEM((total // BLOCK * (width // SLAB), SLAB // HEAD, length, BLOCK), f32),
            pltpu.VMEM((width, total), bf16),
            pltpu.VMEM((total, width), f32),
            pltpu.VMEM((width, total), bf16),
            pltpu.VMEM((total, hidden), bf16),
            pltpu.VMEM((channels, total), bf16),
            pltpu.VMEM((total, hidden), bf16),
            pltpu.VMEM((total, width), bf16),
            pltpu.VMEM((total, 3 * width), bf16),
            pltpu.VMEM((total, width), bf16),
            pltpu.VMEM((8, WORD_SLOT, SLAB), bf16),
            pltpu.SemaphoreType.DMA((2,)),
        ],
        compiler_params=pltpu.CompilerParams(vmem_limit_bytes=20 * MIB),
        cost_estimate=pl.CostEstimate(
            flops=total * width * width * 25 * 4, bytes_accessed=8 * MIB, transcendentals=0
        ),
        name="word_group",
    )(*pooled, *cotangents, word_input, gain_attn, project, output, gain_mlp, expand_w, shrink)


def added(*refs):
    return functools.reduce(lambda a, b: a + b, [ref.astype(f32) for ref in refs]).astype(bf16)


def core_sum_kernel(groups, *refs):
    ins = refs[: 2 * groups]
    outs = refs[-4:]
    for place, out in enumerate(outs):
        at = 0
        for keep, arrived in zip(ins[0::2], ins[1::2]):
            many = keep.shape[0] // len(outs)
            for entry in range(place * many, (place + 1) * many):
                size = keep.shape[1]
                out[at : at + size] = added(keep[entry], arrived[entry])
                at += size


def core_sum(*pairs, after=()):
    rows = sum(keep.shape[0] // 4 * keep.shape[1] for keep, _ in pairs)
    return pl.pallas_call(
        functools.partial(core_sum_kernel, len(pairs)),
        in_specs=[pl.BlockSpec(memory_space=pltpu.VMEM)] * (2 * len(pairs))
        + [pl.BlockSpec(memory_space=pl.ANY)] * len(after),
        out_shape=[jax.ShapeDtypeStruct((rows, SLAB), bf16)] * 4,
        compiler_params=pltpu.CompilerParams(vmem_limit_bytes=14 * MIB),
        name="core_sum",
    )(*[array for pair in pairs for array in pair], *after)


def plane_sum_kernel(*refs):
    first, second, near_ref, far_ref = (refs[:4], refs[4:8], refs[8], refs[9])
    near_ref[:WORD_SLOT] = added(*[ref[:WORD_SLOT] for ref in first])
    size = CHAR_MLP_SLOT
    for half, out in ((0, near_ref), (1, far_ref)):
        start = WORD_SLOT + half * size
        at = WORD_SLOT if half == 0 else 0
        out[at : at + size] = added(*[ref[start : start + size] for ref in first])
        at += size
        start = half * CHAR_ATTN_SLOT
        out[at : at + CHAR_ATTN_SLOT] = added(
            *[ref[start : start + CHAR_ATTN_SLOT] for ref in second]
        )


def plane_sum(first, second):
    rows = CHAR_MLP_SLOT + CHAR_ATTN_SLOT
    return pl.pallas_call(
        plane_sum_kernel,
        out_shape=[
            jax.ShapeDtypeStruct((WORD_SLOT + rows, SLAB), bf16),
            jax.ShapeDtypeStruct((rows, SLAB), bf16),
        ],
        compiler_params=pltpu.CompilerParams(vmem_limit_bytes=12 * MIB),
        name="plane_sum",
    )(*first, *second)


def last_sum_kernel(near_ref, section_ref, high_ref, both_ref, *outs):
    word_rows = WORD_SLOT
    section, me = position()
    own = near_ref[:word_rows].astype(f32)
    other = section_ref[:word_rows].astype(f32)
    halves = (jnp.where(section == 0, own, other), jnp.where(section == 0, other, own))
    char = (
        near_ref[word_rows:].astype(f32)
        + section_ref[word_rows:].astype(f32)
        + high_ref[...].astype(f32)
        + both_ref[...].astype(f32)
    )

    def mine(vector, size):
        turned = pltpu.roll(vector, lax.rem(SLAB - lax.rem(me * size, SLAB), SLAB), 1)
        return turned[:, :size]

    (
        table_ref,
        gain_attn_ref,
        project_ref,
        output_ref,
        gain_mlp_ref,
        expand_ref,
        shrink_ref,
        w_input_ref,
        w_gain_attn_ref,
        w_project_ref,
        w_output_ref,
        w_gain_mlp_ref,
        w_expand_ref,
        w_shrink_ref,
    ) = outs
    at = 0
    for ref in (expand_ref, shrink_ref, project_ref, output_ref):
        size = ref.shape[0]
        for column in range(ref.shape[1] // SLAB):
            ref[:, column * SLAB : (column + 1) * SLAB] = char[at : at + size]
            at += size
    size = gain_attn_ref.shape[1]
    extra = char[at : at + 16]
    turned = mine(extra, size)
    gain_attn_ref[...] = turned[0:1]
    gain_mlp_ref[...] = turned[1:2]
    table_ref[...] = turned[8:16]
    at = 0
    for ref in (w_input_ref, w_project_ref, w_output_ref, w_expand_ref, w_shrink_ref):
        size = ref.shape[0]
        columns = ref.shape[1] // (2 * SLAB)
        for column in range(columns):
            for half in range(2):
                first = (half * columns + column) * SLAB
                ref[:, first : first + SLAB] = halves[half][at : at + size]
            at += size
    size = w_gain_attn_ref.shape[1]
    extra = own[at : at + 8]
    turned = mine(extra, size)
    upper = me * size >= SLAB
    w_gain_attn_ref[...] = jnp.where(upper, turned[1:2], turned[0:1])
    w_gain_mlp_ref[...] = jnp.where(upper, turned[3:4], turned[2:3])


def last_sum(near, arrived, shapes):
    return pl.pallas_call(
        last_sum_kernel,
        out_shape=[jax.ShapeDtypeStruct(shape, f32) for shape in shapes],
        compiler_params=pltpu.CompilerParams(vmem_limit_bytes=12 * MIB),
        name="last_sum",
    )(near, *arrived)


def exchange(value, section_bit, dp_bits):
    shards = lax.axis_size("dp")
    pairs = [
        (s * shards + d, (s ^ section_bit) * shards + (d ^ dp_bits))
        for s in range(lax.axis_size("section"))
        for d in range(shards)
    ]
    return lax.ppermute(value, ("section", "dp"), pairs)


CORE, SIDE, NEAR, FAR = (1, 2, 4, 8)


def plane_exchange(pieces):
    return (pieces[0],) + tuple(
        exchange(piece, 0, bits) for piece, bits in zip(pieces[1:], (SIDE, NEAR, SIDE | NEAR))
    )


def local_grouped(
    chars, counts, languages, language_table, char_weights, word_input, word_weights, cotangent
):
    shards = lax.axis_size("dp")
    micros, _, words, slots, width = chars.shape
    rows = words * slots
    cot = cotangent[:, 0]
    cot_far = exchange(cot, 0, FAR)
    char_weights = tuple(w[None] if w.ndim == 1 else w for w in char_weights)
    word_weights = tuple(w[None] if w.ndim == 1 else w for w in word_weights)
    chars = chars.reshape(micros, rows, width)
    counts = counts.reshape(micros, 1, words)
    pooled, *stored = char_forward(languages, chars, counts, language_table, char_weights, slots)
    others = (exchange(pooled, 0, FAR), exchange(pooled, 1, 0), exchange(pooled, 1, FAR))
    result, dpooled, keep, send = word_group(
        (pooled,) + others, (cot, cot_far), word_input, word_weights, shards
    )
    word = (keep, exchange(send, 0, CORE))
    dmiddle, gain_mlp_grad, keep, send = char_mlp_back(
        counts, char_weights, dpooled, stored, slots, shards
    )
    first = plane_exchange(core_sum(word, (keep, exchange(send, 0, CORE))))
    chars_grad, keep, send = char_attn_back(
        languages,
        chars,
        language_table,
        char_weights,
        dmiddle,
        gain_mlp_grad,
        stored,
        slots,
        shards,
        first[0],
    )
    second = plane_exchange(core_sum((keep, exchange(send, 0, CORE)), after=first[1:]))
    near, far = plane_sum(first, second)
    arrived = (exchange(near, 1, 0), exchange(far, 0, FAR), exchange(far, 1, FAR))
    shapes = [(language_table.shape[0], language_table.shape[1] // shards)]
    for weight in char_weights + (word_input,) + word_weights:
        if weight.shape[0] == 1:
            shapes.append((1, weight.shape[1] // shards))
        else:
            shapes.append((weight.shape[0] // shards, weight.shape[1]))
    totals = last_sum(near, arrived, shapes)
    totals = [total[0] if total.shape[0] == 1 else total for total in totals]
    return (result[None, None], chars_grad.reshape((1, 1, words, slots, width))) + tuple(totals)


def norm_forward(inputs, gain):
    return inputs * lax.rsqrt(jnp.mean(inputs * inputs, axis=-1, keepdims=True) + eps) * gain


def attend_forward(normed, project, head_count, key_mask):
    row_count, length, channels = normed.shape
    head_size = channels // head_count
    qkv = jnp.einsum("blc,cf->blf", normed, project, preferred_element_type=jnp.float32).astype(
        jnp.bfloat16
    )
    pieces = qkv.reshape(row_count, length, 3, head_count, head_size)
    scores = jnp.einsum(
        "bqhd,bkhd->bhqk", pieces[:, :, 0], pieces[:, :, 1], preferred_element_type=jnp.float32
    ) * head_size ** (-0.5)
    scores = jnp.where(key_mask, scores, -1e30)
    row_max = jnp.max(scores, axis=-1, keepdims=True)
    weights_exp = jnp.exp(scores - row_max)
    row_total = jnp.sum(weights_exp, axis=-1, keepdims=True)
    attn_probs = (weights_exp / row_total).astype(jnp.bfloat16)
    mixed_heads = jnp.einsum(
        "bhqk,bkhd->bqhd", attn_probs, pieces[:, :, 2], preferred_element_type=jnp.float32
    )
    mixed_heads = mixed_heads.reshape(row_count, length, channels).astype(jnp.bfloat16)
    return (qkv, row_max + jnp.log(row_total), mixed_heads)


def attend_backward(
    normed, project, output, qkv, logsum, mixed_heads, dmiddle_low, head_count, key_mask
):
    row_count, length, channels = normed.shape
    head_size = channels // head_count
    scaling = head_size ** (-0.5)
    output_grad = jnp.einsum(
        "blc,bld->cd", mixed_heads, dmiddle_low, preferred_element_type=jnp.float32
    )
    dmixed = jnp.einsum(
        "bld,cd->blc", dmiddle_low, output, preferred_element_type=jnp.float32
    ).astype(jnp.bfloat16)
    dmixed = dmixed.reshape(row_count, length, head_count, head_size)
    pieces = qkv.reshape(row_count, length, 3, head_count, head_size)
    scores = (
        jnp.einsum(
            "bqhd,bkhd->bhqk", pieces[:, :, 0], pieces[:, :, 1], preferred_element_type=jnp.float32
        )
        * scaling
    )
    scores = jnp.where(key_mask, scores, -1e30)
    attn_probs = jnp.exp(scores - logsum)
    dprobs = jnp.einsum(
        "bqhd,bkhd->bhqk", dmixed, pieces[:, :, 2], preferred_element_type=jnp.float32
    )
    row_delta = jnp.sum(attn_probs * dprobs, axis=-1, keepdims=True)
    dscores = (attn_probs * (dprobs - row_delta)).astype(jnp.bfloat16)
    dquery = (
        jnp.einsum("bhqk,bkhd->bqhd", dscores, pieces[:, :, 1], preferred_element_type=jnp.float32)
        * scaling
    )
    dkeys = (
        jnp.einsum("bhqk,bqhd->bkhd", dscores, pieces[:, :, 0], preferred_element_type=jnp.float32)
        * scaling
    )
    dvalues = jnp.einsum(
        "bhqk,bqhd->bkhd",
        attn_probs.astype(jnp.bfloat16),
        dmixed,
        preferred_element_type=jnp.float32,
    )
    dqkv = (
        jnp.stack([dquery, dkeys, dvalues], axis=2)
        .reshape(row_count, length, 3 * channels)
        .astype(jnp.bfloat16)
    )
    project_grad = jnp.einsum("blc,blf->cf", normed, dqkv, preferred_element_type=jnp.float32)
    dnormed = jnp.einsum("blf,cf->blc", dqkv, project, preferred_element_type=jnp.float32)
    return (dnormed, project_grad, output_grad)


def block_forward(inputs, weights, head_count, key_mask):
    gain_attn, project, output, gain_mlp, expand, shrink = weights
    normed = norm_forward(inputs, gain_attn).astype(jnp.bfloat16)
    qkv, logsum, mixed_heads = attend_forward(normed, project, head_count, key_mask)
    middle = inputs + jnp.einsum(
        "blc,cd->bld", mixed_heads, output, preferred_element_type=jnp.float32
    )
    normed_mlp = norm_forward(middle, gain_mlp).astype(jnp.bfloat16)
    before = jnp.einsum("blc,cf->blf", normed_mlp, expand, preferred_element_type=jnp.float32)
    hidden = jax.nn.gelu(before).astype(jnp.bfloat16)
    result = middle + jnp.einsum("blf,fc->blc", hidden, shrink, preferred_element_type=jnp.float32)
    return (result, (inputs, normed, qkv, logsum, mixed_heads, middle, normed_mlp, before, hidden))


def block_backward(dresult, stored, weights, head_count, key_mask):
    gain_attn, project, output, gain_mlp, expand, shrink = weights
    inputs, normed, qkv, logsum, mixed_heads, middle, normed_mlp, before, hidden = stored
    grad_low = dresult.astype(jnp.bfloat16)
    shrink_grad = jnp.einsum("blf,blc->fc", hidden, grad_low, preferred_element_type=jnp.float32)
    dhidden = jnp.einsum(
        "blc,fc->blf", grad_low, shrink, preferred_element_type=jnp.float32
    ).astype(jnp.bfloat16)
    gelu_pull = jax.vjp(jax.nn.gelu, before)[1]
    dbefore = gelu_pull(dhidden.astype(jnp.float32))[0].astype(jnp.bfloat16)
    expand_grad = jnp.einsum("blc,blf->cf", normed_mlp, dbefore, preferred_element_type=jnp.float32)
    dnormed_mlp = jnp.einsum("blf,cf->blc", dbefore, expand, preferred_element_type=jnp.float32)
    norm_pull = jax.vjp(norm_forward, middle, gain_mlp)[1]
    dmiddle_norm, gain_mlp_grad = norm_pull(dnormed_mlp)
    dmiddle = dresult + dmiddle_norm
    dnormed, project_grad, output_grad = attend_backward(
        normed,
        project,
        output,
        qkv,
        logsum,
        mixed_heads,
        dmiddle.astype(jnp.bfloat16),
        head_count,
        key_mask,
    )
    first_pull = jax.vjp(norm_forward, inputs, gain_attn)[1]
    dinputs_norm, gain_attn_grad = first_pull(dnormed)
    return (
        dmiddle + dinputs_norm,
        (gain_attn_grad, project_grad, output_grad, gain_mlp_grad, expand_grad, shrink_grad),
    )


def char_front(char_text, char_count, language, lang_table, weights):
    present = lax.broadcasted_iota(jnp.int32, char_text.shape[:2], 1) < char_count[:, None]
    onehot = (lax.broadcasted_iota(jnp.int32, (lang_table.shape[0],), 0) == language).astype(
        jnp.bfloat16
    )
    lang_row = jnp.dot(onehot, lang_table, preferred_element_type=jnp.float32)
    inputs = char_text.astype(jnp.float32) + lang_row
    result, stored = block_forward(inputs, weights, CH, present[:, None, None, :])
    summed = jnp.sum(jnp.where(present[:, :, None], result, 0.0), axis=1)
    pooled = (summed / char_count[:, None].astype(jnp.float32)).astype(jnp.bfloat16)
    return (pooled, stored, present, onehot)


def char_back(stored, present, onehot, char_count, dpooled, weights):
    spread = dpooled.astype(jnp.float32) / char_count[:, None].astype(jnp.float32)
    dresult = jnp.where(present[:, :, None], spread[:, None, :], 0.0)
    dinputs, gradients = block_backward(dresult, stored, weights, CH, present[:, None, None, :])
    table_grad = onehot.astype(jnp.float32)[:, None] * jnp.sum(dinputs, axis=(0, 1))[None, :]
    return (dinputs, (table_grad,) + gradients)


def word_full(pooled, cot_rows, word_input, weights):
    length = pooled.shape[0]
    word_start = jnp.dot(pooled, word_input, preferred_element_type=jnp.float32)[None]
    causal = (
        lax.broadcasted_iota(jnp.int32, (length, length), 0)
        >= lax.broadcasted_iota(jnp.int32, (length, length), 1)
    )[None, None]
    result, stored = block_forward(word_start, weights, H, causal)
    dstart, gradients = block_backward(
        cot_rows.astype(jnp.float32)[None], stored, weights, H, causal
    )
    grad_low = dstart[0].astype(jnp.bfloat16)
    input_grad = jnp.einsum("wc,wd->cd", pooled, grad_low, preferred_element_type=jnp.float32)
    dpooled = jnp.einsum(
        "wd,cd->wc", grad_low, word_input, preferred_element_type=jnp.float32
    ).astype(jnp.bfloat16)
    return (result[0], dpooled, (input_grad,) + gradients)


def reduce_rows(gradients):
    shards = lax.axis_size("dp")
    flat = []
    for place, gradient in enumerate(gradients):
        if place == 0:
            gradient = gradient.T
        flat.append(gradient.astype(jnp.bfloat16).reshape(shards, -1))
    packed = jnp.concatenate(flat, axis=1)
    me = lax.axis_index("dp")
    packed = jnp.take(packed, jnp.arange(shards) ^ me, axis=0)
    bit = 1
    while packed.shape[0] > 1:
        pairs = packed.reshape(packed.shape[0] // 2, 2, packed.shape[1])
        arrived = lax.ppermute(pairs[:, 1], "dp", [(i, i ^ bit) for i in range(shards)])
        packed = (pairs[:, 0].astype(jnp.float32) + arrived.astype(jnp.float32)).astype(
            jnp.bfloat16
        )
        bit *= 2
    arrived = lax.ppermute(packed, "section", [(0, 1), (1, 0)])
    total = (packed.astype(jnp.float32) + arrived.astype(jnp.float32))[0]
    outs = []
    at = 0
    for place, gradient in enumerate(gradients):
        size = gradient.size // shards
        piece = total[at : at + size]
        at += size
        if place == 0:
            outs.append(piece.reshape(-1, gradient.shape[0]).T)
        else:
            outs.append(piece.reshape((gradient.shape[0] // shards,) + gradient.shape[1:]))
    return tuple(outs)


def local(
    chars,
    counts,
    languages,
    language_table,
    char_gain_attn,
    char_project,
    char_output,
    char_gain_mlp,
    char_expand,
    char_shrink,
    word_input,
    word_gain_attn,
    word_project,
    word_output,
    word_gain_mlp,
    word_expand,
    word_shrink,
    cotangent,
):
    char_weights = (
        char_gain_attn,
        char_project,
        char_output,
        char_gain_mlp,
        char_expand,
        char_shrink,
    )
    word_weights = (
        word_gain_attn,
        word_project,
        word_output,
        word_gain_mlp,
        word_expand,
        word_shrink,
    )
    if lax.axis_size("dp") == 16:
        return local_grouped(
            chars,
            counts,
            languages,
            language_table,
            char_weights,
            word_input,
            word_weights,
            cotangent,
        )
    section_index = lax.axis_index("section")
    char_text = chars[section_index, 0]
    char_count = counts[section_index, 0]
    language = languages[section_index, 0]
    cot_rows = cotangent[section_index, 0]
    pooled, stored, present, onehot = char_front(
        char_text, char_count, language, language_table, char_weights
    )
    result, dpooled, word_grads = word_full(pooled, cot_rows, word_input, word_weights)
    text_grad, char_grads = char_back(stored, present, onehot, char_count, dpooled, char_weights)
    totals = reduce_rows(char_grads + word_grads)
    return (result[None, None], text_grad[None, None]) + totals


def solution(mesh):
    placed = (
        P(None, "dp", None, None, None),
        P(None, "dp", None),
        P(None, "dp"),
        P(),
        P(),
        P(),
        P(),
        P(),
        P(),
        P(),
        P(),
        P(),
        P(),
        P(),
        P(),
        P(),
        P(),
        P(None, "dp", None, None),
    )
    return jax.shard_map(
        local,
        mesh=mesh,
        in_specs=placed,
        out_specs=(
            P("section", "dp", None, None),
            P("section", "dp", None, None, None),
            P(None, "dp"),
            P("dp"),
            P("dp", None),
            P("dp", None),
            P("dp"),
            P("dp", None),
            P("dp", None),
            P("dp", None),
            P("dp"),
            P("dp", None),
            P("dp", None),
            P("dp"),
            P("dp", None),
            P("dp", None),
        ),
        check_vma=False,
    )
```

```python
import functools

import jax
import jax.numpy as jnp
from jax import lax
from jax.experimental import pallas as pl
from jax.experimental.pallas import tpu as pltpu
from jax.sharding import PartitionSpec as P

CH = 4
H = 8
HEAD = 64
SLAB = 256
HEADS = SLAB // HEAD
BLOCK = 128
MIB = 1024 * 1024

eps = 1e-05

f32 = jnp.float32
bf16 = jnp.bfloat16


def dot(a, b):
    return jnp.dot(a, b, preferred_element_type=f32)


def dot_nt(a, b):
    return lax.dot_general(a, b, (((1,), (1,)), ((), ())), preferred_element_type=f32)


def position():
    return (lax.axis_index("section"), lax.axis_index("dp"))


def lanes(shape):
    return lax.broadcasted_iota(jnp.int32, shape, 1)


def rows_of(shape):
    return lax.broadcasted_iota(jnp.int32, shape, 0)


def stack_heads(a):
    head = lanes((1, SLAB)) // HEAD
    masks = [jnp.where(head == place, 1.0, 0.0).astype(bf16) for place in range(HEADS)]
    return jnp.concatenate([a * mask for mask in masks], axis=0)


def compact(scores, length):
    group = lanes((length, BLOCK)) // length
    total = scores[:length]
    for place in range(1, BLOCK // length):
        total = jnp.where(group == place, scores[place * length : (place + 1) * length], total)
    return total


def compact_heads(scores, length):
    return [
        compact(scores[:, head * BLOCK : (head + 1) * BLOCK], length) for head in range(HEADS)
    ]


def expand(values, length):
    group = lanes((length, BLOCK)) // length
    return jnp.concatenate(
        [jnp.where(group == place, values, 0.0) for place in range(BLOCK // length)], axis=0
    ).astype(bf16)


def expand_heads(values, tile, length):
    first = tile * HEADS * BLOCK
    return [
        expand(values[:, first + head * BLOCK : first + (head + 1) * BLOCK], length)
        for head in range(HEADS)
    ]


def head_rows(a, head):
    return a[head * HEAD : (head + 1) * HEAD]


def attend(load, tiles, key_mask, length):
    scores = []
    for tile in tiles:
        scores += compact_heads(dot_nt(load(tile, 1), stack_heads(load(tile, 0))), length)
    scores = jnp.concatenate(scores, axis=1) * HEAD**-0.5
    scores = jnp.where(key_mask, scores, -1e30)
    weights = jnp.exp(scores - jnp.max(scores, axis=0, keepdims=True))
    probs = weights / jnp.sum(weights, axis=0, keepdims=True)
    mixed = []
    for number, tile in enumerate(tiles):
        values = load(tile, 2).T
        parts = expand_heads(probs, number, length)
        mixed.append(
            jnp.concatenate(
                [dot(head_rows(values, head), parts[head]) for head in range(HEADS)], axis=0
            ).astype(bf16)
        )
    return (probs, mixed)


def attend_back(load, load_dmixed, tiles, probs, store, length):
    dprobs = []
    for number, tile in enumerate(tiles):
        stacked = stack_heads(load_dmixed(tile))
        dprobs += compact_heads(dot_nt(load(tile, 2), stacked), length)
        parts = jnp.concatenate(expand_heads(probs, number, length), axis=1)
        store(tile, 2, dot(parts, stacked).astype(bf16))
    dprobs = jnp.concatenate(dprobs, axis=1)
    dscores = probs * (dprobs - jnp.sum(probs * dprobs, axis=0, keepdims=True))
    scaling = HEAD**-0.5
    for number, tile in enumerate(tiles):
        parts = expand_heads(dscores, number, length)
        keys = load(tile, 1).T
        dq = jnp.concatenate(
            [dot(head_rows(keys, head), parts[head]) for head in range(HEADS)], axis=0
        )
        store(tile, 0, (dq * scaling).astype(bf16).T)
        dk = dot(jnp.concatenate(parts, axis=1), stack_heads(load(tile, 0)))
        store(tile, 1, (dk * scaling).astype(bf16))


def unit(x):
    scale = lax.rsqrt(jnp.mean(x * x, axis=-1, keepdims=True) + eps)
    return (x * scale, scale)


def unit_back(dnormed, gain, normal, scale):
    weighted = dnormed * gain
    return scale * (weighted - normal * jnp.mean(normal * weighted, axis=-1, keepdims=True))


def gelu_parts(before):
    c = 0.7978845608028654
    square = before * before
    half = 0.5 * jnp.tanh(before * (c + (c * 0.044715) * square)) + 0.5
    value = before * half
    slope = half + value * (1.0 - half) * (2.0 * c + (6.0 * c * 0.044715) * square)
    return (value, slope)


def pick(row, place):
    return jnp.sum(jnp.where(lanes(row.shape) == place, row, 0), axis=1, keepdims=True)


def char_rows(chars, table_ref, language):
    table = table_ref[...].astype(f32)
    row = jnp.sum(jnp.where(rows_of(table.shape) == language, table, 0.0), axis=0, keepdims=True)
    return chars.astype(f32) + row


def counts_by_row(counts, rows, slots):
    words = counts.shape[-1]
    counts = jnp.broadcast_to(counts.astype(f32), (8, words)).astype(bf16)
    shape = (words, rows)
    member = lanes(shape) // slots == rows_of(shape)
    return dot(counts, jnp.where(member, 1.0, 0.0).astype(bf16))[:1]


def counts_column(counts):
    words = counts.shape[-1]
    shape = (words, words)
    spread = jnp.broadcast_to(counts.astype(f32), shape)
    return jnp.sum(
        jnp.where(rows_of(shape) == lanes(shape), spread, 0.0), axis=1, keepdims=True
    )


def fetch_all(sources, targets, sems):
    fetches = [
        pltpu.make_async_copy(source, target, sems.at[place])
        for place, (source, target) in enumerate(zip(sources, targets))
    ]
    for fetch in fetches:
        fetch.start()
    return fetches


def in_hbm(array):
    return pltpu.with_memory_space_constraint(array, pltpu.HBM)


def char_forward_kernel(
    slots,
    chars_hbm,
    languages_hbm,
    counts_hbm,
    table_hbm,
    gain_attn_hbm,
    project_hbm,
    output_hbm,
    gain_mlp_hbm,
    expand_hbm,
    shrink_hbm,
    pooled_ref,
    hidden_sum_ref,
    qkv_ref,
    probs_ref,
    mixed_ref,
    middle_ref,
    slope_ref,
    chars_ref,
    languages_ref,
    counts_ref,
    table_ref,
    gain_attn_ref,
    project_ref,
    output_ref,
    gain_mlp_ref,
    expand_ref,
    shrink_ref,
    sems,
):
    section, _ = position()
    fetches = fetch_all(
        (
            languages_hbm,
            counts_hbm,
            table_hbm,
            gain_attn_hbm,
            chars_hbm.at[section],
            project_hbm,
            output_hbm,
            gain_mlp_hbm,
            expand_hbm,
            shrink_hbm,
        ),
        (
            languages_ref,
            counts_ref,
            table_ref,
            gain_attn_ref,
            chars_ref,
            project_ref,
            output_ref,
            gain_mlp_ref,
            expand_ref,
            shrink_ref,
        ),
        sems,
    )
    for fetch in fetches[:2]:
        fetch.wait()
    counts = counts_ref[section]
    rows = chars_ref.shape[0]
    words = counts.shape[-1]
    row_counts = counts_by_row(counts, rows, slots)
    for fetch in fetches[2:5]:
        fetch.wait()
    x = char_rows(chars_ref[...], table_ref, pick(languages_ref[...], section))
    normal, _ = unit(x)
    normed = (normal * gain_attn_ref[...]).astype(bf16)
    fetches[5].wait()
    qkv_ref[...] = dot(normed, project_ref[...]).astype(bf16)
    blocks = range(rows // BLOCK)

    def load(block, which):
        return qkv_ref[block * BLOCK : (block + 1) * BLOCK, which * SLAB : (which + 1) * SLAB]

    by_head = jnp.concatenate(
        [row_counts[:, block * BLOCK : (block + 1) * BLOCK] for block in blocks for _ in range(HEADS)],
        axis=1,
    )
    key_mask = rows_of((slots, rows * HEADS)).astype(f32) < by_head
    probs, mixed = attend(load, blocks, key_mask, slots)
    probs_ref[...] = probs
    for block in blocks:
        mixed_ref[:, block * BLOCK : (block + 1) * BLOCK] = mixed[block]
    mixed = mixed_ref[...].T
    fetches[6].wait()
    middle = x + dot(mixed, output_ref[...])
    middle_ref[...] = middle
    normal, _ = unit(middle)
    fetches[7].wait()
    normed = (normal * gain_mlp_ref[...]).astype(bf16)
    word_shape = (words, rows)
    lane = lanes(word_shape)
    member = (lane // slots == rows_of(word_shape)) & ((lane % slots).astype(f32) < row_counts)
    member = jnp.where(member, 1.0, 0.0).astype(bf16)
    fetches[8].wait()
    for at in range(0, expand_ref.shape[1], 256):
        part = slice(at, at + 256)
        value, slope = gelu_parts(dot(normed, expand_ref[:, part]))
        slope_ref[:, part] = slope.astype(bf16)
        hidden_sum_ref[:, part] = dot(member, value.astype(bf16)).astype(bf16)
    high = middle.astype(bf16)
    low = (middle - high.astype(f32)).astype(bf16)
    fetches[9].wait()
    total = dot(member, high) + dot(member, low) + dot(hidden_sum_ref[...], shrink_ref[...])
    pooled_ref[...] = (total / counts_column(counts)).astype(bf16)


def char_forward(languages, chars, counts, table, weights, slots):
    rows, width = chars.shape[1:]
    words = rows // slots
    hidden = weights[4].shape[1]
    vmem = pl.BlockSpec(memory_space=pltpu.VMEM)
    hbm = pl.BlockSpec(memory_space=pltpu.HBM)
    fetched = (languages, counts, table) + tuple(weights)
    return pl.pallas_call(
        functools.partial(char_forward_kernel, slots),
        in_specs=[hbm] * 10,
        out_specs=[vmem] * 7,
        out_shape=[
            jax.ShapeDtypeStruct((words, width), bf16),
            jax.ShapeDtypeStruct((words, hidden), bf16),
            jax.ShapeDtypeStruct((rows, 3 * width), bf16),
            jax.ShapeDtypeStruct((slots, rows * HEADS), f32),
            jax.ShapeDtypeStruct((width, rows), bf16),
            jax.ShapeDtypeStruct((rows, width), f32),
            jax.ShapeDtypeStruct((rows, hidden), bf16),
        ],
        scratch_shapes=[pltpu.VMEM(chars.shape[1:], bf16)]
        + [pltpu.VMEM(array.shape, array.dtype) for array in fetched]
        + [pltpu.SemaphoreType.DMA((10,))],
        compiler_params=pltpu.CompilerParams(vmem_limit_bytes=16 * MIB),
        cost_estimate=pl.CostEstimate(
            flops=64 * rows * width * width, bytes_accessed=8 * MIB, transcendentals=0
        ),
        name="char_forward",
    )(*[in_hbm(array) for array in (chars,) + fetched])


CHAR_FIRST_SLOT = 144
CHAR_LAST_SLOT = 64


def char_shard(slot, me):
    return me ^ ((slot >> 3) | (((slot >> 1) & 3) << 1) | ((slot & 1) << 3))


def put_shards(gradient, slots, shard_of, at):
    width = SLAB
    columns = gradient.shape[1] // width
    size = gradient.shape[0] // len(slots)
    for number, (ref, place) in enumerate(slots):
        first = pl.multiple_of(shard_of(number) * size, size)
        for column in range(columns):
            start = at + column * size
            ref[place, start : start + size] = gradient[
                pl.ds(first, size), column * width : (column + 1) * width
            ].astype(bf16)
    return at + size * columns


def slot_refs(*refs):
    return [(ref, place) for ref in refs for place in range(ref.shape[0])]


def char_mlp_back_kernel(
    slots,
    shards,
    counts_hbm,
    gain_mlp_ref,
    expand_ref,
    shrink_ref,
    dpooled_ref,
    hidden_sum_ref,
    mixed_ref,
    middle_ref,
    slope_ref,
    dmiddle_ref,
    gain_ref,
    keep_ref,
    send_ref,
    counts_ref,
    dhidden_words,
    dbefore,
    expand_grad,
    shrink_grad,
    output_grad,
    sem,
):
    section, me = position()
    fetch = pltpu.make_async_copy(counts_hbm, counts_ref, sem)
    fetch.start()
    fetch.wait()
    counts = counts_ref[section]
    rows, width = middle_ref.shape
    words = counts.shape[-1]
    spread = dpooled_ref[...].astype(f32) / counts_column(counts)
    spread_high = spread.astype(bf16)
    spread_low = (spread - spread_high.astype(f32)).astype(bf16)
    dhidden_words[...] = dot_nt(spread_high, shrink_ref[...]).astype(bf16)
    shape = (rows, words)
    row = rows_of(shape)
    member = (row // slots == lanes(shape)) & (row % slots < counts)
    member = jnp.where(member, 1.0, 0.0).astype(bf16)
    for at in range(0, expand_ref.shape[1], 256):
        part = slice(at, at + 256)
        dbefore[:, part] = dot(member, dhidden_words[:, part]).astype(bf16) * slope_ref[:, part]
    dnormed = dot_nt(dbefore[...], expand_ref[...])
    normal, scale = unit(middle_ref[...])
    normed_t = (normal * gain_mlp_ref[...]).astype(bf16).T
    gain_ref[...] = jnp.broadcast_to(
        jnp.sum(dnormed * normal, axis=0, keepdims=True), gain_ref.shape
    )
    dmiddle = (
        dot(member, spread_high)
        + dot(member, spread_low)
        + unit_back(dnormed, gain_mlp_ref[...], normal, scale)
    )
    dmiddle_ref[...] = dmiddle
    expand_grad[...] = dot(normed_t, dbefore[...])
    shrink_grad[...] = dot(hidden_sum_ref[...].T, spread_high)
    output_grad[...] = dot(mixed_ref[...], dmiddle.astype(bf16))
    targets = slot_refs(keep_ref, send_ref)
    at = 0
    for gradient in (expand_grad, shrink_grad, output_grad):
        at = put_shards(gradient, targets, lambda slot: char_shard(slot, me), at)


def char_mlp_back(counts, weights, dpooled, stored, slots, shards):
    _, _, output, gain_mlp, expand_w, shrink = weights
    hidden_sum, _, _, mixed, middle, slope = stored
    rows, width = middle.shape
    words = rows // slots
    hidden = expand_w.shape[1]
    half = (shards // 2, CHAR_FIRST_SLOT, width)
    vmem = pl.BlockSpec(memory_space=pltpu.VMEM)
    hbm = pl.BlockSpec(memory_space=pltpu.HBM)
    return pl.pallas_call(
        functools.partial(char_mlp_back_kernel, slots, shards),
        in_specs=[hbm] + [vmem] * 8,
        out_specs=[vmem] * 4,
        out_shape=[
            jax.ShapeDtypeStruct((rows, width), f32),
            jax.ShapeDtypeStruct((8, width), f32),
            jax.ShapeDtypeStruct(half, bf16),
            jax.ShapeDtypeStruct(half, bf16),
        ],
        scratch_shapes=[
            pltpu.VMEM(counts.shape, counts.dtype),
            pltpu.VMEM((words, hidden), bf16),
            pltpu.VMEM((rows, hidden), bf16),
            pltpu.VMEM(expand_w.shape, f32),
            pltpu.VMEM(shrink.shape, f32),
            pltpu.VMEM(output.shape, f32),
            pltpu.SemaphoreType.DMA,
        ],
        compiler_params=pltpu.CompilerParams(vmem_limit_bytes=16 * MIB),
        cost_estimate=pl.CostEstimate(
            flops=64 * rows * width * width, bytes_accessed=8 * MIB, transcendentals=0
        ),
        name="char_mlp_back",
    )(in_hbm(counts), gain_mlp, expand_w, shrink, dpooled, hidden_sum, mixed, middle, slope)


def char_attn_back_kernel(
    slots,
    shards,
    _,
    chars_hbm,
    languages_hbm,
    table_ref,
    gain_attn_ref,
    project_ref,
    output_ref,
    dmiddle_ref,
    gain_mlp_grad_ref,
    qkv_ref,
    probs_ref,
    grad_hbm,
    keep_ref,
    send_ref,
    send_more_ref,
    chars_ref,
    languages_ref,
    dmixed,
    dqkv,
    grad,
    project_grad,
    sems,
):
    section, me = position()
    fetches = fetch_all(
        (chars_hbm.at[section], languages_hbm), (chars_ref, languages_ref), sems
    )
    rows, width = dmiddle_ref.shape
    dmixed[...] = dot_nt(dmiddle_ref[...].astype(bf16), output_ref[...]).astype(bf16)

    def load(block, which):
        return qkv_ref[block * BLOCK : (block + 1) * BLOCK, which * SLAB : (which + 1) * SLAB]

    def load_dmixed(block):
        return dmixed[block * BLOCK : (block + 1) * BLOCK]

    def store(block, which, value):
        dqkv[block * BLOCK : (block + 1) * BLOCK, which * SLAB : (which + 1) * SLAB] = value

    attend_back(load, load_dmixed, range(rows // BLOCK), probs_ref[...], store, slots)
    dnormed = dot_nt(dqkv[...], project_ref[...])
    for fetch in fetches:
        fetch.wait()
    language = pick(languages_ref[...], section)
    normal, scale = unit(char_rows(chars_ref[...], table_ref, language))
    gain_attn_grad = jnp.sum(dnormed * normal, axis=0, keepdims=True)
    dx = dmiddle_ref[...] + unit_back(dnormed, gain_attn_ref[...], normal, scale)
    grad[...] = dx
    leave = pltpu.make_async_copy(grad, grad_hbm, sems.at[2])
    leave.start()
    row_sum = jnp.sum(dx, axis=0, keepdims=True)
    normed_t = (normal * gain_attn_ref[...]).astype(bf16).T
    project_grad[...] = dot(normed_t, dqkv[...])
    targets = slot_refs(keep_ref, send_ref, send_more_ref)
    at = put_shards(project_grad, targets, lambda slot: char_shard(slot, me), 0)
    extra = jnp.concatenate(
        [
            gain_attn_grad,
            gain_mlp_grad_ref[:7],
            jnp.where(rows_of((8, 1)) == language, row_sum, 0.0),
        ],
        axis=0,
    ).astype(bf16)
    for ref, place in targets:
        ref[place, at : at + 16] = extra
    leave.wait()


def char_attn_back(
    languages, chars, table, weights, dmiddle, gain_mlp_grad, stored, slots, shards, after
):
    gain_attn, project, output, _, _, _ = weights
    _, qkv, probs, _, _, _ = stored
    rows, width = dmiddle.shape
    half = (shards // 2, CHAR_LAST_SLOT, width)
    quarter = (shards // 4, CHAR_LAST_SLOT, width)
    vmem = pl.BlockSpec(memory_space=pltpu.VMEM)
    hbm = pl.BlockSpec(memory_space=pltpu.HBM)
    return pl.pallas_call(
        functools.partial(char_attn_back_kernel, slots, shards),
        in_specs=[pl.BlockSpec(memory_space=pl.ANY), hbm, hbm] + [vmem] * 8,
        out_specs=[hbm, vmem, vmem, vmem],
        out_shape=[
            jax.ShapeDtypeStruct((rows, width), f32),
            jax.ShapeDtypeStruct(half, bf16),
            jax.ShapeDtypeStruct(quarter, bf16),
            jax.ShapeDtypeStruct(quarter, bf16),
        ],
        scratch_shapes=[
            pltpu.VMEM((rows, width), bf16),
            pltpu.VMEM(languages.shape, languages.dtype),
            pltpu.VMEM((rows, width), bf16),
            pltpu.VMEM((rows, 3 * width), bf16),
            pltpu.VMEM((rows, width), f32),
            pltpu.VMEM(project.shape, f32),
            pltpu.SemaphoreType.DMA((3,)),
        ],
        compiler_params=pltpu.CompilerParams(vmem_limit_bytes=16 * MIB),
        cost_estimate=pl.CostEstimate(
            flops=64 * rows * width * width, bytes_accessed=8 * MIB, transcendentals=0
        ),
        name="char_attn_back",
    )(
        after,
        in_hbm(chars),
        in_hbm(languages),
        table,
        gain_attn,
        project,
        output,
        dmiddle,
        gain_mlp_grad,
        qkv,
        probs,
    )


WORD_SLOT = 416


def word_kernel(
    length,
    shards,
    own_ref,
    far_ref,
    section_ref,
    both_ref,
    cot_ref,
    cot_far_ref,
    input_ref,
    gain_attn_ref,
    project_ref,
    output_ref,
    gain_mlp_ref,
    expand_ref,
    shrink_ref,
    result_hbm,
    dpooled_ref,
    keep_ref,
    send_ref,
    pooled,
    pooled_t,
    dz,
    start,
    normed_t,
    qkv,
    kept,
    mixed_t,
    middle,
    normed_mlp_t,
    hidden,
    dbefore,
    dmixed,
    dqkv,
    dy,
    dstart,
    result,
    input_grad,
    project_grad,
    output_grad,
    expand_grad,
    shrink_grad,
    sem,
):
    total = pooled.shape[0]
    width = output_ref.shape[0]
    section, me = position()
    slabs = width // SLAB
    for place, ref in enumerate((own_ref, far_ref, section_ref, both_ref)):
        pooled[place * length : (place + 1) * length] = ref[...]
    for place, (ref, other) in enumerate(
        ((cot_ref, section), (cot_far_ref, section), (cot_ref, 1 - section), (cot_far_ref, 1 - section))
    ):
        dz[place * length : (place + 1) * length] = ref[other]

    x = dot(pooled[...], input_ref[...])
    start[...] = x
    normal, _ = unit(x)
    low = (normal * gain_attn_ref[...]).astype(bf16)
    normed_t[...] = low.T
    qkv[...] = dot(low, project_ref[...]).astype(bf16)
    tiles = [(block, slab) for block in range(total // BLOCK) for slab in range(slabs)]

    def load(tile, which):
        block, slab = tile
        at = which * width + slab * SLAB
        return qkv[block * BLOCK : (block + 1) * BLOCK, at : at + SLAB]

    mask_shape = (length, len(tiles) * HEADS * BLOCK)
    causal = rows_of(mask_shape) <= lanes(mask_shape) % length
    probs, mixed = attend(load, tiles, causal, length)
    kept[...] = probs
    for (block, slab), piece in zip(tiles, mixed):
        mixed_t[slab * SLAB : (slab + 1) * SLAB, block * BLOCK : (block + 1) * BLOCK] = piece
    x = x + dot(mixed_t[...].T, output_ref[...])
    middle[...] = x
    normal, _ = unit(x)
    low = (normal * gain_mlp_ref[...]).astype(bf16)
    normed_mlp_t[...] = low.T
    dz_all = dz[...]
    for at in range(0, expand_ref.shape[1], 256):
        part = slice(at, at + 256)
        value, bend = gelu_parts(dot(low, expand_ref[:, part]))
        hidden[:, part] = value.astype(bf16)
        dhidden = dot_nt(dz_all, shrink_ref[part, :]).astype(bf16)
        dbefore[:, part] = dhidden * bend.astype(bf16)
    result[...] = middle[:length] + dot(hidden[:length], shrink_ref[...])
    leave = pltpu.make_async_copy(result, result_hbm, sem)
    leave.start()

    dnormed = dot_nt(dbefore[...], expand_ref[...])
    normal, scale = unit(middle[...])
    gain_mlp_grad = jnp.sum(dnormed * normal, axis=0, keepdims=True)
    dmiddle = dz_all.astype(f32) + unit_back(dnormed, gain_mlp_ref[...], normal, scale)
    dy_low = dmiddle.astype(bf16)
    dy[...] = dy_low
    dmixed[...] = dot_nt(dy_low, output_ref[...]).astype(bf16)

    def load_dmixed(tile):
        block, slab = tile
        return dmixed[block * BLOCK : (block + 1) * BLOCK, slab * SLAB : (slab + 1) * SLAB]

    def store(tile, which, value):
        block, slab = tile
        at = which * width + slab * SLAB
        dqkv[block * BLOCK : (block + 1) * BLOCK, at : at + SLAB] = value

    attend_back(load, load_dmixed, tiles, kept[...], store, length)
    dnormed = dot_nt(dqkv[...], project_ref[...])
    normal, scale = unit(start[...])
    gain_attn_grad = jnp.sum(dnormed * normal, axis=0, keepdims=True)
    dword = (dmiddle + unit_back(dnormed, gain_attn_ref[...], normal, scale)).astype(bf16)
    dpooled_ref[...] = dot_nt(dword[:length], input_ref[...]).astype(bf16)
    dstart[...] = dword

    def shard_of(slot):
        return (me & 7) ^ ((slot >> 2) | ((slot & 3) << 1))

    def own_rows(flipped):
        many = flipped.shape[0] // 2
        return flipped[pl.ds(pl.multiple_of((me >> 3) * many, many), many), :]

    def half_columns(ref, place):
        many = ref.shape[1] // 2
        return ref[:, pl.ds(pl.multiple_of(place * many, many), many)]

    def own_columns(ref):
        return half_columns(ref, section)

    pooled_t[...] = pooled[...].T
    hidden_t = half_columns(hidden, me >> 3).T
    targets = slot_refs(keep_ref, send_ref)
    at = 0
    for lhs, rhs, ref in (
        (own_rows(pooled_t), own_columns(dstart), input_grad),
        (own_rows(normed_t), own_columns(dqkv), project_grad),
        (own_rows(mixed_t), own_columns(dy), output_grad),
        (own_rows(normed_mlp_t), own_columns(dbefore), expand_grad),
        (hidden_t, own_columns(dz), shrink_grad),
    ):
        ref[...] = dot(lhs, rhs)
        at = put_shards(ref, targets, shard_of, at)
    extra = jnp.concatenate(
        [gain_attn_grad[:, :SLAB], gain_attn_grad[:, SLAB:]]
        + [gain_mlp_grad[:, :SLAB], gain_mlp_grad[:, SLAB:]]
        + [jnp.zeros((12, SLAB), f32)],
        axis=0,
    ).astype(bf16)
    for ref, place in targets:
        ref[place, at : at + 16] = extra
    leave.wait()


def word_group(pooled, cotangents, word_input, weights, shards):
    gain_attn, project, output, gain_mlp, expand_w, shrink = weights
    length, channels = pooled[0].shape
    width = output.shape[0]
    hidden = expand_w.shape[1]
    total = 4 * length
    half = (4, WORD_SLOT, SLAB)
    vmem = pl.BlockSpec(memory_space=pltpu.VMEM)
    hbm = pl.BlockSpec(memory_space=pltpu.HBM)
    return pl.pallas_call(
        functools.partial(word_kernel, length, shards),
        in_specs=[vmem] * 13,
        out_specs=[hbm, vmem, vmem, vmem],
        out_shape=[
            jax.ShapeDtypeStruct((length, width), f32),
            jax.ShapeDtypeStruct((length, channels), bf16),
            jax.ShapeDtypeStruct(half, bf16),
            jax.ShapeDtypeStruct(half, bf16),
        ],
        scratch_shapes=[
            pltpu.VMEM((total, channels), bf16),
            pltpu.VMEM((channels, total), bf16),
            pltpu.VMEM((total, width), bf16),
            pltpu.VMEM((total, width), f32),
            pltpu.VMEM((width, total), bf16),
            pltpu.VMEM((total, 3 * width), bf16),
            pltpu.VMEM((length, total * (width // HEAD)), f32),
            pltpu.VMEM((width, total), bf16),
            pltpu.VMEM((total, width), f32),
            pltpu.VMEM((width, total), bf16),
            pltpu.VMEM((total, hidden), bf16),
            pltpu.VMEM((total, hidden), bf16),
            pltpu.VMEM((total, width), bf16),
            pltpu.VMEM((total, 3 * width), bf16),
            pltpu.VMEM((total, width), bf16),
            pltpu.VMEM((total, width), bf16),
            pltpu.VMEM((length, width), f32),
            pltpu.VMEM((channels // 2, width // 2), f32),
            pltpu.VMEM((width // 2, 3 * width // 2), f32),
            pltpu.VMEM((width // 2, width // 2), f32),
            pltpu.VMEM((width // 2, hidden // 2), f32),
            pltpu.VMEM((hidden // 2, width // 2), f32),
            pltpu.SemaphoreType.DMA,
        ],
        compiler_params=pltpu.CompilerParams(vmem_limit_bytes=20 * MIB),
        cost_estimate=pl.CostEstimate(
            flops=total * width * width * 25 * 4, bytes_accessed=8 * MIB, transcendentals=0
        ),
        name="word_group",
    )(*pooled, *cotangents, word_input, gain_attn, project, output, gain_mlp, expand_w, shrink)


def summed(*parts):
    return functools.reduce(lambda a, b: a + b, [part.astype(f32) for part in parts])


def added(*parts):
    return summed(*parts).astype(bf16)


def by_section(section, low, high):
    return (jnp.where(section == 0, low, high), jnp.where(section == 0, high, low))


def first_sum_kernel(word_keep, word_arrived, char_keep, char_arrived, *outs):
    *word, stay_ref, go_ref = outs
    section, _ = position()
    for place, ref in enumerate(word):
        ref[...] = added(word_keep[place], word_arrived[place])
    half = SLAB // 2
    for place in range(char_keep.shape[0]):
        total = added(char_keep[place], char_arrived[place])
        stay_ref[place], go_ref[place] = by_section(section, total[:, :half], total[:, half:])


def first_sum(word, char):
    half = jax.ShapeDtypeStruct(char[0].shape[:2] + (SLAB // 2,), bf16)
    *pieces, stay, go = pl.pallas_call(
        first_sum_kernel,
        out_shape=[jax.ShapeDtypeStruct((WORD_SLOT, SLAB), bf16)] * 4 + [half, half],
        compiler_params=pltpu.CompilerParams(vmem_limit_bytes=12 * MIB),
        name="first_sum",
    )(*word, *char)
    return (pieces, stay, go)


def second_sum_kernel(char, last_keep, arrived, arrived_more, *outs):
    half = SLAB // 2
    for place, out in enumerate(outs):
        at = CHAR_FIRST_SLOT
        for far in range(2):
            entry = 2 * place + far
            out[:CHAR_FIRST_SLOT, far * half : (far + 1) * half] = char[entry]
            many = arrived.shape[0]
            other = arrived[entry] if entry < many else arrived_more[entry - many]
            out[at : at + CHAR_LAST_SLOT] = added(last_keep[entry], other)
            at += CHAR_LAST_SLOT


def middle_sum_kernel(*refs):
    *pieces, stay, arrived, word_ref, char_ref = refs
    word_ref[...] = added(*[ref[...] for ref in pieces])
    char_ref[...] = added(stay[...], arrived[...])


def middle_sum(pieces, stay, arrived):
    return pl.pallas_call(
        middle_sum_kernel,
        out_shape=[
            jax.ShapeDtypeStruct(pieces[0].shape, bf16),
            jax.ShapeDtypeStruct(stay.shape, bf16),
        ],
        compiler_params=pltpu.CompilerParams(vmem_limit_bytes=12 * MIB),
        cost_estimate=pl.CostEstimate(
            flops=20_000_000_000, bytes_accessed=8 * MIB, transcendentals=0
        ),
        name="middle_sum",
    )(*pieces, stay, arrived)


def second_sum(first, last):
    rows = CHAR_FIRST_SLOT + 2 * CHAR_LAST_SLOT
    return pl.pallas_call(
        second_sum_kernel,
        out_shape=[jax.ShapeDtypeStruct((rows, SLAB), bf16)] * 4,
        compiler_params=pltpu.CompilerParams(vmem_limit_bytes=12 * MIB),
        name="second_sum",
    )(first, *last)


FOLD = 80


def plane_sum_kernel(*refs):
    word, char, near_ref, far_ref = (refs[0], refs[1:5], refs[5], refs[6])
    near_ref[:WORD_SLOT] = word[...]
    half = SLAB // 2
    for far, out, at in ((0, near_ref, WORD_SLOT), (1, far_ref, 0)):
        columns = slice(far * half, (far + 1) * half)
        total = added(*[ref[:CHAR_FIRST_SLOT, columns] for ref in char])
        out[at : at + FOLD, :half] = total[:FOLD]
        out[at : at + FOLD, half:] = total[CHAR_FIRST_SLOT - FOLD :]
        first = CHAR_FIRST_SLOT + far * CHAR_LAST_SLOT
        at += FOLD
        out[at : at + CHAR_LAST_SLOT] = added(
            *[ref[first : first + CHAR_LAST_SLOT] for ref in char]
        )


def plane_sum(word, char):
    rows = FOLD + CHAR_LAST_SLOT
    return pl.pallas_call(
        plane_sum_kernel,
        out_shape=[
            jax.ShapeDtypeStruct((WORD_SLOT + rows, SLAB), bf16),
            jax.ShapeDtypeStruct((rows, SLAB), bf16),
        ],
        compiler_params=pltpu.CompilerParams(vmem_limit_bytes=12 * MIB),
        name="plane_sum",
    )(word, *char)


def last_sum_kernel(near_ref, section_ref, high_ref, both_ref, *outs):
    word_rows = WORD_SLOT
    section, me = position()
    own = near_ref[:word_rows].astype(f32)
    halves = by_section(section, own, section_ref[:word_rows].astype(f32))
    half = SLAB // 2

    def unfold(near, far):
        total = summed(near[word_rows : word_rows + FOLD], far[:FOLD])
        return jnp.concatenate(
            [total[:, :half], total[2 * FOLD - CHAR_FIRST_SLOT :, half:]], axis=0
        )

    first = jnp.concatenate(
        by_section(section, unfold(near_ref, high_ref), unfold(section_ref, both_ref)), axis=1
    )
    last = summed(
        near_ref[word_rows + FOLD :],
        section_ref[word_rows + FOLD :],
        high_ref[FOLD:],
        both_ref[FOLD:],
    )

    def mine(vector, size):
        turned = pltpu.roll(vector, lax.rem(SLAB - lax.rem(me * size, SLAB), SLAB), 1)
        return turned[:, :size]

    (
        table_ref,
        gain_attn_ref,
        project_ref,
        output_ref,
        gain_mlp_ref,
        expand_ref,
        shrink_ref,
        w_input_ref,
        w_gain_attn_ref,
        w_project_ref,
        w_output_ref,
        w_gain_mlp_ref,
        w_expand_ref,
        w_shrink_ref,
    ) = outs
    for char, refs in ((first, (expand_ref, shrink_ref, output_ref)), (last, (project_ref,))):
        at = 0
        for ref in refs:
            size = ref.shape[0]
            for column in range(ref.shape[1] // SLAB):
                ref[:, column * SLAB : (column + 1) * SLAB] = char[at : at + size]
                at += size
    size = gain_attn_ref.shape[1]
    extra = last[at : at + 16]
    turned = mine(extra, size)
    gain_attn_ref[...] = turned[0:1]
    gain_mlp_ref[...] = turned[1:2]
    table_ref[...] = turned[8:16]
    at = 0
    for ref in (w_input_ref, w_project_ref, w_output_ref, w_expand_ref, w_shrink_ref):
        size = ref.shape[0]
        columns = ref.shape[1] // (2 * SLAB)
        for column in range(columns):
            for half in range(2):
                first = (half * columns + column) * SLAB
                ref[:, first : first + SLAB] = halves[half][at : at + size]
            at += size
    size = w_gain_attn_ref.shape[1]
    extra = own[at : at + 8]
    turned = mine(extra, size)
    upper = me * size >= SLAB
    w_gain_attn_ref[...] = jnp.where(upper, turned[1:2], turned[0:1])
    w_gain_mlp_ref[...] = jnp.where(upper, turned[3:4], turned[2:3])


def last_sum(near, arrived, shapes):
    return pl.pallas_call(
        last_sum_kernel,
        out_shape=[jax.ShapeDtypeStruct(shape, f32) for shape in shapes],
        compiler_params=pltpu.CompilerParams(vmem_limit_bytes=12 * MIB),
        name="last_sum",
    )(near, *arrived)


def exchange(value, section_bit, dp_bits):
    shards = lax.axis_size("dp")
    pairs = [
        (s * shards + d, (s ^ section_bit) * shards + (d ^ dp_bits))
        for s in range(lax.axis_size("section"))
        for d in range(shards)
    ]
    return lax.ppermute(value, ("section", "dp"), pairs)


CORE, SIDE, NEAR, FAR = (1, 2, 4, 8)


def plane_exchange(pieces):
    return (pieces[0],) + tuple(
        exchange(piece, 0, bits) for piece, bits in zip(pieces[1:], (SIDE, NEAR, SIDE | NEAR))
    )


def local_grouped(
    chars, counts, languages, language_table, char_weights, word_input, word_weights, cotangent
):
    shards = lax.axis_size("dp")
    micros, _, words, slots, width = chars.shape
    rows = words * slots
    cot = cotangent[:, 0]
    cot_far = exchange(cot, 0, FAR)
    char_weights = tuple(w[None] if w.ndim == 1 else w for w in char_weights)
    word_weights = tuple(w[None] if w.ndim == 1 else w for w in word_weights)
    chars = chars.reshape(micros, rows, width)
    counts = counts.reshape(micros, 1, words)
    languages = languages.reshape(1, micros)
    pooled, *stored = char_forward(languages, chars, counts, language_table, char_weights, slots)
    others = (exchange(pooled, 0, FAR), exchange(pooled, 1, 0), exchange(pooled, 1, FAR))
    result, dpooled, keep, send = word_group(
        (pooled,) + others, (cot, cot_far), word_input, word_weights, shards
    )
    word = (keep, exchange(send, 0, CORE))
    dmiddle, gain_mlp_grad, keep, send = char_mlp_back(
        counts, char_weights, dpooled, stored, slots, shards
    )
    pieces, stay, go = first_sum(word, (keep, exchange(send, 0, CORE)))
    word = plane_exchange(pieces)
    arrived = exchange(go, 1, 0)
    chars_grad, keep, *sends = char_attn_back(
        languages,
        chars,
        language_table,
        char_weights,
        dmiddle,
        gain_mlp_grad,
        stored,
        slots,
        shards,
        stay,
    )
    last = (keep,) + tuple(exchange(send, 0, CORE) for send in sends)
    word, first = middle_sum(word, stay, arrived)
    char = plane_exchange(second_sum(first, last))
    near, far = plane_sum(word, char)
    arrived = (exchange(near, 1, 0), exchange(far, 0, FAR), exchange(far, 1, FAR))
    shapes = [(language_table.shape[0], language_table.shape[1] // shards)]
    for weight in char_weights + (word_input,) + word_weights:
        if weight.shape[0] == 1:
            shapes.append((1, weight.shape[1] // shards))
        else:
            shapes.append((weight.shape[0] // shards, weight.shape[1]))
    totals = last_sum(near, arrived, shapes)
    totals = [total[0] if total.shape[0] == 1 else total for total in totals]
    return (result[None, None], chars_grad.reshape((1, 1, words, slots, width))) + tuple(totals)


def norm_forward(inputs, gain):
    return inputs * lax.rsqrt(jnp.mean(inputs * inputs, axis=-1, keepdims=True) + eps) * gain


def attend_forward(normed, project, head_count, key_mask):
    row_count, length, channels = normed.shape
    head_size = channels // head_count
    qkv = jnp.einsum("blc,cf->blf", normed, project, preferred_element_type=jnp.float32).astype(
        jnp.bfloat16
    )
    pieces = qkv.reshape(row_count, length, 3, head_count, head_size)
    scores = jnp.einsum(
        "bqhd,bkhd->bhqk", pieces[:, :, 0], pieces[:, :, 1], preferred_element_type=jnp.float32
    ) * head_size ** (-0.5)
    scores = jnp.where(key_mask, scores, -1e30)
    row_max = jnp.max(scores, axis=-1, keepdims=True)
    weights_exp = jnp.exp(scores - row_max)
    row_total = jnp.sum(weights_exp, axis=-1, keepdims=True)
    attn_probs = (weights_exp / row_total).astype(jnp.bfloat16)
    mixed_heads = jnp.einsum(
        "bhqk,bkhd->bqhd", attn_probs, pieces[:, :, 2], preferred_element_type=jnp.float32
    )
    mixed_heads = mixed_heads.reshape(row_count, length, channels).astype(jnp.bfloat16)
    return (qkv, row_max + jnp.log(row_total), mixed_heads)


def attend_backward(
    normed, project, output, qkv, logsum, mixed_heads, dmiddle_low, head_count, key_mask
):
    row_count, length, channels = normed.shape
    head_size = channels // head_count
    scaling = head_size ** (-0.5)
    output_grad = jnp.einsum(
        "blc,bld->cd", mixed_heads, dmiddle_low, preferred_element_type=jnp.float32
    )
    dmixed = jnp.einsum(
        "bld,cd->blc", dmiddle_low, output, preferred_element_type=jnp.float32
    ).astype(jnp.bfloat16)
    dmixed = dmixed.reshape(row_count, length, head_count, head_size)
    pieces = qkv.reshape(row_count, length, 3, head_count, head_size)
    scores = (
        jnp.einsum(
            "bqhd,bkhd->bhqk", pieces[:, :, 0], pieces[:, :, 1], preferred_element_type=jnp.float32
        )
        * scaling
    )
    scores = jnp.where(key_mask, scores, -1e30)
    attn_probs = jnp.exp(scores - logsum)
    dprobs = jnp.einsum(
        "bqhd,bkhd->bhqk", dmixed, pieces[:, :, 2], preferred_element_type=jnp.float32
    )
    row_delta = jnp.sum(attn_probs * dprobs, axis=-1, keepdims=True)
    dscores = (attn_probs * (dprobs - row_delta)).astype(jnp.bfloat16)
    dquery = (
        jnp.einsum("bhqk,bkhd->bqhd", dscores, pieces[:, :, 1], preferred_element_type=jnp.float32)
        * scaling
    )
    dkeys = (
        jnp.einsum("bhqk,bqhd->bkhd", dscores, pieces[:, :, 0], preferred_element_type=jnp.float32)
        * scaling
    )
    dvalues = jnp.einsum(
        "bhqk,bqhd->bkhd",
        attn_probs.astype(jnp.bfloat16),
        dmixed,
        preferred_element_type=jnp.float32,
    )
    dqkv = (
        jnp.stack([dquery, dkeys, dvalues], axis=2)
        .reshape(row_count, length, 3 * channels)
        .astype(jnp.bfloat16)
    )
    project_grad = jnp.einsum("blc,blf->cf", normed, dqkv, preferred_element_type=jnp.float32)
    dnormed = jnp.einsum("blf,cf->blc", dqkv, project, preferred_element_type=jnp.float32)
    return (dnormed, project_grad, output_grad)


def block_forward(inputs, weights, head_count, key_mask):
    gain_attn, project, output, gain_mlp, expand, shrink = weights
    normed = norm_forward(inputs, gain_attn).astype(jnp.bfloat16)
    qkv, logsum, mixed_heads = attend_forward(normed, project, head_count, key_mask)
    middle = inputs + jnp.einsum(
        "blc,cd->bld", mixed_heads, output, preferred_element_type=jnp.float32
    )
    normed_mlp = norm_forward(middle, gain_mlp).astype(jnp.bfloat16)
    before = jnp.einsum("blc,cf->blf", normed_mlp, expand, preferred_element_type=jnp.float32)
    hidden = jax.nn.gelu(before).astype(jnp.bfloat16)
    result = middle + jnp.einsum("blf,fc->blc", hidden, shrink, preferred_element_type=jnp.float32)
    return (result, (inputs, normed, qkv, logsum, mixed_heads, middle, normed_mlp, before, hidden))


def block_backward(dresult, stored, weights, head_count, key_mask):
    gain_attn, project, output, gain_mlp, expand, shrink = weights
    inputs, normed, qkv, logsum, mixed_heads, middle, normed_mlp, before, hidden = stored
    grad_low = dresult.astype(jnp.bfloat16)
    shrink_grad = jnp.einsum("blf,blc->fc", hidden, grad_low, preferred_element_type=jnp.float32)
    dhidden = jnp.einsum(
        "blc,fc->blf", grad_low, shrink, preferred_element_type=jnp.float32
    ).astype(jnp.bfloat16)
    gelu_pull = jax.vjp(jax.nn.gelu, before)[1]
    dbefore = gelu_pull(dhidden.astype(jnp.float32))[0].astype(jnp.bfloat16)
    expand_grad = jnp.einsum("blc,blf->cf", normed_mlp, dbefore, preferred_element_type=jnp.float32)
    dnormed_mlp = jnp.einsum("blf,cf->blc", dbefore, expand, preferred_element_type=jnp.float32)
    norm_pull = jax.vjp(norm_forward, middle, gain_mlp)[1]
    dmiddle_norm, gain_mlp_grad = norm_pull(dnormed_mlp)
    dmiddle = dresult + dmiddle_norm
    dnormed, project_grad, output_grad = attend_backward(
        normed,
        project,
        output,
        qkv,
        logsum,
        mixed_heads,
        dmiddle.astype(jnp.bfloat16),
        head_count,
        key_mask,
    )
    first_pull = jax.vjp(norm_forward, inputs, gain_attn)[1]
    dinputs_norm, gain_attn_grad = first_pull(dnormed)
    return (
        dmiddle + dinputs_norm,
        (gain_attn_grad, project_grad, output_grad, gain_mlp_grad, expand_grad, shrink_grad),
    )


def char_front(char_text, char_count, language, lang_table, weights):
    present = lax.broadcasted_iota(jnp.int32, char_text.shape[:2], 1) < char_count[:, None]
    onehot = (lax.broadcasted_iota(jnp.int32, (lang_table.shape[0],), 0) == language).astype(
        jnp.bfloat16
    )
    lang_row = jnp.dot(onehot, lang_table, preferred_element_type=jnp.float32)
    inputs = char_text.astype(jnp.float32) + lang_row
    result, stored = block_forward(inputs, weights, CH, present[:, None, None, :])
    summed = jnp.sum(jnp.where(present[:, :, None], result, 0.0), axis=1)
    pooled = (summed / char_count[:, None].astype(jnp.float32)).astype(jnp.bfloat16)
    return (pooled, stored, present, onehot)


def char_back(stored, present, onehot, char_count, dpooled, weights):
    spread = dpooled.astype(jnp.float32) / char_count[:, None].astype(jnp.float32)
    dresult = jnp.where(present[:, :, None], spread[:, None, :], 0.0)
    dinputs, gradients = block_backward(dresult, stored, weights, CH, present[:, None, None, :])
    table_grad = onehot.astype(jnp.float32)[:, None] * jnp.sum(dinputs, axis=(0, 1))[None, :]
    return (dinputs, (table_grad,) + gradients)


def word_full(pooled, cot_rows, word_input, weights):
    length = pooled.shape[0]
    word_start = jnp.dot(pooled, word_input, preferred_element_type=jnp.float32)[None]
    causal = (
        lax.broadcasted_iota(jnp.int32, (length, length), 0)
        >= lax.broadcasted_iota(jnp.int32, (length, length), 1)
    )[None, None]
    result, stored = block_forward(word_start, weights, H, causal)
    dstart, gradients = block_backward(
        cot_rows.astype(jnp.float32)[None], stored, weights, H, causal
    )
    grad_low = dstart[0].astype(jnp.bfloat16)
    input_grad = jnp.einsum("wc,wd->cd", pooled, grad_low, preferred_element_type=jnp.float32)
    dpooled = jnp.einsum(
        "wd,cd->wc", grad_low, word_input, preferred_element_type=jnp.float32
    ).astype(jnp.bfloat16)
    return (result[0], dpooled, (input_grad,) + gradients)


def reduce_rows(gradients):
    shards = lax.axis_size("dp")
    flat = []
    for place, gradient in enumerate(gradients):
        if place == 0:
            gradient = gradient.T
        flat.append(gradient.astype(jnp.bfloat16).reshape(shards, -1))
    packed = jnp.concatenate(flat, axis=1)
    me = lax.axis_index("dp")
    packed = jnp.take(packed, jnp.arange(shards) ^ me, axis=0)
    bit = 1
    while packed.shape[0] > 1:
        pairs = packed.reshape(packed.shape[0] // 2, 2, packed.shape[1])
        arrived = lax.ppermute(pairs[:, 1], "dp", [(i, i ^ bit) for i in range(shards)])
        packed = (pairs[:, 0].astype(jnp.float32) + arrived.astype(jnp.float32)).astype(
            jnp.bfloat16
        )
        bit *= 2
    arrived = lax.ppermute(packed, "section", [(0, 1), (1, 0)])
    total = (packed.astype(jnp.float32) + arrived.astype(jnp.float32))[0]
    outs = []
    at = 0
    for place, gradient in enumerate(gradients):
        size = gradient.size // shards
        piece = total[at : at + size]
        at += size
        if place == 0:
            outs.append(piece.reshape(-1, gradient.shape[0]).T)
        else:
            outs.append(piece.reshape((gradient.shape[0] // shards,) + gradient.shape[1:]))
    return tuple(outs)


def local(
    chars,
    counts,
    languages,
    language_table,
    char_gain_attn,
    char_project,
    char_output,
    char_gain_mlp,
    char_expand,
    char_shrink,
    word_input,
    word_gain_attn,
    word_project,
    word_output,
    word_gain_mlp,
    word_expand,
    word_shrink,
    cotangent,
):
    char_weights = (
        char_gain_attn,
        char_project,
        char_output,
        char_gain_mlp,
        char_expand,
        char_shrink,
    )
    word_weights = (
        word_gain_attn,
        word_project,
        word_output,
        word_gain_mlp,
        word_expand,
        word_shrink,
    )
    if lax.axis_size("dp") == 16:
        return local_grouped(
            chars,
            counts,
            languages,
            language_table,
            char_weights,
            word_input,
            word_weights,
            cotangent,
        )
    section_index = lax.axis_index("section")
    char_text = chars[section_index, 0]
    char_count = counts[section_index, 0]
    language = languages[section_index, 0]
    cot_rows = cotangent[section_index, 0]
    pooled, stored, present, onehot = char_front(
        char_text, char_count, language, language_table, char_weights
    )
    result, dpooled, word_grads = word_full(pooled, cot_rows, word_input, word_weights)
    text_grad, char_grads = char_back(stored, present, onehot, char_count, dpooled, char_weights)
    totals = reduce_rows(char_grads + word_grads)
    return (result[None, None], text_grad[None, None]) + totals


def solution(mesh):
    placed = (
        P(None, "dp", None, None, None),
        P(None, "dp", None),
        P(None, "dp"),
        P(),
        P(),
        P(),
        P(),
        P(),
        P(),
        P(),
        P(),
        P(),
        P(),
        P(),
        P(),
        P(),
        P(),
        P(None, "dp", None, None),
    )
    return jax.shard_map(
        local,
        mesh=mesh,
        in_specs=placed,
        out_specs=(
            P("section", "dp", None, None),
            P("section", "dp", None, None, None),
            P(None, "dp"),
            P("dp"),
            P("dp", None),
            P("dp", None),
            P("dp"),
            P("dp", None),
            P("dp", None),
            P("dp", None),
            P("dp"),
            P("dp", None),
            P("dp", None),
            P("dp"),
            P("dp", None),
            P("dp", None),
        ),
        check_vma=False,
    )
```

```python
import functools

import jax
import jax.numpy as jnp
from jax import lax
from jax.experimental import pallas as pl
from jax.experimental.pallas import tpu as pltpu
from jax.sharding import PartitionSpec as P

CH = 4
H = 8
HEAD = 64
SLAB = 256
HEADS = SLAB // HEAD
BLOCK = 128
MIB = 1024 * 1024

eps = 1e-05

f32 = jnp.float32
bf16 = jnp.bfloat16


def dot(a, b):
    return jnp.dot(a, b, preferred_element_type=f32)


def dot_nt(a, b):
    return lax.dot_general(a, b, (((1,), (1,)), ((), ())), preferred_element_type=f32)


def position():
    return (lax.axis_index("section"), lax.axis_index("dp"))


def lanes(shape):
    return lax.broadcasted_iota(jnp.int32, shape, 1)


def rows_of(shape):
    return lax.broadcasted_iota(jnp.int32, shape, 0)


def stack_heads(a):
    head = lanes((1, SLAB)) // HEAD
    masks = [jnp.where(head == place, 1.0, 0.0).astype(bf16) for place in range(HEADS)]
    return jnp.concatenate([a * mask for mask in masks], axis=0)


def compact(scores, length):
    group = lanes((length, BLOCK)) // length
    total = scores[:length]
    for place in range(1, BLOCK // length):
        total = jnp.where(group == place, scores[place * length : (place + 1) * length], total)
    return total


def compact_heads(scores, length):
    return [
        compact(scores[:, head * BLOCK : (head + 1) * BLOCK], length) for head in range(HEADS)
    ]


def expand(values, length):
    group = lanes((length, BLOCK)) // length
    return jnp.concatenate(
        [jnp.where(group == place, values, 0.0) for place in range(BLOCK // length)], axis=0
    ).astype(bf16)


def expand_heads(values, tile, length):
    first = tile * HEADS * BLOCK
    return [
        expand(values[:, first + head * BLOCK : first + (head + 1) * BLOCK], length)
        for head in range(HEADS)
    ]


def head_rows(a, head):
    return a[head * HEAD : (head + 1) * HEAD]


def attend(load, tiles, key_mask, length):
    scores = []
    for tile in tiles:
        scores += compact_heads(dot_nt(load(tile, 1), stack_heads(load(tile, 0))), length)
    scores = jnp.concatenate(scores, axis=1) * HEAD**-0.5
    scores = jnp.where(key_mask, scores, -1e30)
    weights = jnp.exp(scores - jnp.max(scores, axis=0, keepdims=True))
    probs = weights / jnp.sum(weights, axis=0, keepdims=True)
    mixed = []
    for number, tile in enumerate(tiles):
        values = load(tile, 2).T
        parts = expand_heads(probs, number, length)
        mixed.append(
            jnp.concatenate(
                [dot(head_rows(values, head), parts[head]) for head in range(HEADS)], axis=0
            ).astype(bf16)
        )
    return (probs, mixed)


def attend_back(load, load_dmixed, tiles, probs, store, length):
    dprobs = []
    for number, tile in enumerate(tiles):
        stacked = stack_heads(load_dmixed(tile))
        dprobs += compact_heads(dot_nt(load(tile, 2), stacked), length)
        parts = jnp.concatenate(expand_heads(probs, number, length), axis=1)
        store(tile, 2, dot(parts, stacked).astype(bf16))
    dprobs = jnp.concatenate(dprobs, axis=1)
    dscores = probs * (dprobs - jnp.sum(probs * dprobs, axis=0, keepdims=True))
    scaling = HEAD**-0.5
    for number, tile in enumerate(tiles):
        parts = expand_heads(dscores, number, length)
        keys = load(tile, 1).T
        dq = jnp.concatenate(
            [dot(head_rows(keys, head), parts[head]) for head in range(HEADS)], axis=0
        )
        store(tile, 0, (dq * scaling).astype(bf16).T)
        dk = dot(jnp.concatenate(parts, axis=1), stack_heads(load(tile, 0)))
        store(tile, 1, (dk * scaling).astype(bf16))


def unit(x):
    scale = lax.rsqrt(jnp.mean(x * x, axis=-1, keepdims=True) + eps)
    return (x * scale, scale)


def unit_back(dnormed, gain, normal, scale):
    weighted = dnormed * gain
    return scale * (weighted - normal * jnp.mean(normal * weighted, axis=-1, keepdims=True))


def gelu_parts(before):
    c = 0.7978845608028654
    before = before.astype(bf16)
    square = before * before
    half = bf16(0.5) * jnp.tanh(before * (bf16(c) + bf16(c * 0.044715) * square)) + bf16(0.5)
    value = before * half
    slope = half + value * (bf16(1.0) - half) * (bf16(2.0 * c) + bf16(6.0 * c * 0.044715) * square)
    return (value, slope)


def pick(row, place):
    return jnp.sum(jnp.where(lanes(row.shape) == place, row, 0), axis=1, keepdims=True)


def char_rows(chars, table_ref, language):
    table = table_ref[...].astype(f32)
    row = jnp.sum(jnp.where(rows_of(table.shape) == language, table, 0.0), axis=0, keepdims=True)
    return chars.astype(f32) + row


def counts_by_row(counts, rows, slots):
    words = counts.shape[-1]
    counts = jnp.broadcast_to(counts.astype(f32), (8, words)).astype(bf16)
    shape = (words, rows)
    member = lanes(shape) // slots == rows_of(shape)
    return dot(counts, jnp.where(member, 1.0, 0.0).astype(bf16))[:1]


def counts_column(counts):
    words = counts.shape[-1]
    shape = (words, words)
    spread = jnp.broadcast_to(counts.astype(f32), shape)
    return jnp.sum(
        jnp.where(rows_of(shape) == lanes(shape), spread, 0.0), axis=1, keepdims=True
    )


def fetch_all(sources, targets, sems):
    fetches = [
        pltpu.make_async_copy(source, target, sems.at[place])
        for place, (source, target) in enumerate(zip(sources, targets))
    ]
    for fetch in fetches:
        fetch.start()
    return fetches


def in_hbm(array):
    return pltpu.with_memory_space_constraint(array, pltpu.HBM)


def char_forward_kernel(
    slots,
    chars_hbm,
    languages_hbm,
    counts_hbm,
    table_hbm,
    gain_attn_hbm,
    project_hbm,
    output_hbm,
    gain_mlp_hbm,
    expand_hbm,
    shrink_hbm,
    pooled_ref,
    hidden_sum_ref,
    qkv_ref,
    probs_ref,
    mixed_ref,
    middle_ref,
    slope_ref,
    chars_ref,
    languages_ref,
    counts_ref,
    table_ref,
    gain_attn_ref,
    project_ref,
    output_ref,
    gain_mlp_ref,
    expand_ref,
    shrink_ref,
    sems,
):
    section, _ = position()
    fetches = fetch_all(
        (
            languages_hbm,
            counts_hbm,
            table_hbm,
            gain_attn_hbm,
            chars_hbm.at[section],
            project_hbm,
            output_hbm,
            gain_mlp_hbm,
            expand_hbm,
            shrink_hbm,
        ),
        (
            languages_ref,
            counts_ref,
            table_ref,
            gain_attn_ref,
            chars_ref,
            project_ref,
            output_ref,
            gain_mlp_ref,
            expand_ref,
            shrink_ref,
        ),
        sems,
    )
    for fetch in fetches[:2]:
        fetch.wait()
    counts = counts_ref[section]
    rows = chars_ref.shape[0]
    words = counts.shape[-1]
    row_counts = counts_by_row(counts, rows, slots)
    for fetch in fetches[2:5]:
        fetch.wait()
    x = char_rows(chars_ref[...], table_ref, pick(languages_ref[...], section))
    normal, _ = unit(x)
    normed = (normal * gain_attn_ref[...]).astype(bf16)
    fetches[5].wait()
    qkv_ref[...] = dot(normed, project_ref[...]).astype(bf16)
    blocks = range(rows // BLOCK)

    def load(block, which):
        return qkv_ref[block * BLOCK : (block + 1) * BLOCK, which * SLAB : (which + 1) * SLAB]

    by_head = jnp.concatenate(
        [row_counts[:, block * BLOCK : (block + 1) * BLOCK] for block in blocks for _ in range(HEADS)],
        axis=1,
    )
    key_mask = rows_of((slots, rows * HEADS)).astype(f32) < by_head
    probs, mixed = attend(load, blocks, key_mask, slots)
    probs_ref[...] = probs
    for block in blocks:
        mixed_ref[:, block * BLOCK : (block + 1) * BLOCK] = mixed[block]
    mixed = mixed_ref[...].T
    fetches[6].wait()
    middle = x + dot(mixed, output_ref[...])
    middle_ref[...] = middle
    normal, _ = unit(middle)
    fetches[7].wait()
    normed = (normal * gain_mlp_ref[...]).astype(bf16)
    word_shape = (words, rows)
    lane = lanes(word_shape)
    member = (lane // slots == rows_of(word_shape)) & ((lane % slots).astype(f32) < row_counts)
    member = jnp.where(member, 1.0, 0.0).astype(bf16)
    fetches[8].wait()
    for at in range(0, expand_ref.shape[1], 256):
        part = slice(at, at + 256)
        value, slope = gelu_parts(dot(normed, expand_ref[:, part]))
        slope_ref[:, part] = slope
        hidden_sum_ref[:, part] = dot(member, value).astype(bf16)
    high = middle.astype(bf16)
    low = (middle - high.astype(f32)).astype(bf16)
    fetches[9].wait()
    total = dot(member, high) + dot(member, low) + dot(hidden_sum_ref[...], shrink_ref[...])
    pooled_ref[...] = (total / counts_column(counts)).astype(bf16)


def char_forward(languages, chars, counts, table, weights, slots):
    rows, width = chars.shape[1:]
    words = rows // slots
    hidden = weights[4].shape[1]
    vmem = pl.BlockSpec(memory_space=pltpu.VMEM)
    hbm = pl.BlockSpec(memory_space=pltpu.HBM)
    fetched = (languages, counts, table) + tuple(weights)
    return pl.pallas_call(
        functools.partial(char_forward_kernel, slots),
        in_specs=[hbm] * 10,
        out_specs=[vmem] * 7,
        out_shape=[
            jax.ShapeDtypeStruct((words, width), bf16),
            jax.ShapeDtypeStruct((words, hidden), bf16),
            jax.ShapeDtypeStruct((rows, 3 * width), bf16),
            jax.ShapeDtypeStruct((slots, rows * HEADS), f32),
            jax.ShapeDtypeStruct((width, rows), bf16),
            jax.ShapeDtypeStruct((rows, width), f32),
            jax.ShapeDtypeStruct((rows, hidden), bf16),
        ],
        scratch_shapes=[pltpu.VMEM(chars.shape[1:], bf16)]
        + [pltpu.VMEM(array.shape, array.dtype) for array in fetched]
        + [pltpu.SemaphoreType.DMA((10,))],
        compiler_params=pltpu.CompilerParams(vmem_limit_bytes=16 * MIB),
        cost_estimate=pl.CostEstimate(
            flops=64 * rows * width * width, bytes_accessed=8 * MIB, transcendentals=0
        ),
        name="char_forward",
    )(*[in_hbm(array) for array in (chars,) + fetched])


CHAR_FIRST_SLOT = 144
CHAR_LAST_SLOT = 48


def char_shard(slot, me):
    return me ^ ((slot >> 3) | (((slot >> 1) & 3) << 1) | ((slot & 1) << 3))


def put_shards(gradient, slots, shard_of, at):
    width = SLAB
    columns = gradient.shape[1] // width
    size = gradient.shape[0] // len(slots)
    for number, slot in enumerate(slots):
        first = pl.multiple_of(shard_of(number) * size, size)
        for column in range(columns):
            start = at + column * size
            slot[start : start + size] = gradient[
                pl.ds(first, size), column * width : (column + 1) * width
            ].astype(bf16)
    return at + size * columns


def slot_refs(*refs):
    return [ref.at[place] for ref in refs for place in range(ref.shape[0])]


def char_mlp_back_kernel(
    slots,
    shards,
    counts_hbm,
    gain_mlp_ref,
    expand_ref,
    shrink_ref,
    dpooled_ref,
    hidden_sum_ref,
    mixed_ref,
    middle_ref,
    slope_ref,
    dmiddle_ref,
    gain_ref,
    keep_ref,
    send_ref,
    counts_ref,
    dhidden_words,
    dbefore,
    expand_grad,
    shrink_grad,
    output_grad,
    sem,
):
    section, me = position()
    fetch = pltpu.make_async_copy(counts_hbm, counts_ref, sem)
    fetch.start()
    fetch.wait()
    counts = counts_ref[section]
    rows, width = middle_ref.shape
    words = counts.shape[-1]
    spread = dpooled_ref[...].astype(f32) / counts_column(counts)
    spread_high = spread.astype(bf16)
    spread_low = (spread - spread_high.astype(f32)).astype(bf16)
    dhidden_words[...] = dot_nt(spread_high, shrink_ref[...]).astype(bf16)
    shape = (rows, words)
    row = rows_of(shape)
    member = (row // slots == lanes(shape)) & (row % slots < counts)
    member = jnp.where(member, 1.0, 0.0).astype(bf16)
    for at in range(0, expand_ref.shape[1], 256):
        part = slice(at, at + 256)
        dbefore[:, part] = dot(member, dhidden_words[:, part]).astype(bf16) * slope_ref[:, part]
    dnormed = dot_nt(dbefore[...], expand_ref[...])
    normal, scale = unit(middle_ref[...])
    normed_t = (normal * gain_mlp_ref[...]).astype(bf16).T
    gain_ref[...] = jnp.broadcast_to(
        jnp.sum(dnormed * normal, axis=0, keepdims=True), gain_ref.shape
    )
    dmiddle = (
        dot(member, spread_high)
        + dot(member, spread_low)
        + unit_back(dnormed, gain_mlp_ref[...], normal, scale)
    )
    dmiddle_ref[...] = dmiddle
    expand_grad[...] = dot(normed_t, dbefore[...])
    shrink_grad[...] = dot(hidden_sum_ref[...].T, spread_high)
    output_grad[...] = dot(mixed_ref[...], dmiddle.astype(bf16))
    targets = slot_refs(keep_ref, send_ref)
    at = 0
    for gradient in (expand_grad, shrink_grad, output_grad):
        at = put_shards(gradient, targets, lambda slot: char_shard(slot, me), at)


def char_mlp_back(counts, weights, dpooled, stored, slots, shards):
    _, _, output, gain_mlp, expand_w, shrink = weights
    hidden_sum, _, _, mixed, middle, slope = stored
    rows, width = middle.shape
    words = rows // slots
    hidden = expand_w.shape[1]
    half = (shards // 2, CHAR_FIRST_SLOT, width)
    vmem = pl.BlockSpec(memory_space=pltpu.VMEM)
    hbm = pl.BlockSpec(memory_space=pltpu.HBM)
    return pl.pallas_call(
        functools.partial(char_mlp_back_kernel, slots, shards),
        in_specs=[hbm] + [vmem] * 8,
        out_specs=[vmem] * 4,
        out_shape=[
            jax.ShapeDtypeStruct((rows, width), f32),
            jax.ShapeDtypeStruct((8, width), f32),
            jax.ShapeDtypeStruct(half, bf16),
            jax.ShapeDtypeStruct(half, bf16),
        ],
        scratch_shapes=[
            pltpu.VMEM(counts.shape, counts.dtype),
            pltpu.VMEM((words, hidden), bf16),
            pltpu.VMEM((rows, hidden), bf16),
            pltpu.VMEM(expand_w.shape, f32),
            pltpu.VMEM(shrink.shape, f32),
            pltpu.VMEM(output.shape, f32),
            pltpu.SemaphoreType.DMA,
        ],
        compiler_params=pltpu.CompilerParams(vmem_limit_bytes=16 * MIB),
        cost_estimate=pl.CostEstimate(
            flops=64 * rows * width * width, bytes_accessed=8 * MIB, transcendentals=0
        ),
        name="char_mlp_back",
    )(in_hbm(counts), gain_mlp, expand_w, shrink, dpooled, hidden_sum, mixed, middle, slope)


def char_attn_back_kernel(
    slots,
    shards,
    _,
    chars_hbm,
    languages_hbm,
    table_ref,
    gain_attn_ref,
    project_ref,
    output_ref,
    dmiddle_ref,
    gain_mlp_grad_ref,
    qkv_ref,
    probs_ref,
    grad_hbm,
    keep_ref,
    send_ref,
    chars_ref,
    languages_ref,
    dmixed,
    dqkv,
    grad,
    project_grad,
    sems,
):
    section, me = position()
    fetches = fetch_all(
        (chars_hbm.at[section], languages_hbm), (chars_ref, languages_ref), sems
    )
    rows, width = dmiddle_ref.shape
    dmixed[...] = dot_nt(dmiddle_ref[...].astype(bf16), output_ref[...]).astype(bf16)

    def load(block, which):
        return qkv_ref[block * BLOCK : (block + 1) * BLOCK, which * SLAB : (which + 1) * SLAB]

    def load_dmixed(block):
        return dmixed[block * BLOCK : (block + 1) * BLOCK]

    def store(block, which, value):
        dqkv[block * BLOCK : (block + 1) * BLOCK, which * SLAB : (which + 1) * SLAB] = value

    attend_back(load, load_dmixed, range(rows // BLOCK), probs_ref[...], store, slots)
    dnormed = dot_nt(dqkv[...], project_ref[...])
    for fetch in fetches:
        fetch.wait()
    language = pick(languages_ref[...], section)
    normal, scale = unit(char_rows(chars_ref[...], table_ref, language))
    gain_attn_grad = jnp.sum(dnormed * normal, axis=0, keepdims=True)
    dx = dmiddle_ref[...] + unit_back(dnormed, gain_attn_ref[...], normal, scale)
    grad[...] = dx
    leave = pltpu.make_async_copy(grad, grad_hbm, sems.at[2])
    leave.start()
    row_sum = jnp.sum(dx, axis=0, keepdims=True)
    normed_t = (normal * gain_attn_ref[...]).astype(bf16).T
    project_grad[...] = dot(normed_t, dqkv[...])
    targets = [
        ref.at[pl.ds(place * CHAR_LAST_SLOT, CHAR_LAST_SLOT)]
        for ref in (keep_ref, send_ref)
        for place in range(shards // 2)
    ]
    put_shards(project_grad, targets, lambda slot: char_shard(slot, me), 0)
    extra = jnp.concatenate(
        [
            gain_attn_grad,
            gain_mlp_grad_ref[:7],
            jnp.where(rows_of((8, 1)) == language, row_sum, 0.0),
        ],
        axis=0,
    ).astype(bf16)
    at = shards // 2 * CHAR_LAST_SLOT
    for ref in (keep_ref, send_ref):
        ref[at : at + 16] = extra
    leave.wait()


def char_attn_back(
    languages, chars, table, weights, dmiddle, gain_mlp_grad, stored, slots, shards, after
):
    gain_attn, project, output, _, _, _ = weights
    _, qkv, probs, _, _, _ = stored
    rows, width = dmiddle.shape
    half = (shards // 2 * CHAR_LAST_SLOT + 16, width)
    vmem = pl.BlockSpec(memory_space=pltpu.VMEM)
    hbm = pl.BlockSpec(memory_space=pltpu.HBM)
    return pl.pallas_call(
        functools.partial(char_attn_back_kernel, slots, shards),
        in_specs=[pl.BlockSpec(memory_space=pl.ANY), hbm, hbm] + [vmem] * 8,
        out_specs=[hbm, vmem, vmem],
        out_shape=[
            jax.ShapeDtypeStruct((rows, width), f32),
            jax.ShapeDtypeStruct(half, bf16),
            jax.ShapeDtypeStruct(half, bf16),
        ],
        scratch_shapes=[
            pltpu.VMEM((rows, width), bf16),
            pltpu.VMEM(languages.shape, languages.dtype),
            pltpu.VMEM((rows, width), bf16),
            pltpu.VMEM((rows, 3 * width), bf16),
            pltpu.VMEM((rows, width), f32),
            pltpu.VMEM(project.shape, f32),
            pltpu.SemaphoreType.DMA((3,)),
        ],
        compiler_params=pltpu.CompilerParams(vmem_limit_bytes=16 * MIB),
        cost_estimate=pl.CostEstimate(
            flops=0, bytes_accessed=0, transcendentals=0
        ),
        name="char_attn_back",
    )(
        after,
        in_hbm(chars),
        in_hbm(languages),
        table,
        gain_attn,
        project,
        output,
        dmiddle,
        gain_mlp_grad,
        qkv,
        probs,
    )


WORD_SLOT = 416


def word_kernel(
    length,
    shards,
    own_ref,
    far_ref,
    section_ref,
    both_ref,
    cot_ref,
    cot_far_ref,
    input_ref,
    gain_attn_ref,
    project_ref,
    output_ref,
    gain_mlp_ref,
    expand_ref,
    shrink_ref,
    result_hbm,
    dpooled_ref,
    keep_ref,
    send_ref,
    pooled,
    pooled_t,
    dz,
    start,
    normed_t,
    qkv,
    kept,
    mixed_t,
    middle,
    normed_mlp_t,
    hidden,
    dbefore,
    dmixed,
    dqkv,
    dy,
    dstart,
    result,
    input_grad,
    project_grad,
    output_grad,
    expand_grad,
    shrink_grad,
    sem,
):
    total = pooled.shape[0]
    width = output_ref.shape[0]
    section, me = position()
    slabs = width // SLAB
    for place, ref in enumerate((own_ref, far_ref, section_ref, both_ref)):
        pooled[place * length : (place + 1) * length] = ref[...]
    for place, (ref, other) in enumerate(
        ((cot_ref, section), (cot_far_ref, section), (cot_ref, 1 - section), (cot_far_ref, 1 - section))
    ):
        dz[place * length : (place + 1) * length] = ref[other]

    x = dot(pooled[...], input_ref[...])
    start[...] = x
    normal, _ = unit(x)
    low = (normal * gain_attn_ref[...]).astype(bf16)
    normed_t[...] = low.T
    qkv[...] = dot(low, project_ref[...]).astype(bf16)
    tiles = [(block, slab) for block in range(total // BLOCK) for slab in range(slabs)]

    def load(tile, which):
        block, slab = tile
        at = which * width + slab * SLAB
        return qkv[block * BLOCK : (block + 1) * BLOCK, at : at + SLAB]

    mask_shape = (length, len(tiles) * HEADS * BLOCK)
    causal = rows_of(mask_shape) <= lanes(mask_shape) % length
    probs, mixed = attend(load, tiles, causal, length)
    kept[...] = probs
    for (block, slab), piece in zip(tiles, mixed):
        mixed_t[slab * SLAB : (slab + 1) * SLAB, block * BLOCK : (block + 1) * BLOCK] = piece
    x = x + dot(mixed_t[...].T, output_ref[...])
    middle[...] = x
    normal, _ = unit(x)
    low = (normal * gain_mlp_ref[...]).astype(bf16)
    normed_mlp_t[...] = low.T
    dz_all = dz[...]
    for at in range(0, expand_ref.shape[1], 256):
        part = slice(at, at + 256)
        value, bend = gelu_parts(dot(low, expand_ref[:, part]))
        hidden[:, part] = value
        dhidden = dot_nt(dz_all, shrink_ref[part, :]).astype(bf16)
        dbefore[:, part] = dhidden * bend
    result[...] = middle[:length] + dot(hidden[:length], shrink_ref[...])
    leave = pltpu.make_async_copy(result, result_hbm, sem)
    leave.start()

    dnormed = dot_nt(dbefore[...], expand_ref[...])
    normal, scale = unit(middle[...])
    gain_mlp_grad = jnp.sum(dnormed * normal, axis=0, keepdims=True)
    dmiddle = dz_all.astype(f32) + unit_back(dnormed, gain_mlp_ref[...], normal, scale)
    dy_low = dmiddle.astype(bf16)
    dy[...] = dy_low
    dmixed[...] = dot_nt(dy_low, output_ref[...]).astype(bf16)

    def load_dmixed(tile):
        block, slab = tile
        return dmixed[block * BLOCK : (block + 1) * BLOCK, slab * SLAB : (slab + 1) * SLAB]

    def store(tile, which, value):
        block, slab = tile
        at = which * width + slab * SLAB
        dqkv[block * BLOCK : (block + 1) * BLOCK, at : at + SLAB] = value

    attend_back(load, load_dmixed, tiles, kept[...], store, length)
    dnormed = dot_nt(dqkv[...], project_ref[...])
    normal, scale = unit(start[...])
    gain_attn_grad = jnp.sum(dnormed * normal, axis=0, keepdims=True)
    dword = (dmiddle + unit_back(dnormed, gain_attn_ref[...], normal, scale)).astype(bf16)
    dpooled_ref[...] = dot_nt(dword[:length], input_ref[...]).astype(bf16)
    dstart[...] = dword

    def shard_of(slot):
        return (me & 7) ^ ((slot >> 2) | ((slot & 3) << 1))

    def own_rows(flipped):
        many = flipped.shape[0] // 2
        return flipped[pl.ds(pl.multiple_of((me >> 3) * many, many), many), :]

    def half_columns(ref, place):
        many = ref.shape[1] // 2
        return ref[:, pl.ds(pl.multiple_of(place * many, many), many)]

    def own_columns(ref):
        return half_columns(ref, section)

    pooled_t[...] = pooled[...].T
    hidden_t = half_columns(hidden, me >> 3).T
    targets = slot_refs(keep_ref, send_ref)
    at = 0
    for lhs, rhs, ref in (
        (own_rows(pooled_t), own_columns(dstart), input_grad),
        (own_rows(normed_t), own_columns(dqkv), project_grad),
        (own_rows(mixed_t), own_columns(dy), output_grad),
        (own_rows(normed_mlp_t), own_columns(dbefore), expand_grad),
        (hidden_t, own_columns(dz), shrink_grad),
    ):
        ref[...] = dot(lhs, rhs)
        at = put_shards(ref, targets, shard_of, at)
    extra = jnp.concatenate(
        [gain_attn_grad[:, :SLAB], gain_attn_grad[:, SLAB:]]
        + [gain_mlp_grad[:, :SLAB], gain_mlp_grad[:, SLAB:]]
        + [jnp.zeros((12, SLAB), f32)],
        axis=0,
    ).astype(bf16)
    for target in targets:
        target[at : at + 16] = extra
    leave.wait()


def word_group(pooled, cotangents, word_input, weights, shards):
    gain_attn, project, output, gain_mlp, expand_w, shrink = weights
    length, channels = pooled[0].shape
    width = output.shape[0]
    hidden = expand_w.shape[1]
    total = 4 * length
    half = (4, WORD_SLOT, SLAB)
    vmem = pl.BlockSpec(memory_space=pltpu.VMEM)
    hbm = pl.BlockSpec(memory_space=pltpu.HBM)
    return pl.pallas_call(
        functools.partial(word_kernel, length, shards),
        in_specs=[vmem] * 13,
        out_specs=[hbm, vmem, vmem, vmem],
        out_shape=[
            jax.ShapeDtypeStruct((length, width), f32),
            jax.ShapeDtypeStruct((length, channels), bf16),
            jax.ShapeDtypeStruct(half, bf16),
            jax.ShapeDtypeStruct(half, bf16),
        ],
        scratch_shapes=[
            pltpu.VMEM((total, channels), bf16),
            pltpu.VMEM((channels, total), bf16),
            pltpu.VMEM((total, width), bf16),
            pltpu.VMEM((total, width), f32),
            pltpu.VMEM((width, total), bf16),
            pltpu.VMEM((total, 3 * width), bf16),
            pltpu.VMEM((length, total * (width // HEAD)), f32),
            pltpu.VMEM((width, total), bf16),
            pltpu.VMEM((total, width), f32),
            pltpu.VMEM((width, total), bf16),
            pltpu.VMEM((total, hidden), bf16),
            pltpu.VMEM((total, hidden), bf16),
            pltpu.VMEM((total, width), bf16),
            pltpu.VMEM((total, 3 * width), bf16),
            pltpu.VMEM((total, width), bf16),
            pltpu.VMEM((total, width), bf16),
            pltpu.VMEM((length, width), f32),
            pltpu.VMEM((channels // 2, width // 2), f32),
            pltpu.VMEM((width // 2, 3 * width // 2), f32),
            pltpu.VMEM((width // 2, width // 2), f32),
            pltpu.VMEM((width // 2, hidden // 2), f32),
            pltpu.VMEM((hidden // 2, width // 2), f32),
            pltpu.SemaphoreType.DMA,
        ],
        compiler_params=pltpu.CompilerParams(vmem_limit_bytes=20 * MIB),
        cost_estimate=pl.CostEstimate(
            flops=total * width * width * 25 * 4, bytes_accessed=8 * MIB, transcendentals=0
        ),
        name="word_group",
    )(*pooled, *cotangents, word_input, gain_attn, project, output, gain_mlp, expand_w, shrink)


def summed(*parts):
    return functools.reduce(lambda a, b: a + b, [part.astype(f32) for part in parts])


def added(*parts):
    return summed(*parts).astype(bf16)


def by_section(section, low, high):
    return (jnp.where(section == 0, low, high), jnp.where(section == 0, high, low))


def word_sum_kernel(keep, arrived, *outs):
    for place, ref in enumerate(outs):
        ref[...] = added(keep[place], arrived[place])


def word_sum(keep, arrived):
    return pl.pallas_call(
        word_sum_kernel,
        out_shape=[jax.ShapeDtypeStruct((WORD_SLOT, SLAB), bf16)] * 4,
        compiler_params=pltpu.CompilerParams(vmem_limit_bytes=12 * MIB),
        name="word_sum",
    )(keep, arrived)


def first_sum_kernel(keep, arrived, stay_ref, go_ref):
    section, _ = position()
    half = SLAB // 2
    for place in range(keep.shape[0]):
        total = added(keep[place], arrived[place])
        stay_ref[place], go_ref[place] = by_section(section, total[:, :half], total[:, half:])


def first_sum(keep, arrived):
    half = jax.ShapeDtypeStruct(keep.shape[:2] + (SLAB // 2,), bf16)
    return pl.pallas_call(
        first_sum_kernel,
        out_shape=[half, half],
        compiler_params=pltpu.CompilerParams(vmem_limit_bytes=12 * MIB),
        name="first_sum",
    )(keep, arrived)


def second_sum_kernel(first, keep, arrived, *outs):
    _, me = position()
    half = SLAB // 2
    extra = summed(keep[-16:], arrived[-16:])
    for place, out in enumerate(outs):
        at = CHAR_FIRST_SLOT
        for far in range(2):
            entry = 2 * place + far
            columns = slice(far * half, (far + 1) * half)
            out[:CHAR_FIRST_SLOT, columns] = first[entry]
            rows = slice(entry * CHAR_LAST_SLOT, (entry + 1) * CHAR_LAST_SLOT)
            out[at : at + CHAR_LAST_SLOT] = added(keep[rows], arrived[rows])
            at += CHAR_LAST_SLOT
            turn = lax.rem(SLAB - char_shard(entry, me) * 16, SLAB)
            out[-16:, columns] = pltpu.roll(extra, turn, 1)[:, :half].astype(bf16)


LONG = pl.CostEstimate(flops=20_000_000_000, bytes_accessed=8 * MIB, transcendentals=0)


def total_kernel(*refs):
    refs[-1][...] = added(*[ref[...] for ref in refs[:-1]])


def total_of(*pieces):
    return pl.pallas_call(
        total_kernel,
        out_shape=jax.ShapeDtypeStruct(pieces[0].shape, bf16),
        compiler_params=pltpu.CompilerParams(vmem_limit_bytes=12 * MIB),
        cost_estimate=LONG,
        name="total",
    )(*pieces)


def pair_kernel(one, other, _, out):
    out[...] = added(one[...], other[...])


def pair_of(one, other, after):
    vmem = pl.BlockSpec(memory_space=pltpu.VMEM)
    return pl.pallas_call(
        pair_kernel,
        in_specs=[vmem, vmem, pl.BlockSpec(memory_space=pl.ANY)],
        out_shape=jax.ShapeDtypeStruct(one.shape, bf16),
        compiler_params=pltpu.CompilerParams(vmem_limit_bytes=12 * MIB),
        cost_estimate=LONG,
        name="pair",
    )(one, other, after)


def second_sum(first, last):
    rows = CHAR_FIRST_SLOT + 2 * CHAR_LAST_SLOT + 16
    return pl.pallas_call(
        second_sum_kernel,
        out_shape=[jax.ShapeDtypeStruct((rows, SLAB), bf16)] * 4,
        compiler_params=pltpu.CompilerParams(vmem_limit_bytes=12 * MIB),
        name="second_sum",
    )(first, *last)


FOLD = 80


def plane_sum_kernel(*refs):
    word, char, near_ref, far_ref = (refs[0], refs[1:5], refs[5], refs[6])
    near_ref[:WORD_SLOT] = word[...]
    half = SLAB // 2
    for far, out, at in ((0, near_ref, WORD_SLOT), (1, far_ref, 0)):
        columns = slice(far * half, (far + 1) * half)
        total = added(*[ref[:CHAR_FIRST_SLOT, columns] for ref in char])
        out[at : at + FOLD, :half] = total[:FOLD]
        out[at : at + FOLD, half:] = total[CHAR_FIRST_SLOT - FOLD :]
        out[at : at + 16, half:] = added(*[ref[-16:, columns] for ref in char])
        first = CHAR_FIRST_SLOT + far * CHAR_LAST_SLOT
        at += FOLD
        out[at : at + CHAR_LAST_SLOT] = added(
            *[ref[first : first + CHAR_LAST_SLOT] for ref in char]
        )


def plane_sum(word, char):
    rows = FOLD + CHAR_LAST_SLOT
    return pl.pallas_call(
        plane_sum_kernel,
        out_shape=[
            jax.ShapeDtypeStruct((WORD_SLOT + rows, SLAB), bf16),
            jax.ShapeDtypeStruct((rows, SLAB), bf16),
        ],
        compiler_params=pltpu.CompilerParams(vmem_limit_bytes=12 * MIB),
        name="plane_sum",
    )(word, *char)


def last_sum_kernel(near_ref, section_ref, high_ref, both_ref, *outs):
    word_rows = WORD_SLOT
    section, me = position()
    own = near_ref[:word_rows].astype(f32)
    halves = by_section(section, own, section_ref[:word_rows].astype(f32))
    half = SLAB // 2

    mine_too = summed(near_ref[word_rows : word_rows + FOLD], high_ref[:FOLD])
    theirs = summed(section_ref[word_rows : word_rows + FOLD], both_ref[:FOLD])

    def unfold(total):
        return jnp.concatenate(
            [total[:, :half], total[2 * FOLD - CHAR_FIRST_SLOT :, half:]], axis=0
        )

    first = jnp.concatenate(by_section(section, unfold(mine_too), unfold(theirs)), axis=1)
    extra = mine_too[:16, half:] + theirs[:16, half:]
    last = summed(
        near_ref[word_rows + FOLD :],
        section_ref[word_rows + FOLD :],
        high_ref[FOLD:],
        both_ref[FOLD:],
    )

    def mine(vector, size):
        turned = pltpu.roll(vector, lax.rem(SLAB - lax.rem(me * size, SLAB), SLAB), 1)
        return turned[:, :size]

    (
        table_ref,
        gain_attn_ref,
        project_ref,
        output_ref,
        gain_mlp_ref,
        expand_ref,
        shrink_ref,
        w_input_ref,
        w_gain_attn_ref,
        w_project_ref,
        w_output_ref,
        w_gain_mlp_ref,
        w_expand_ref,
        w_shrink_ref,
    ) = outs
    for char, refs in ((first, (expand_ref, shrink_ref, output_ref)), (last, (project_ref,))):
        at = 0
        for ref in refs:
            size = ref.shape[0]
            for column in range(ref.shape[1] // SLAB):
                ref[:, column * SLAB : (column + 1) * SLAB] = char[at : at + size]
                at += size
    size = gain_attn_ref.shape[1]
    gain_attn_ref[...] = extra[0:1, :size]
    gain_mlp_ref[...] = extra[1:2, :size]
    table_ref[...] = extra[8:16, :size]
    at = 0
    for ref in (w_input_ref, w_project_ref, w_output_ref, w_expand_ref, w_shrink_ref):
        size = ref.shape[0]
        columns = ref.shape[1] // (2 * SLAB)
        for column in range(columns):
            for half in range(2):
                first = (half * columns + column) * SLAB
                ref[:, first : first + SLAB] = halves[half][at : at + size]
            at += size
    size = w_gain_attn_ref.shape[1]
    extra = own[at : at + 8]
    turned = mine(extra, size)
    upper = me * size >= SLAB
    w_gain_attn_ref[...] = jnp.where(upper, turned[1:2], turned[0:1])
    w_gain_mlp_ref[...] = jnp.where(upper, turned[3:4], turned[2:3])


def last_sum(near, arrived, shapes):
    return pl.pallas_call(
        last_sum_kernel,
        out_shape=[jax.ShapeDtypeStruct(shape, f32) for shape in shapes],
        compiler_params=pltpu.CompilerParams(vmem_limit_bytes=12 * MIB),
        name="last_sum",
    )(near, *arrived)


def exchange(value, section_bit, dp_bits):
    shards = lax.axis_size("dp")
    pairs = [
        (s * shards + d, (s ^ section_bit) * shards + (d ^ dp_bits))
        for s in range(lax.axis_size("section"))
        for d in range(shards)
    ]
    return lax.ppermute(value, ("section", "dp"), pairs)


CORE, SIDE, NEAR, FAR = (1, 2, 4, 8)


def plane_exchange(pieces):
    return (pieces[0],) + tuple(
        exchange(piece, 0, bits) for piece, bits in zip(pieces[1:], (SIDE, NEAR, SIDE | NEAR))
    )


def local_grouped(
    chars, counts, languages, language_table, char_weights, word_input, word_weights, cotangent
):
    shards = lax.axis_size("dp")
    micros, _, words, slots, width = chars.shape
    rows = words * slots
    cot = cotangent[:, 0]
    cot_far = exchange(cot, 0, FAR)
    char_weights = tuple(w[None] if w.ndim == 1 else w for w in char_weights)
    word_weights = tuple(w[None] if w.ndim == 1 else w for w in word_weights)
    chars = chars.reshape(micros, rows, width)
    counts = counts.reshape(micros, 1, words)
    languages = languages.reshape(1, micros)
    pooled, *stored = char_forward(languages, chars, counts, language_table, char_weights, slots)
    others = (exchange(pooled, 0, FAR), exchange(pooled, 1, 0), exchange(pooled, 1, FAR))
    result, dpooled, keep, send = word_group(
        (pooled,) + others, (cot, cot_far), word_input, word_weights, shards
    )
    word = plane_exchange(word_sum(keep, exchange(send, 0, CORE)))
    dmiddle, gain_mlp_grad, keep, send = char_mlp_back(
        counts, char_weights, dpooled, stored, slots, shards
    )
    stay, go = first_sum(keep, exchange(send, 0, CORE))
    arrived = exchange(go, 1, 0)
    chars_grad, keep, send = char_attn_back(
        languages,
        chars,
        language_table,
        char_weights,
        dmiddle,
        gain_mlp_grad,
        stored,
        slots,
        shards,
        stay,
    )
    last = (keep, exchange(send, 0, CORE))
    word = total_of(*word)
    first = pair_of(stay, arrived, word)
    char = plane_exchange(second_sum(first, last))
    near, far = plane_sum(word, char)
    arrived = (exchange(near, 1, 0), exchange(far, 0, FAR), exchange(far, 1, FAR))
    shapes = [(language_table.shape[0], language_table.shape[1] // shards)]
    for weight in char_weights + (word_input,) + word_weights:
        if weight.shape[0] == 1:
            shapes.append((1, weight.shape[1] // shards))
        else:
            shapes.append((weight.shape[0] // shards, weight.shape[1]))
    totals = last_sum(near, arrived, shapes)
    totals = [total[0] if total.shape[0] == 1 else total for total in totals]
    return (result[None, None], chars_grad.reshape((1, 1, words, slots, width))) + tuple(totals)


def norm_forward(inputs, gain):
    return inputs * lax.rsqrt(jnp.mean(inputs * inputs, axis=-1, keepdims=True) + eps) * gain


def attend_forward(normed, project, head_count, key_mask):
    row_count, length, channels = normed.shape
    head_size = channels // head_count
    qkv = jnp.einsum("blc,cf->blf", normed, project, preferred_element_type=jnp.float32).astype(
        jnp.bfloat16
    )
    pieces = qkv.reshape(row_count, length, 3, head_count, head_size)
    scores = jnp.einsum(
        "bqhd,bkhd->bhqk", pieces[:, :, 0], pieces[:, :, 1], preferred_element_type=jnp.float32
    ) * head_size ** (-0.5)
    scores = jnp.where(key_mask, scores, -1e30)
    row_max = jnp.max(scores, axis=-1, keepdims=True)
    weights_exp = jnp.exp(scores - row_max)
    row_total = jnp.sum(weights_exp, axis=-1, keepdims=True)
    attn_probs = (weights_exp / row_total).astype(jnp.bfloat16)
    mixed_heads = jnp.einsum(
        "bhqk,bkhd->bqhd", attn_probs, pieces[:, :, 2], preferred_element_type=jnp.float32
    )
    mixed_heads = mixed_heads.reshape(row_count, length, channels).astype(jnp.bfloat16)
    return (qkv, row_max + jnp.log(row_total), mixed_heads)


def attend_backward(
    normed, project, output, qkv, logsum, mixed_heads, dmiddle_low, head_count, key_mask
):
    row_count, length, channels = normed.shape
    head_size = channels // head_count
    scaling = head_size ** (-0.5)
    output_grad = jnp.einsum(
        "blc,bld->cd", mixed_heads, dmiddle_low, preferred_element_type=jnp.float32
    )
    dmixed = jnp.einsum(
        "bld,cd->blc", dmiddle_low, output, preferred_element_type=jnp.float32
    ).astype(jnp.bfloat16)
    dmixed = dmixed.reshape(row_count, length, head_count, head_size)
    pieces = qkv.reshape(row_count, length, 3, head_count, head_size)
    scores = (
        jnp.einsum(
            "bqhd,bkhd->bhqk", pieces[:, :, 0], pieces[:, :, 1], preferred_element_type=jnp.float32
        )
        * scaling
    )
    scores = jnp.where(key_mask, scores, -1e30)
    attn_probs = jnp.exp(scores - logsum)
    dprobs = jnp.einsum(
        "bqhd,bkhd->bhqk", dmixed, pieces[:, :, 2], preferred_element_type=jnp.float32
    )
    row_delta = jnp.sum(attn_probs * dprobs, axis=-1, keepdims=True)
    dscores = (attn_probs * (dprobs - row_delta)).astype(jnp.bfloat16)
    dquery = (
        jnp.einsum("bhqk,bkhd->bqhd", dscores, pieces[:, :, 1], preferred_element_type=jnp.float32)
        * scaling
    )
    dkeys = (
        jnp.einsum("bhqk,bqhd->bkhd", dscores, pieces[:, :, 0], preferred_element_type=jnp.float32)
        * scaling
    )
    dvalues = jnp.einsum(
        "bhqk,bqhd->bkhd",
        attn_probs.astype(jnp.bfloat16),
        dmixed,
        preferred_element_type=jnp.float32,
    )
    dqkv = (
        jnp.stack([dquery, dkeys, dvalues], axis=2)
        .reshape(row_count, length, 3 * channels)
        .astype(jnp.bfloat16)
    )
    project_grad = jnp.einsum("blc,blf->cf", normed, dqkv, preferred_element_type=jnp.float32)
    dnormed = jnp.einsum("blf,cf->blc", dqkv, project, preferred_element_type=jnp.float32)
    return (dnormed, project_grad, output_grad)


def block_forward(inputs, weights, head_count, key_mask):
    gain_attn, project, output, gain_mlp, expand, shrink = weights
    normed = norm_forward(inputs, gain_attn).astype(jnp.bfloat16)
    qkv, logsum, mixed_heads = attend_forward(normed, project, head_count, key_mask)
    middle = inputs + jnp.einsum(
        "blc,cd->bld", mixed_heads, output, preferred_element_type=jnp.float32
    )
    normed_mlp = norm_forward(middle, gain_mlp).astype(jnp.bfloat16)
    before = jnp.einsum("blc,cf->blf", normed_mlp, expand, preferred_element_type=jnp.float32)
    hidden = jax.nn.gelu(before).astype(jnp.bfloat16)
    result = middle + jnp.einsum("blf,fc->blc", hidden, shrink, preferred_element_type=jnp.float32)
    return (result, (inputs, normed, qkv, logsum, mixed_heads, middle, normed_mlp, before, hidden))


def block_backward(dresult, stored, weights, head_count, key_mask):
    gain_attn, project, output, gain_mlp, expand, shrink = weights
    inputs, normed, qkv, logsum, mixed_heads, middle, normed_mlp, before, hidden = stored
    grad_low = dresult.astype(jnp.bfloat16)
    shrink_grad = jnp.einsum("blf,blc->fc", hidden, grad_low, preferred_element_type=jnp.float32)
    dhidden = jnp.einsum(
        "blc,fc->blf", grad_low, shrink, preferred_element_type=jnp.float32
    ).astype(jnp.bfloat16)
    gelu_pull = jax.vjp(jax.nn.gelu, before)[1]
    dbefore = gelu_pull(dhidden.astype(jnp.float32))[0].astype(jnp.bfloat16)
    expand_grad = jnp.einsum("blc,blf->cf", normed_mlp, dbefore, preferred_element_type=jnp.float32)
    dnormed_mlp = jnp.einsum("blf,cf->blc", dbefore, expand, preferred_element_type=jnp.float32)
    norm_pull = jax.vjp(norm_forward, middle, gain_mlp)[1]
    dmiddle_norm, gain_mlp_grad = norm_pull(dnormed_mlp)
    dmiddle = dresult + dmiddle_norm
    dnormed, project_grad, output_grad = attend_backward(
        normed,
        project,
        output,
        qkv,
        logsum,
        mixed_heads,
        dmiddle.astype(jnp.bfloat16),
        head_count,
        key_mask,
    )
    first_pull = jax.vjp(norm_forward, inputs, gain_attn)[1]
    dinputs_norm, gain_attn_grad = first_pull(dnormed)
    return (
        dmiddle + dinputs_norm,
        (gain_attn_grad, project_grad, output_grad, gain_mlp_grad, expand_grad, shrink_grad),
    )


def char_front(char_text, char_count, language, lang_table, weights):
    present = lax.broadcasted_iota(jnp.int32, char_text.shape[:2], 1) < char_count[:, None]
    onehot = (lax.broadcasted_iota(jnp.int32, (lang_table.shape[0],), 0) == language).astype(
        jnp.bfloat16
    )
    lang_row = jnp.dot(onehot, lang_table, preferred_element_type=jnp.float32)
    inputs = char_text.astype(jnp.float32) + lang_row
    result, stored = block_forward(inputs, weights, CH, present[:, None, None, :])
    summed = jnp.sum(jnp.where(present[:, :, None], result, 0.0), axis=1)
    pooled = (summed / char_count[:, None].astype(jnp.float32)).astype(jnp.bfloat16)
    return (pooled, stored, present, onehot)


def char_back(stored, present, onehot, char_count, dpooled, weights):
    spread = dpooled.astype(jnp.float32) / char_count[:, None].astype(jnp.float32)
    dresult = jnp.where(present[:, :, None], spread[:, None, :], 0.0)
    dinputs, gradients = block_backward(dresult, stored, weights, CH, present[:, None, None, :])
    table_grad = onehot.astype(jnp.float32)[:, None] * jnp.sum(dinputs, axis=(0, 1))[None, :]
    return (dinputs, (table_grad,) + gradients)


def word_full(pooled, cot_rows, word_input, weights):
    length = pooled.shape[0]
    word_start = jnp.dot(pooled, word_input, preferred_element_type=jnp.float32)[None]
    causal = (
        lax.broadcasted_iota(jnp.int32, (length, length), 0)
        >= lax.broadcasted_iota(jnp.int32, (length, length), 1)
    )[None, None]
    result, stored = block_forward(word_start, weights, H, causal)
    dstart, gradients = block_backward(
        cot_rows.astype(jnp.float32)[None], stored, weights, H, causal
    )
    grad_low = dstart[0].astype(jnp.bfloat16)
    input_grad = jnp.einsum("wc,wd->cd", pooled, grad_low, preferred_element_type=jnp.float32)
    dpooled = jnp.einsum(
        "wd,cd->wc", grad_low, word_input, preferred_element_type=jnp.float32
    ).astype(jnp.bfloat16)
    return (result[0], dpooled, (input_grad,) + gradients)


def reduce_rows(gradients):
    shards = lax.axis_size("dp")
    flat = []
    for place, gradient in enumerate(gradients):
        if place == 0:
            gradient = gradient.T
        flat.append(gradient.astype(jnp.bfloat16).reshape(shards, -1))
    packed = jnp.concatenate(flat, axis=1)
    me = lax.axis_index("dp")
    packed = jnp.take(packed, jnp.arange(shards) ^ me, axis=0)
    bit = 1
    while packed.shape[0] > 1:
        pairs = packed.reshape(packed.shape[0] // 2, 2, packed.shape[1])
        arrived = lax.ppermute(pairs[:, 1], "dp", [(i, i ^ bit) for i in range(shards)])
        packed = (pairs[:, 0].astype(jnp.float32) + arrived.astype(jnp.float32)).astype(
            jnp.bfloat16
        )
        bit *= 2
    arrived = lax.ppermute(packed, "section", [(0, 1), (1, 0)])
    total = (packed.astype(jnp.float32) + arrived.astype(jnp.float32))[0]
    outs = []
    at = 0
    for place, gradient in enumerate(gradients):
        size = gradient.size // shards
        piece = total[at : at + size]
        at += size
        if place == 0:
            outs.append(piece.reshape(-1, gradient.shape[0]).T)
        else:
            outs.append(piece.reshape((gradient.shape[0] // shards,) + gradient.shape[1:]))
    return tuple(outs)


def local(
    chars,
    counts,
    languages,
    language_table,
    char_gain_attn,
    char_project,
    char_output,
    char_gain_mlp,
    char_expand,
    char_shrink,
    word_input,
    word_gain_attn,
    word_project,
    word_output,
    word_gain_mlp,
    word_expand,
    word_shrink,
    cotangent,
):
    char_weights = (
        char_gain_attn,
        char_project,
        char_output,
        char_gain_mlp,
        char_expand,
        char_shrink,
    )
    word_weights = (
        word_gain_attn,
        word_project,
        word_output,
        word_gain_mlp,
        word_expand,
        word_shrink,
    )
    if lax.axis_size("dp") == 16:
        return local_grouped(
            chars,
            counts,
            languages,
            language_table,
            char_weights,
            word_input,
            word_weights,
            cotangent,
        )
    section_index = lax.axis_index("section")
    char_text = chars[section_index, 0]
    char_count = counts[section_index, 0]
    language = languages[section_index, 0]
    cot_rows = cotangent[section_index, 0]
    pooled, stored, present, onehot = char_front(
        char_text, char_count, language, language_table, char_weights
    )
    result, dpooled, word_grads = word_full(pooled, cot_rows, word_input, word_weights)
    text_grad, char_grads = char_back(stored, present, onehot, char_count, dpooled, char_weights)
    totals = reduce_rows(char_grads + word_grads)
    return (result[None, None], text_grad[None, None]) + totals


def solution(mesh):
    placed = (
        P(None, "dp", None, None, None),
        P(None, "dp", None),
        P(None, "dp"),
        P(),
        P(),
        P(),
        P(),
        P(),
        P(),
        P(),
        P(),
        P(),
        P(),
        P(),
        P(),
        P(),
        P(),
        P(None, "dp", None, None),
    )
    return jax.shard_map(
        local,
        mesh=mesh,
        in_specs=placed,
        out_specs=(
            P("section", "dp", None, None),
            P("section", "dp", None, None, None),
            P(None, "dp"),
            P("dp"),
            P("dp", None),
            P("dp", None),
            P("dp"),
            P("dp", None),
            P("dp", None),
            P("dp", None),
            P("dp"),
            P("dp", None),
            P("dp", None),
            P("dp"),
            P("dp", None),
            P("dp", None),
        ),
        check_vma=False,
    )
```

```python
import functools

import jax
import jax.numpy as jnp
from jax import lax
from jax.experimental import pallas as pl
from jax.experimental.pallas import tpu as pltpu
from jax.sharding import PartitionSpec as P

CH = 4
H = 8
HEAD = 64
SLAB = 256
HEADS = SLAB // HEAD
BLOCK = 128
MIB = 1024 * 1024

eps = 1e-05

f32 = jnp.float32
bf16 = jnp.bfloat16


def dot(a, b):
    return jnp.dot(a, b, preferred_element_type=f32)


def dot_nt(a, b):
    return lax.dot_general(a, b, (((1,), (1,)), ((), ())), preferred_element_type=f32)


def position():
    return (lax.axis_index("section"), lax.axis_index("dp"))


def lanes(shape):
    return lax.broadcasted_iota(jnp.int32, shape, 1)


def rows_of(shape):
    return lax.broadcasted_iota(jnp.int32, shape, 0)


def stack_heads(a):
    head = lanes((1, SLAB)) // HEAD
    masks = [jnp.where(head == place, 1.0, 0.0).astype(bf16) for place in range(HEADS)]
    return jnp.concatenate([a * mask for mask in masks], axis=0)


def compact(scores, length):
    group = lanes((length, BLOCK)) // length
    total = scores[:length]
    for place in range(1, BLOCK // length):
        total = jnp.where(group == place, scores[place * length : (place + 1) * length], total)
    return total


def compact_heads(scores, length):
    return [
        compact(scores[:, head * BLOCK : (head + 1) * BLOCK], length) for head in range(HEADS)
    ]


def expand(values, length):
    group = lanes((length, BLOCK)) // length
    return jnp.concatenate(
        [jnp.where(group == place, values, 0.0) for place in range(BLOCK // length)], axis=0
    ).astype(bf16)


def expand_heads(values, tile, length):
    first = tile * HEADS * BLOCK
    return [
        expand(values[:, first + head * BLOCK : first + (head + 1) * BLOCK], length)
        for head in range(HEADS)
    ]


def head_rows(a, head):
    return a[head * HEAD : (head + 1) * HEAD]


def attend(load, tiles, key_mask, length):
    scores = []
    for tile in tiles:
        scores += compact_heads(dot_nt(load(tile, 1), stack_heads(load(tile, 0))), length)
    scores = jnp.concatenate(scores, axis=1) * HEAD**-0.5
    scores = jnp.where(key_mask, scores, -1e30)
    weights = jnp.exp(scores - jnp.max(scores, axis=0, keepdims=True))
    probs = weights / jnp.sum(weights, axis=0, keepdims=True)
    mixed = []
    for number, tile in enumerate(tiles):
        values = load(tile, 2).T
        parts = expand_heads(probs, number, length)
        mixed.append(
            jnp.concatenate(
                [dot(head_rows(values, head), parts[head]) for head in range(HEADS)], axis=0
            ).astype(bf16)
        )
    return (probs, mixed)


def attend_back(load, load_dmixed, tiles, probs, store, length):
    dprobs = []
    for number, tile in enumerate(tiles):
        stacked = stack_heads(load_dmixed(tile))
        dprobs += compact_heads(dot_nt(load(tile, 2), stacked), length)
        parts = jnp.concatenate(expand_heads(probs, number, length), axis=1)
        store(tile, 2, dot(parts, stacked).astype(bf16))
    dprobs = jnp.concatenate(dprobs, axis=1)
    dscores = probs * (dprobs - jnp.sum(probs * dprobs, axis=0, keepdims=True))
    scaling = HEAD**-0.5
    for number, tile in enumerate(tiles):
        parts = expand_heads(dscores, number, length)
        keys = load(tile, 1).T
        dq = jnp.concatenate(
            [dot(head_rows(keys, head), parts[head]) for head in range(HEADS)], axis=0
        )
        store(tile, 0, (dq * scaling).astype(bf16).T)
        dk = dot(jnp.concatenate(parts, axis=1), stack_heads(load(tile, 0)))
        store(tile, 1, (dk * scaling).astype(bf16))


def unit(x):
    scale = lax.rsqrt(jnp.mean(x * x, axis=-1, keepdims=True) + eps)
    return (x * scale, scale)


def unit_back(dnormed, gain, normal, scale):
    weighted = dnormed * gain
    return scale * (weighted - normal * jnp.mean(normal * weighted, axis=-1, keepdims=True))


def gelu_parts(before):
    c = 0.7978845608028654
    before = before.astype(bf16)
    square = before * before
    half = bf16(0.5) * jnp.tanh(before * (bf16(c) + bf16(c * 0.044715) * square)) + bf16(0.5)
    value = before * half
    slope = half + value * (bf16(1.0) - half) * (bf16(2.0 * c) + bf16(6.0 * c * 0.044715) * square)
    return (value, slope)


def pick(row, place):
    return jnp.sum(jnp.where(lanes(row.shape) == place, row, 0), axis=1, keepdims=True)


def char_rows(chars, table_ref, language):
    table = table_ref[...].astype(f32)
    row = jnp.sum(jnp.where(rows_of(table.shape) == language, table, 0.0), axis=0, keepdims=True)
    return chars.astype(f32) + row


def counts_by_row(counts, rows, slots):
    words = counts.shape[-1]
    counts = jnp.broadcast_to(counts.astype(f32), (8, words)).astype(bf16)
    shape = (words, rows)
    member = lanes(shape) // slots == rows_of(shape)
    return dot(counts, jnp.where(member, 1.0, 0.0).astype(bf16))[:1]


def counts_column(counts):
    words = counts.shape[-1]
    shape = (words, words)
    spread = jnp.broadcast_to(counts.astype(f32), shape)
    return jnp.sum(
        jnp.where(rows_of(shape) == lanes(shape), spread, 0.0), axis=1, keepdims=True
    )


def fetch_all(sources, targets, sems):
    fetches = [
        pltpu.make_async_copy(source, target, sems.at[place])
        for place, (source, target) in enumerate(zip(sources, targets))
    ]
    for fetch in fetches:
        fetch.start()
    return fetches


def in_hbm(array):
    return pltpu.with_memory_space_constraint(array, pltpu.HBM)


def char_forward_kernel(
    slots,
    chars_hbm,
    languages_hbm,
    counts_hbm,
    table_hbm,
    gain_attn_hbm,
    project_hbm,
    output_hbm,
    gain_mlp_hbm,
    expand_hbm,
    shrink_hbm,
    pooled_ref,
    hidden_sum_ref,
    qkv_ref,
    probs_ref,
    mixed_ref,
    middle_ref,
    slope_ref,
    chars_ref,
    languages_ref,
    counts_ref,
    table_ref,
    gain_attn_ref,
    project_ref,
    output_ref,
    gain_mlp_ref,
    expand_ref,
    shrink_ref,
    sems,
):
    section, _ = position()
    fetches = fetch_all(
        (
            languages_hbm,
            counts_hbm,
            table_hbm,
            gain_attn_hbm,
            chars_hbm.at[section],
            project_hbm,
            output_hbm,
            gain_mlp_hbm,
            expand_hbm,
            shrink_hbm,
        ),
        (
            languages_ref,
            counts_ref,
            table_ref,
            gain_attn_ref,
            chars_ref,
            project_ref,
            output_ref,
            gain_mlp_ref,
            expand_ref,
            shrink_ref,
        ),
        sems,
    )
    for fetch in fetches[:2]:
        fetch.wait()
    counts = counts_ref[section]
    rows = chars_ref.shape[0]
    words = counts.shape[-1]
    row_counts = counts_by_row(counts, rows, slots)
    for fetch in fetches[2:5]:
        fetch.wait()
    x = char_rows(chars_ref[...], table_ref, pick(languages_ref[...], section))
    normal, _ = unit(x)
    normed = (normal * gain_attn_ref[...]).astype(bf16)
    fetches[5].wait()
    qkv_ref[...] = dot(normed, project_ref[...]).astype(bf16)
    blocks = range(rows // BLOCK)

    def load(block, which):
        return qkv_ref[block * BLOCK : (block + 1) * BLOCK, which * SLAB : (which + 1) * SLAB]

    by_head = jnp.concatenate(
        [row_counts[:, block * BLOCK : (block + 1) * BLOCK] for block in blocks for _ in range(HEADS)],
        axis=1,
    )
    key_mask = rows_of((slots, rows * HEADS)).astype(f32) < by_head
    probs, mixed = attend(load, blocks, key_mask, slots)
    probs_ref[...] = probs
    for block in blocks:
        mixed_ref[:, block * BLOCK : (block + 1) * BLOCK] = mixed[block]
    mixed = mixed_ref[...].T
    fetches[6].wait()
    middle = x + dot(mixed, output_ref[...])
    middle_ref[...] = middle
    normal, _ = unit(middle)
    fetches[7].wait()
    normed = (normal * gain_mlp_ref[...]).astype(bf16)
    word_shape = (words, rows)
    lane = lanes(word_shape)
    member = (lane // slots == rows_of(word_shape)) & ((lane % slots).astype(f32) < row_counts)
    member = jnp.where(member, 1.0, 0.0).astype(bf16)
    fetches[8].wait()
    parts = [slice(at, at + 256) for at in range(0, expand_ref.shape[1], 256)]
    before = dot(normed, expand_ref[:, parts[0]])
    for number, part in enumerate(parts):
        value, slope = gelu_parts(before)
        if number + 1 < len(parts):
            before = dot(normed, expand_ref[:, parts[number + 1]])
        slope_ref[:, part] = slope
        hidden_sum_ref[:, part] = dot(member, value).astype(bf16)
    high = middle.astype(bf16)
    low = (middle - high.astype(f32)).astype(bf16)
    fetches[9].wait()
    total = dot(member, high) + dot(member, low) + dot(hidden_sum_ref[...], shrink_ref[...])
    pooled_ref[...] = (total / counts_column(counts)).astype(bf16)


def char_forward(languages, chars, counts, table, weights, slots):
    rows, width = chars.shape[1:]
    words = rows // slots
    hidden = weights[4].shape[1]
    vmem = pl.BlockSpec(memory_space=pltpu.VMEM)
    hbm = pl.BlockSpec(memory_space=pltpu.HBM)
    fetched = (languages, counts, table) + tuple(weights)
    return pl.pallas_call(
        functools.partial(char_forward_kernel, slots),
        in_specs=[hbm] * 10,
        out_specs=[vmem] * 7,
        out_shape=[
            jax.ShapeDtypeStruct((words, width), bf16),
            jax.ShapeDtypeStruct((words, hidden), bf16),
            jax.ShapeDtypeStruct((rows, 3 * width), bf16),
            jax.ShapeDtypeStruct((slots, rows * HEADS), f32),
            jax.ShapeDtypeStruct((width, rows), bf16),
            jax.ShapeDtypeStruct((rows, width), f32),
            jax.ShapeDtypeStruct((rows, hidden), bf16),
        ],
        scratch_shapes=[pltpu.VMEM(chars.shape[1:], bf16)]
        + [pltpu.VMEM(array.shape, array.dtype) for array in fetched]
        + [pltpu.SemaphoreType.DMA((10,))],
        compiler_params=pltpu.CompilerParams(vmem_limit_bytes=16 * MIB),
        cost_estimate=pl.CostEstimate(
            flops=64 * rows * width * width, bytes_accessed=8 * MIB, transcendentals=0
        ),
        name="char_forward",
    )(*[in_hbm(array) for array in (chars,) + fetched])


CHAR_FIRST_SLOT = 144
CHAR_LAST_SLOT = 48


def char_shard(slot, me):
    return me ^ ((slot >> 3) | (((slot >> 1) & 3) << 1) | ((slot & 1) << 3))


def put_shards(gradient, slots, shard_of, at):
    width = SLAB
    columns = gradient.shape[1] // width
    size = gradient.shape[0] // len(slots)
    for number, slot in enumerate(slots):
        first = pl.multiple_of(shard_of(number) * size, size)
        for column in range(columns):
            start = at + column * size
            slot[start : start + size] = gradient[
                pl.ds(first, size), column * width : (column + 1) * width
            ].astype(bf16)
    return at + size * columns


def slot_refs(*refs):
    return [ref.at[place] for ref in refs for place in range(ref.shape[0])]


def char_mlp_back_kernel(
    slots,
    shards,
    counts_hbm,
    gain_mlp_ref,
    expand_ref,
    shrink_ref,
    dpooled_ref,
    hidden_sum_ref,
    mixed_ref,
    middle_ref,
    slope_ref,
    dmiddle_ref,
    gain_ref,
    keep_ref,
    send_ref,
    counts_ref,
    dhidden_words,
    dbefore,
    expand_grad,
    shrink_grad,
    output_grad,
    sem,
):
    section, me = position()
    fetch = pltpu.make_async_copy(counts_hbm, counts_ref, sem)
    fetch.start()
    fetch.wait()
    counts = counts_ref[section]
    rows, width = middle_ref.shape
    words = counts.shape[-1]
    spread = dpooled_ref[...].astype(f32) / counts_column(counts)
    spread_high = spread.astype(bf16)
    spread_low = (spread - spread_high.astype(f32)).astype(bf16)
    dhidden_words[...] = dot_nt(spread_high, shrink_ref[...]).astype(bf16)
    shape = (rows, words)
    row = rows_of(shape)
    member = (row // slots == lanes(shape)) & (row % slots < counts)
    member = jnp.where(member, 1.0, 0.0).astype(bf16)
    for at in range(0, expand_ref.shape[1], 256):
        part = slice(at, at + 256)
        dbefore[:, part] = dot(member, dhidden_words[:, part]).astype(bf16) * slope_ref[:, part]
    normal, scale = unit(middle_ref[...])
    normed_t = (normal * gain_mlp_ref[...]).astype(bf16).T
    hidden_sum_t = hidden_sum_ref[...].T
    targets = slot_refs(keep_ref, send_ref)

    def put(gradient, at):
        return put_shards(gradient, targets, lambda slot: char_shard(slot, me), at)

    dnormed = dot_nt(dbefore[...], expand_ref[...])
    expand_grad[...] = dot(normed_t, dbefore[...])
    shrink_grad[...] = dot(hidden_sum_t, spread_high)
    dmiddle = (
        dot(member, spread_high)
        + dot(member, spread_low)
        + unit_back(dnormed, gain_mlp_ref[...], normal, scale)
    )
    dmiddle_ref[...] = dmiddle
    output_grad[...] = dot(mixed_ref[...], dmiddle.astype(bf16))
    gain_ref[...] = jnp.broadcast_to(
        jnp.sum(dnormed * normal, axis=0, keepdims=True), gain_ref.shape
    )
    at = put(expand_grad, 0)
    at = put(shrink_grad, at)
    put(output_grad, at)


def char_mlp_back(counts, weights, dpooled, stored, slots, shards):
    _, _, output, gain_mlp, expand_w, shrink = weights
    hidden_sum, _, _, mixed, middle, slope = stored
    rows, width = middle.shape
    words = rows // slots
    hidden = expand_w.shape[1]
    half = (shards // 2, CHAR_FIRST_SLOT, width)
    vmem = pl.BlockSpec(memory_space=pltpu.VMEM)
    hbm = pl.BlockSpec(memory_space=pltpu.HBM)
    return pl.pallas_call(
        functools.partial(char_mlp_back_kernel, slots, shards),
        in_specs=[hbm] + [vmem] * 8,
        out_specs=[vmem] * 4,
        out_shape=[
            jax.ShapeDtypeStruct((rows, width), f32),
            jax.ShapeDtypeStruct((8, width), f32),
            jax.ShapeDtypeStruct(half, bf16),
            jax.ShapeDtypeStruct(half, bf16),
        ],
        scratch_shapes=[
            pltpu.VMEM(counts.shape, counts.dtype),
            pltpu.VMEM((words, hidden), bf16),
            pltpu.VMEM((rows, hidden), bf16),
            pltpu.VMEM(expand_w.shape, f32),
            pltpu.VMEM(shrink.shape, f32),
            pltpu.VMEM(output.shape, f32),
            pltpu.SemaphoreType.DMA,
        ],
        compiler_params=pltpu.CompilerParams(vmem_limit_bytes=16 * MIB),
        cost_estimate=pl.CostEstimate(
            flops=64 * rows * width * width, bytes_accessed=8 * MIB, transcendentals=0
        ),
        name="char_mlp_back",
    )(in_hbm(counts), gain_mlp, expand_w, shrink, dpooled, hidden_sum, mixed, middle, slope)


def char_attn_back_kernel(
    slots,
    shards,
    _,
    chars_hbm,
    languages_hbm,
    table_ref,
    gain_attn_ref,
    project_ref,
    output_ref,
    dmiddle_ref,
    gain_mlp_grad_ref,
    qkv_ref,
    probs_ref,
    grad_hbm,
    keep_ref,
    send_ref,
    chars_ref,
    languages_ref,
    dmixed,
    dqkv,
    grad,
    project_grad,
    sems,
):
    section, me = position()
    fetches = fetch_all(
        (chars_hbm.at[section], languages_hbm), (chars_ref, languages_ref), sems
    )
    rows, width = dmiddle_ref.shape
    dmixed[...] = dot_nt(dmiddle_ref[...].astype(bf16), output_ref[...]).astype(bf16)

    def load(block, which):
        return qkv_ref[block * BLOCK : (block + 1) * BLOCK, which * SLAB : (which + 1) * SLAB]

    def load_dmixed(block):
        return dmixed[block * BLOCK : (block + 1) * BLOCK]

    def store(block, which, value):
        dqkv[block * BLOCK : (block + 1) * BLOCK, which * SLAB : (which + 1) * SLAB] = value

    attend_back(load, load_dmixed, range(rows // BLOCK), probs_ref[...], store, slots)
    for fetch in fetches:
        fetch.wait()
    language = pick(languages_ref[...], section)
    normal, scale = unit(char_rows(chars_ref[...], table_ref, language))
    normed_t = (normal * gain_attn_ref[...]).astype(bf16).T
    dnormed = dot_nt(dqkv[...], project_ref[...])
    project_grad[...] = dot(normed_t, dqkv[...])
    gain_attn_grad = jnp.sum(dnormed * normal, axis=0, keepdims=True)
    dx = dmiddle_ref[...] + unit_back(dnormed, gain_attn_ref[...], normal, scale)
    grad[...] = dx
    leave = pltpu.make_async_copy(grad, grad_hbm, sems.at[2])
    leave.start()
    row_sum = jnp.sum(dx, axis=0, keepdims=True)
    targets = [
        ref.at[pl.ds(place * CHAR_LAST_SLOT, CHAR_LAST_SLOT)]
        for ref in (keep_ref, send_ref)
        for place in range(shards // 2)
    ]
    put_shards(project_grad, targets, lambda slot: char_shard(slot, me), 0)
    extra = jnp.concatenate(
        [
            gain_attn_grad,
            gain_mlp_grad_ref[:7],
            jnp.where(rows_of((8, 1)) == language, row_sum, 0.0),
        ],
        axis=0,
    ).astype(bf16)
    at = shards // 2 * CHAR_LAST_SLOT
    for ref in (keep_ref, send_ref):
        ref[at : at + 16] = extra
    leave.wait()


def char_attn_back(
    languages, chars, table, weights, dmiddle, gain_mlp_grad, stored, slots, shards, after
):
    gain_attn, project, output, _, _, _ = weights
    _, qkv, probs, _, _, _ = stored
    rows, width = dmiddle.shape
    half = (shards // 2 * CHAR_LAST_SLOT + 16, width)
    vmem = pl.BlockSpec(memory_space=pltpu.VMEM)
    hbm = pl.BlockSpec(memory_space=pltpu.HBM)
    return pl.pallas_call(
        functools.partial(char_attn_back_kernel, slots, shards),
        in_specs=[pl.BlockSpec(memory_space=pl.ANY), hbm, hbm] + [vmem] * 8,
        out_specs=[hbm, vmem, vmem],
        out_shape=[
            jax.ShapeDtypeStruct((rows, width), f32),
            jax.ShapeDtypeStruct(half, bf16),
            jax.ShapeDtypeStruct(half, bf16),
        ],
        scratch_shapes=[
            pltpu.VMEM((rows, width), bf16),
            pltpu.VMEM(languages.shape, languages.dtype),
            pltpu.VMEM((rows, width), bf16),
            pltpu.VMEM((rows, 3 * width), bf16),
            pltpu.VMEM((rows, width), f32),
            pltpu.VMEM(project.shape, f32),
            pltpu.SemaphoreType.DMA((3,)),
        ],
        compiler_params=pltpu.CompilerParams(vmem_limit_bytes=16 * MIB),
        cost_estimate=pl.CostEstimate(
            flops=0, bytes_accessed=0, transcendentals=0
        ),
        name="char_attn_back",
    )(
        after,
        in_hbm(chars),
        in_hbm(languages),
        table,
        gain_attn,
        project,
        output,
        dmiddle,
        gain_mlp_grad,
        qkv,
        probs,
    )


WORD_SLOT = 416


def word_kernel(
    length,
    shards,
    own_ref,
    both_ref,
    section_ref,
    far_ref,
    cot_ref,
    cot_far_ref,
    input_ref,
    gain_attn_ref,
    project_ref,
    output_ref,
    gain_mlp_ref,
    expand_ref,
    shrink_ref,
    result_hbm,
    dpooled_ref,
    keep_ref,
    send_ref,
    pooled,
    pooled_t,
    dz,
    start,
    normed_t,
    qkv,
    kept,
    mixed_t,
    middle,
    normed_mlp_t,
    hidden,
    dbefore,
    dmixed,
    dqkv,
    dy,
    dstart,
    result,
    input_grad,
    project_grad,
    output_grad,
    expand_grad,
    shrink_grad,
    sem,
):
    total = pooled.shape[0]
    width = output_ref.shape[0]
    section, me = position()
    slabs = width // SLAB
    for place, ref in enumerate((own_ref, far_ref, section_ref, both_ref)):
        pooled[place * length : (place + 1) * length] = ref[...]
    for place, (ref, other) in enumerate(
        ((cot_ref, section), (cot_far_ref, section), (cot_ref, 1 - section), (cot_far_ref, 1 - section))
    ):
        dz[place * length : (place + 1) * length] = ref[other]

    x = dot(pooled[...], input_ref[...])
    start[...] = x
    normal, _ = unit(x)
    low = (normal * gain_attn_ref[...]).astype(bf16)
    normed_t[...] = low.T
    qkv[...] = dot(low, project_ref[...]).astype(bf16)
    tiles = [(block, slab) for block in range(total // BLOCK) for slab in range(slabs)]

    def load(tile, which):
        block, slab = tile
        at = which * width + slab * SLAB
        return qkv[block * BLOCK : (block + 1) * BLOCK, at : at + SLAB]

    mask_shape = (length, len(tiles) * HEADS * BLOCK)
    causal = rows_of(mask_shape) <= lanes(mask_shape) % length
    probs, mixed = attend(load, tiles, causal, length)
    kept[...] = probs
    for (block, slab), piece in zip(tiles, mixed):
        mixed_t[slab * SLAB : (slab + 1) * SLAB, block * BLOCK : (block + 1) * BLOCK] = piece
    x = x + dot(mixed_t[...].T, output_ref[...])
    middle[...] = x
    normal, _ = unit(x)
    low = (normal * gain_mlp_ref[...]).astype(bf16)
    normed_mlp_t[...] = low.T
    dz_all = dz[...]
    for at in range(0, expand_ref.shape[1], 256):
        part = slice(at, at + 256)
        value, bend = gelu_parts(dot(low, expand_ref[:, part]))
        hidden[:, part] = value
        dhidden = dot_nt(dz_all, shrink_ref[part, :]).astype(bf16)
        dbefore[:, part] = dhidden * bend

    def shard_of(slot):
        return (me & 7) ^ ((slot >> 2) | ((slot & 3) << 1))

    def own_rows(flipped):
        many = flipped.shape[0] // 2
        return flipped[pl.ds(pl.multiple_of((me >> 3) * many, many), many), :]

    def half_columns(ref, place):
        many = ref.shape[1] // 2
        return ref[:, pl.ds(pl.multiple_of(place * many, many), many)]

    def own_columns(ref):
        return half_columns(ref, section)

    targets = slot_refs(keep_ref, send_ref)
    hidden_t = half_columns(hidden, me >> 3).T
    pooled_t[...] = pooled[...].T
    normal, scale = unit(middle[...])
    dnormed = dot_nt(dbefore[...], expand_ref[...])
    expand_grad[...] = dot(own_rows(normed_mlp_t), own_columns(dbefore))
    shrink_grad[...] = dot(hidden_t, own_columns(dz))
    dmiddle = dz_all.astype(f32) + unit_back(dnormed, gain_mlp_ref[...], normal, scale)
    dy_low = dmiddle.astype(bf16)
    dy[...] = dy_low
    dmixed[...] = dot_nt(dy_low, output_ref[...]).astype(bf16)
    gain_mlp_grad = jnp.sum(dnormed * normal, axis=0, keepdims=True)
    result[...] = middle[:length] + dot(hidden[:length], shrink_ref[...])
    leave = pltpu.make_async_copy(result, result_hbm, sem)
    leave.start()
    output_grad[...] = dot(own_rows(mixed_t), own_columns(dy))

    def load_dmixed(tile):
        block, slab = tile
        return dmixed[block * BLOCK : (block + 1) * BLOCK, slab * SLAB : (slab + 1) * SLAB]

    def store(tile, which, value):
        block, slab = tile
        at = which * width + slab * SLAB
        dqkv[block * BLOCK : (block + 1) * BLOCK, at : at + SLAB] = value

    attend_back(load, load_dmixed, tiles, kept[...], store, length)
    normal, scale = unit(start[...])
    dnormed = dot_nt(dqkv[...], project_ref[...])
    project_grad[...] = dot(own_rows(normed_t), own_columns(dqkv))
    dword = (dmiddle + unit_back(dnormed, gain_attn_ref[...], normal, scale)).astype(bf16)
    dpooled_ref[...] = dot_nt(dword[:length], input_ref[...]).astype(bf16)
    dstart[...] = dword
    gain_attn_grad = jnp.sum(dnormed * normal, axis=0, keepdims=True)
    input_grad[...] = dot(own_rows(pooled_t), own_columns(dstart))
    at = 0
    for ref in (input_grad, project_grad, output_grad, expand_grad, shrink_grad):
        at = put_shards(ref, targets, shard_of, at)
    extra = jnp.concatenate(
        [gain_attn_grad[:, :SLAB], gain_attn_grad[:, SLAB:]]
        + [gain_mlp_grad[:, :SLAB], gain_mlp_grad[:, SLAB:]]
        + [jnp.zeros((12, SLAB), f32)],
        axis=0,
    ).astype(bf16)
    for target in targets:
        target[at : at + 16] = extra
    leave.wait()


def word_group(pooled, cotangents, word_input, weights, shards):
    gain_attn, project, output, gain_mlp, expand_w, shrink = weights
    length, channels = pooled[0].shape
    width = output.shape[0]
    hidden = expand_w.shape[1]
    total = 4 * length
    half = (4, WORD_SLOT, SLAB)
    vmem = pl.BlockSpec(memory_space=pltpu.VMEM)
    hbm = pl.BlockSpec(memory_space=pltpu.HBM)
    return pl.pallas_call(
        functools.partial(word_kernel, length, shards),
        in_specs=[vmem] * 13,
        out_specs=[hbm, vmem, vmem, vmem],
        out_shape=[
            jax.ShapeDtypeStruct((length, width), f32),
            jax.ShapeDtypeStruct((length, channels), bf16),
            jax.ShapeDtypeStruct(half, bf16),
            jax.ShapeDtypeStruct(half, bf16),
        ],
        scratch_shapes=[
            pltpu.VMEM((total, channels), bf16),
            pltpu.VMEM((channels, total), bf16),
            pltpu.VMEM((total, width), bf16),
            pltpu.VMEM((total, width), f32),
            pltpu.VMEM((width, total), bf16),
            pltpu.VMEM((total, 3 * width), bf16),
            pltpu.VMEM((length, total * (width // HEAD)), f32),
            pltpu.VMEM((width, total), bf16),
            pltpu.VMEM((total, width), f32),
            pltpu.VMEM((width, total), bf16),
            pltpu.VMEM((total, hidden), bf16),
            pltpu.VMEM((total, hidden), bf16),
            pltpu.VMEM((total, width), bf16),
            pltpu.VMEM((total, 3 * width), bf16),
            pltpu.VMEM((total, width), bf16),
            pltpu.VMEM((total, width), bf16),
            pltpu.VMEM((length, width), f32),
            pltpu.VMEM((channels // 2, width // 2), f32),
            pltpu.VMEM((width // 2, 3 * width // 2), f32),
            pltpu.VMEM((width // 2, width // 2), f32),
            pltpu.VMEM((width // 2, hidden // 2), f32),
            pltpu.VMEM((hidden // 2, width // 2), f32),
            pltpu.SemaphoreType.DMA,
        ],
        compiler_params=pltpu.CompilerParams(vmem_limit_bytes=20 * MIB),
        cost_estimate=pl.CostEstimate(
            flops=total * width * width * 25 * 4, bytes_accessed=8 * MIB, transcendentals=0
        ),
        name="word_group",
    )(*pooled, *cotangents, word_input, gain_attn, project, output, gain_mlp, expand_w, shrink)


def summed(*parts):
    return functools.reduce(lambda a, b: a + b, [part.astype(f32) for part in parts])


def added(*parts):
    return summed(*parts).astype(bf16)


def by_section(section, low, high):
    return (jnp.where(section == 0, low, high), jnp.where(section == 0, high, low))


def word_sum_kernel(keep, arrived, *outs):
    for place, ref in enumerate(outs):
        ref[...] = added(keep[place], arrived[place])


def word_sum(keep, arrived):
    return pl.pallas_call(
        word_sum_kernel,
        out_shape=[jax.ShapeDtypeStruct((WORD_SLOT, SLAB), bf16)] * 4,
        compiler_params=pltpu.CompilerParams(vmem_limit_bytes=12 * MIB),
        name="word_sum",
    )(keep, arrived)


def first_sum_kernel(keep, arrived, stay_ref, go_ref):
    section, _ = position()
    half = SLAB // 2
    for place in range(keep.shape[0]):
        total = added(keep[place], arrived[place])
        stay_ref[place], go_ref[place] = by_section(section, total[:, :half], total[:, half:])


def first_sum(keep, arrived):
    half = jax.ShapeDtypeStruct(keep.shape[:2] + (SLAB // 2,), bf16)
    return pl.pallas_call(
        first_sum_kernel,
        out_shape=[half, half],
        compiler_params=pltpu.CompilerParams(vmem_limit_bytes=12 * MIB),
        name="first_sum",
    )(keep, arrived)


def second_sum_kernel(first, keep, arrived, *outs):
    _, me = position()
    half = SLAB // 2
    extra = summed(keep[-16:], arrived[-16:])
    for place, out in enumerate(outs):
        at = CHAR_FIRST_SLOT
        for far in range(2):
            entry = 2 * place + far
            columns = slice(far * half, (far + 1) * half)
            out[:CHAR_FIRST_SLOT, columns] = first[entry]
            rows = slice(entry * CHAR_LAST_SLOT, (entry + 1) * CHAR_LAST_SLOT)
            out[at : at + CHAR_LAST_SLOT] = added(keep[rows], arrived[rows])
            at += CHAR_LAST_SLOT
            turn = lax.rem(SLAB - char_shard(entry, me) * 16, SLAB)
            out[-16:, columns] = pltpu.roll(extra, turn, 1)[:, :half].astype(bf16)


LONG = pl.CostEstimate(flops=20_000_000_000, bytes_accessed=8 * MIB, transcendentals=0)


def total_kernel(*refs):
    refs[-1][...] = added(*[ref[...] for ref in refs[:-1]])


def total_of(*pieces):
    return pl.pallas_call(
        total_kernel,
        out_shape=jax.ShapeDtypeStruct(pieces[0].shape, bf16),
        compiler_params=pltpu.CompilerParams(vmem_limit_bytes=12 * MIB),
        cost_estimate=LONG,
        name="total",
    )(*pieces)


def pair_kernel(one, other, _, out):
    out[...] = added(one[...], other[...])


def pair_of(one, other, after):
    vmem = pl.BlockSpec(memory_space=pltpu.VMEM)
    return pl.pallas_call(
        pair_kernel,
        in_specs=[vmem, vmem, pl.BlockSpec(memory_space=pl.ANY)],
        out_shape=jax.ShapeDtypeStruct(one.shape, bf16),
        compiler_params=pltpu.CompilerParams(vmem_limit_bytes=12 * MIB),
        cost_estimate=LONG,
        name="pair",
    )(one, other, after)


def second_sum(first, last):
    rows = CHAR_FIRST_SLOT + 2 * CHAR_LAST_SLOT + 16
    return pl.pallas_call(
        second_sum_kernel,
        out_shape=[jax.ShapeDtypeStruct((rows, SLAB), bf16)] * 4,
        compiler_params=pltpu.CompilerParams(vmem_limit_bytes=12 * MIB),
        name="second_sum",
    )(first, *last)


FOLD = 80


def plane_sum_kernel(*refs):
    word, char, near_ref, far_ref = (refs[0], refs[1:5], refs[5], refs[6])
    near_ref[:WORD_SLOT] = word[...]
    half = SLAB // 2
    for far, out, at in ((0, near_ref, WORD_SLOT), (1, far_ref, 0)):
        columns = slice(far * half, (far + 1) * half)
        total = added(*[ref[:CHAR_FIRST_SLOT, columns] for ref in char])
        out[at : at + FOLD, :half] = total[:FOLD]
        out[at : at + FOLD, half:] = total[CHAR_FIRST_SLOT - FOLD :]
        out[at : at + 16, half:] = added(*[ref[-16:, columns] for ref in char])
        first = CHAR_FIRST_SLOT + far * CHAR_LAST_SLOT
        at += FOLD
        out[at : at + CHAR_LAST_SLOT] = added(
            *[ref[first : first + CHAR_LAST_SLOT] for ref in char]
        )


def plane_sum(word, char):
    rows = FOLD + CHAR_LAST_SLOT
    return pl.pallas_call(
        plane_sum_kernel,
        out_shape=[
            jax.ShapeDtypeStruct((WORD_SLOT + rows, SLAB), bf16),
            jax.ShapeDtypeStruct((rows, SLAB), bf16),
        ],
        compiler_params=pltpu.CompilerParams(vmem_limit_bytes=12 * MIB),
        name="plane_sum",
    )(word, *char)


def last_sum_kernel(near_ref, both_ref, high_ref, section_ref, *outs):
    word_rows = WORD_SLOT
    section, me = position()
    own = near_ref[:word_rows].astype(f32)
    halves = by_section(section, own, section_ref[:word_rows].astype(f32))
    half = SLAB // 2

    mine_too = summed(near_ref[word_rows : word_rows + FOLD], high_ref[:FOLD])
    theirs = summed(section_ref[word_rows : word_rows + FOLD], both_ref[:FOLD])

    def unfold(total):
        return jnp.concatenate(
            [total[:, :half], total[2 * FOLD - CHAR_FIRST_SLOT :, half:]], axis=0
        )

    first = jnp.concatenate(by_section(section, unfold(mine_too), unfold(theirs)), axis=1)
    extra = mine_too[:16, half:] + theirs[:16, half:]
    last = summed(
        near_ref[word_rows + FOLD :],
        section_ref[word_rows + FOLD :],
        high_ref[FOLD:],
        both_ref[FOLD:],
    )

    def mine(vector, size):
        turned = pltpu.roll(vector, lax.rem(SLAB - lax.rem(me * size, SLAB), SLAB), 1)
        return turned[:, :size]

    (
        table_ref,
        gain_attn_ref,
        project_ref,
        output_ref,
        gain_mlp_ref,
        expand_ref,
        shrink_ref,
        w_input_ref,
        w_gain_attn_ref,
        w_project_ref,
        w_output_ref,
        w_gain_mlp_ref,
        w_expand_ref,
        w_shrink_ref,
    ) = outs
    for char, refs in ((first, (expand_ref, shrink_ref, output_ref)), (last, (project_ref,))):
        at = 0
        for ref in refs:
            size = ref.shape[0]
            for column in range(ref.shape[1] // SLAB):
                ref[:, column * SLAB : (column + 1) * SLAB] = char[at : at + size]
                at += size
    size = gain_attn_ref.shape[1]
    gain_attn_ref[...] = extra[0:1, :size]
    gain_mlp_ref[...] = extra[1:2, :size]
    table_ref[...] = extra[8:16, :size]
    at = 0
    for ref in (w_input_ref, w_project_ref, w_output_ref, w_expand_ref, w_shrink_ref):
        size = ref.shape[0]
        columns = ref.shape[1] // (2 * SLAB)
        for column in range(columns):
            for half in range(2):
                first = (half * columns + column) * SLAB
                ref[:, first : first + SLAB] = halves[half][at : at + size]
            at += size
    size = w_gain_attn_ref.shape[1]
    extra = own[at : at + 8]
    turned = mine(extra, size)
    upper = me * size >= SLAB
    w_gain_attn_ref[...] = jnp.where(upper, turned[1:2], turned[0:1])
    w_gain_mlp_ref[...] = jnp.where(upper, turned[3:4], turned[2:3])


def last_sum(near, arrived, shapes):
    return pl.pallas_call(
        last_sum_kernel,
        out_shape=[jax.ShapeDtypeStruct(shape, f32) for shape in shapes],
        compiler_params=pltpu.CompilerParams(vmem_limit_bytes=12 * MIB),
        name="last_sum",
    )(near, *arrived)


def exchange(value, section_bit, dp_bits):
    shards = lax.axis_size("dp")
    pairs = [
        (s * shards + d, (s ^ section_bit) * shards + (d ^ dp_bits))
        for s in range(lax.axis_size("section"))
        for d in range(shards)
    ]
    return lax.ppermute(value, ("section", "dp"), pairs)


CORE, SIDE, NEAR, FAR = (1, 2, 4, 8)


def plane_exchange(pieces):
    return tuple(
        exchange(piece, 0, bits) for piece, bits in zip(pieces[:0:-1], (SIDE | NEAR, NEAR, SIDE))
    ) + (pieces[0],)


def local_grouped(
    chars, counts, languages, language_table, char_weights, word_input, word_weights, cotangent
):
    shards = lax.axis_size("dp")
    micros, _, words, slots, width = chars.shape
    rows = words * slots
    cot = cotangent[:, 0]
    cot_far = exchange(cot, 0, FAR)
    char_weights = tuple(w[None] if w.ndim == 1 else w for w in char_weights)
    word_weights = tuple(w[None] if w.ndim == 1 else w for w in word_weights)
    chars = chars.reshape(micros, rows, width)
    counts = counts.reshape(micros, 1, words)
    languages = languages.reshape(1, micros)
    pooled, *stored = char_forward(languages, chars, counts, language_table, char_weights, slots)
    others = (exchange(pooled, 1, FAR), exchange(pooled, 1, 0), exchange(pooled, 0, FAR))
    result, dpooled, keep, send = word_group(
        (pooled,) + others, (cot, cot_far), word_input, word_weights, shards
    )
    word = plane_exchange(word_sum(keep, exchange(send, 0, CORE)))
    dmiddle, gain_mlp_grad, keep, send = char_mlp_back(
        counts, char_weights, dpooled, stored, slots, shards
    )
    stay, go = first_sum(keep, exchange(send, 0, CORE))
    arrived = exchange(go, 1, 0)
    chars_grad, keep, send = char_attn_back(
        languages,
        chars,
        language_table,
        char_weights,
        dmiddle,
        gain_mlp_grad,
        stored,
        slots,
        shards,
        stay,
    )
    last = (keep, exchange(send, 0, CORE))
    word = total_of(*word)
    first = pair_of(stay, arrived, word)
    char = plane_exchange(second_sum(first, last))
    near, far = plane_sum(word, char)
    arrived = (exchange(far, 1, FAR), exchange(far, 0, FAR), exchange(near, 1, 0))
    shapes = [(language_table.shape[0], language_table.shape[1] // shards)]
    for weight in char_weights + (word_input,) + word_weights:
        if weight.shape[0] == 1:
            shapes.append((1, weight.shape[1] // shards))
        else:
            shapes.append((weight.shape[0] // shards, weight.shape[1]))
    totals = last_sum(near, arrived, shapes)
    totals = [total[0] if total.shape[0] == 1 else total for total in totals]
    return (result[None, None], chars_grad.reshape((1, 1, words, slots, width))) + tuple(totals)


def norm_forward(inputs, gain):
    return inputs * lax.rsqrt(jnp.mean(inputs * inputs, axis=-1, keepdims=True) + eps) * gain


def attend_forward(normed, project, head_count, key_mask):
    row_count, length, channels = normed.shape
    head_size = channels // head_count
    qkv = jnp.einsum("blc,cf->blf", normed, project, preferred_element_type=jnp.float32).astype(
        jnp.bfloat16
    )
    pieces = qkv.reshape(row_count, length, 3, head_count, head_size)
    scores = jnp.einsum(
        "bqhd,bkhd->bhqk", pieces[:, :, 0], pieces[:, :, 1], preferred_element_type=jnp.float32
    ) * head_size ** (-0.5)
    scores = jnp.where(key_mask, scores, -1e30)
    row_max = jnp.max(scores, axis=-1, keepdims=True)
    weights_exp = jnp.exp(scores - row_max)
    row_total = jnp.sum(weights_exp, axis=-1, keepdims=True)
    attn_probs = (weights_exp / row_total).astype(jnp.bfloat16)
    mixed_heads = jnp.einsum(
        "bhqk,bkhd->bqhd", attn_probs, pieces[:, :, 2], preferred_element_type=jnp.float32
    )
    mixed_heads = mixed_heads.reshape(row_count, length, channels).astype(jnp.bfloat16)
    return (qkv, row_max + jnp.log(row_total), mixed_heads)


def attend_backward(
    normed, project, output, qkv, logsum, mixed_heads, dmiddle_low, head_count, key_mask
):
    row_count, length, channels = normed.shape
    head_size = channels // head_count
    scaling = head_size ** (-0.5)
    output_grad = jnp.einsum(
        "blc,bld->cd", mixed_heads, dmiddle_low, preferred_element_type=jnp.float32
    )
    dmixed = jnp.einsum(
        "bld,cd->blc", dmiddle_low, output, preferred_element_type=jnp.float32
    ).astype(jnp.bfloat16)
    dmixed = dmixed.reshape(row_count, length, head_count, head_size)
    pieces = qkv.reshape(row_count, length, 3, head_count, head_size)
    scores = (
        jnp.einsum(
            "bqhd,bkhd->bhqk", pieces[:, :, 0], pieces[:, :, 1], preferred_element_type=jnp.float32
        )
        * scaling
    )
    scores = jnp.where(key_mask, scores, -1e30)
    attn_probs = jnp.exp(scores - logsum)
    dprobs = jnp.einsum(
        "bqhd,bkhd->bhqk", dmixed, pieces[:, :, 2], preferred_element_type=jnp.float32
    )
    row_delta = jnp.sum(attn_probs * dprobs, axis=-1, keepdims=True)
    dscores = (attn_probs * (dprobs - row_delta)).astype(jnp.bfloat16)
    dquery = (
        jnp.einsum("bhqk,bkhd->bqhd", dscores, pieces[:, :, 1], preferred_element_type=jnp.float32)
        * scaling
    )
    dkeys = (
        jnp.einsum("bhqk,bqhd->bkhd", dscores, pieces[:, :, 0], preferred_element_type=jnp.float32)
        * scaling
    )
    dvalues = jnp.einsum(
        "bhqk,bqhd->bkhd",
        attn_probs.astype(jnp.bfloat16),
        dmixed,
        preferred_element_type=jnp.float32,
    )
    dqkv = (
        jnp.stack([dquery, dkeys, dvalues], axis=2)
        .reshape(row_count, length, 3 * channels)
        .astype(jnp.bfloat16)
    )
    project_grad = jnp.einsum("blc,blf->cf", normed, dqkv, preferred_element_type=jnp.float32)
    dnormed = jnp.einsum("blf,cf->blc", dqkv, project, preferred_element_type=jnp.float32)
    return (dnormed, project_grad, output_grad)


def block_forward(inputs, weights, head_count, key_mask):
    gain_attn, project, output, gain_mlp, expand, shrink = weights
    normed = norm_forward(inputs, gain_attn).astype(jnp.bfloat16)
    qkv, logsum, mixed_heads = attend_forward(normed, project, head_count, key_mask)
    middle = inputs + jnp.einsum(
        "blc,cd->bld", mixed_heads, output, preferred_element_type=jnp.float32
    )
    normed_mlp = norm_forward(middle, gain_mlp).astype(jnp.bfloat16)
    before = jnp.einsum("blc,cf->blf", normed_mlp, expand, preferred_element_type=jnp.float32)
    hidden = jax.nn.gelu(before).astype(jnp.bfloat16)
    result = middle + jnp.einsum("blf,fc->blc", hidden, shrink, preferred_element_type=jnp.float32)
    return (result, (inputs, normed, qkv, logsum, mixed_heads, middle, normed_mlp, before, hidden))


def block_backward(dresult, stored, weights, head_count, key_mask):
    gain_attn, project, output, gain_mlp, expand, shrink = weights
    inputs, normed, qkv, logsum, mixed_heads, middle, normed_mlp, before, hidden = stored
    grad_low = dresult.astype(jnp.bfloat16)
    shrink_grad = jnp.einsum("blf,blc->fc", hidden, grad_low, preferred_element_type=jnp.float32)
    dhidden = jnp.einsum(
        "blc,fc->blf", grad_low, shrink, preferred_element_type=jnp.float32
    ).astype(jnp.bfloat16)
    gelu_pull = jax.vjp(jax.nn.gelu, before)[1]
    dbefore = gelu_pull(dhidden.astype(jnp.float32))[0].astype(jnp.bfloat16)
    expand_grad = jnp.einsum("blc,blf->cf", normed_mlp, dbefore, preferred_element_type=jnp.float32)
    dnormed_mlp = jnp.einsum("blf,cf->blc", dbefore, expand, preferred_element_type=jnp.float32)
    norm_pull = jax.vjp(norm_forward, middle, gain_mlp)[1]
    dmiddle_norm, gain_mlp_grad = norm_pull(dnormed_mlp)
    dmiddle = dresult + dmiddle_norm
    dnormed, project_grad, output_grad = attend_backward(
        normed,
        project,
        output,
        qkv,
        logsum,
        mixed_heads,
        dmiddle.astype(jnp.bfloat16),
        head_count,
        key_mask,
    )
    first_pull = jax.vjp(norm_forward, inputs, gain_attn)[1]
    dinputs_norm, gain_attn_grad = first_pull(dnormed)
    return (
        dmiddle + dinputs_norm,
        (gain_attn_grad, project_grad, output_grad, gain_mlp_grad, expand_grad, shrink_grad),
    )


def char_front(char_text, char_count, language, lang_table, weights):
    present = lax.broadcasted_iota(jnp.int32, char_text.shape[:2], 1) < char_count[:, None]
    onehot = (lax.broadcasted_iota(jnp.int32, (lang_table.shape[0],), 0) == language).astype(
        jnp.bfloat16
    )
    lang_row = jnp.dot(onehot, lang_table, preferred_element_type=jnp.float32)
    inputs = char_text.astype(jnp.float32) + lang_row
    result, stored = block_forward(inputs, weights, CH, present[:, None, None, :])
    summed = jnp.sum(jnp.where(present[:, :, None], result, 0.0), axis=1)
    pooled = (summed / char_count[:, None].astype(jnp.float32)).astype(jnp.bfloat16)
    return (pooled, stored, present, onehot)


def char_back(stored, present, onehot, char_count, dpooled, weights):
    spread = dpooled.astype(jnp.float32) / char_count[:, None].astype(jnp.float32)
    dresult = jnp.where(present[:, :, None], spread[:, None, :], 0.0)
    dinputs, gradients = block_backward(dresult, stored, weights, CH, present[:, None, None, :])
    table_grad = onehot.astype(jnp.float32)[:, None] * jnp.sum(dinputs, axis=(0, 1))[None, :]
    return (dinputs, (table_grad,) + gradients)


def word_full(pooled, cot_rows, word_input, weights):
    length = pooled.shape[0]
    word_start = jnp.dot(pooled, word_input, preferred_element_type=jnp.float32)[None]
    causal = (
        lax.broadcasted_iota(jnp.int32, (length, length), 0)
        >= lax.broadcasted_iota(jnp.int32, (length, length), 1)
    )[None, None]
    result, stored = block_forward(word_start, weights, H, causal)
    dstart, gradients = block_backward(
        cot_rows.astype(jnp.float32)[None], stored, weights, H, causal
    )
    grad_low = dstart[0].astype(jnp.bfloat16)
    input_grad = jnp.einsum("wc,wd->cd", pooled, grad_low, preferred_element_type=jnp.float32)
    dpooled = jnp.einsum(
        "wd,cd->wc", grad_low, word_input, preferred_element_type=jnp.float32
    ).astype(jnp.bfloat16)
    return (result[0], dpooled, (input_grad,) + gradients)


def reduce_rows(gradients):
    shards = lax.axis_size("dp")
    flat = []
    for place, gradient in enumerate(gradients):
        if place == 0:
            gradient = gradient.T
        flat.append(gradient.astype(jnp.bfloat16).reshape(shards, -1))
    packed = jnp.concatenate(flat, axis=1)
    me = lax.axis_index("dp")
    packed = jnp.take(packed, jnp.arange(shards) ^ me, axis=0)
    bit = 1
    while packed.shape[0] > 1:
        pairs = packed.reshape(packed.shape[0] // 2, 2, packed.shape[1])
        arrived = lax.ppermute(pairs[:, 1], "dp", [(i, i ^ bit) for i in range(shards)])
        packed = (pairs[:, 0].astype(jnp.float32) + arrived.astype(jnp.float32)).astype(
            jnp.bfloat16
        )
        bit *= 2
    arrived = lax.ppermute(packed, "section", [(0, 1), (1, 0)])
    total = (packed.astype(jnp.float32) + arrived.astype(jnp.float32))[0]
    outs = []
    at = 0
    for place, gradient in enumerate(gradients):
        size = gradient.size // shards
        piece = total[at : at + size]
        at += size
        if place == 0:
            outs.append(piece.reshape(-1, gradient.shape[0]).T)
        else:
            outs.append(piece.reshape((gradient.shape[0] // shards,) + gradient.shape[1:]))
    return tuple(outs)


def local(
    chars,
    counts,
    languages,
    language_table,
    char_gain_attn,
    char_project,
    char_output,
    char_gain_mlp,
    char_expand,
    char_shrink,
    word_input,
    word_gain_attn,
    word_project,
    word_output,
    word_gain_mlp,
    word_expand,
    word_shrink,
    cotangent,
):
    char_weights = (
        char_gain_attn,
        char_project,
        char_output,
        char_gain_mlp,
        char_expand,
        char_shrink,
    )
    word_weights = (
        word_gain_attn,
        word_project,
        word_output,
        word_gain_mlp,
        word_expand,
        word_shrink,
    )
    if lax.axis_size("dp") == 16:
        return local_grouped(
            chars,
            counts,
            languages,
            language_table,
            char_weights,
            word_input,
            word_weights,
            cotangent,
        )
    section_index = lax.axis_index("section")
    char_text = chars[section_index, 0]
    char_count = counts[section_index, 0]
    language = languages[section_index, 0]
    cot_rows = cotangent[section_index, 0]
    pooled, stored, present, onehot = char_front(
        char_text, char_count, language, language_table, char_weights
    )
    result, dpooled, word_grads = word_full(pooled, cot_rows, word_input, word_weights)
    text_grad, char_grads = char_back(stored, present, onehot, char_count, dpooled, char_weights)
    totals = reduce_rows(char_grads + word_grads)
    return (result[None, None], text_grad[None, None]) + totals


def solution(mesh):
    placed = (
        P(None, "dp", None, None, None),
        P(None, "dp", None),
        P(None, "dp"),
        P(),
        P(),
        P(),
        P(),
        P(),
        P(),
        P(),
        P(),
        P(),
        P(),
        P(),
        P(),
        P(),
        P(),
        P(None, "dp", None, None),
    )
    return jax.shard_map(
        local,
        mesh=mesh,
        in_specs=placed,
        out_specs=(
            P("section", "dp", None, None),
            P("section", "dp", None, None, None),
            P(None, "dp"),
            P("dp"),
            P("dp", None),
            P("dp", None),
            P("dp"),
            P("dp", None),
            P("dp", None),
            P("dp", None),
            P("dp"),
            P("dp", None),
            P("dp", None),
            P("dp"),
            P("dp", None),
            P("dp", None),
        ),
        check_vma=False,
    )
```

```python
import functools

import jax
import jax.numpy as jnp
from jax import lax
from jax.experimental import pallas as pl
from jax.experimental.pallas import tpu as pltpu
from jax.sharding import PartitionSpec as P

CH = 4
H = 8
HEAD = 64
SLAB = 256
HEADS = SLAB // HEAD
BLOCK = 128
MIB = 1024 * 1024

eps = 1e-05

f32 = jnp.float32
bf16 = jnp.bfloat16


def dot(a, b):
    return jnp.dot(a, b, preferred_element_type=f32)


def dot_nt(a, b):
    return lax.dot_general(a, b, (((1,), (1,)), ((), ())), preferred_element_type=f32)


def position():
    return (lax.axis_index("section"), lax.axis_index("dp"))


def lanes(shape):
    return lax.broadcasted_iota(jnp.int32, shape, 1)


def rows_of(shape):
    return lax.broadcasted_iota(jnp.int32, shape, 0)


def stack_heads(a):
    head = lanes((1, SLAB)) // HEAD
    masks = [jnp.where(head == place, 1.0, 0.0).astype(bf16) for place in range(HEADS)]
    return jnp.concatenate([a * mask for mask in masks], axis=0)


def compact(scores, length):
    group = lanes((length, BLOCK)) // length
    total = scores[:length]
    for place in range(1, BLOCK // length):
        total = jnp.where(group == place, scores[place * length : (place + 1) * length], total)
    return total


def compact_heads(scores, length):
    return [
        compact(scores[:, head * BLOCK : (head + 1) * BLOCK], length) for head in range(HEADS)
    ]


def expand(values, length):
    group = lanes((length, BLOCK)) // length
    return jnp.concatenate(
        [jnp.where(group == place, values, 0.0) for place in range(BLOCK // length)], axis=0
    ).astype(bf16)


def expand_heads(values, tile, length):
    first = tile * HEADS * BLOCK
    return [
        expand(values[:, first + head * BLOCK : first + (head + 1) * BLOCK], length)
        for head in range(HEADS)
    ]


def head_rows(a, head):
    return a[head * HEAD : (head + 1) * HEAD]


def attend(load, tiles, key_mask, length):
    scores = []
    for tile in tiles:
        scores += compact_heads(dot_nt(load(tile, 1), stack_heads(load(tile, 0))), length)
    scores = jnp.concatenate(scores, axis=1) * HEAD**-0.5
    scores = jnp.where(key_mask, scores, -1e30)
    weights = jnp.exp(scores - jnp.max(scores, axis=0, keepdims=True))
    probs = weights / jnp.sum(weights, axis=0, keepdims=True)
    mixed = []
    for number, tile in enumerate(tiles):
        values = load(tile, 2).T
        parts = expand_heads(probs, number, length)
        mixed.append(
            jnp.concatenate(
                [dot(head_rows(values, head), parts[head]) for head in range(HEADS)], axis=0
            ).astype(bf16)
        )
    return (probs, mixed)


def attend_back(load, load_dmixed, tiles, probs, store, length):
    dprobs = []
    for number, tile in enumerate(tiles):
        stacked = stack_heads(load_dmixed(tile))
        dprobs += compact_heads(dot_nt(load(tile, 2), stacked), length)
        parts = jnp.concatenate(expand_heads(probs, number, length), axis=1)
        store(tile, 2, dot(parts, stacked).astype(bf16))
    dprobs = jnp.concatenate(dprobs, axis=1)
    dscores = probs * (dprobs - jnp.sum(probs * dprobs, axis=0, keepdims=True))
    scaling = HEAD**-0.5
    for number, tile in enumerate(tiles):
        parts = expand_heads(dscores, number, length)
        keys = load(tile, 1).T
        dq = jnp.concatenate(
            [dot(head_rows(keys, head), parts[head]) for head in range(HEADS)], axis=0
        )
        store(tile, 0, (dq * scaling).astype(bf16).T)
        dk = dot(jnp.concatenate(parts, axis=1), stack_heads(load(tile, 0)))
        store(tile, 1, (dk * scaling).astype(bf16))


def unit(x):
    scale = lax.rsqrt(jnp.mean(x * x, axis=-1, keepdims=True) + eps)
    return (x * scale, scale)


def unit_back(dnormed, gain, normal, scale):
    weighted = dnormed * gain
    return scale * (weighted - normal * jnp.mean(normal * weighted, axis=-1, keepdims=True))


def gelu_parts(before):
    c = 0.7978845608028654
    before = before.astype(bf16)
    square = before * before
    half = bf16(0.5) * jnp.tanh(before * (bf16(c) + bf16(c * 0.044715) * square)) + bf16(0.5)
    value = before * half
    slope = half + value * (bf16(1.0) - half) * (bf16(2.0 * c) + bf16(6.0 * c * 0.044715) * square)
    return (value, slope)


def pick(row, place):
    return jnp.sum(jnp.where(lanes(row.shape) == place, row, 0), axis=1, keepdims=True)


def char_rows(chars, table_ref, language):
    table = table_ref[...].astype(f32)
    row = jnp.sum(jnp.where(rows_of(table.shape) == language, table, 0.0), axis=0, keepdims=True)
    return chars.astype(f32) + row


def counts_by_row(counts, rows, slots):
    words = counts.shape[-1]
    counts = jnp.broadcast_to(counts.astype(f32), (8, words)).astype(bf16)
    shape = (words, rows)
    member = lanes(shape) // slots == rows_of(shape)
    return dot(counts, jnp.where(member, 1.0, 0.0).astype(bf16))[:1]


def counts_column(counts):
    words = counts.shape[-1]
    shape = (words, words)
    spread = jnp.broadcast_to(counts.astype(f32), shape)
    return jnp.sum(
        jnp.where(rows_of(shape) == lanes(shape), spread, 0.0), axis=1, keepdims=True
    )


def fetch_all(sources, targets, sems):
    fetches = [
        pltpu.make_async_copy(source, target, sems.at[place])
        for place, (source, target) in enumerate(zip(sources, targets))
    ]
    for fetch in fetches:
        fetch.start()
    return fetches


def in_hbm(array):
    return pltpu.with_memory_space_constraint(array, pltpu.HBM)


def char_forward_kernel(
    slots,
    chars_hbm,
    languages_hbm,
    counts_hbm,
    table_hbm,
    gain_attn_hbm,
    project_hbm,
    output_hbm,
    gain_mlp_hbm,
    expand_hbm,
    shrink_hbm,
    pooled_ref,
    hidden_sum_ref,
    counts_ref,
    qkv_ref,
    probs_ref,
    mixed_ref,
    middle_ref,
    slope_ref,
    chars_ref,
    languages_ref,
    table_ref,
    gain_attn_ref,
    project_ref,
    output_ref,
    gain_mlp_ref,
    expand_ref,
    shrink_ref,
    sems,
):
    section, _ = position()
    fetches = fetch_all(
        (
            languages_hbm,
            counts_hbm,
            table_hbm,
            gain_attn_hbm,
            chars_hbm.at[section],
            project_hbm,
            output_hbm,
            gain_mlp_hbm,
            expand_hbm,
            shrink_hbm,
        ),
        (
            languages_ref,
            counts_ref,
            table_ref,
            gain_attn_ref,
            chars_ref,
            project_ref,
            output_ref,
            gain_mlp_ref,
            expand_ref,
            shrink_ref,
        ),
        sems,
    )
    for fetch in fetches[:2]:
        fetch.wait()
    counts = counts_ref[section]
    rows = chars_ref.shape[0]
    words = counts.shape[-1]
    row_counts = counts_by_row(counts, rows, slots)
    for fetch in fetches[2:5]:
        fetch.wait()
    x = char_rows(chars_ref[...], table_ref, pick(languages_ref[...], section))
    normal, _ = unit(x)
    normed = (normal * gain_attn_ref[...]).astype(bf16)
    fetches[5].wait()
    qkv_ref[...] = dot(normed, project_ref[...]).astype(bf16)
    blocks = range(rows // BLOCK)

    def load(block, which):
        return qkv_ref[block * BLOCK : (block + 1) * BLOCK, which * SLAB : (which + 1) * SLAB]

    by_head = jnp.concatenate(
        [row_counts[:, block * BLOCK : (block + 1) * BLOCK] for block in blocks for _ in range(HEADS)],
        axis=1,
    )
    key_mask = rows_of((slots, rows * HEADS)).astype(f32) < by_head
    probs, mixed = attend(load, blocks, key_mask, slots)
    probs_ref[...] = probs
    for block in blocks:
        mixed_ref[:, block * BLOCK : (block + 1) * BLOCK] = mixed[block]
    mixed = mixed_ref[...].T
    fetches[6].wait()
    middle = x + dot(mixed, output_ref[...])
    middle_ref[...] = middle
    normal, _ = unit(middle)
    fetches[7].wait()
    normed = (normal * gain_mlp_ref[...]).astype(bf16)
    word_shape = (words, rows)
    lane = lanes(word_shape)
    member = (lane // slots == rows_of(word_shape)) & ((lane % slots).astype(f32) < row_counts)
    member = jnp.where(member, 1.0, 0.0).astype(bf16)
    fetches[8].wait()
    parts = [slice(at, at + 256) for at in range(0, expand_ref.shape[1], 256)]
    before = dot(normed, expand_ref[:, parts[0]])
    for number, part in enumerate(parts):
        value, slope = gelu_parts(before)
        if number + 1 < len(parts):
            before = dot(normed, expand_ref[:, parts[number + 1]])
        slope_ref[:, part] = slope
        hidden_sum_ref[:, part] = dot(member, value).astype(bf16)
    high = middle.astype(bf16)
    low = (middle - high.astype(f32)).astype(bf16)
    fetches[9].wait()
    total = dot(member, high) + dot(member, low) + dot(hidden_sum_ref[...], shrink_ref[...])
    pooled_ref[...] = (total / counts_column(counts)).astype(bf16)


def char_forward(languages, chars, counts, table, weights, slots):
    rows, width = chars.shape[1:]
    words = rows // slots
    hidden = weights[4].shape[1]
    vmem = pl.BlockSpec(memory_space=pltpu.VMEM)
    hbm = pl.BlockSpec(memory_space=pltpu.HBM)
    fetched = (languages, counts, table) + tuple(weights)
    return pl.pallas_call(
        functools.partial(char_forward_kernel, slots),
        in_specs=[hbm] * 10,
        out_specs=[vmem] * 8,
        out_shape=[
            jax.ShapeDtypeStruct((words, width), bf16),
            jax.ShapeDtypeStruct((words, hidden), bf16),
            jax.ShapeDtypeStruct(counts.shape, counts.dtype),
            jax.ShapeDtypeStruct((rows, 3 * width), bf16),
            jax.ShapeDtypeStruct((slots, rows * HEADS), f32),
            jax.ShapeDtypeStruct((width, rows), bf16),
            jax.ShapeDtypeStruct((rows, width), f32),
            jax.ShapeDtypeStruct((rows, hidden), bf16),
        ],
        scratch_shapes=[pltpu.VMEM(chars.shape[1:], bf16)]
        + [pltpu.VMEM(array.shape, array.dtype) for array in fetched if array is not counts]
        + [pltpu.SemaphoreType.DMA((10,))],
        compiler_params=pltpu.CompilerParams(vmem_limit_bytes=16 * MIB),
        cost_estimate=pl.CostEstimate(
            flops=64 * rows * width * width, bytes_accessed=8 * MIB, transcendentals=0
        ),
        name="char_forward",
    )(*[in_hbm(array) for array in (chars,) + fetched])


CHAR_FIRST_SLOT = 144
CHAR_SECTION_SLOT = 80
CHAR_CORE_SLOT = 112
CHAR_LAST_SLOT = 48


def char_shard(slot, me):
    return me ^ ((slot >> 3) | (((slot >> 1) & 3) << 1) | ((slot & 1) << 3))


def put_shards(gradient, slots, shard_of, at):
    width = SLAB
    columns = gradient.shape[1] // width
    size = gradient.shape[0] // len(slots)
    for number, slot in enumerate(slots):
        first = pl.multiple_of(shard_of(number) * size, size)
        for column in range(columns):
            start = at + column * size
            slot[start : start + size] = gradient[
                pl.ds(first, size), column * width : (column + 1) * width
            ].astype(bf16)
    return at + size * columns


def slot_refs(*refs):
    return [ref.at[place] for ref in refs for place in range(ref.shape[0])]


def char_mlp_back_kernel(
    slots,
    shards,
    counts_ref,
    gain_mlp_ref,
    expand_ref,
    shrink_ref,
    dpooled_ref,
    hidden_sum_ref,
    other_sum_ref,
    mixed_ref,
    middle_ref,
    slope_ref,
    dmiddle_ref,
    gain_ref,
    keep_ref,
    send_ref,
    dhidden_words,
    dz,
    dbefore,
    expand_grad,
    shrink_grad,
    output_grad,
):
    section, me = position()
    counts = counts_ref[section]
    rows, width = middle_ref.shape
    words = counts.shape[-1]
    spread = dpooled_ref[:words].astype(f32) / counts_column(counts)
    spread_high = spread.astype(bf16)
    spread_low = (spread - spread_high.astype(f32)).astype(bf16)
    dhidden_words[...] = dot_nt(spread_high, shrink_ref[...]).astype(bf16)
    dz[:words] = spread_high
    other = dpooled_ref[words:].astype(f32) / counts_column(counts_ref[1 - section])
    dz[words:] = other.astype(bf16)
    shape = (rows, words)
    row = rows_of(shape)
    member = (row // slots == lanes(shape)) & (row % slots < counts)
    member = jnp.where(member, 1.0, 0.0).astype(bf16)
    for at in range(0, expand_ref.shape[1], 256):
        part = slice(at, at + 256)
        dbefore[:, part] = dot(member, dhidden_words[:, part]).astype(bf16) * slope_ref[:, part]
    normal, scale = unit(middle_ref[...])
    normed_t = (normal * gain_mlp_ref[...]).astype(bf16).T
    hidden_sums = jnp.concatenate([hidden_sum_ref[...], other_sum_ref[...]], axis=0)
    hidden_sums_t = hidden_sums.T

    dnormed = dot_nt(dbefore[...], expand_ref[...])
    expand_grad[...] = dot(normed_t, dbefore[...])
    half = width // 2
    own_half = dz[:, pl.ds(pl.multiple_of(section * half, half), half)]
    shrink_grad[...] = dot(hidden_sums_t, own_half)
    dmiddle = (
        dot(member, spread_high)
        + dot(member, spread_low)
        + unit_back(dnormed, gain_mlp_ref[...], normal, scale)
    )
    dmiddle_ref[...] = dmiddle
    output_grad[...] = dot(mixed_ref[...], dmiddle.astype(bf16))
    gain_ref[...] = jnp.broadcast_to(
        jnp.sum(dnormed * normal, axis=0, keepdims=True), gain_ref.shape
    )
    targets = slot_refs(keep_ref, send_ref)
    at = 0
    for gradient in (expand_grad, output_grad):
        at = put_shards(gradient, targets, lambda slot: char_shard(slot, me), at)
    size = shrink_grad.shape[0] // shards
    for number, target in enumerate(targets):
        first = pl.multiple_of(char_shard(number, me) * size, size)
        piece = shrink_grad[pl.ds(first, size), :].astype(bf16)
        target[at:, :half] = piece[: size // 2]
        target[at:, half:] = piece[size // 2 :]


def char_mlp_back(counts, weights, dpooled, stored, other_sum, slots, shards):
    _, _, output, gain_mlp, expand_w, shrink = weights
    hidden_sum, _, _, mixed, middle, slope = stored
    rows, width = middle.shape
    words = rows // slots
    hidden = expand_w.shape[1]
    half = (shards // 2, CHAR_CORE_SLOT, width)
    vmem = pl.BlockSpec(memory_space=pltpu.VMEM)
    return pl.pallas_call(
        functools.partial(char_mlp_back_kernel, slots, shards),
        in_specs=[vmem] * 10,
        out_specs=[vmem] * 4,
        out_shape=[
            jax.ShapeDtypeStruct((rows, width), f32),
            jax.ShapeDtypeStruct((8, width), f32),
            jax.ShapeDtypeStruct(half, bf16),
            jax.ShapeDtypeStruct(half, bf16),
        ],
        scratch_shapes=[
            pltpu.VMEM((words, hidden), bf16),
            pltpu.VMEM((2 * words, width), bf16),
            pltpu.VMEM((rows, hidden), bf16),
            pltpu.VMEM(expand_w.shape, f32),
            pltpu.VMEM((hidden, width // 2), f32),
            pltpu.VMEM(output.shape, f32),
        ],
        compiler_params=pltpu.CompilerParams(vmem_limit_bytes=16 * MIB),
        cost_estimate=pl.CostEstimate(
            flops=64 * rows * width * width, bytes_accessed=8 * MIB, transcendentals=0
        ),
        name="char_mlp_back",
    )(
        counts,
        gain_mlp,
        expand_w,
        shrink,
        dpooled,
        hidden_sum,
        other_sum,
        mixed,
        middle,
        slope,
    )


def char_attn_back_kernel(
    slots,
    shards,
    _,
    chars_hbm,
    languages_hbm,
    table_ref,
    gain_attn_ref,
    project_ref,
    output_ref,
    dmiddle_ref,
    gain_mlp_grad_ref,
    qkv_ref,
    probs_ref,
    grad_hbm,
    keep_ref,
    send_ref,
    chars_ref,
    languages_ref,
    dmixed,
    dqkv,
    grad,
    project_grad,
    sems,
):
    section, me = position()
    fetches = fetch_all(
        (chars_hbm.at[section], languages_hbm), (chars_ref, languages_ref), sems
    )
    rows, width = dmiddle_ref.shape
    dmixed[...] = dot_nt(dmiddle_ref[...].astype(bf16), output_ref[...]).astype(bf16)

    def load(block, which):
        return qkv_ref[block * BLOCK : (block + 1) * BLOCK, which * SLAB : (which + 1) * SLAB]

    def load_dmixed(block):
        return dmixed[block * BLOCK : (block + 1) * BLOCK]

    def store(block, which, value):
        dqkv[block * BLOCK : (block + 1) * BLOCK, which * SLAB : (which + 1) * SLAB] = value

    attend_back(load, load_dmixed, range(rows // BLOCK), probs_ref[...], store, slots)
    for fetch in fetches:
        fetch.wait()
    language = pick(languages_ref[...], section)
    normal, scale = unit(char_rows(chars_ref[...], table_ref, language))
    normed_t = (normal * gain_attn_ref[...]).astype(bf16).T
    dnormed = dot_nt(dqkv[...], project_ref[...])
    project_grad[...] = dot(normed_t, dqkv[...])
    gain_attn_grad = jnp.sum(dnormed * normal, axis=0, keepdims=True)
    dx = dmiddle_ref[...] + unit_back(dnormed, gain_attn_ref[...], normal, scale)
    grad[...] = dx
    leave = pltpu.make_async_copy(grad, grad_hbm, sems.at[2])
    leave.start()
    row_sum = jnp.sum(dx, axis=0, keepdims=True)
    targets = [
        ref.at[pl.ds(place * CHAR_LAST_SLOT, CHAR_LAST_SLOT)]
        for ref in (keep_ref, send_ref)
        for place in range(shards // 2)
    ]
    put_shards(project_grad, targets, lambda slot: char_shard(slot, me), 0)
    extra = jnp.concatenate(
        [
            gain_attn_grad,
            gain_mlp_grad_ref[:7],
            jnp.where(rows_of((8, 1)) == language, row_sum, 0.0),
        ],
        axis=0,
    ).astype(bf16)
    for ref in (keep_ref, send_ref):
        ref[ref.shape[0] - 16 :] = extra
    leave.wait()


def char_attn_back(
    languages, chars, table, weights, dmiddle, gain_mlp_grad, stored, slots, shards, after
):
    gain_attn, project, output, _, _, _ = weights
    _, qkv, probs, _, _, _ = stored
    rows, width = dmiddle.shape
    half = (shards // 2 * CHAR_LAST_SLOT + 16, width)
    vmem = pl.BlockSpec(memory_space=pltpu.VMEM)
    hbm = pl.BlockSpec(memory_space=pltpu.HBM)
    return pl.pallas_call(
        functools.partial(char_attn_back_kernel, slots, shards),
        in_specs=[pl.BlockSpec(memory_space=pl.ANY), hbm, hbm] + [vmem] * 8,
        out_specs=[hbm, vmem, vmem],
        out_shape=[
            jax.ShapeDtypeStruct((rows, width), f32),
            jax.ShapeDtypeStruct(half, bf16),
            jax.ShapeDtypeStruct(half, bf16),
        ],
        scratch_shapes=[
            pltpu.VMEM((rows, width), bf16),
            pltpu.VMEM(languages.shape, languages.dtype),
            pltpu.VMEM((rows, width), bf16),
            pltpu.VMEM((rows, 3 * width), bf16),
            pltpu.VMEM((rows, width), f32),
            pltpu.VMEM(project.shape, f32),
            pltpu.SemaphoreType.DMA((3,)),
        ],
        compiler_params=pltpu.CompilerParams(vmem_limit_bytes=16 * MIB),
        cost_estimate=pl.CostEstimate(
            flops=0, bytes_accessed=0, transcendentals=0
        ),
        name="char_attn_back",
    )(
        after,
        in_hbm(chars),
        in_hbm(languages),
        table,
        gain_attn,
        project,
        output,
        dmiddle,
        gain_mlp_grad,
        qkv,
        probs,
    )


LONG = pl.CostEstimate(flops=20_000_000_000, bytes_accessed=8 * MIB, transcendentals=0)

WORD_SLOT = 416

SHORT_FLOPS = 475_000_000


def word_kernel(
    length,
    shards,
    own_ref,
    both_ref,
    section_ref,
    far_ref,
    cot_ref,
    cot_far_ref,
    input_ref,
    gain_attn_ref,
    project_ref,
    output_ref,
    gain_mlp_ref,
    expand_ref,
    shrink_ref,
    result_hbm,
    dpooled_ref,
    keep_ref,
    send_ref,
    pooled,
    pooled_t,
    dz,
    start,
    normed_t,
    qkv,
    kept,
    mixed_t,
    middle,
    normed_mlp_t,
    hidden,
    dbefore,
    dmixed,
    dqkv,
    dy,
    dstart,
    result,
    input_grad,
    project_grad,
    output_grad,
    expand_grad,
    shrink_grad,
    sem,
):
    total = pooled.shape[0]
    width = output_ref.shape[0]
    section, me = position()
    slabs = width // SLAB
    for place, ref in enumerate((own_ref, section_ref, far_ref, both_ref)):
        pooled[place * length : (place + 1) * length] = ref[...]
    for place, (ref, other) in enumerate(
        ((cot_ref, section), (cot_ref, 1 - section), (cot_far_ref, section), (cot_far_ref, 1 - section))
    ):
        dz[place * length : (place + 1) * length] = ref[other]

    x = dot(pooled[...], input_ref[...])
    start[...] = x
    normal, _ = unit(x)
    low = (normal * gain_attn_ref[...]).astype(bf16)
    normed_t[...] = low.T
    qkv[...] = dot(low, project_ref[...]).astype(bf16)
    tiles = [(block, slab) for block in range(total // BLOCK) for slab in range(slabs)]

    def load(tile, which):
        block, slab = tile
        at = which * width + slab * SLAB
        return qkv[block * BLOCK : (block + 1) * BLOCK, at : at + SLAB]

    mask_shape = (length, len(tiles) * HEADS * BLOCK)
    causal = rows_of(mask_shape) <= lanes(mask_shape) % length
    probs, mixed = attend(load, tiles, causal, length)
    kept[...] = probs
    for (block, slab), piece in zip(tiles, mixed):
        mixed_t[slab * SLAB : (slab + 1) * SLAB, block * BLOCK : (block + 1) * BLOCK] = piece
    x = x + dot(mixed_t[...].T, output_ref[...])
    middle[...] = x
    normal, _ = unit(x)
    low = (normal * gain_mlp_ref[...]).astype(bf16)
    normed_mlp_t[...] = low.T
    dz_all = dz[...]
    for at in range(0, expand_ref.shape[1], 256):
        part = slice(at, at + 256)
        value, bend = gelu_parts(dot(low, expand_ref[:, part]))
        hidden[:, part] = value
        dhidden = dot_nt(dz_all, shrink_ref[part, :]).astype(bf16)
        dbefore[:, part] = dhidden * bend

    def shard_of(slot):
        return (me & 7) ^ ((slot >> 2) | ((slot & 3) << 1))

    def own_rows(flipped):
        many = flipped.shape[0] // 2
        return flipped[pl.ds(pl.multiple_of((me >> 3) * many, many), many), :]

    def half_columns(ref, place):
        many = ref.shape[1] // 2
        return ref[:, pl.ds(pl.multiple_of(place * many, many), many)]

    def own_columns(ref):
        return half_columns(ref, section)

    targets = slot_refs(keep_ref, send_ref)
    hidden_t = half_columns(hidden, me >> 3).T
    pooled_t[...] = pooled[...].T
    normal, scale = unit(middle[...])
    dnormed = dot_nt(dbefore[...], expand_ref[...])
    expand_grad[...] = dot(own_rows(normed_mlp_t), own_columns(dbefore))
    shrink_grad[...] = dot(hidden_t, own_columns(dz))
    dmiddle = dz_all.astype(f32) + unit_back(dnormed, gain_mlp_ref[...], normal, scale)
    dy_low = dmiddle.astype(bf16)
    dy[...] = dy_low
    dmixed[...] = dot_nt(dy_low, output_ref[...]).astype(bf16)
    gain_mlp_grad = jnp.sum(dnormed * normal, axis=0, keepdims=True)
    result[...] = middle[:length] + dot(hidden[:length], shrink_ref[...])
    leave = pltpu.make_async_copy(result, result_hbm, sem)
    leave.start()
    output_grad[...] = dot(own_rows(mixed_t), own_columns(dy))

    def load_dmixed(tile):
        block, slab = tile
        return dmixed[block * BLOCK : (block + 1) * BLOCK, slab * SLAB : (slab + 1) * SLAB]

    def store(tile, which, value):
        block, slab = tile
        at = which * width + slab * SLAB
        dqkv[block * BLOCK : (block + 1) * BLOCK, at : at + SLAB] = value

    attend_back(load, load_dmixed, tiles, kept[...], store, length)
    normal, scale = unit(start[...])
    dnormed = dot_nt(dqkv[...], project_ref[...])
    project_grad[...] = dot(own_rows(normed_t), own_columns(dqkv))
    dword = (dmiddle + unit_back(dnormed, gain_attn_ref[...], normal, scale)).astype(bf16)
    dpooled_ref[...] = dot_nt(dword[: 2 * length], input_ref[...]).astype(bf16)
    dstart[...] = dword
    gain_attn_grad = jnp.sum(dnormed * normal, axis=0, keepdims=True)
    input_grad[...] = dot(own_rows(pooled_t), own_columns(dstart))
    at = 0
    for ref in (input_grad, project_grad, output_grad, expand_grad, shrink_grad):
        at = put_shards(ref, targets, shard_of, at)
    extra = jnp.concatenate(
        [gain_attn_grad[:, :SLAB], gain_attn_grad[:, SLAB:]]
        + [gain_mlp_grad[:, :SLAB], gain_mlp_grad[:, SLAB:]]
        + [jnp.zeros((12, SLAB), f32)],
        axis=0,
    ).astype(bf16)
    for target in targets:
        target[at : at + 16] = extra
    leave.wait()


def word_group(pooled, cotangents, word_input, weights, shards):
    gain_attn, project, output, gain_mlp, expand_w, shrink = weights
    length, channels = pooled[0].shape
    width = output.shape[0]
    hidden = expand_w.shape[1]
    total = 4 * length
    half = (4, WORD_SLOT, SLAB)
    vmem = pl.BlockSpec(memory_space=pltpu.VMEM)
    hbm = pl.BlockSpec(memory_space=pltpu.HBM)
    return pl.pallas_call(
        functools.partial(word_kernel, length, shards),
        in_specs=[vmem] * 13,
        out_specs=[hbm, vmem, vmem, vmem],
        out_shape=[
            jax.ShapeDtypeStruct((length, width), f32),
            jax.ShapeDtypeStruct((2 * length, channels), bf16),
            jax.ShapeDtypeStruct(half, bf16),
            jax.ShapeDtypeStruct(half, bf16),
        ],
        scratch_shapes=[
            pltpu.VMEM((total, channels), bf16),
            pltpu.VMEM((channels, total), bf16),
            pltpu.VMEM((total, width), bf16),
            pltpu.VMEM((total, width), f32),
            pltpu.VMEM((width, total), bf16),
            pltpu.VMEM((total, 3 * width), bf16),
            pltpu.VMEM((length, total * (width // HEAD)), f32),
            pltpu.VMEM((width, total), bf16),
            pltpu.VMEM((total, width), f32),
            pltpu.VMEM((width, total), bf16),
            pltpu.VMEM((total, hidden), bf16),
            pltpu.VMEM((total, hidden), bf16),
            pltpu.VMEM((total, width), bf16),
            pltpu.VMEM((total, 3 * width), bf16),
            pltpu.VMEM((total, width), bf16),
            pltpu.VMEM((total, width), bf16),
            pltpu.VMEM((length, width), f32),
            pltpu.VMEM((channels // 2, width // 2), f32),
            pltpu.VMEM((width // 2, 3 * width // 2), f32),
            pltpu.VMEM((width // 2, width // 2), f32),
            pltpu.VMEM((width // 2, hidden // 2), f32),
            pltpu.VMEM((hidden // 2, width // 2), f32),
            pltpu.SemaphoreType.DMA,
        ],
        compiler_params=pltpu.CompilerParams(vmem_limit_bytes=20 * MIB),
        cost_estimate=pl.CostEstimate(
            flops=total * width * width * 25 * 4, bytes_accessed=8 * MIB, transcendentals=0
        ),
        name="word_group",
    )(*pooled, *cotangents, word_input, gain_attn, project, output, gain_mlp, expand_w, shrink)


def summed(*parts):
    return functools.reduce(lambda a, b: a + b, [part.astype(f32) for part in parts])


def added(*parts):
    return summed(*parts).astype(bf16)


def by_section(section, low, high):
    return (jnp.where(section == 0, low, high), jnp.where(section == 0, high, low))


def word_sum_kernel(keep, arrived, *outs):
    for place, ref in enumerate(outs):
        ref[...] = added(keep[place], arrived[place])


def word_sum(keep, arrived):
    return pl.pallas_call(
        word_sum_kernel,
        out_shape=[jax.ShapeDtypeStruct((WORD_SLOT, SLAB), bf16)] * 4,
        compiler_params=pltpu.CompilerParams(vmem_limit_bytes=12 * MIB),
        name="word_sum",
    )(keep, arrived)


def first_sum_kernel(keep, arrived, stay_ref, go_ref, shrink_ref):
    section, _ = position()
    half = SLAB // 2
    for place in range(keep.shape[0]):
        total = added(keep[place], arrived[place])
        rows = total[:CHAR_SECTION_SLOT]
        stay_ref[place], go_ref[place] = by_section(section, rows[:, :half], rows[:, half:])
        rows = total[CHAR_SECTION_SLOT:]
        shrink_ref[place] = jnp.concatenate([rows[:, :half], rows[:, half:]], axis=0)


def first_sum(keep, arrived):
    half = jax.ShapeDtypeStruct((keep.shape[0], CHAR_SECTION_SLOT, SLAB // 2), bf16)
    shrink = jax.ShapeDtypeStruct(
        (keep.shape[0], CHAR_FIRST_SLOT - CHAR_SECTION_SLOT, SLAB // 2), bf16
    )
    return pl.pallas_call(
        first_sum_kernel,
        out_shape=[half, half, shrink],
        compiler_params=pltpu.CompilerParams(vmem_limit_bytes=12 * MIB),
        name="first_sum",
    )(keep, arrived)


def section_sum_kernel(stay, arrived, out):
    out[...] = added(stay[...], arrived[...])


def section_sum(stay, arrived):
    return pl.pallas_call(
        section_sum_kernel,
        out_shape=jax.ShapeDtypeStruct(stay.shape, bf16),
        compiler_params=pltpu.CompilerParams(vmem_limit_bytes=12 * MIB),
        cost_estimate=pl.CostEstimate(flops=SHORT_FLOPS, bytes_accessed=0, transcendentals=0),
        name="section_sum",
    )(stay, arrived)


def second_sum_kernel(first, shrink, keep, core_arrived, *outs):
    _, me = position()
    half = SLAB // 2
    extra = summed(keep[-16:], core_arrived[-16:])
    for place, out in enumerate(outs):
        at = CHAR_FIRST_SLOT
        for far in range(2):
            entry = 2 * place + far
            columns = slice(far * half, (far + 1) * half)
            total = first[entry]
            middle = CHAR_SECTION_SLOT - 16
            out[:middle, columns] = total[:middle]
            out[middle : CHAR_FIRST_SLOT - 16, columns] = shrink[entry]
            out[CHAR_FIRST_SLOT - 16 : CHAR_FIRST_SLOT, columns] = total[middle:]
            rows = slice(entry * CHAR_LAST_SLOT, (entry + 1) * CHAR_LAST_SLOT)
            out[at : at + CHAR_LAST_SLOT] = added(keep[rows], core_arrived[rows])
            at += CHAR_LAST_SLOT
            turn = lax.rem(SLAB - char_shard(entry, me) * 16, SLAB)
            out[-16:, columns] = pltpu.roll(extra, turn, 1)[:, :half].astype(bf16)


def total_kernel(*refs):
    refs[-1][...] = added(*[ref[...] for ref in refs[:-1]])


def total_of(*pieces):
    return pl.pallas_call(
        total_kernel,
        out_shape=jax.ShapeDtypeStruct(pieces[0].shape, bf16),
        compiler_params=pltpu.CompilerParams(vmem_limit_bytes=12 * MIB),
        cost_estimate=LONG,
        name="total",
    )(*pieces)


def second_sum(first, last):
    rows = CHAR_FIRST_SLOT + 2 * CHAR_LAST_SLOT + 16
    return pl.pallas_call(
        second_sum_kernel,
        out_shape=[jax.ShapeDtypeStruct((rows, SLAB), bf16)] * 4,
        compiler_params=pltpu.CompilerParams(vmem_limit_bytes=12 * MIB),
        name="second_sum",
    )(*first, *last)


FOLD = 80


def plane_sum_kernel(*refs):
    half = SLAB // 2
    pieces = refs[:4]
    for far, out in enumerate(refs[5:]):
        columns = slice(far * half, (far + 1) * half)
        total = added(*[ref[:CHAR_FIRST_SLOT, columns] for ref in pieces])
        out[:FOLD, :half] = total[:FOLD]
        out[:FOLD, half:] = total[CHAR_FIRST_SLOT - FOLD :]
        out[:16, half:] = added(*[ref[-16:, columns] for ref in pieces])
        first = CHAR_FIRST_SLOT + far * CHAR_LAST_SLOT
        out[FOLD:] = added(*[ref[first : first + CHAR_LAST_SLOT] for ref in pieces])


def plane_sum(pieces, after):
    return pl.pallas_call(
        plane_sum_kernel,
        in_specs=[pl.BlockSpec(memory_space=pltpu.VMEM)] * 4 + [pl.BlockSpec(memory_space=pl.ANY)],
        out_shape=[jax.ShapeDtypeStruct((FOLD + CHAR_LAST_SLOT, SLAB), bf16)] * 2,
        compiler_params=pltpu.CompilerParams(vmem_limit_bytes=12 * MIB),
        cost_estimate=LONG,
        name="plane_sum",
    )(*pieces, after)


def char_last_kernel(near_ref, both_ref, far_ref, section_ref, _, *outs):
    section, _ = position()
    half = SLAB // 2
    mine = summed(near_ref[:FOLD], far_ref[:FOLD])
    theirs = summed(section_ref[:FOLD], both_ref[:FOLD])

    def unfold(total):
        return jnp.concatenate(
            [total[:, :half], total[2 * FOLD - CHAR_FIRST_SLOT :, half:]], axis=0
        )

    first = jnp.concatenate(by_section(section, unfold(mine), unfold(theirs)), axis=1)
    extra = mine[:16, half:] + theirs[:16, half:]
    last = summed(near_ref[FOLD:], section_ref[FOLD:], far_ref[FOLD:], both_ref[FOLD:])
    table_ref, gain_attn_ref, project_ref, output_ref, gain_mlp_ref, expand_ref, shrink_ref = outs
    for total, refs in ((first, (expand_ref, shrink_ref, output_ref)), (last, (project_ref,))):
        at = 0
        for ref in refs:
            size = ref.shape[0]
            for column in range(ref.shape[1] // SLAB):
                ref[:, column * SLAB : (column + 1) * SLAB] = total[at : at + size]
                at += size
    size = gain_attn_ref.shape[1]
    gain_attn_ref[...] = extra[0:1, :size]
    gain_mlp_ref[...] = extra[1:2, :size]
    table_ref[...] = extra[8:16, :size]


def char_last(near, arrived, shapes, after):
    return pl.pallas_call(
        char_last_kernel,
        in_specs=[pl.BlockSpec(memory_space=pltpu.VMEM)] * 4 + [pl.BlockSpec(memory_space=pltpu.HBM)],
        out_shape=[jax.ShapeDtypeStruct(shape, f32) for shape in shapes],
        compiler_params=pltpu.CompilerParams(vmem_limit_bytes=12 * MIB),
        name="char_last",
    )(near, *arrived, in_hbm(after))


def word_last_kernel(own_ref, other_ref, *outs):
    section, me = position()
    own = own_ref[...].astype(f32)
    halves = by_section(section, own, other_ref[...].astype(f32))
    input_ref, gain_attn_ref, project_ref, output_ref, gain_mlp_ref, expand_ref, shrink_ref = outs
    at = 0
    for ref in (input_ref, project_ref, output_ref, expand_ref, shrink_ref):
        size = ref.shape[0]
        columns = ref.shape[1] // (2 * SLAB)
        for column in range(columns):
            for half in range(2):
                first = (half * columns + column) * SLAB
                ref[:, first : first + SLAB] = halves[half][at : at + size]
            at += size
    size = gain_attn_ref.shape[1]
    turn = lax.rem(SLAB - lax.rem(me * size, SLAB), SLAB)
    turned = pltpu.roll(own[at : at + 8], turn, 1)[:, :size]
    upper = me * size >= SLAB
    gain_attn_ref[...] = jnp.where(upper, turned[1:2], turned[0:1])
    gain_mlp_ref[...] = jnp.where(upper, turned[3:4], turned[2:3])


def word_last(own, other, shapes):
    return pl.pallas_call(
        word_last_kernel,
        out_shape=[jax.ShapeDtypeStruct(shape, f32) for shape in shapes],
        compiler_params=pltpu.CompilerParams(vmem_limit_bytes=12 * MIB),
        name="word_last",
    )(own, other)


def exchange(value, section_bit, dp_bits):
    shards = lax.axis_size("dp")
    pairs = [
        (s * shards + d, (s ^ section_bit) * shards + (d ^ dp_bits))
        for s in range(lax.axis_size("section"))
        for d in range(shards)
    ]
    return lax.ppermute(value, ("section", "dp"), pairs)


CORE, SIDE, NEAR, FAR = (1, 2, 4, 8)


def plane_exchange(pieces):
    return tuple(
        exchange(piece, 0, bits) for piece, bits in zip(pieces[:0:-1], (SIDE | NEAR, NEAR, SIDE))
    ) + (pieces[0],)


def local_grouped(
    chars, counts, languages, language_table, char_weights, word_input, word_weights, cotangent
):
    shards = lax.axis_size("dp")
    micros, _, words, slots, width = chars.shape
    rows = words * slots
    cot = cotangent[:, 0]
    cot_far = exchange(cot, 0, FAR)
    char_weights = tuple(w[None] if w.ndim == 1 else w for w in char_weights)
    word_weights = tuple(w[None] if w.ndim == 1 else w for w in word_weights)
    chars = chars.reshape(micros, rows, width)
    counts = counts.reshape(micros, 1, words)
    languages = languages.reshape(1, micros)
    pooled, hidden_sum, own_counts, *stored = char_forward(
        languages, chars, counts, language_table, char_weights, slots
    )
    stored = (hidden_sum, *stored)
    other_sum = exchange(hidden_sum, 1, 0)
    others = (exchange(pooled, 1, FAR), exchange(pooled, 1, 0), exchange(pooled, 0, FAR))
    result, dpooled, keep, send = word_group(
        (pooled,) + others, (cot, cot_far), word_input, word_weights, shards
    )
    word = plane_exchange(word_sum(keep, exchange(send, 0, CORE)))
    dmiddle, gain_mlp_grad, keep, send = char_mlp_back(
        own_counts, char_weights, dpooled, stored, other_sum, slots, shards
    )
    stay, go, shrink = first_sum(keep, exchange(send, 0, CORE))
    first = (section_sum(stay, exchange(go, 1, 0)), shrink)
    chars_grad, keep, send = char_attn_back(
        languages,
        chars,
        language_table,
        char_weights,
        dmiddle,
        gain_mlp_grad,
        stored,
        slots,
        shards,
        stay,
    )
    last = (keep, exchange(send, 0, CORE))
    char = plane_exchange(second_sum(first, last))
    word = total_of(*word)
    near, far = plane_sum(char, word)
    arrived = (exchange(far, 1, FAR), exchange(far, 0, FAR), exchange(near, 1, 0))

    def shard_shapes(weights):
        for weight in weights:
            if weight.shape[0] == 1:
                yield (1, weight.shape[1] // shards)
            else:
                yield (weight.shape[0] // shards, weight.shape[1])

    table_shape = (language_table.shape[0], language_table.shape[1] // shards)
    word_shapes = list(shard_shapes((word_input,) + word_weights))
    word_totals = word_last(word, exchange(word, 1, 0), word_shapes)
    char_shapes = [table_shape, *shard_shapes(char_weights)]
    char_totals = char_last(near, arrived, char_shapes, word_totals[0])
    totals = [total[0] if total.shape[0] == 1 else total for total in char_totals + word_totals]
    return (result[None, None], chars_grad.reshape((1, 1, words, slots, width))) + tuple(totals)


def norm_forward(inputs, gain):
    return inputs * lax.rsqrt(jnp.mean(inputs * inputs, axis=-1, keepdims=True) + eps) * gain


def attend_forward(normed, project, head_count, key_mask):
    row_count, length, channels = normed.shape
    head_size = channels // head_count
    qkv = jnp.einsum("blc,cf->blf", normed, project, preferred_element_type=jnp.float32).astype(
        jnp.bfloat16
    )
    pieces = qkv.reshape(row_count, length, 3, head_count, head_size)
    scores = jnp.einsum(
        "bqhd,bkhd->bhqk", pieces[:, :, 0], pieces[:, :, 1], preferred_element_type=jnp.float32
    ) * head_size ** (-0.5)
    scores = jnp.where(key_mask, scores, -1e30)
    row_max = jnp.max(scores, axis=-1, keepdims=True)
    weights_exp = jnp.exp(scores - row_max)
    row_total = jnp.sum(weights_exp, axis=-1, keepdims=True)
    attn_probs = (weights_exp / row_total).astype(jnp.bfloat16)
    mixed_heads = jnp.einsum(
        "bhqk,bkhd->bqhd", attn_probs, pieces[:, :, 2], preferred_element_type=jnp.float32
    )
    mixed_heads = mixed_heads.reshape(row_count, length, channels).astype(jnp.bfloat16)
    return (qkv, row_max + jnp.log(row_total), mixed_heads)


def attend_backward(
    normed, project, output, qkv, logsum, mixed_heads, dmiddle_low, head_count, key_mask
):
    row_count, length, channels = normed.shape
    head_size = channels // head_count
    scaling = head_size ** (-0.5)
    output_grad = jnp.einsum(
        "blc,bld->cd", mixed_heads, dmiddle_low, preferred_element_type=jnp.float32
    )
    dmixed = jnp.einsum(
        "bld,cd->blc", dmiddle_low, output, preferred_element_type=jnp.float32
    ).astype(jnp.bfloat16)
    dmixed = dmixed.reshape(row_count, length, head_count, head_size)
    pieces = qkv.reshape(row_count, length, 3, head_count, head_size)
    scores = (
        jnp.einsum(
            "bqhd,bkhd->bhqk", pieces[:, :, 0], pieces[:, :, 1], preferred_element_type=jnp.float32
        )
        * scaling
    )
    scores = jnp.where(key_mask, scores, -1e30)
    attn_probs = jnp.exp(scores - logsum)
    dprobs = jnp.einsum(
        "bqhd,bkhd->bhqk", dmixed, pieces[:, :, 2], preferred_element_type=jnp.float32
    )
    row_delta = jnp.sum(attn_probs * dprobs, axis=-1, keepdims=True)
    dscores = (attn_probs * (dprobs - row_delta)).astype(jnp.bfloat16)
    dquery = (
        jnp.einsum("bhqk,bkhd->bqhd", dscores, pieces[:, :, 1], preferred_element_type=jnp.float32)
        * scaling
    )
    dkeys = (
        jnp.einsum("bhqk,bqhd->bkhd", dscores, pieces[:, :, 0], preferred_element_type=jnp.float32)
        * scaling
    )
    dvalues = jnp.einsum(
        "bhqk,bqhd->bkhd",
        attn_probs.astype(jnp.bfloat16),
        dmixed,
        preferred_element_type=jnp.float32,
    )
    dqkv = (
        jnp.stack([dquery, dkeys, dvalues], axis=2)
        .reshape(row_count, length, 3 * channels)
        .astype(jnp.bfloat16)
    )
    project_grad = jnp.einsum("blc,blf->cf", normed, dqkv, preferred_element_type=jnp.float32)
    dnormed = jnp.einsum("blf,cf->blc", dqkv, project, preferred_element_type=jnp.float32)
    return (dnormed, project_grad, output_grad)


def block_forward(inputs, weights, head_count, key_mask):
    gain_attn, project, output, gain_mlp, expand, shrink = weights
    normed = norm_forward(inputs, gain_attn).astype(jnp.bfloat16)
    qkv, logsum, mixed_heads = attend_forward(normed, project, head_count, key_mask)
    middle = inputs + jnp.einsum(
        "blc,cd->bld", mixed_heads, output, preferred_element_type=jnp.float32
    )
    normed_mlp = norm_forward(middle, gain_mlp).astype(jnp.bfloat16)
    before = jnp.einsum("blc,cf->blf", normed_mlp, expand, preferred_element_type=jnp.float32)
    hidden = jax.nn.gelu(before).astype(jnp.bfloat16)
    result = middle + jnp.einsum("blf,fc->blc", hidden, shrink, preferred_element_type=jnp.float32)
    return (result, (inputs, normed, qkv, logsum, mixed_heads, middle, normed_mlp, before, hidden))


def block_backward(dresult, stored, weights, head_count, key_mask):
    gain_attn, project, output, gain_mlp, expand, shrink = weights
    inputs, normed, qkv, logsum, mixed_heads, middle, normed_mlp, before, hidden = stored
    grad_low = dresult.astype(jnp.bfloat16)
    shrink_grad = jnp.einsum("blf,blc->fc", hidden, grad_low, preferred_element_type=jnp.float32)
    dhidden = jnp.einsum(
        "blc,fc->blf", grad_low, shrink, preferred_element_type=jnp.float32
    ).astype(jnp.bfloat16)
    gelu_pull = jax.vjp(jax.nn.gelu, before)[1]
    dbefore = gelu_pull(dhidden.astype(jnp.float32))[0].astype(jnp.bfloat16)
    expand_grad = jnp.einsum("blc,blf->cf", normed_mlp, dbefore, preferred_element_type=jnp.float32)
    dnormed_mlp = jnp.einsum("blf,cf->blc", dbefore, expand, preferred_element_type=jnp.float32)
    norm_pull = jax.vjp(norm_forward, middle, gain_mlp)[1]
    dmiddle_norm, gain_mlp_grad = norm_pull(dnormed_mlp)
    dmiddle = dresult + dmiddle_norm
    dnormed, project_grad, output_grad = attend_backward(
        normed,
        project,
        output,
        qkv,
        logsum,
        mixed_heads,
        dmiddle.astype(jnp.bfloat16),
        head_count,
        key_mask,
    )
    first_pull = jax.vjp(norm_forward, inputs, gain_attn)[1]
    dinputs_norm, gain_attn_grad = first_pull(dnormed)
    return (
        dmiddle + dinputs_norm,
        (gain_attn_grad, project_grad, output_grad, gain_mlp_grad, expand_grad, shrink_grad),
    )


def char_front(char_text, char_count, language, lang_table, weights):
    present = lax.broadcasted_iota(jnp.int32, char_text.shape[:2], 1) < char_count[:, None]
    onehot = (lax.broadcasted_iota(jnp.int32, (lang_table.shape[0],), 0) == language).astype(
        jnp.bfloat16
    )
    lang_row = jnp.dot(onehot, lang_table, preferred_element_type=jnp.float32)
    inputs = char_text.astype(jnp.float32) + lang_row
    result, stored = block_forward(inputs, weights, CH, present[:, None, None, :])
    summed = jnp.sum(jnp.where(present[:, :, None], result, 0.0), axis=1)
    pooled = (summed / char_count[:, None].astype(jnp.float32)).astype(jnp.bfloat16)
    return (pooled, stored, present, onehot)


def char_back(stored, present, onehot, char_count, dpooled, weights):
    spread = dpooled.astype(jnp.float32) / char_count[:, None].astype(jnp.float32)
    dresult = jnp.where(present[:, :, None], spread[:, None, :], 0.0)
    dinputs, gradients = block_backward(dresult, stored, weights, CH, present[:, None, None, :])
    table_grad = onehot.astype(jnp.float32)[:, None] * jnp.sum(dinputs, axis=(0, 1))[None, :]
    return (dinputs, (table_grad,) + gradients)


def word_full(pooled, cot_rows, word_input, weights):
    length = pooled.shape[0]
    word_start = jnp.dot(pooled, word_input, preferred_element_type=jnp.float32)[None]
    causal = (
        lax.broadcasted_iota(jnp.int32, (length, length), 0)
        >= lax.broadcasted_iota(jnp.int32, (length, length), 1)
    )[None, None]
    result, stored = block_forward(word_start, weights, H, causal)
    dstart, gradients = block_backward(
        cot_rows.astype(jnp.float32)[None], stored, weights, H, causal
    )
    grad_low = dstart[0].astype(jnp.bfloat16)
    input_grad = jnp.einsum("wc,wd->cd", pooled, grad_low, preferred_element_type=jnp.float32)
    dpooled = jnp.einsum(
        "wd,cd->wc", grad_low, word_input, preferred_element_type=jnp.float32
    ).astype(jnp.bfloat16)
    return (result[0], dpooled, (input_grad,) + gradients)


def reduce_rows(gradients):
    shards = lax.axis_size("dp")
    flat = []
    for place, gradient in enumerate(gradients):
        if place == 0:
            gradient = gradient.T
        flat.append(gradient.astype(jnp.bfloat16).reshape(shards, -1))
    packed = jnp.concatenate(flat, axis=1)
    me = lax.axis_index("dp")
    packed = jnp.take(packed, jnp.arange(shards) ^ me, axis=0)
    bit = 1
    while packed.shape[0] > 1:
        pairs = packed.reshape(packed.shape[0] // 2, 2, packed.shape[1])
        arrived = lax.ppermute(pairs[:, 1], "dp", [(i, i ^ bit) for i in range(shards)])
        packed = (pairs[:, 0].astype(jnp.float32) + arrived.astype(jnp.float32)).astype(
            jnp.bfloat16
        )
        bit *= 2
    arrived = lax.ppermute(packed, "section", [(0, 1), (1, 0)])
    total = (packed.astype(jnp.float32) + arrived.astype(jnp.float32))[0]
    outs = []
    at = 0
    for place, gradient in enumerate(gradients):
        size = gradient.size // shards
        piece = total[at : at + size]
        at += size
        if place == 0:
            outs.append(piece.reshape(-1, gradient.shape[0]).T)
        else:
            outs.append(piece.reshape((gradient.shape[0] // shards,) + gradient.shape[1:]))
    return tuple(outs)


def local(
    chars,
    counts,
    languages,
    language_table,
    char_gain_attn,
    char_project,
    char_output,
    char_gain_mlp,
    char_expand,
    char_shrink,
    word_input,
    word_gain_attn,
    word_project,
    word_output,
    word_gain_mlp,
    word_expand,
    word_shrink,
    cotangent,
):
    char_weights = (
        char_gain_attn,
        char_project,
        char_output,
        char_gain_mlp,
        char_expand,
        char_shrink,
    )
    word_weights = (
        word_gain_attn,
        word_project,
        word_output,
        word_gain_mlp,
        word_expand,
        word_shrink,
    )
    if lax.axis_size("dp") == 16:
        return local_grouped(
            chars,
            counts,
            languages,
            language_table,
            char_weights,
            word_input,
            word_weights,
            cotangent,
        )
    section_index = lax.axis_index("section")
    char_text = chars[section_index, 0]
    char_count = counts[section_index, 0]
    language = languages[section_index, 0]
    cot_rows = cotangent[section_index, 0]
    pooled, stored, present, onehot = char_front(
        char_text, char_count, language, language_table, char_weights
    )
    result, dpooled, word_grads = word_full(pooled, cot_rows, word_input, word_weights)
    text_grad, char_grads = char_back(stored, present, onehot, char_count, dpooled, char_weights)
    totals = reduce_rows(char_grads + word_grads)
    return (result[None, None], text_grad[None, None]) + totals


def solution(mesh):
    placed = (
        P(None, "dp", None, None, None),
        P(None, "dp", None),
        P(None, "dp"),
        P(),
        P(),
        P(),
        P(),
        P(),
        P(),
        P(),
        P(),
        P(),
        P(),
        P(),
        P(),
        P(),
        P(),
        P(None, "dp", None, None),
    )
    return jax.shard_map(
        local,
        mesh=mesh,
        in_specs=placed,
        out_specs=(
            P("section", "dp", None, None),
            P("section", "dp", None, None, None),
            P(None, "dp"),
            P("dp"),
            P("dp", None),
            P("dp", None),
            P("dp"),
            P("dp", None),
            P("dp", None),
            P("dp", None),
            P("dp"),
            P("dp", None),
            P("dp", None),
            P("dp"),
            P("dp", None),
            P("dp", None),
        ),
        check_vma=False,
    )
```

```python
import functools

import jax
import jax.numpy as jnp
from jax import lax
from jax.experimental import pallas as pl
from jax.experimental.pallas import tpu as pltpu
from jax.sharding import PartitionSpec as P

CH = 4
H = 8
HEAD = 64
SLAB = 256
HEADS = SLAB // HEAD
BLOCK = 128
MIB = 1024 * 1024

eps = 1e-05

f32 = jnp.float32
bf16 = jnp.bfloat16


def dot(a, b):
    return jnp.dot(a, b, preferred_element_type=f32)


def dot_nt(a, b):
    return lax.dot_general(a, b, (((1,), (1,)), ((), ())), preferred_element_type=f32)


def position():
    return (lax.axis_index("section"), lax.axis_index("dp"))


def lanes(shape):
    return lax.broadcasted_iota(jnp.int32, shape, 1)


def rows_of(shape):
    return lax.broadcasted_iota(jnp.int32, shape, 0)


def stack_heads(a):
    head = lanes((1, SLAB)) // HEAD
    masks = [jnp.where(head == place, 1.0, 0.0).astype(bf16) for place in range(HEADS)]
    return jnp.concatenate([a * mask for mask in masks], axis=0)


def compact(scores, length):
    group = lanes((length, BLOCK)) // length
    total = scores[:length]
    for place in range(1, BLOCK // length):
        total = jnp.where(group == place, scores[place * length : (place + 1) * length], total)
    return total


def compact_heads(scores, length):
    return [
        compact(scores[:, head * BLOCK : (head + 1) * BLOCK], length) for head in range(HEADS)
    ]


def expand(values, length):
    group = lanes((length, BLOCK)) // length
    return jnp.concatenate(
        [jnp.where(group == place, values, 0.0) for place in range(BLOCK // length)], axis=0
    ).astype(bf16)


def expand_heads(values, tile, length):
    first = tile * HEADS * BLOCK
    return [
        expand(values[:, first + head * BLOCK : first + (head + 1) * BLOCK], length)
        for head in range(HEADS)
    ]


def head_rows(a, head):
    return a[head * HEAD : (head + 1) * HEAD]


def attend(load, tiles, key_mask, length):
    scores = []
    for tile in tiles:
        scores += compact_heads(dot_nt(load(tile, 1), stack_heads(load(tile, 0))), length)
    scores = jnp.concatenate(scores, axis=1) * HEAD**-0.5
    scores = jnp.where(key_mask, scores, -1e30)
    weights = jnp.exp(scores - jnp.max(scores, axis=0, keepdims=True))
    probs = weights / jnp.sum(weights, axis=0, keepdims=True)
    mixed = []
    for number, tile in enumerate(tiles):
        values = load(tile, 2).T
        parts = expand_heads(probs, number, length)
        mixed.append(
            jnp.concatenate(
                [dot(head_rows(values, head), parts[head]) for head in range(HEADS)], axis=0
            ).astype(bf16)
        )
    return (probs, mixed)


def attend_back(load, load_dmixed, tiles, probs, store, length):
    dprobs = []
    for number, tile in enumerate(tiles):
        grads = load_dmixed(tile)
        stacked = stack_heads(grads)
        scores = dot_nt(stack_heads(load(tile, 2)), grads)
        dprobs += [compact(scores[head * BLOCK : (head + 1) * BLOCK], length) for head in range(HEADS)]
        parts = jnp.concatenate(expand_heads(probs, number, length), axis=1)
        store(tile, 2, dot(parts, stacked).astype(bf16))
    dprobs = jnp.concatenate(dprobs, axis=1)
    dscores = probs * (dprobs - jnp.sum(probs * dprobs, axis=0, keepdims=True))
    scaling = HEAD**-0.5
    for number, tile in enumerate(tiles):
        parts = expand_heads(dscores, number, length)
        keys = load(tile, 1).T
        dq = jnp.concatenate(
            [dot(head_rows(keys, head), parts[head]) for head in range(HEADS)], axis=0
        )
        store(tile, 0, (dq * scaling).astype(bf16).T)
        dk = dot(jnp.concatenate(parts, axis=1), stack_heads(load(tile, 0)))
        store(tile, 1, (dk * scaling).astype(bf16))


def unit(x):
    scale = lax.rsqrt(jnp.mean(x * x, axis=-1, keepdims=True) + eps)
    return (x * scale, scale)


def unit_back(dnormed, gain, normal, scale):
    weighted = dnormed * gain
    return scale * (weighted - normal * jnp.mean(normal * weighted, axis=-1, keepdims=True))


def gelu_parts(before):
    c = 0.7978845608028654
    before = before.astype(bf16)
    square = before * before
    half = bf16(0.5) * jnp.tanh(before * (bf16(c) + bf16(c * 0.044715) * square)) + bf16(0.5)
    value = before * half
    slope = half + value * (bf16(1.0) - half) * (bf16(2.0 * c) + bf16(6.0 * c * 0.044715) * square)
    return (value, slope)


def pick(row, place):
    return jnp.sum(jnp.where(lanes(row.shape) == place, row, 0), axis=1, keepdims=True)


def char_rows(chars, table_ref, language):
    table = table_ref[...].astype(f32)
    row = jnp.sum(jnp.where(rows_of(table.shape) == language, table, 0.0), axis=0, keepdims=True)
    return chars.astype(f32) + row


def counts_by_row(counts, rows, slots):
    words = counts.shape[-1]
    counts = jnp.broadcast_to(counts.astype(f32), (8, words)).astype(bf16)
    shape = (words, rows)
    member = lanes(shape) // slots == rows_of(shape)
    return dot(counts, jnp.where(member, 1.0, 0.0).astype(bf16))[:1]


def counts_column(counts):
    words = counts.shape[-1]
    shape = (words, words)
    spread = jnp.broadcast_to(counts.astype(f32), shape)
    return jnp.sum(
        jnp.where(rows_of(shape) == lanes(shape), spread, 0.0), axis=1, keepdims=True
    )


def fetch_all(sources, targets, sems):
    fetches = [
        pltpu.make_async_copy(source, target, sems.at[place])
        for place, (source, target) in enumerate(zip(sources, targets))
    ]
    for fetch in fetches:
        fetch.start()
    return fetches


def in_hbm(array):
    return pltpu.with_memory_space_constraint(array, pltpu.HBM)


def char_forward_kernel(
    slots,
    chars_hbm,
    languages_hbm,
    counts_hbm,
    table_hbm,
    gain_attn_hbm,
    project_hbm,
    output_hbm,
    gain_mlp_hbm,
    expand_hbm,
    shrink_hbm,
    pooled_ref,
    hidden_sum_ref,
    counts_ref,
    qkv_ref,
    probs_ref,
    mixed_ref,
    middle_ref,
    slope_ref,
    chars_ref,
    languages_ref,
    table_ref,
    gain_attn_ref,
    project_ref,
    output_ref,
    gain_mlp_ref,
    expand_ref,
    shrink_ref,
    sems,
):
    section, _ = position()
    fetches = fetch_all(
        (
            languages_hbm,
            counts_hbm,
            table_hbm,
            gain_attn_hbm,
            chars_hbm.at[section],
            project_hbm,
            output_hbm,
            gain_mlp_hbm,
            expand_hbm,
            shrink_hbm,
        ),
        (
            languages_ref,
            counts_ref,
            table_ref,
            gain_attn_ref,
            chars_ref,
            project_ref,
            output_ref,
            gain_mlp_ref,
            expand_ref,
            shrink_ref,
        ),
        sems,
    )
    for fetch in fetches[:2]:
        fetch.wait()
    counts = counts_ref[section]
    rows = chars_ref.shape[0]
    words = counts.shape[-1]
    row_counts = counts_by_row(counts, rows, slots)
    for fetch in fetches[2:5]:
        fetch.wait()
    x = char_rows(chars_ref[...], table_ref, pick(languages_ref[...], section))
    normal, _ = unit(x)
    normed = (normal * gain_attn_ref[...]).astype(bf16)
    fetches[5].wait()
    qkv_ref[...] = dot(normed, project_ref[...]).astype(bf16)
    blocks = range(rows // BLOCK)

    def load(block, which):
        return qkv_ref[block * BLOCK : (block + 1) * BLOCK, which * SLAB : (which + 1) * SLAB]

    by_head = jnp.concatenate(
        [row_counts[:, block * BLOCK : (block + 1) * BLOCK] for block in blocks for _ in range(HEADS)],
        axis=1,
    )
    key_mask = rows_of((slots, rows * HEADS)).astype(f32) < by_head
    probs, mixed = attend(load, blocks, key_mask, slots)
    probs_ref[...] = probs
    for block in blocks:
        mixed_ref[:, block * BLOCK : (block + 1) * BLOCK] = mixed[block]
    mixed = mixed_ref[...].T
    fetches[6].wait()
    middle = x + dot(mixed, output_ref[...])
    middle_ref[...] = middle
    normal, _ = unit(middle)
    fetches[7].wait()
    normed = (normal * gain_mlp_ref[...]).astype(bf16)
    word_shape = (words, rows)
    lane = lanes(word_shape)
    member = (lane // slots == rows_of(word_shape)) & ((lane % slots).astype(f32) < row_counts)
    member = jnp.where(member, 1.0, 0.0).astype(bf16)
    fetches[8].wait()
    parts = [slice(at, at + 256) for at in range(0, expand_ref.shape[1], 256)]
    before = dot(normed, expand_ref[:, parts[0]])
    for number, part in enumerate(parts):
        value, slope = gelu_parts(before)
        if number + 1 < len(parts):
            before = dot(normed, expand_ref[:, parts[number + 1]])
        slope_ref[:, part] = slope
        hidden_sum_ref[:, part] = dot(member, value).astype(bf16)
    high = middle.astype(bf16)
    fetches[9].wait()
    total = dot(member, high) + dot(hidden_sum_ref[...], shrink_ref[...])
    pooled_ref[...] = (total / counts_column(counts)).astype(bf16)


def char_forward(languages, chars, counts, table, weights, slots):
    rows, width = chars.shape[1:]
    words = rows // slots
    hidden = weights[4].shape[1]
    vmem = pl.BlockSpec(memory_space=pltpu.VMEM)
    hbm = pl.BlockSpec(memory_space=pltpu.HBM)
    fetched = (languages, counts, table) + tuple(weights)
    return pl.pallas_call(
        functools.partial(char_forward_kernel, slots),
        in_specs=[hbm] * 10,
        out_specs=[vmem] * 8,
        out_shape=[
            jax.ShapeDtypeStruct((words, width), bf16),
            jax.ShapeDtypeStruct((words, hidden), bf16),
            jax.ShapeDtypeStruct(counts.shape, counts.dtype),
            jax.ShapeDtypeStruct((rows, 3 * width), bf16),
            jax.ShapeDtypeStruct((slots, rows * HEADS), f32),
            jax.ShapeDtypeStruct((width, rows), bf16),
            jax.ShapeDtypeStruct((rows, width), f32),
            jax.ShapeDtypeStruct((rows, hidden), bf16),
        ],
        scratch_shapes=[pltpu.VMEM(chars.shape[1:], bf16)]
        + [pltpu.VMEM(array.shape, array.dtype) for array in fetched if array is not counts]
        + [pltpu.SemaphoreType.DMA((10,))],
        compiler_params=pltpu.CompilerParams(vmem_limit_bytes=16 * MIB),
        cost_estimate=pl.CostEstimate(
            flops=64 * rows * width * width, bytes_accessed=8 * MIB, transcendentals=0
        ),
        name="char_forward",
    )(*[in_hbm(array) for array in (chars,) + fetched])


CHAR_FIRST_SLOT = 144
CHAR_SECTION_SLOT = 80
CHAR_CORE_SLOT = 112
CHAR_LAST_SLOT = 48


def char_shard(slot, me):
    return me ^ ((slot >> 3) | (((slot >> 1) & 3) << 1) | ((slot & 1) << 3))


def put_shards(gradient, slots, shard_of, at):
    width = SLAB
    columns = gradient.shape[1] // width
    size = gradient.shape[0] // len(slots)
    for number, slot in enumerate(slots):
        first = pl.multiple_of(shard_of(number) * size, size)
        for column in range(columns):
            start = at + column * size
            slot[start : start + size] = gradient[
                pl.ds(first, size), column * width : (column + 1) * width
            ].astype(bf16)
    return at + size * columns


def slot_refs(*refs):
    return [ref.at[place] for ref in refs for place in range(ref.shape[0])]


def char_mlp_back_kernel(
    slots,
    shards,
    counts_ref,
    gain_mlp_ref,
    expand_ref,
    shrink_ref,
    dpooled_ref,
    hidden_sum_ref,
    other_sum_ref,
    mixed_ref,
    middle_ref,
    slope_ref,
    dmiddle_ref,
    gain_ref,
    keep_ref,
    send_ref,
    counts_wide,
    spread,
    dhidden_words,
    dz,
    dbefore,
    expand_grad,
    shrink_grad,
    output_grad,
):
    section, me = position()
    counts = counts_ref[section]
    rows, width = middle_ref.shape
    words = counts.shape[-1]
    column = counts_column(counts)
    counts_wide[...] = jnp.broadcast_to(column, counts_wide.shape)
    spread_value = dpooled_ref[:words].astype(f32) / column
    spread[...] = spread_value
    spread_high = spread_value.astype(bf16)
    dhidden_words[...] = dot_nt(spread_high, shrink_ref[...]).astype(bf16).astype(f32)
    dz[:words] = spread_high
    other = dpooled_ref[words:].astype(f32) / counts_column(counts_ref[1 - section])
    dz[words:] = other.astype(bf16)
    slot = rows_of((slots, 128)).astype(f32)
    for word in range(words):
        at_word = slice(word * slots, (word + 1) * slots)
        present = slot < counts_wide[word : word + 1, :]
        for at in range(0, expand_ref.shape[1], 128):
            part = slice(at, at + 128)
            piece = jnp.where(present, dhidden_words[word : word + 1, part], 0.0).astype(bf16)
            dbefore[at_word, part] = piece * slope_ref[at_word, part]
        for at in range(0, width, 128):
            part = slice(at, at + 128)
            dmiddle_ref[at_word, part] = jnp.where(present, spread[word : word + 1, part], 0.0)
    normal, scale = unit(middle_ref[...])
    normed_t = (normal * gain_mlp_ref[...]).astype(bf16).T
    hidden_sums = jnp.concatenate([hidden_sum_ref[...], other_sum_ref[...]], axis=0)
    hidden_sums_t = hidden_sums.T

    dnormed = dot_nt(dbefore[...], expand_ref[...])
    expand_grad[...] = dot(normed_t, dbefore[...])
    half = width // 2
    own_half = dz[:, pl.ds(pl.multiple_of(section * half, half), half)]
    shrink_grad[...] = dot(hidden_sums_t, own_half)
    dmiddle = dmiddle_ref[...] + unit_back(dnormed, gain_mlp_ref[...], normal, scale)
    dmiddle_ref[...] = dmiddle
    output_grad[...] = dot(mixed_ref[...], dmiddle.astype(bf16))
    gain_ref[...] = jnp.broadcast_to(
        jnp.sum(dnormed * normal, axis=0, keepdims=True), gain_ref.shape
    )
    targets = slot_refs(keep_ref, send_ref)
    at = 0
    for gradient in (expand_grad, output_grad):
        at = put_shards(gradient, targets, lambda slot: char_shard(slot, me), at)
    size = shrink_grad.shape[0] // shards
    for number, target in enumerate(targets):
        first = pl.multiple_of(char_shard(number, me) * size, size)
        piece = shrink_grad[pl.ds(first, size), :].astype(bf16)
        target[at:, :half] = piece[: size // 2]
        target[at:, half:] = piece[size // 2 :]


def char_mlp_back(counts, weights, dpooled, stored, other_sum, slots, shards):
    _, _, output, gain_mlp, expand_w, shrink = weights
    hidden_sum, _, _, mixed, middle, slope = stored
    rows, width = middle.shape
    words = rows // slots
    hidden = expand_w.shape[1]
    half = (shards // 2, CHAR_CORE_SLOT, width)
    vmem = pl.BlockSpec(memory_space=pltpu.VMEM)
    return pl.pallas_call(
        functools.partial(char_mlp_back_kernel, slots, shards),
        in_specs=[vmem] * 10,
        out_specs=[vmem] * 4,
        out_shape=[
            jax.ShapeDtypeStruct((rows, width), f32),
            jax.ShapeDtypeStruct((8, width), f32),
            jax.ShapeDtypeStruct(half, bf16),
            jax.ShapeDtypeStruct(half, bf16),
        ],
        scratch_shapes=[
            pltpu.VMEM((words, 128), f32),
            pltpu.VMEM((words, width), f32),
            pltpu.VMEM((words, hidden), f32),
            pltpu.VMEM((2 * words, width), bf16),
            pltpu.VMEM((rows, hidden), bf16),
            pltpu.VMEM(expand_w.shape, f32),
            pltpu.VMEM((hidden, width // 2), f32),
            pltpu.VMEM(output.shape, f32),
        ],
        compiler_params=pltpu.CompilerParams(vmem_limit_bytes=16 * MIB),
        cost_estimate=pl.CostEstimate(
            flops=64 * rows * width * width, bytes_accessed=8 * MIB, transcendentals=0
        ),
        name="char_mlp_back",
    )(
        counts,
        gain_mlp,
        expand_w,
        shrink,
        dpooled,
        hidden_sum,
        other_sum,
        mixed,
        middle,
        slope,
    )


def char_attn_back_kernel(
    slots,
    shards,
    _,
    chars_hbm,
    languages_hbm,
    table_ref,
    gain_attn_ref,
    project_ref,
    output_ref,
    dmiddle_ref,
    gain_mlp_grad_ref,
    qkv_ref,
    probs_ref,
    grad_hbm,
    keep_ref,
    send_ref,
    chars_ref,
    languages_ref,
    dmixed,
    dqkv,
    grad,
    project_grad,
    sems,
):
    section, me = position()
    fetches = fetch_all(
        (chars_hbm.at[section], languages_hbm), (chars_ref, languages_ref), sems
    )
    rows, width = dmiddle_ref.shape
    dmixed[...] = dot_nt(dmiddle_ref[...].astype(bf16), output_ref[...]).astype(bf16)

    def load(block, which):
        return qkv_ref[block * BLOCK : (block + 1) * BLOCK, which * SLAB : (which + 1) * SLAB]

    def load_dmixed(block):
        return dmixed[block * BLOCK : (block + 1) * BLOCK]

    def store(block, which, value):
        dqkv[block * BLOCK : (block + 1) * BLOCK, which * SLAB : (which + 1) * SLAB] = value

    attend_back(load, load_dmixed, range(rows // BLOCK), probs_ref[...], store, slots)
    for fetch in fetches:
        fetch.wait()
    language = pick(languages_ref[...], section)
    normal, scale = unit(char_rows(chars_ref[...], table_ref, language))
    normed_t = (normal * gain_attn_ref[...]).astype(bf16).T
    dnormed = dot_nt(dqkv[...], project_ref[...])
    project_grad[...] = dot(normed_t, dqkv[...])
    gain_attn_grad = jnp.sum(dnormed * normal, axis=0, keepdims=True)
    dx = dmiddle_ref[...] + unit_back(dnormed, gain_attn_ref[...], normal, scale)
    grad[...] = dx
    leave = pltpu.make_async_copy(grad, grad_hbm, sems.at[2])
    leave.start()
    row_sum = jnp.sum(dx, axis=0, keepdims=True)
    targets = [
        ref.at[pl.ds(place * CHAR_LAST_SLOT, CHAR_LAST_SLOT)]
        for ref in (keep_ref, send_ref)
        for place in range(shards // 2)
    ]
    put_shards(project_grad, targets, lambda slot: char_shard(slot, me), 0)
    extra = jnp.concatenate(
        [
            gain_attn_grad,
            gain_mlp_grad_ref[:7],
            jnp.where(rows_of((8, 1)) == language, row_sum, 0.0),
        ],
        axis=0,
    ).astype(bf16)
    for ref in (keep_ref, send_ref):
        ref[ref.shape[0] - 16 :] = extra
    leave.wait()


def char_attn_back(
    languages, chars, table, weights, dmiddle, gain_mlp_grad, stored, slots, shards, after
):
    gain_attn, project, output, _, _, _ = weights
    _, qkv, probs, _, _, _ = stored
    rows, width = dmiddle.shape
    half = (shards // 2 * CHAR_LAST_SLOT + 16, width)
    vmem = pl.BlockSpec(memory_space=pltpu.VMEM)
    hbm = pl.BlockSpec(memory_space=pltpu.HBM)
    return pl.pallas_call(
        functools.partial(char_attn_back_kernel, slots, shards),
        in_specs=[pl.BlockSpec(memory_space=pl.ANY), hbm, hbm] + [vmem] * 8,
        out_specs=[hbm, vmem, vmem],
        out_shape=[
            jax.ShapeDtypeStruct((rows, width), f32),
            jax.ShapeDtypeStruct(half, bf16),
            jax.ShapeDtypeStruct(half, bf16),
        ],
        scratch_shapes=[
            pltpu.VMEM((rows, width), bf16),
            pltpu.VMEM(languages.shape, languages.dtype),
            pltpu.VMEM((rows, width), bf16),
            pltpu.VMEM((rows, 3 * width), bf16),
            pltpu.VMEM((rows, width), f32),
            pltpu.VMEM(project.shape, f32),
            pltpu.SemaphoreType.DMA((3,)),
        ],
        compiler_params=pltpu.CompilerParams(vmem_limit_bytes=16 * MIB),
        cost_estimate=pl.CostEstimate(
            flops=0, bytes_accessed=0, transcendentals=0
        ),
        name="char_attn_back",
    )(
        after,
        in_hbm(chars),
        in_hbm(languages),
        table,
        gain_attn,
        project,
        output,
        dmiddle,
        gain_mlp_grad,
        qkv,
        probs,
    )


LONG = pl.CostEstimate(flops=20_000_000_000, bytes_accessed=8 * MIB, transcendentals=0)

WORD_SLOT = 416

SHORT_FLOPS = 475_000_000


def word_kernel(
    length,
    shards,
    own_ref,
    both_ref,
    section_ref,
    far_ref,
    cot_ref,
    cot_far_ref,
    input_ref,
    gain_attn_ref,
    project_ref,
    output_ref,
    gain_mlp_ref,
    expand_ref,
    shrink_ref,
    result_hbm,
    dpooled_ref,
    keep_ref,
    send_ref,
    pooled,
    pooled_t,
    dz,
    start,
    normed_t,
    qkv,
    kept,
    mixed_t,
    middle,
    normed_mlp_t,
    hidden,
    dbefore,
    dmixed,
    dqkv,
    dy,
    dstart,
    result,
    input_grad,
    project_grad,
    output_grad,
    expand_grad,
    shrink_grad,
    sem,
):
    total = pooled.shape[0]
    width = output_ref.shape[0]
    section, me = position()
    slabs = width // SLAB
    for place, ref in enumerate((own_ref, section_ref, far_ref, both_ref)):
        pooled[place * length : (place + 1) * length] = ref[...]
    for place, (ref, other) in enumerate(
        ((cot_ref, section), (cot_ref, 1 - section), (cot_far_ref, section), (cot_far_ref, 1 - section))
    ):
        dz[place * length : (place + 1) * length] = ref[other]

    x = dot(pooled[...], input_ref[...])
    start[...] = x
    normal, _ = unit(x)
    low = (normal * gain_attn_ref[...]).astype(bf16)
    normed_t[...] = low.T
    qkv[...] = dot(low, project_ref[...]).astype(bf16)
    tiles = [(block, slab) for block in range(total // BLOCK) for slab in range(slabs)]

    def load(tile, which):
        block, slab = tile
        at = which * width + slab * SLAB
        return qkv[block * BLOCK : (block + 1) * BLOCK, at : at + SLAB]

    mask_shape = (length, len(tiles) * HEADS * BLOCK)
    causal = rows_of(mask_shape) <= lanes(mask_shape) % length
    probs, mixed = attend(load, tiles, causal, length)
    kept[...] = probs
    for (block, slab), piece in zip(tiles, mixed):
        mixed_t[slab * SLAB : (slab + 1) * SLAB, block * BLOCK : (block + 1) * BLOCK] = piece
    x = x + dot(mixed_t[...].T, output_ref[...])
    middle[...] = x
    normal, _ = unit(x)
    low = (normal * gain_mlp_ref[...]).astype(bf16)
    normed_mlp_t[...] = low.T
    dz_all = dz[...]
    for at in range(0, expand_ref.shape[1], 256):
        part = slice(at, at + 256)
        value, bend = gelu_parts(dot(low, expand_ref[:, part]))
        hidden[:, part] = value
        dhidden = dot_nt(dz_all, shrink_ref[part, :]).astype(bf16)
        dbefore[:, part] = dhidden * bend

    def shard_of(slot):
        return (me & 7) ^ ((slot >> 2) | ((slot & 3) << 1))

    def own_rows(flipped):
        many = flipped.shape[0] // 2
        return flipped[pl.ds(pl.multiple_of((me >> 3) * many, many), many), :]

    def half_columns(ref, place):
        many = ref.shape[1] // 2
        return ref[:, pl.ds(pl.multiple_of(place * many, many), many)]

    def own_columns(ref):
        return half_columns(ref, section)

    targets = slot_refs(keep_ref, send_ref)
    hidden_t = half_columns(hidden, me >> 3).T
    pooled_t[...] = pooled[...].T
    normal, scale = unit(middle[...])
    dnormed = dot_nt(dbefore[...], expand_ref[...])
    expand_grad[...] = dot(own_rows(normed_mlp_t), own_columns(dbefore))
    shrink_grad[...] = dot(hidden_t, own_columns(dz))
    dmiddle = dz_all.astype(f32) + unit_back(dnormed, gain_mlp_ref[...], normal, scale)
    dy_low = dmiddle.astype(bf16)
    dy[...] = dy_low
    dmixed[...] = dot_nt(dy_low, output_ref[...]).astype(bf16)
    gain_mlp_grad = jnp.sum(dnormed * normal, axis=0, keepdims=True)
    result[...] = middle[:length] + dot(hidden[:length], shrink_ref[...])
    leave = pltpu.make_async_copy(result, result_hbm, sem)
    leave.start()
    output_grad[...] = dot(own_rows(mixed_t), own_columns(dy))

    def load_dmixed(tile):
        block, slab = tile
        return dmixed[block * BLOCK : (block + 1) * BLOCK, slab * SLAB : (slab + 1) * SLAB]

    def store(tile, which, value):
        block, slab = tile
        at = which * width + slab * SLAB
        dqkv[block * BLOCK : (block + 1) * BLOCK, at : at + SLAB] = value

    attend_back(load, load_dmixed, tiles, kept[...], store, length)
    normal, scale = unit(start[...])
    dnormed = dot_nt(dqkv[...], project_ref[...])
    project_grad[...] = dot(own_rows(normed_t), own_columns(dqkv))
    dword = (dmiddle + unit_back(dnormed, gain_attn_ref[...], normal, scale)).astype(bf16)
    dpooled_ref[...] = dot_nt(dword[: 2 * length], input_ref[...]).astype(bf16)
    dstart[...] = dword
    gain_attn_grad = jnp.sum(dnormed * normal, axis=0, keepdims=True)
    input_grad[...] = dot(own_rows(pooled_t), own_columns(dstart))
    at = 0
    for ref in (input_grad, project_grad, output_grad, expand_grad, shrink_grad):
        at = put_shards(ref, targets, shard_of, at)
    extra = jnp.concatenate(
        [gain_attn_grad[:, :SLAB], gain_attn_grad[:, SLAB:]]
        + [gain_mlp_grad[:, :SLAB], gain_mlp_grad[:, SLAB:]]
        + [jnp.zeros((12, SLAB), f32)],
        axis=0,
    ).astype(bf16)
    for target in targets:
        target[at : at + 16] = extra
    leave.wait()


def word_group(pooled, cotangents, word_input, weights, shards):
    gain_attn, project, output, gain_mlp, expand_w, shrink = weights
    length, channels = pooled[0].shape
    width = output.shape[0]
    hidden = expand_w.shape[1]
    total = 4 * length
    half = (4, WORD_SLOT, SLAB)
    vmem = pl.BlockSpec(memory_space=pltpu.VMEM)
    hbm = pl.BlockSpec(memory_space=pltpu.HBM)
    return pl.pallas_call(
        functools.partial(word_kernel, length, shards),
        in_specs=[vmem] * 13,
        out_specs=[hbm, vmem, vmem, vmem],
        out_shape=[
            jax.ShapeDtypeStruct((length, width), f32),
            jax.ShapeDtypeStruct((2 * length, channels), bf16),
            jax.ShapeDtypeStruct(half, bf16),
            jax.ShapeDtypeStruct(half, bf16),
        ],
        scratch_shapes=[
            pltpu.VMEM((total, channels), bf16),
            pltpu.VMEM((channels, total), bf16),
            pltpu.VMEM((total, width), bf16),
            pltpu.VMEM((total, width), f32),
            pltpu.VMEM((width, total), bf16),
            pltpu.VMEM((total, 3 * width), bf16),
            pltpu.VMEM((length, total * (width // HEAD)), f32),
            pltpu.VMEM((width, total), bf16),
            pltpu.VMEM((total, width), f32),
            pltpu.VMEM((width, total), bf16),
            pltpu.VMEM((total, hidden), bf16),
            pltpu.VMEM((total, hidden), bf16),
            pltpu.VMEM((total, width), bf16),
            pltpu.VMEM((total, 3 * width), bf16),
            pltpu.VMEM((total, width), bf16),
            pltpu.VMEM((total, width), bf16),
            pltpu.VMEM((length, width), f32),
            pltpu.VMEM((channels // 2, width // 2), f32),
            pltpu.VMEM((width // 2, 3 * width // 2), f32),
            pltpu.VMEM((width // 2, width // 2), f32),
            pltpu.VMEM((width // 2, hidden // 2), f32),
            pltpu.VMEM((hidden // 2, width // 2), f32),
            pltpu.SemaphoreType.DMA,
        ],
        compiler_params=pltpu.CompilerParams(vmem_limit_bytes=20 * MIB),
        cost_estimate=pl.CostEstimate(
            flops=total * width * width * 25 * 4, bytes_accessed=8 * MIB, transcendentals=0
        ),
        name="word_group",
    )(*pooled, *cotangents, word_input, gain_attn, project, output, gain_mlp, expand_w, shrink)


def summed(*parts):
    return functools.reduce(lambda a, b: a + b, [part.astype(f32) for part in parts])


def added(*parts):
    return summed(*parts).astype(bf16)


def by_section(section, low, high):
    return (jnp.where(section == 0, low, high), jnp.where(section == 0, high, low))


def word_sum_kernel(keep, arrived, *outs):
    for place, ref in enumerate(outs):
        ref[...] = added(keep[place], arrived[place])


def word_sum(keep, arrived):
    return pl.pallas_call(
        word_sum_kernel,
        out_shape=[jax.ShapeDtypeStruct((WORD_SLOT, SLAB), bf16)] * 4,
        compiler_params=pltpu.CompilerParams(vmem_limit_bytes=12 * MIB),
        name="word_sum",
    )(keep, arrived)


def first_sum_kernel(keep, arrived, stay_ref, go_ref, shrink_ref):
    section, _ = position()
    half = SLAB // 2
    for place in range(keep.shape[0]):
        total = added(keep[place], arrived[place])
        rows = total[:CHAR_SECTION_SLOT]
        stay_ref[place], go_ref[place] = by_section(section, rows[:, :half], rows[:, half:])
        rows = total[CHAR_SECTION_SLOT:]
        shrink_ref[place] = jnp.concatenate([rows[:, :half], rows[:, half:]], axis=0)


def first_sum(keep, arrived):
    half = jax.ShapeDtypeStruct((keep.shape[0], CHAR_SECTION_SLOT, SLAB // 2), bf16)
    shrink = jax.ShapeDtypeStruct(
        (keep.shape[0], CHAR_FIRST_SLOT - CHAR_SECTION_SLOT, SLAB // 2), bf16
    )
    return pl.pallas_call(
        first_sum_kernel,
        out_shape=[half, half, shrink],
        compiler_params=pltpu.CompilerParams(vmem_limit_bytes=12 * MIB),
        name="first_sum",
    )(keep, arrived)


def section_sum_kernel(stay, arrived, out):
    out[...] = added(stay[...], arrived[...])


def section_sum(stay, arrived):
    return pl.pallas_call(
        section_sum_kernel,
        out_shape=jax.ShapeDtypeStruct(stay.shape, bf16),
        compiler_params=pltpu.CompilerParams(vmem_limit_bytes=12 * MIB),
        cost_estimate=pl.CostEstimate(flops=SHORT_FLOPS, bytes_accessed=0, transcendentals=0),
        name="section_sum",
    )(stay, arrived)


def second_sum_kernel(first, shrink, keep, core_arrived, *outs):
    _, me = position()
    half = SLAB // 2
    extra = summed(keep[-16:], core_arrived[-16:])
    for place, out in enumerate(outs):
        at = CHAR_FIRST_SLOT
        for far in range(2):
            entry = 2 * place + far
            columns = slice(far * half, (far + 1) * half)
            total = first[entry]
            middle = CHAR_SECTION_SLOT - 16
            out[:middle, columns] = total[:middle]
            out[middle : CHAR_FIRST_SLOT - 16, columns] = shrink[entry]
            out[CHAR_FIRST_SLOT - 16 : CHAR_FIRST_SLOT, columns] = total[middle:]
            rows = slice(entry * CHAR_LAST_SLOT, (entry + 1) * CHAR_LAST_SLOT)
            out[at : at + CHAR_LAST_SLOT] = added(keep[rows], core_arrived[rows])
            at += CHAR_LAST_SLOT
            turn = lax.rem(SLAB - char_shard(entry, me) * 16, SLAB)
            out[-16:, columns] = pltpu.roll(extra, turn, 1)[:, :half].astype(bf16)


def total_kernel(*refs):
    refs[-1][...] = added(*[ref[...] for ref in refs[:-1]])


def total_of(*pieces):
    return pl.pallas_call(
        total_kernel,
        out_shape=jax.ShapeDtypeStruct(pieces[0].shape, bf16),
        compiler_params=pltpu.CompilerParams(vmem_limit_bytes=12 * MIB),
        cost_estimate=LONG,
        name="total",
    )(*pieces)


def second_sum(first, last):
    rows = CHAR_FIRST_SLOT + 2 * CHAR_LAST_SLOT + 16
    return pl.pallas_call(
        second_sum_kernel,
        out_shape=[jax.ShapeDtypeStruct((rows, SLAB), bf16)] * 4,
        compiler_params=pltpu.CompilerParams(vmem_limit_bytes=12 * MIB),
        name="second_sum",
    )(*first, *last)


FOLD = 80


def plane_sum_kernel(*refs):
    half = SLAB // 2
    pieces = refs[:4]
    for far, out in enumerate(refs[5:]):
        columns = slice(far * half, (far + 1) * half)
        total = added(*[ref[:CHAR_FIRST_SLOT, columns] for ref in pieces])
        out[:FOLD, :half] = total[:FOLD]
        out[:FOLD, half:] = total[CHAR_FIRST_SLOT - FOLD :]
        out[:16, half:] = added(*[ref[-16:, columns] for ref in pieces])
        first = CHAR_FIRST_SLOT + far * CHAR_LAST_SLOT
        out[FOLD:] = added(*[ref[first : first + CHAR_LAST_SLOT] for ref in pieces])


def plane_sum(pieces, after):
    return pl.pallas_call(
        plane_sum_kernel,
        in_specs=[pl.BlockSpec(memory_space=pltpu.VMEM)] * 4 + [pl.BlockSpec(memory_space=pl.ANY)],
        out_shape=[jax.ShapeDtypeStruct((FOLD + CHAR_LAST_SLOT, SLAB), bf16)] * 2,
        compiler_params=pltpu.CompilerParams(vmem_limit_bytes=12 * MIB),
        cost_estimate=LONG,
        name="plane_sum",
    )(*pieces, after)


def char_last_kernel(near_ref, both_ref, far_ref, section_ref, _, *outs):
    section, _ = position()
    half = SLAB // 2
    mine = summed(near_ref[:FOLD], far_ref[:FOLD])
    theirs = summed(section_ref[:FOLD], both_ref[:FOLD])

    def unfold(total):
        return jnp.concatenate(
            [total[:, :half], total[2 * FOLD - CHAR_FIRST_SLOT :, half:]], axis=0
        )

    first = jnp.concatenate(by_section(section, unfold(mine), unfold(theirs)), axis=1)
    extra = mine[:16, half:] + theirs[:16, half:]
    last = summed(near_ref[FOLD:], section_ref[FOLD:], far_ref[FOLD:], both_ref[FOLD:])
    table_ref, gain_attn_ref, project_ref, output_ref, gain_mlp_ref, expand_ref, shrink_ref = outs
    for total, refs in ((first, (expand_ref, shrink_ref, output_ref)), (last, (project_ref,))):
        at = 0
        for ref in refs:
            size = ref.shape[0]
            for column in range(ref.shape[1] // SLAB):
                ref[:, column * SLAB : (column + 1) * SLAB] = total[at : at + size]
                at += size
    size = gain_attn_ref.shape[1]
    gain_attn_ref[...] = extra[0:1, :size]
    gain_mlp_ref[...] = extra[1:2, :size]
    table_ref[...] = extra[8:16, :size]


def char_last(near, arrived, shapes, after):
    return pl.pallas_call(
        char_last_kernel,
        in_specs=[pl.BlockSpec(memory_space=pltpu.VMEM)] * 4 + [pl.BlockSpec(memory_space=pltpu.HBM)],
        out_shape=[jax.ShapeDtypeStruct(shape, f32) for shape in shapes],
        compiler_params=pltpu.CompilerParams(vmem_limit_bytes=12 * MIB),
        name="char_last",
    )(near, *arrived, in_hbm(after))


def word_last_kernel(own_ref, other_ref, *outs):
    section, me = position()
    own = own_ref[...].astype(f32)
    halves = by_section(section, own, other_ref[...].astype(f32))
    input_ref, gain_attn_ref, project_ref, output_ref, gain_mlp_ref, expand_ref, shrink_ref = outs
    at = 0
    for ref in (input_ref, project_ref, output_ref, expand_ref, shrink_ref):
        size = ref.shape[0]
        columns = ref.shape[1] // (2 * SLAB)
        for column in range(columns):
            for half in range(2):
                first = (half * columns + column) * SLAB
                ref[:, first : first + SLAB] = halves[half][at : at + size]
            at += size
    size = gain_attn_ref.shape[1]
    turn = lax.rem(SLAB - lax.rem(me * size, SLAB), SLAB)
    turned = pltpu.roll(own[at : at + 8], turn, 1)[:, :size]
    upper = me * size >= SLAB
    gain_attn_ref[...] = jnp.where(upper, turned[1:2], turned[0:1])
    gain_mlp_ref[...] = jnp.where(upper, turned[3:4], turned[2:3])


def word_last(own, other, shapes):
    return pl.pallas_call(
        word_last_kernel,
        out_shape=[jax.ShapeDtypeStruct(shape, f32) for shape in shapes],
        compiler_params=pltpu.CompilerParams(vmem_limit_bytes=12 * MIB),
        name="word_last",
    )(own, other)


def exchange(value, section_bit, dp_bits):
    shards = lax.axis_size("dp")
    pairs = [
        (s * shards + d, (s ^ section_bit) * shards + (d ^ dp_bits))
        for s in range(lax.axis_size("section"))
        for d in range(shards)
    ]
    return lax.ppermute(value, ("section", "dp"), pairs)


CORE, SIDE, NEAR, FAR = (1, 2, 4, 8)


def plane_exchange(pieces):
    return tuple(
        exchange(piece, 0, bits) for piece, bits in zip(pieces[:0:-1], (SIDE | NEAR, NEAR, SIDE))
    ) + (pieces[0],)


def local_grouped(
    chars, counts, languages, language_table, char_weights, word_input, word_weights, cotangent
):
    shards = lax.axis_size("dp")
    micros, _, words, slots, width = chars.shape
    rows = words * slots
    cot = cotangent[:, 0]
    cot_far = exchange(cot, 0, FAR)
    char_weights = tuple(w[None] if w.ndim == 1 else w for w in char_weights)
    word_weights = tuple(w[None] if w.ndim == 1 else w for w in word_weights)
    chars = chars.reshape(micros, rows, width)
    counts = counts.reshape(micros, 1, words)
    languages = languages.reshape(1, micros)
    pooled, hidden_sum, own_counts, *stored = char_forward(
        languages, chars, counts, language_table, char_weights, slots
    )
    stored = (hidden_sum, *stored)
    other_sum = exchange(hidden_sum, 1, 0)
    others = (exchange(pooled, 1, FAR), exchange(pooled, 1, 0), exchange(pooled, 0, FAR))
    result, dpooled, keep, send = word_group(
        (pooled,) + others, (cot, cot_far), word_input, word_weights, shards
    )
    word = plane_exchange(word_sum(keep, exchange(send, 0, CORE)))
    dmiddle, gain_mlp_grad, keep, send = char_mlp_back(
        own_counts, char_weights, dpooled, stored, other_sum, slots, shards
    )
    stay, go, shrink = first_sum(keep, exchange(send, 0, CORE))
    first = (section_sum(stay, exchange(go, 1, 0)), shrink)
    chars_grad, keep, send = char_attn_back(
        languages,
        chars,
        language_table,
        char_weights,
        dmiddle,
        gain_mlp_grad,
        stored,
        slots,
        shards,
        stay,
    )
    last = (keep, exchange(send, 0, CORE))
    char = plane_exchange(second_sum(first, last))
    word = total_of(*word)
    near, far = plane_sum(char, word)
    arrived = (exchange(far, 1, FAR), exchange(far, 0, FAR), exchange(near, 1, 0))

    def shard_shapes(weights):
        for weight in weights:
            if weight.shape[0] == 1:
                yield (1, weight.shape[1] // shards)
            else:
                yield (weight.shape[0] // shards, weight.shape[1])

    table_shape = (language_table.shape[0], language_table.shape[1] // shards)
    word_shapes = list(shard_shapes((word_input,) + word_weights))
    word_totals = word_last(word, exchange(word, 1, 0), word_shapes)
    char_shapes = [table_shape, *shard_shapes(char_weights)]
    char_totals = char_last(near, arrived, char_shapes, word_totals[0])
    totals = [total[0] if total.shape[0] == 1 else total for total in char_totals + word_totals]
    return (result[None, None], chars_grad.reshape((1, 1, words, slots, width))) + tuple(totals)


def norm_forward(inputs, gain):
    return inputs * lax.rsqrt(jnp.mean(inputs * inputs, axis=-1, keepdims=True) + eps) * gain


def attend_forward(normed, project, head_count, key_mask):
    row_count, length, channels = normed.shape
    head_size = channels // head_count
    qkv = jnp.einsum("blc,cf->blf", normed, project, preferred_element_type=jnp.float32).astype(
        jnp.bfloat16
    )
    pieces = qkv.reshape(row_count, length, 3, head_count, head_size)
    scores = jnp.einsum(
        "bqhd,bkhd->bhqk", pieces[:, :, 0], pieces[:, :, 1], preferred_element_type=jnp.float32
    ) * head_size ** (-0.5)
    scores = jnp.where(key_mask, scores, -1e30)
    row_max = jnp.max(scores, axis=-1, keepdims=True)
    weights_exp = jnp.exp(scores - row_max)
    row_total = jnp.sum(weights_exp, axis=-1, keepdims=True)
    attn_probs = (weights_exp / row_total).astype(jnp.bfloat16)
    mixed_heads = jnp.einsum(
        "bhqk,bkhd->bqhd", attn_probs, pieces[:, :, 2], preferred_element_type=jnp.float32
    )
    mixed_heads = mixed_heads.reshape(row_count, length, channels).astype(jnp.bfloat16)
    return (qkv, row_max + jnp.log(row_total), mixed_heads)


def attend_backward(
    normed, project, output, qkv, logsum, mixed_heads, dmiddle_low, head_count, key_mask
):
    row_count, length, channels = normed.shape
    head_size = channels // head_count
    scaling = head_size ** (-0.5)
    output_grad = jnp.einsum(
        "blc,bld->cd", mixed_heads, dmiddle_low, preferred_element_type=jnp.float32
    )
    dmixed = jnp.einsum(
        "bld,cd->blc", dmiddle_low, output, preferred_element_type=jnp.float32
    ).astype(jnp.bfloat16)
    dmixed = dmixed.reshape(row_count, length, head_count, head_size)
    pieces = qkv.reshape(row_count, length, 3, head_count, head_size)
    scores = (
        jnp.einsum(
            "bqhd,bkhd->bhqk", pieces[:, :, 0], pieces[:, :, 1], preferred_element_type=jnp.float32
        )
        * scaling
    )
    scores = jnp.where(key_mask, scores, -1e30)
    attn_probs = jnp.exp(scores - logsum)
    dprobs = jnp.einsum(
        "bqhd,bkhd->bhqk", dmixed, pieces[:, :, 2], preferred_element_type=jnp.float32
    )
    row_delta = jnp.sum(attn_probs * dprobs, axis=-1, keepdims=True)
    dscores = (attn_probs * (dprobs - row_delta)).astype(jnp.bfloat16)
    dquery = (
        jnp.einsum("bhqk,bkhd->bqhd", dscores, pieces[:, :, 1], preferred_element_type=jnp.float32)
        * scaling
    )
    dkeys = (
        jnp.einsum("bhqk,bqhd->bkhd", dscores, pieces[:, :, 0], preferred_element_type=jnp.float32)
        * scaling
    )
    dvalues = jnp.einsum(
        "bhqk,bqhd->bkhd",
        attn_probs.astype(jnp.bfloat16),
        dmixed,
        preferred_element_type=jnp.float32,
    )
    dqkv = (
        jnp.stack([dquery, dkeys, dvalues], axis=2)
        .reshape(row_count, length, 3 * channels)
        .astype(jnp.bfloat16)
    )
    project_grad = jnp.einsum("blc,blf->cf", normed, dqkv, preferred_element_type=jnp.float32)
    dnormed = jnp.einsum("blf,cf->blc", dqkv, project, preferred_element_type=jnp.float32)
    return (dnormed, project_grad, output_grad)


def block_forward(inputs, weights, head_count, key_mask):
    gain_attn, project, output, gain_mlp, expand, shrink = weights
    normed = norm_forward(inputs, gain_attn).astype(jnp.bfloat16)
    qkv, logsum, mixed_heads = attend_forward(normed, project, head_count, key_mask)
    middle = inputs + jnp.einsum(
        "blc,cd->bld", mixed_heads, output, preferred_element_type=jnp.float32
    )
    normed_mlp = norm_forward(middle, gain_mlp).astype(jnp.bfloat16)
    before = jnp.einsum("blc,cf->blf", normed_mlp, expand, preferred_element_type=jnp.float32)
    hidden = jax.nn.gelu(before).astype(jnp.bfloat16)
    result = middle + jnp.einsum("blf,fc->blc", hidden, shrink, preferred_element_type=jnp.float32)
    return (result, (inputs, normed, qkv, logsum, mixed_heads, middle, normed_mlp, before, hidden))


def block_backward(dresult, stored, weights, head_count, key_mask):
    gain_attn, project, output, gain_mlp, expand, shrink = weights
    inputs, normed, qkv, logsum, mixed_heads, middle, normed_mlp, before, hidden = stored
    grad_low = dresult.astype(jnp.bfloat16)
    shrink_grad = jnp.einsum("blf,blc->fc", hidden, grad_low, preferred_element_type=jnp.float32)
    dhidden = jnp.einsum(
        "blc,fc->blf", grad_low, shrink, preferred_element_type=jnp.float32
    ).astype(jnp.bfloat16)
    gelu_pull = jax.vjp(jax.nn.gelu, before)[1]
    dbefore = gelu_pull(dhidden.astype(jnp.float32))[0].astype(jnp.bfloat16)
    expand_grad = jnp.einsum("blc,blf->cf", normed_mlp, dbefore, preferred_element_type=jnp.float32)
    dnormed_mlp = jnp.einsum("blf,cf->blc", dbefore, expand, preferred_element_type=jnp.float32)
    norm_pull = jax.vjp(norm_forward, middle, gain_mlp)[1]
    dmiddle_norm, gain_mlp_grad = norm_pull(dnormed_mlp)
    dmiddle = dresult + dmiddle_norm
    dnormed, project_grad, output_grad = attend_backward(
        normed,
        project,
        output,
        qkv,
        logsum,
        mixed_heads,
        dmiddle.astype(jnp.bfloat16),
        head_count,
        key_mask,
    )
    first_pull = jax.vjp(norm_forward, inputs, gain_attn)[1]
    dinputs_norm, gain_attn_grad = first_pull(dnormed)
    return (
        dmiddle + dinputs_norm,
        (gain_attn_grad, project_grad, output_grad, gain_mlp_grad, expand_grad, shrink_grad),
    )


def char_front(char_text, char_count, language, lang_table, weights):
    present = lax.broadcasted_iota(jnp.int32, char_text.shape[:2], 1) < char_count[:, None]
    onehot = (lax.broadcasted_iota(jnp.int32, (lang_table.shape[0],), 0) == language).astype(
        jnp.bfloat16
    )
    lang_row = jnp.dot(onehot, lang_table, preferred_element_type=jnp.float32)
    inputs = char_text.astype(jnp.float32) + lang_row
    result, stored = block_forward(inputs, weights, CH, present[:, None, None, :])
    summed = jnp.sum(jnp.where(present[:, :, None], result, 0.0), axis=1)
    pooled = (summed / char_count[:, None].astype(jnp.float32)).astype(jnp.bfloat16)
    return (pooled, stored, present, onehot)


def char_back(stored, present, onehot, char_count, dpooled, weights):
    spread = dpooled.astype(jnp.float32) / char_count[:, None].astype(jnp.float32)
    dresult = jnp.where(present[:, :, None], spread[:, None, :], 0.0)
    dinputs, gradients = block_backward(dresult, stored, weights, CH, present[:, None, None, :])
    table_grad = onehot.astype(jnp.float32)[:, None] * jnp.sum(dinputs, axis=(0, 1))[None, :]
    return (dinputs, (table_grad,) + gradients)


def word_full(pooled, cot_rows, word_input, weights):
    length = pooled.shape[0]
    word_start = jnp.dot(pooled, word_input, preferred_element_type=jnp.float32)[None]
    causal = (
        lax.broadcasted_iota(jnp.int32, (length, length), 0)
        >= lax.broadcasted_iota(jnp.int32, (length, length), 1)
    )[None, None]
    result, stored = block_forward(word_start, weights, H, causal)
    dstart, gradients = block_backward(
        cot_rows.astype(jnp.float32)[None], stored, weights, H, causal
    )
    grad_low = dstart[0].astype(jnp.bfloat16)
    input_grad = jnp.einsum("wc,wd->cd", pooled, grad_low, preferred_element_type=jnp.float32)
    dpooled = jnp.einsum(
        "wd,cd->wc", grad_low, word_input, preferred_element_type=jnp.float32
    ).astype(jnp.bfloat16)
    return (result[0], dpooled, (input_grad,) + gradients)


def reduce_rows(gradients):
    shards = lax.axis_size("dp")
    flat = []
    for place, gradient in enumerate(gradients):
        if place == 0:
            gradient = gradient.T
        flat.append(gradient.astype(jnp.bfloat16).reshape(shards, -1))
    packed = jnp.concatenate(flat, axis=1)
    me = lax.axis_index("dp")
    packed = jnp.take(packed, jnp.arange(shards) ^ me, axis=0)
    bit = 1
    while packed.shape[0] > 1:
        pairs = packed.reshape(packed.shape[0] // 2, 2, packed.shape[1])
        arrived = lax.ppermute(pairs[:, 1], "dp", [(i, i ^ bit) for i in range(shards)])
        packed = (pairs[:, 0].astype(jnp.float32) + arrived.astype(jnp.float32)).astype(
            jnp.bfloat16
        )
        bit *= 2
    arrived = lax.ppermute(packed, "section", [(0, 1), (1, 0)])
    total = (packed.astype(jnp.float32) + arrived.astype(jnp.float32))[0]
    outs = []
    at = 0
    for place, gradient in enumerate(gradients):
        size = gradient.size // shards
        piece = total[at : at + size]
        at += size
        if place == 0:
            outs.append(piece.reshape(-1, gradient.shape[0]).T)
        else:
            outs.append(piece.reshape((gradient.shape[0] // shards,) + gradient.shape[1:]))
    return tuple(outs)


def local(
    chars,
    counts,
    languages,
    language_table,
    char_gain_attn,
    char_project,
    char_output,
    char_gain_mlp,
    char_expand,
    char_shrink,
    word_input,
    word_gain_attn,
    word_project,
    word_output,
    word_gain_mlp,
    word_expand,
    word_shrink,
    cotangent,
):
    char_weights = (
        char_gain_attn,
        char_project,
        char_output,
        char_gain_mlp,
        char_expand,
        char_shrink,
    )
    word_weights = (
        word_gain_attn,
        word_project,
        word_output,
        word_gain_mlp,
        word_expand,
        word_shrink,
    )
    if lax.axis_size("dp") == 16:
        return local_grouped(
            chars,
            counts,
            languages,
            language_table,
            char_weights,
            word_input,
            word_weights,
            cotangent,
        )
    section_index = lax.axis_index("section")
    char_text = chars[section_index, 0]
    char_count = counts[section_index, 0]
    language = languages[section_index, 0]
    cot_rows = cotangent[section_index, 0]
    pooled, stored, present, onehot = char_front(
        char_text, char_count, language, language_table, char_weights
    )
    result, dpooled, word_grads = word_full(pooled, cot_rows, word_input, word_weights)
    text_grad, char_grads = char_back(stored, present, onehot, char_count, dpooled, char_weights)
    totals = reduce_rows(char_grads + word_grads)
    return (result[None, None], text_grad[None, None]) + totals


def solution(mesh):
    placed = (
        P(None, "dp", None, None, None),
        P(None, "dp", None),
        P(None, "dp"),
        P(),
        P(),
        P(),
        P(),
        P(),
        P(),
        P(),
        P(),
        P(),
        P(),
        P(),
        P(),
        P(),
        P(),
        P(None, "dp", None, None),
    )
    return jax.shard_map(
        local,
        mesh=mesh,
        in_specs=placed,
        out_specs=(
            P("section", "dp", None, None),
            P("section", "dp", None, None, None),
            P(None, "dp"),
            P("dp"),
            P("dp", None),
            P("dp", None),
            P("dp"),
            P("dp", None),
            P("dp", None),
            P("dp", None),
            P("dp"),
            P("dp", None),
            P("dp", None),
            P("dp"),
            P("dp", None),
            P("dp", None),
        ),
        check_vma=False,
    )
```

```python
import functools

import jax
import jax.numpy as jnp
from jax import lax
from jax.experimental import pallas as pl
from jax.experimental.pallas import tpu as pltpu
from jax.sharding import PartitionSpec as P

CH = 4
H = 8
HEAD = 64
SLAB = 256
HEADS = SLAB // HEAD
BLOCK = 128
MIB = 1024 * 1024

eps = 1e-05

f32 = jnp.float32
bf16 = jnp.bfloat16


def dot(a, b):
    return jnp.dot(a, b, preferred_element_type=f32)


def dot_nt(a, b):
    return lax.dot_general(a, b, (((1,), (1,)), ((), ())), preferred_element_type=f32)


def position():
    return (lax.axis_index("section"), lax.axis_index("dp"))


def lanes(shape):
    return lax.broadcasted_iota(jnp.int32, shape, 1)


def rows_of(shape):
    return lax.broadcasted_iota(jnp.int32, shape, 0)


def stack_heads(a):
    head = lanes((1, SLAB)) // HEAD
    masks = [jnp.where(head == place, 1.0, 0.0).astype(bf16) for place in range(HEADS)]
    return jnp.concatenate([a * mask for mask in masks], axis=0)


def compact(scores, length):
    group = lanes((length, BLOCK)) // length
    total = scores[:length]
    for place in range(1, BLOCK // length):
        total = jnp.where(group == place, scores[place * length : (place + 1) * length], total)
    return total


def compact_heads(scores, length):
    return [
        compact(scores[:, head * BLOCK : (head + 1) * BLOCK], length) for head in range(HEADS)
    ]


def expand(values, length):
    group = lanes((length, BLOCK)) // length
    return jnp.concatenate(
        [jnp.where(group == place, values, 0.0) for place in range(BLOCK // length)], axis=0
    ).astype(bf16)


def expand_heads(values, tile, length):
    first = tile * HEADS * BLOCK
    return [
        expand(values[:, first + head * BLOCK : first + (head + 1) * BLOCK], length)
        for head in range(HEADS)
    ]


def head_rows(a, head):
    return a[head * HEAD : (head + 1) * HEAD]


def attend(load, tiles, key_mask, length):
    scores = []
    for tile in tiles:
        scores += compact_heads(dot_nt(load(tile, 1), stack_heads(load(tile, 0))), length)
    scores = jnp.concatenate(scores, axis=1) * HEAD**-0.5
    scores = jnp.where(key_mask, scores, -1e30)
    weights = jnp.exp(scores - jnp.max(scores, axis=0, keepdims=True))
    probs = weights / jnp.sum(weights, axis=0, keepdims=True)
    mixed = []
    for number, tile in enumerate(tiles):
        values = load(tile, 2).T
        parts = expand_heads(probs, number, length)
        mixed.append(
            jnp.concatenate(
                [dot(head_rows(values, head), parts[head]) for head in range(HEADS)], axis=0
            ).astype(bf16)
        )
    return (probs, mixed)


def attend_back(load, load_dmixed, tiles, probs, store, length):
    dprobs = []
    for number, tile in enumerate(tiles):
        grads = load_dmixed(tile)
        stacked = stack_heads(grads)
        scores = dot_nt(stack_heads(load(tile, 2)), grads)
        dprobs += [compact(scores[head * BLOCK : (head + 1) * BLOCK], length) for head in range(HEADS)]
        parts = jnp.concatenate(expand_heads(probs, number, length), axis=1)
        store(tile, 2, dot(parts, stacked).astype(bf16))
    dprobs = jnp.concatenate(dprobs, axis=1)
    dscores = probs * (dprobs - jnp.sum(probs * dprobs, axis=0, keepdims=True))
    scaling = HEAD**-0.5
    for number, tile in enumerate(tiles):
        parts = expand_heads(dscores, number, length)
        keys = load(tile, 1).T
        dq = jnp.concatenate(
            [dot(head_rows(keys, head), parts[head]) for head in range(HEADS)], axis=0
        )
        store(tile, 0, (dq * scaling).astype(bf16).T)
        dk = dot(jnp.concatenate(parts, axis=1), stack_heads(load(tile, 0)))
        store(tile, 1, (dk * scaling).astype(bf16))


def unit(x):
    scale = lax.rsqrt(jnp.mean(x * x, axis=-1, keepdims=True) + eps)
    return (x * scale, scale)


def unit_back(dnormed, gain, normal, scale):
    weighted = dnormed * gain
    return scale * (weighted - normal * jnp.mean(normal * weighted, axis=-1, keepdims=True))


def gelu_parts(before):
    c = 0.7978845608028654
    before = before.astype(bf16)
    square = before * before
    half = bf16(0.5) * jnp.tanh(before * (bf16(c) + bf16(c * 0.044715) * square)) + bf16(0.5)
    value = before * half
    slope = half + value * (bf16(1.0) - half) * (bf16(2.0 * c) + bf16(6.0 * c * 0.044715) * square)
    return (value, slope)


def pick(row, place):
    return jnp.sum(jnp.where(lanes(row.shape) == place, row, 0), axis=1, keepdims=True)


def char_rows(chars, table_ref, language):
    table = table_ref[...].astype(f32)
    row = jnp.sum(jnp.where(rows_of(table.shape) == language, table, 0.0), axis=0, keepdims=True)
    return chars.astype(f32) + row


def counts_by_row(counts, rows, slots):
    words = counts.shape[-1]
    counts = jnp.broadcast_to(counts.astype(f32), (8, words)).astype(bf16)
    shape = (words, rows)
    member = lanes(shape) // slots == rows_of(shape)
    return dot(counts, jnp.where(member, 1.0, 0.0).astype(bf16))[:1]


def counts_column(counts):
    words = counts.shape[-1]
    shape = (words, words)
    spread = jnp.broadcast_to(counts.astype(f32), shape)
    return jnp.sum(
        jnp.where(rows_of(shape) == lanes(shape), spread, 0.0), axis=1, keepdims=True
    )


def fetch_all(sources, targets, sems):
    fetches = [
        pltpu.make_async_copy(source, target, sems.at[place])
        for place, (source, target) in enumerate(zip(sources, targets))
    ]
    for fetch in fetches:
        fetch.start()
    return fetches


def in_hbm(array):
    return pltpu.with_memory_space_constraint(array, pltpu.HBM)


def char_forward_kernel(
    slots,
    chars_hbm,
    languages_hbm,
    counts_hbm,
    table_hbm,
    gain_attn_hbm,
    project_hbm,
    output_hbm,
    gain_mlp_hbm,
    expand_hbm,
    shrink_hbm,
    pooled_ref,
    hidden_sum_ref,
    counts_ref,
    qkv_ref,
    probs_ref,
    mixed_ref,
    middle_ref,
    slope_ref,
    chars_ref,
    languages_ref,
    table_ref,
    gain_attn_ref,
    project_ref,
    output_ref,
    gain_mlp_ref,
    expand_ref,
    shrink_ref,
    sems,
):
    section, _ = position()
    fetches = fetch_all(
        (
            languages_hbm,
            counts_hbm,
            table_hbm,
            gain_attn_hbm,
            chars_hbm.at[section],
            project_hbm,
            output_hbm,
            gain_mlp_hbm,
            expand_hbm,
            shrink_hbm,
        ),
        (
            languages_ref,
            counts_ref,
            table_ref,
            gain_attn_ref,
            chars_ref,
            project_ref,
            output_ref,
            gain_mlp_ref,
            expand_ref,
            shrink_ref,
        ),
        sems,
    )
    for fetch in fetches[:2]:
        fetch.wait()
    counts = counts_ref[section]
    rows = chars_ref.shape[0]
    words = counts.shape[-1]
    row_counts = counts_by_row(counts, rows, slots)
    for fetch in fetches[2:5]:
        fetch.wait()
    x = char_rows(chars_ref[...], table_ref, pick(languages_ref[...], section))
    normal, _ = unit(x)
    normed = (normal * gain_attn_ref[...]).astype(bf16)
    fetches[5].wait()
    qkv_ref[...] = dot(normed, project_ref[...]).astype(bf16)
    blocks = range(rows // BLOCK)

    def load(block, which):
        return qkv_ref[block * BLOCK : (block + 1) * BLOCK, which * SLAB : (which + 1) * SLAB]

    by_head = jnp.concatenate(
        [row_counts[:, block * BLOCK : (block + 1) * BLOCK] for block in blocks for _ in range(HEADS)],
        axis=1,
    )
    key_mask = rows_of((slots, rows * HEADS)).astype(f32) < by_head
    probs, mixed = attend(load, blocks, key_mask, slots)
    probs_ref[...] = probs
    for block in blocks:
        mixed_ref[:, block * BLOCK : (block + 1) * BLOCK] = mixed[block]
    mixed = mixed_ref[...].T
    fetches[6].wait()
    middle = x + dot(mixed, output_ref[...])
    middle_ref[...] = middle
    normal, _ = unit(middle)
    fetches[7].wait()
    normed = (normal * gain_mlp_ref[...]).astype(bf16)
    word_shape = (words, rows)
    lane = lanes(word_shape)
    member = (lane // slots == rows_of(word_shape)) & ((lane % slots).astype(f32) < row_counts)
    member = jnp.where(member, 1.0, 0.0).astype(bf16)
    fetches[8].wait()
    parts = [slice(at, at + 256) for at in range(0, expand_ref.shape[1], 256)]
    before = dot(normed, expand_ref[:, parts[0]])
    for number, part in enumerate(parts):
        value, slope = gelu_parts(before)
        if number + 1 < len(parts):
            before = dot(normed, expand_ref[:, parts[number + 1]])
        slope_ref[:, part] = slope
        hidden_sum_ref[:, part] = dot(member, value).astype(bf16)
    high = middle.astype(bf16)
    fetches[9].wait()
    total = dot(member, high) + dot(hidden_sum_ref[...], shrink_ref[...])
    pooled_ref[...] = (total / counts_column(counts)).astype(bf16)


def char_forward(languages, chars, counts, table, weights, slots):
    rows, width = chars.shape[1:]
    words = rows // slots
    hidden = weights[4].shape[1]
    vmem = pl.BlockSpec(memory_space=pltpu.VMEM)
    hbm = pl.BlockSpec(memory_space=pltpu.HBM)
    fetched = (languages, counts, table) + tuple(weights)
    return pl.pallas_call(
        functools.partial(char_forward_kernel, slots),
        in_specs=[hbm] * 10,
        out_specs=[vmem] * 8,
        out_shape=[
            jax.ShapeDtypeStruct((words, width), bf16),
            jax.ShapeDtypeStruct((words, hidden), bf16),
            jax.ShapeDtypeStruct(counts.shape, counts.dtype),
            jax.ShapeDtypeStruct((rows, 3 * width), bf16),
            jax.ShapeDtypeStruct((slots, rows * HEADS), f32),
            jax.ShapeDtypeStruct((width, rows), bf16),
            jax.ShapeDtypeStruct((rows, width), f32),
            jax.ShapeDtypeStruct((rows, hidden), bf16),
        ],
        scratch_shapes=[pltpu.VMEM(chars.shape[1:], bf16)]
        + [pltpu.VMEM(array.shape, array.dtype) for array in fetched if array is not counts]
        + [pltpu.SemaphoreType.DMA((10,))],
        compiler_params=pltpu.CompilerParams(vmem_limit_bytes=16 * MIB),
        cost_estimate=pl.CostEstimate(
            flops=64 * rows * width * width, bytes_accessed=8 * MIB, transcendentals=0
        ),
        name="char_forward",
    )(*[in_hbm(array) for array in (chars,) + fetched])


CHAR_FIRST_SLOT = 144
CHAR_SECTION_SLOT = 80
CHAR_CORE_SLOT = 112
CHAR_LAST_SLOT = 48


def char_shard(slot, me):
    return me ^ ((slot >> 3) | (((slot >> 1) & 3) << 1) | ((slot & 1) << 3))


def put_shards(gradient, slots, shard_of, at):
    width = SLAB
    columns = gradient.shape[1] // width
    size = gradient.shape[0] // len(slots)
    for number, slot in enumerate(slots):
        first = pl.multiple_of(shard_of(number) * size, size)
        for column in range(columns):
            start = at + column * size
            slot[start : start + size] = gradient[
                pl.ds(first, size), column * width : (column + 1) * width
            ].astype(bf16)
    return at + size * columns


def slot_refs(*refs):
    return [ref.at[place] for ref in refs for place in range(ref.shape[0])]


def char_mlp_back_kernel(
    slots,
    shards,
    counts_ref,
    gain_mlp_ref,
    expand_ref,
    shrink_ref,
    dpooled_ref,
    hidden_sum_ref,
    other_sum_ref,
    mixed_ref,
    middle_ref,
    slope_ref,
    dmiddle_ref,
    gain_ref,
    keep_ref,
    send_ref,
    counts_wide,
    spread,
    dhidden_words,
    dz,
    dbefore,
    expand_grad,
    shrink_grad,
    output_grad,
):
    section, me = position()
    counts = counts_ref[section]
    rows, width = middle_ref.shape
    words = counts.shape[-1]
    column = counts_column(counts)
    counts_wide[...] = jnp.broadcast_to(column, counts_wide.shape)
    spread_value = dpooled_ref[:words].astype(f32) / column
    spread[...] = spread_value
    spread_high = spread_value.astype(bf16)
    dhidden_words[...] = dot_nt(spread_high, shrink_ref[...]).astype(bf16).astype(f32)
    dz[:words] = spread_high
    other = dpooled_ref[words:].astype(f32) / counts_column(counts_ref[1 - section])
    dz[words:] = other.astype(bf16)
    slot = rows_of((slots, 128)).astype(f32)
    for word in range(words):
        at_word = slice(word * slots, (word + 1) * slots)
        present = slot < counts_wide[word : word + 1, :]
        for at in range(0, expand_ref.shape[1], 128):
            part = slice(at, at + 128)
            piece = jnp.where(present, dhidden_words[word : word + 1, part], 0.0).astype(bf16)
            dbefore[at_word, part] = piece * slope_ref[at_word, part]
        for at in range(0, width, 128):
            part = slice(at, at + 128)
            dmiddle_ref[at_word, part] = jnp.where(present, spread[word : word + 1, part], 0.0)
    normal, scale = unit(middle_ref[...])
    normed_t = (normal * gain_mlp_ref[...]).astype(bf16).T
    hidden_sums = jnp.concatenate([hidden_sum_ref[...], other_sum_ref[...]], axis=0)
    hidden_sums_t = hidden_sums.T

    dnormed = dot_nt(dbefore[...], expand_ref[...])
    expand_grad[...] = dot(normed_t, dbefore[...])
    half = width // 2
    own_half = dz[:, pl.ds(pl.multiple_of(section * half, half), half)]
    shrink_grad[...] = dot(hidden_sums_t, own_half)
    dmiddle = dmiddle_ref[...] + unit_back(dnormed, gain_mlp_ref[...], normal, scale)
    dmiddle_ref[...] = dmiddle
    output_grad[...] = dot(mixed_ref[...], dmiddle.astype(bf16))
    gain_ref[...] = jnp.broadcast_to(
        jnp.sum(dnormed * normal, axis=0, keepdims=True), gain_ref.shape
    )
    targets = slot_refs(keep_ref, send_ref)
    at = 0
    for gradient in (expand_grad, output_grad):
        at = put_shards(gradient, targets, lambda slot: char_shard(slot, me), at)
    size = shrink_grad.shape[0] // shards
    for number, target in enumerate(targets):
        first = pl.multiple_of(char_shard(number, me) * size, size)
        piece = shrink_grad[pl.ds(first, size), :].astype(bf16)
        target[at:, :half] = piece[: size // 2]
        target[at:, half:] = piece[size // 2 :]


def char_mlp_back(counts, weights, dpooled, stored, other_sum, slots, shards):
    _, _, output, gain_mlp, expand_w, shrink = weights
    hidden_sum, _, _, mixed, middle, slope = stored
    rows, width = middle.shape
    words = rows // slots
    hidden = expand_w.shape[1]
    half = (shards // 2, CHAR_CORE_SLOT, width)
    vmem = pl.BlockSpec(memory_space=pltpu.VMEM)
    return pl.pallas_call(
        functools.partial(char_mlp_back_kernel, slots, shards),
        in_specs=[vmem] * 10,
        out_specs=[vmem] * 4,
        out_shape=[
            jax.ShapeDtypeStruct((rows, width), f32),
            jax.ShapeDtypeStruct((8, width), f32),
            jax.ShapeDtypeStruct(half, bf16),
            jax.ShapeDtypeStruct(half, bf16),
        ],
        scratch_shapes=[
            pltpu.VMEM((words, 128), f32),
            pltpu.VMEM((words, width), f32),
            pltpu.VMEM((words, hidden), f32),
            pltpu.VMEM((2 * words, width), bf16),
            pltpu.VMEM((rows, hidden), bf16),
            pltpu.VMEM(expand_w.shape, f32),
            pltpu.VMEM((hidden, width // 2), f32),
            pltpu.VMEM(output.shape, f32),
        ],
        compiler_params=pltpu.CompilerParams(vmem_limit_bytes=16 * MIB),
        cost_estimate=pl.CostEstimate(
            flops=64 * rows * width * width, bytes_accessed=8 * MIB, transcendentals=0
        ),
        name="char_mlp_back",
    )(
        counts,
        gain_mlp,
        expand_w,
        shrink,
        dpooled,
        hidden_sum,
        other_sum,
        mixed,
        middle,
        slope,
    )


def char_attn_back_kernel(
    slots,
    shards,
    _,
    chars_hbm,
    languages_hbm,
    table_ref,
    gain_attn_ref,
    project_ref,
    output_ref,
    dmiddle_ref,
    gain_mlp_grad_ref,
    word_gains_ref,
    qkv_ref,
    probs_ref,
    grad_ref,
    keep_ref,
    send_ref,
    extra_ref,
    chars_ref,
    languages_ref,
    dmixed,
    dqkv,
    project_grad,
    sems,
):
    section, me = position()
    fetches = fetch_all(
        (chars_hbm.at[section], languages_hbm), (chars_ref, languages_ref), sems
    )
    rows, width = dmiddle_ref.shape
    dmixed[...] = dot_nt(dmiddle_ref[...].astype(bf16), output_ref[...]).astype(bf16)

    def load(block, which):
        return qkv_ref[block * BLOCK : (block + 1) * BLOCK, which * SLAB : (which + 1) * SLAB]

    def load_dmixed(block):
        return dmixed[block * BLOCK : (block + 1) * BLOCK]

    def store(block, which, value):
        dqkv[block * BLOCK : (block + 1) * BLOCK, which * SLAB : (which + 1) * SLAB] = value

    attend_back(load, load_dmixed, range(rows // BLOCK), probs_ref[...], store, slots)
    for fetch in fetches:
        fetch.wait()
    language = pick(languages_ref[...], section)
    normal, scale = unit(char_rows(chars_ref[...], table_ref, language))
    normed_t = (normal * gain_attn_ref[...]).astype(bf16).T
    dnormed = dot_nt(dqkv[...], project_ref[...])
    project_grad[...] = dot(normed_t, dqkv[...])
    gain_attn_grad = jnp.sum(dnormed * normal, axis=0, keepdims=True)
    dx = dmiddle_ref[...] + unit_back(dnormed, gain_attn_ref[...], normal, scale)
    grad_ref[...] = dx
    row_sum = jnp.sum(dx, axis=0, keepdims=True)
    targets = [
        ref.at[pl.ds(place * CHAR_LAST_SLOT, CHAR_LAST_SLOT)]
        for ref in (keep_ref, send_ref)
        for place in range(shards // 2)
    ]
    put_shards(project_grad, targets, lambda slot: char_shard(slot, me), 0)
    extra = jnp.concatenate(
        [
            gain_attn_grad,
            gain_mlp_grad_ref[:1],
            word_gains_ref[:6],
            jnp.where(rows_of((8, 1)) == language, row_sum, 0.0),
        ],
        axis=0,
    ).astype(bf16)
    extra_ref[...] = extra


def char_attn_back(
    languages,
    chars,
    table,
    weights,
    dmiddle,
    gain_mlp_grad,
    word_gains,
    stored,
    slots,
    shards,
    after,
):
    gain_attn, project, output, _, _, _ = weights
    _, qkv, probs, _, _, _ = stored
    rows, width = dmiddle.shape
    half = (shards // 2 * CHAR_LAST_SLOT, width)
    vmem = pl.BlockSpec(memory_space=pltpu.VMEM)
    hbm = pl.BlockSpec(memory_space=pltpu.HBM)
    return pl.pallas_call(
        functools.partial(char_attn_back_kernel, slots, shards),
        in_specs=[pl.BlockSpec(memory_space=pl.ANY), hbm, hbm] + [vmem] * 9,
        out_specs=[vmem] * 4,
        out_shape=[
            jax.ShapeDtypeStruct((rows, width), f32),
            jax.ShapeDtypeStruct(half, bf16),
            jax.ShapeDtypeStruct(half, bf16),
            jax.ShapeDtypeStruct((16, width), bf16),
        ],
        scratch_shapes=[
            pltpu.VMEM((rows, width), bf16),
            pltpu.VMEM(languages.shape, languages.dtype),
            pltpu.VMEM((rows, width), bf16),
            pltpu.VMEM((rows, 3 * width), bf16),
            pltpu.VMEM(project.shape, f32),
            pltpu.SemaphoreType.DMA((2,)),
        ],
        compiler_params=pltpu.CompilerParams(vmem_limit_bytes=16 * MIB),
        cost_estimate=pl.CostEstimate(
            flops=0, bytes_accessed=0, transcendentals=0
        ),
        name="char_attn_back",
    )(
        after,
        in_hbm(chars),
        in_hbm(languages),
        table,
        gain_attn,
        project,
        output,
        dmiddle,
        gain_mlp_grad,
        word_gains,
        qkv,
        probs,
    )


LONG = pl.CostEstimate(flops=20_000_000_000, bytes_accessed=8 * MIB, transcendentals=0)

WORD_SLOT = 400

SHORT_FLOPS = 400_000_000


def word_kernel(
    length,
    shards,
    own_ref,
    both_ref,
    section_ref,
    far_ref,
    cot_ref,
    cot_far_ref,
    input_ref,
    gain_attn_ref,
    project_ref,
    output_ref,
    gain_mlp_ref,
    expand_ref,
    shrink_ref,
    result_hbm,
    dpooled_ref,
    gains_ref,
    keep_ref,
    send_ref,
    pooled,
    pooled_t,
    dz,
    start,
    normed_t,
    qkv,
    kept,
    mixed_t,
    middle,
    normed_mlp_t,
    hidden,
    dbefore,
    dmixed,
    dqkv,
    dy,
    dstart,
    result,
    input_grad,
    project_grad,
    output_grad,
    expand_grad,
    shrink_grad,
    sem,
):
    total = pooled.shape[0]
    width = output_ref.shape[0]
    section, me = position()
    slabs = width // SLAB
    for place, ref in enumerate((own_ref, section_ref, far_ref, both_ref)):
        pooled[place * length : (place + 1) * length] = ref[...]
    for place, (ref, other) in enumerate(
        ((cot_ref, section), (cot_ref, 1 - section), (cot_far_ref, section), (cot_far_ref, 1 - section))
    ):
        dz[place * length : (place + 1) * length] = ref[other]

    x = dot(pooled[...], input_ref[...])
    start[...] = x
    normal, _ = unit(x)
    low = (normal * gain_attn_ref[...]).astype(bf16)
    normed_t[...] = low.T
    qkv[...] = dot(low, project_ref[...]).astype(bf16)
    tiles = [(block, slab) for block in range(total // BLOCK) for slab in range(slabs)]

    def load(tile, which):
        block, slab = tile
        at = which * width + slab * SLAB
        return qkv[block * BLOCK : (block + 1) * BLOCK, at : at + SLAB]

    mask_shape = (length, len(tiles) * HEADS * BLOCK)
    causal = rows_of(mask_shape) <= lanes(mask_shape) % length
    probs, mixed = attend(load, tiles, causal, length)
    kept[...] = probs
    for (block, slab), piece in zip(tiles, mixed):
        mixed_t[slab * SLAB : (slab + 1) * SLAB, block * BLOCK : (block + 1) * BLOCK] = piece
    x = x + dot(mixed_t[...].T, output_ref[...])
    middle[...] = x
    normal, _ = unit(x)
    low = (normal * gain_mlp_ref[...]).astype(bf16)
    normed_mlp_t[...] = low.T
    dz_all = dz[...]
    for at in range(0, expand_ref.shape[1], 256):
        part = slice(at, at + 256)
        value, bend = gelu_parts(dot(low, expand_ref[:, part]))
        hidden[:, part] = value
        dhidden = dot_nt(dz_all, shrink_ref[part, :]).astype(bf16)
        dbefore[:, part] = dhidden * bend

    def shard_of(slot):
        return (me & 7) ^ ((slot >> 2) | ((slot & 3) << 1))

    def own_rows(flipped):
        many = flipped.shape[0] // 2
        return flipped[pl.ds(pl.multiple_of((me >> 3) * many, many), many), :]

    def half_columns(ref, place):
        many = ref.shape[1] // 2
        return ref[:, pl.ds(pl.multiple_of(place * many, many), many)]

    def own_columns(ref):
        return half_columns(ref, section)

    targets = slot_refs(keep_ref, send_ref)
    hidden_t = half_columns(hidden, me >> 3).T
    pooled_t[...] = pooled[...].T
    normal, scale = unit(middle[...])
    dnormed = dot_nt(dbefore[...], expand_ref[...])
    expand_grad[...] = dot(own_rows(normed_mlp_t), own_columns(dbefore))
    shrink_grad[...] = dot(hidden_t, own_columns(dz))
    dmiddle = dz_all.astype(f32) + unit_back(dnormed, gain_mlp_ref[...], normal, scale)
    dy_low = dmiddle.astype(bf16)
    dy[...] = dy_low
    dmixed[...] = dot_nt(dy_low, output_ref[...]).astype(bf16)
    gain_mlp_grad = jnp.sum(dnormed * normal, axis=0, keepdims=True)
    result[...] = middle[:length] + dot(hidden[:length], shrink_ref[...])
    leave = pltpu.make_async_copy(result, result_hbm, sem)
    leave.start()
    output_grad[...] = dot(own_rows(mixed_t), own_columns(dy))

    def load_dmixed(tile):
        block, slab = tile
        return dmixed[block * BLOCK : (block + 1) * BLOCK, slab * SLAB : (slab + 1) * SLAB]

    def store(tile, which, value):
        block, slab = tile
        at = which * width + slab * SLAB
        dqkv[block * BLOCK : (block + 1) * BLOCK, at : at + SLAB] = value

    attend_back(load, load_dmixed, tiles, kept[...], store, length)
    normal, scale = unit(start[...])
    dnormed = dot_nt(dqkv[...], project_ref[...])
    project_grad[...] = dot(own_rows(normed_t), own_columns(dqkv))
    dword = (dmiddle + unit_back(dnormed, gain_attn_ref[...], normal, scale)).astype(bf16)
    dpooled_ref[...] = dot_nt(dword[: 2 * length], input_ref[...]).astype(bf16)
    dstart[...] = dword
    gain_attn_grad = jnp.sum(dnormed * normal, axis=0, keepdims=True)
    input_grad[...] = dot(own_rows(pooled_t), own_columns(dstart))
    at = 0
    for ref in (input_grad, project_grad, output_grad, expand_grad, shrink_grad):
        at = put_shards(ref, targets, shard_of, at)
    gains_ref[...] = 0.25 * jnp.concatenate(
        [gain_attn_grad[:, :SLAB], gain_attn_grad[:, SLAB:]]
        + [gain_mlp_grad[:, :SLAB], gain_mlp_grad[:, SLAB:]]
        + [jnp.zeros((4, SLAB), f32)],
        axis=0,
    )
    leave.wait()


def word_group(pooled, cotangents, word_input, weights, shards):
    gain_attn, project, output, gain_mlp, expand_w, shrink = weights
    length, channels = pooled[0].shape
    width = output.shape[0]
    hidden = expand_w.shape[1]
    total = 4 * length
    half = (4, WORD_SLOT, SLAB)
    vmem = pl.BlockSpec(memory_space=pltpu.VMEM)
    hbm = pl.BlockSpec(memory_space=pltpu.HBM)
    return pl.pallas_call(
        functools.partial(word_kernel, length, shards),
        in_specs=[vmem] * 13,
        out_specs=[hbm, vmem, vmem, vmem, vmem],
        out_shape=[
            jax.ShapeDtypeStruct((length, width), f32),
            jax.ShapeDtypeStruct((2 * length, channels), bf16),
            jax.ShapeDtypeStruct((8, SLAB), f32),
            jax.ShapeDtypeStruct(half, bf16),
            jax.ShapeDtypeStruct(half, bf16),
        ],
        scratch_shapes=[
            pltpu.VMEM((total, channels), bf16),
            pltpu.VMEM((channels, total), bf16),
            pltpu.VMEM((total, width), bf16),
            pltpu.VMEM((total, width), f32),
            pltpu.VMEM((width, total), bf16),
            pltpu.VMEM((total, 3 * width), bf16),
            pltpu.VMEM((length, total * (width // HEAD)), f32),
            pltpu.VMEM((width, total), bf16),
            pltpu.VMEM((total, width), f32),
            pltpu.VMEM((width, total), bf16),
            pltpu.VMEM((total, hidden), bf16),
            pltpu.VMEM((total, hidden), bf16),
            pltpu.VMEM((total, width), bf16),
            pltpu.VMEM((total, 3 * width), bf16),
            pltpu.VMEM((total, width), bf16),
            pltpu.VMEM((total, width), bf16),
            pltpu.VMEM((length, width), f32),
            pltpu.VMEM((channels // 2, width // 2), f32),
            pltpu.VMEM((width // 2, 3 * width // 2), f32),
            pltpu.VMEM((width // 2, width // 2), f32),
            pltpu.VMEM((width // 2, hidden // 2), f32),
            pltpu.VMEM((hidden // 2, width // 2), f32),
            pltpu.SemaphoreType.DMA,
        ],
        compiler_params=pltpu.CompilerParams(vmem_limit_bytes=20 * MIB),
        cost_estimate=pl.CostEstimate(
            flops=total * width * width * 25 * 4, bytes_accessed=8 * MIB, transcendentals=0
        ),
        name="word_group",
    )(*pooled, *cotangents, word_input, gain_attn, project, output, gain_mlp, expand_w, shrink)


def summed(*parts):
    return functools.reduce(lambda a, b: a + b, [part.astype(f32) for part in parts])


def added(*parts):
    return summed(*parts).astype(bf16)


def by_section(section, low, high):
    return (jnp.where(section == 0, low, high), jnp.where(section == 0, high, low))


def word_sum_kernel(keep, arrived, *outs):
    for place, ref in enumerate(outs):
        ref[...] = added(keep[place], arrived[place])


def word_sum(keep, arrived):
    return pl.pallas_call(
        word_sum_kernel,
        out_shape=[jax.ShapeDtypeStruct((WORD_SLOT, SLAB), bf16)] * 4,
        compiler_params=pltpu.CompilerParams(vmem_limit_bytes=12 * MIB),
        name="word_sum",
    )(keep, arrived)


def first_sum_kernel(keep, arrived, stay_ref, go_ref, shrink_ref):
    section, _ = position()
    half = SLAB // 2
    for place in range(keep.shape[0]):
        total = added(keep[place], arrived[place])
        rows = total[:CHAR_SECTION_SLOT]
        stay_ref[place], go_ref[place] = by_section(section, rows[:, :half], rows[:, half:])
        rows = total[CHAR_SECTION_SLOT:]
        shrink_ref[place] = jnp.concatenate([rows[:, :half], rows[:, half:]], axis=0)


def first_sum(keep, arrived):
    half = jax.ShapeDtypeStruct((keep.shape[0], CHAR_SECTION_SLOT, SLAB // 2), bf16)
    shrink = jax.ShapeDtypeStruct(
        (keep.shape[0], CHAR_FIRST_SLOT - CHAR_SECTION_SLOT, SLAB // 2), bf16
    )
    return pl.pallas_call(
        first_sum_kernel,
        out_shape=[half, half, shrink],
        compiler_params=pltpu.CompilerParams(vmem_limit_bytes=12 * MIB),
        name="first_sum",
    )(keep, arrived)


def section_sum_kernel(stay, arrived, out):
    out[...] = added(stay[...], arrived[...])


def section_sum(stay, arrived):
    return pl.pallas_call(
        section_sum_kernel,
        out_shape=jax.ShapeDtypeStruct(stay.shape, bf16),
        compiler_params=pltpu.CompilerParams(vmem_limit_bytes=12 * MIB),
        cost_estimate=pl.CostEstimate(flops=SHORT_FLOPS, bytes_accessed=0, transcendentals=0),
        name="section_sum",
    )(stay, arrived)


def second_sum_kernel(first, shrink, keep, core_arrived, own_extra, core_extra, *outs):
    _, me = position()
    half = SLAB // 2
    extra = summed(own_extra[...], core_extra[...])
    for place, out in enumerate(outs):
        at = CHAR_FIRST_SLOT
        for far in range(2):
            entry = 2 * place + far
            columns = slice(far * half, (far + 1) * half)
            total = first[entry]
            middle = CHAR_SECTION_SLOT - 16
            out[:middle, columns] = total[:middle]
            out[middle : CHAR_FIRST_SLOT - 16, columns] = shrink[entry]
            out[CHAR_FIRST_SLOT - 16 : CHAR_FIRST_SLOT, columns] = total[middle:]
            rows = slice(entry * CHAR_LAST_SLOT, (entry + 1) * CHAR_LAST_SLOT)
            out[at : at + CHAR_LAST_SLOT] = added(keep[rows], core_arrived[rows])
            at += CHAR_LAST_SLOT
            shard = char_shard(entry, me)
            turned = pltpu.roll(extra, lax.rem(SLAB - shard * 16, SLAB), 1)
            word = pltpu.roll(extra, lax.rem(2 * SLAB - shard * 32, SLAB), 1)
            upper = shard * 32 >= SLAB
            block = jnp.concatenate(
                [
                    turned[:2],
                    jnp.where(upper, word[3:4], word[2:3]),
                    jnp.where(upper, word[5:6], word[4:5]),
                    turned[4:],
                ],
                axis=0,
            )
            out[-16:, columns] = block[:, :half].astype(bf16)


def total_kernel(*refs):
    *pieces, chars_ref, out, chars_hbm, sem = refs
    leave = pltpu.make_async_copy(chars_ref, chars_hbm, sem)
    leave.start()
    out[...] = added(*[ref[...] for ref in pieces])
    leave.wait()


def total_of(*pieces, chars_grad):
    vmem = pl.BlockSpec(memory_space=pltpu.VMEM)
    return pl.pallas_call(
        total_kernel,
        in_specs=[vmem] * (len(pieces) + 1),
        out_specs=[vmem, pl.BlockSpec(memory_space=pltpu.HBM)],
        out_shape=[
            jax.ShapeDtypeStruct(pieces[0].shape, bf16),
            jax.ShapeDtypeStruct(chars_grad.shape, f32),
        ],
        scratch_shapes=[pltpu.SemaphoreType.DMA],
        compiler_params=pltpu.CompilerParams(vmem_limit_bytes=12 * MIB),
        cost_estimate=LONG,
        name="total",
    )(*pieces, chars_grad)


def second_sum(first, last):
    rows = CHAR_FIRST_SLOT + 2 * CHAR_LAST_SLOT + 16
    return pl.pallas_call(
        second_sum_kernel,
        out_shape=[jax.ShapeDtypeStruct((rows, SLAB), bf16)] * 4,
        compiler_params=pltpu.CompilerParams(vmem_limit_bytes=12 * MIB),
        name="second_sum",
    )(*first, *last)


FOLD = 80


def plane_sum_kernel(*refs):
    half = SLAB // 2
    pieces = refs[:4]
    for far, out in enumerate(refs[5:]):
        columns = slice(far * half, (far + 1) * half)
        total = added(*[ref[:CHAR_FIRST_SLOT, columns] for ref in pieces])
        out[:FOLD, :half] = total[:FOLD]
        out[:FOLD, half:] = total[CHAR_FIRST_SLOT - FOLD :]
        out[:16, half:] = added(*[ref[-16:, columns] for ref in pieces])
        first = CHAR_FIRST_SLOT + far * CHAR_LAST_SLOT
        out[FOLD:] = added(*[ref[first : first + CHAR_LAST_SLOT] for ref in pieces])


def plane_sum(pieces, after):
    return pl.pallas_call(
        plane_sum_kernel,
        in_specs=[pl.BlockSpec(memory_space=pltpu.VMEM)] * 4 + [pl.BlockSpec(memory_space=pl.ANY)],
        out_shape=[jax.ShapeDtypeStruct((FOLD + CHAR_LAST_SLOT, SLAB), bf16)] * 2,
        compiler_params=pltpu.CompilerParams(vmem_limit_bytes=12 * MIB),
        cost_estimate=LONG,
        name="plane_sum",
    )(*pieces, after)


def char_last_kernel(near_ref, both_ref, far_ref, section_ref, _, *outs):
    section, _ = position()
    half = SLAB // 2
    mine = summed(near_ref[:FOLD], far_ref[:FOLD])
    theirs = summed(section_ref[:FOLD], both_ref[:FOLD])

    def unfold(total):
        return jnp.concatenate(
            [total[:, :half], total[2 * FOLD - CHAR_FIRST_SLOT :, half:]], axis=0
        )

    first = jnp.concatenate(by_section(section, unfold(mine), unfold(theirs)), axis=1)
    extra = mine[:16, half:] + theirs[:16, half:]
    last = summed(near_ref[FOLD:], section_ref[FOLD:], far_ref[FOLD:], both_ref[FOLD:])
    (
        table_ref,
        gain_attn_ref,
        project_ref,
        output_ref,
        gain_mlp_ref,
        expand_ref,
        shrink_ref,
        word_gain_attn_ref,
        word_gain_mlp_ref,
    ) = outs
    for total, refs in ((first, (expand_ref, shrink_ref, output_ref)), (last, (project_ref,))):
        at = 0
        for ref in refs:
            size = ref.shape[0]
            for column in range(ref.shape[1] // SLAB):
                ref[:, column * SLAB : (column + 1) * SLAB] = total[at : at + size]
                at += size
    size = gain_attn_ref.shape[1]
    gain_attn_ref[...] = extra[0:1, :size]
    gain_mlp_ref[...] = extra[1:2, :size]
    table_ref[...] = extra[8:16, :size]
    size = word_gain_attn_ref.shape[1]
    word_gain_attn_ref[...] = extra[2:3, :size]
    word_gain_mlp_ref[...] = extra[3:4, :size]


def char_last(near, arrived, shapes, after):
    return pl.pallas_call(
        char_last_kernel,
        in_specs=[pl.BlockSpec(memory_space=pltpu.VMEM)] * 4 + [pl.BlockSpec(memory_space=pltpu.HBM)],
        out_shape=[jax.ShapeDtypeStruct(shape, f32) for shape in shapes],
        compiler_params=pltpu.CompilerParams(vmem_limit_bytes=12 * MIB),
        name="char_last",
    )(near, *arrived, in_hbm(after))


def word_last_kernel(own_ref, other_ref, *outs):
    section, _ = position()
    own = own_ref[...].astype(f32)
    halves = by_section(section, own, other_ref[...].astype(f32))
    at = 0
    for ref in outs:
        size = ref.shape[0]
        columns = ref.shape[1] // (2 * SLAB)
        for column in range(columns):
            for half in range(2):
                first = (half * columns + column) * SLAB
                ref[:, first : first + SLAB] = halves[half][at : at + size]
            at += size


def word_last(own, other, shapes):
    return pl.pallas_call(
        word_last_kernel,
        out_shape=[jax.ShapeDtypeStruct(shape, f32) for shape in shapes],
        compiler_params=pltpu.CompilerParams(vmem_limit_bytes=12 * MIB),
        name="word_last",
    )(own, other)


def exchange(value, section_bit, dp_bits):
    shards = lax.axis_size("dp")
    pairs = [
        (s * shards + d, (s ^ section_bit) * shards + (d ^ dp_bits))
        for s in range(lax.axis_size("section"))
        for d in range(shards)
    ]
    return lax.ppermute(value, ("section", "dp"), pairs)


CORE, SIDE, NEAR, FAR = (1, 2, 4, 8)


def plane_exchange(pieces):
    return tuple(
        exchange(piece, 0, bits) for piece, bits in zip(pieces[:0:-1], (SIDE | NEAR, NEAR, SIDE))
    ) + (pieces[0],)


def local_grouped(
    chars, counts, languages, language_table, char_weights, word_input, word_weights, cotangent
):
    shards = lax.axis_size("dp")
    micros, _, words, slots, width = chars.shape
    rows = words * slots
    cot = cotangent[:, 0]
    cot_far = exchange(cot, 0, FAR)
    char_weights = tuple(w[None] if w.ndim == 1 else w for w in char_weights)
    word_weights = tuple(w[None] if w.ndim == 1 else w for w in word_weights)
    chars = chars.reshape(micros, rows, width)
    counts = counts.reshape(micros, 1, words)
    languages = languages.reshape(1, micros)
    pooled, hidden_sum, own_counts, *stored = char_forward(
        languages, chars, counts, language_table, char_weights, slots
    )
    stored = (hidden_sum, *stored)
    other_sum = exchange(hidden_sum, 1, 0)
    others = (exchange(pooled, 1, FAR), exchange(pooled, 1, 0), exchange(pooled, 0, FAR))
    result, dpooled, word_gains, keep, send = word_group(
        (pooled,) + others, (cot, cot_far), word_input, word_weights, shards
    )
    word = plane_exchange(word_sum(keep, exchange(send, 0, CORE)))
    dmiddle, gain_mlp_grad, keep, send = char_mlp_back(
        own_counts, char_weights, dpooled, stored, other_sum, slots, shards
    )
    stay, go, shrink = first_sum(keep, exchange(send, 0, CORE))
    first = (section_sum(stay, exchange(go, 1, 0)), shrink)
    chars_grad, keep, send, extra = char_attn_back(
        languages,
        chars,
        language_table,
        char_weights,
        dmiddle,
        gain_mlp_grad,
        word_gains,
        stored,
        slots,
        shards,
        stay,
    )
    last = (keep, exchange(send, 0, CORE), extra, exchange(extra, 0, CORE))
    char = plane_exchange(second_sum(first, last))
    word, chars_grad = total_of(*word, chars_grad=chars_grad)
    near, far = plane_sum(char, word)
    arrived = (exchange(far, 1, FAR), exchange(far, 0, FAR), exchange(near, 1, 0))

    def shard_shapes(weights):
        for weight in weights:
            if weight.shape[0] == 1:
                yield (1, weight.shape[1] // shards)
            else:
                yield (weight.shape[0] // shards, weight.shape[1])

    table_shape = (language_table.shape[0], language_table.shape[1] // shards)
    input_shape, attn_shape, project_shape, output_shape, mlp_shape, expand_shape, shrink_shape = (
        shard_shapes((word_input,) + word_weights)
    )
    word_shapes = [input_shape, project_shape, output_shape, expand_shape, shrink_shape]
    word_totals = word_last(word, exchange(word, 1, 0), word_shapes)
    char_shapes = [table_shape, *shard_shapes(char_weights), attn_shape, mlp_shape]
    *char_totals, attn, mlp = char_last(near, arrived, char_shapes, word_totals[0])
    totals = [*char_totals, word_totals[0], attn, *word_totals[1:3], mlp, *word_totals[3:]]
    totals = [total[0] if total.shape[0] == 1 else total for total in totals]
    return (result[None, None], chars_grad.reshape((1, 1, words, slots, width))) + tuple(totals)


def norm_forward(inputs, gain):
    return inputs * lax.rsqrt(jnp.mean(inputs * inputs, axis=-1, keepdims=True) + eps) * gain


def attend_forward(normed, project, head_count, key_mask):
    row_count, length, channels = normed.shape
    head_size = channels // head_count
    qkv = jnp.einsum("blc,cf->blf", normed, project, preferred_element_type=jnp.float32).astype(
        jnp.bfloat16
    )
    pieces = qkv.reshape(row_count, length, 3, head_count, head_size)
    scores = jnp.einsum(
        "bqhd,bkhd->bhqk", pieces[:, :, 0], pieces[:, :, 1], preferred_element_type=jnp.float32
    ) * head_size ** (-0.5)
    scores = jnp.where(key_mask, scores, -1e30)
    row_max = jnp.max(scores, axis=-1, keepdims=True)
    weights_exp = jnp.exp(scores - row_max)
    row_total = jnp.sum(weights_exp, axis=-1, keepdims=True)
    attn_probs = (weights_exp / row_total).astype(jnp.bfloat16)
    mixed_heads = jnp.einsum(
        "bhqk,bkhd->bqhd", attn_probs, pieces[:, :, 2], preferred_element_type=jnp.float32
    )
    mixed_heads = mixed_heads.reshape(row_count, length, channels).astype(jnp.bfloat16)
    return (qkv, row_max + jnp.log(row_total), mixed_heads)


def attend_backward(
    normed, project, output, qkv, logsum, mixed_heads, dmiddle_low, head_count, key_mask
):
    row_count, length, channels = normed.shape
    head_size = channels // head_count
    scaling = head_size ** (-0.5)
    output_grad = jnp.einsum(
        "blc,bld->cd", mixed_heads, dmiddle_low, preferred_element_type=jnp.float32
    )
    dmixed = jnp.einsum(
        "bld,cd->blc", dmiddle_low, output, preferred_element_type=jnp.float32
    ).astype(jnp.bfloat16)
    dmixed = dmixed.reshape(row_count, length, head_count, head_size)
    pieces = qkv.reshape(row_count, length, 3, head_count, head_size)
    scores = (
        jnp.einsum(
            "bqhd,bkhd->bhqk", pieces[:, :, 0], pieces[:, :, 1], preferred_element_type=jnp.float32
        )
        * scaling
    )
    scores = jnp.where(key_mask, scores, -1e30)
    attn_probs = jnp.exp(scores - logsum)
    dprobs = jnp.einsum(
        "bqhd,bkhd->bhqk", dmixed, pieces[:, :, 2], preferred_element_type=jnp.float32
    )
    row_delta = jnp.sum(attn_probs * dprobs, axis=-1, keepdims=True)
    dscores = (attn_probs * (dprobs - row_delta)).astype(jnp.bfloat16)
    dquery = (
        jnp.einsum("bhqk,bkhd->bqhd", dscores, pieces[:, :, 1], preferred_element_type=jnp.float32)
        * scaling
    )
    dkeys = (
        jnp.einsum("bhqk,bqhd->bkhd", dscores, pieces[:, :, 0], preferred_element_type=jnp.float32)
        * scaling
    )
    dvalues = jnp.einsum(
        "bhqk,bqhd->bkhd",
        attn_probs.astype(jnp.bfloat16),
        dmixed,
        preferred_element_type=jnp.float32,
    )
    dqkv = (
        jnp.stack([dquery, dkeys, dvalues], axis=2)
        .reshape(row_count, length, 3 * channels)
        .astype(jnp.bfloat16)
    )
    project_grad = jnp.einsum("blc,blf->cf", normed, dqkv, preferred_element_type=jnp.float32)
    dnormed = jnp.einsum("blf,cf->blc", dqkv, project, preferred_element_type=jnp.float32)
    return (dnormed, project_grad, output_grad)


def block_forward(inputs, weights, head_count, key_mask):
    gain_attn, project, output, gain_mlp, expand, shrink = weights
    normed = norm_forward(inputs, gain_attn).astype(jnp.bfloat16)
    qkv, logsum, mixed_heads = attend_forward(normed, project, head_count, key_mask)
    middle = inputs + jnp.einsum(
        "blc,cd->bld", mixed_heads, output, preferred_element_type=jnp.float32
    )
    normed_mlp = norm_forward(middle, gain_mlp).astype(jnp.bfloat16)
    before = jnp.einsum("blc,cf->blf", normed_mlp, expand, preferred_element_type=jnp.float32)
    hidden = jax.nn.gelu(before).astype(jnp.bfloat16)
    result = middle + jnp.einsum("blf,fc->blc", hidden, shrink, preferred_element_type=jnp.float32)
    return (result, (inputs, normed, qkv, logsum, mixed_heads, middle, normed_mlp, before, hidden))


def block_backward(dresult, stored, weights, head_count, key_mask):
    gain_attn, project, output, gain_mlp, expand, shrink = weights
    inputs, normed, qkv, logsum, mixed_heads, middle, normed_mlp, before, hidden = stored
    grad_low = dresult.astype(jnp.bfloat16)
    shrink_grad = jnp.einsum("blf,blc->fc", hidden, grad_low, preferred_element_type=jnp.float32)
    dhidden = jnp.einsum(
        "blc,fc->blf", grad_low, shrink, preferred_element_type=jnp.float32
    ).astype(jnp.bfloat16)
    gelu_pull = jax.vjp(jax.nn.gelu, before)[1]
    dbefore = gelu_pull(dhidden.astype(jnp.float32))[0].astype(jnp.bfloat16)
    expand_grad = jnp.einsum("blc,blf->cf", normed_mlp, dbefore, preferred_element_type=jnp.float32)
    dnormed_mlp = jnp.einsum("blf,cf->blc", dbefore, expand, preferred_element_type=jnp.float32)
    norm_pull = jax.vjp(norm_forward, middle, gain_mlp)[1]
    dmiddle_norm, gain_mlp_grad = norm_pull(dnormed_mlp)
    dmiddle = dresult + dmiddle_norm
    dnormed, project_grad, output_grad = attend_backward(
        normed,
        project,
        output,
        qkv,
        logsum,
        mixed_heads,
        dmiddle.astype(jnp.bfloat16),
        head_count,
        key_mask,
    )
    first_pull = jax.vjp(norm_forward, inputs, gain_attn)[1]
    dinputs_norm, gain_attn_grad = first_pull(dnormed)
    return (
        dmiddle + dinputs_norm,
        (gain_attn_grad, project_grad, output_grad, gain_mlp_grad, expand_grad, shrink_grad),
    )


def char_front(char_text, char_count, language, lang_table, weights):
    present = lax.broadcasted_iota(jnp.int32, char_text.shape[:2], 1) < char_count[:, None]
    onehot = (lax.broadcasted_iota(jnp.int32, (lang_table.shape[0],), 0) == language).astype(
        jnp.bfloat16
    )
    lang_row = jnp.dot(onehot, lang_table, preferred_element_type=jnp.float32)
    inputs = char_text.astype(jnp.float32) + lang_row
    result, stored = block_forward(inputs, weights, CH, present[:, None, None, :])
    summed = jnp.sum(jnp.where(present[:, :, None], result, 0.0), axis=1)
    pooled = (summed / char_count[:, None].astype(jnp.float32)).astype(jnp.bfloat16)
    return (pooled, stored, present, onehot)


def char_back(stored, present, onehot, char_count, dpooled, weights):
    spread = dpooled.astype(jnp.float32) / char_count[:, None].astype(jnp.float32)
    dresult = jnp.where(present[:, :, None], spread[:, None, :], 0.0)
    dinputs, gradients = block_backward(dresult, stored, weights, CH, present[:, None, None, :])
    table_grad = onehot.astype(jnp.float32)[:, None] * jnp.sum(dinputs, axis=(0, 1))[None, :]
    return (dinputs, (table_grad,) + gradients)


def word_full(pooled, cot_rows, word_input, weights):
    length = pooled.shape[0]
    word_start = jnp.dot(pooled, word_input, preferred_element_type=jnp.float32)[None]
    causal = (
        lax.broadcasted_iota(jnp.int32, (length, length), 0)
        >= lax.broadcasted_iota(jnp.int32, (length, length), 1)
    )[None, None]
    result, stored = block_forward(word_start, weights, H, causal)
    dstart, gradients = block_backward(
        cot_rows.astype(jnp.float32)[None], stored, weights, H, causal
    )
    grad_low = dstart[0].astype(jnp.bfloat16)
    input_grad = jnp.einsum("wc,wd->cd", pooled, grad_low, preferred_element_type=jnp.float32)
    dpooled = jnp.einsum(
        "wd,cd->wc", grad_low, word_input, preferred_element_type=jnp.float32
    ).astype(jnp.bfloat16)
    return (result[0], dpooled, (input_grad,) + gradients)


def reduce_rows(gradients):
    shards = lax.axis_size("dp")
    flat = []
    for place, gradient in enumerate(gradients):
        if place == 0:
            gradient = gradient.T
        flat.append(gradient.astype(jnp.bfloat16).reshape(shards, -1))
    packed = jnp.concatenate(flat, axis=1)
    me = lax.axis_index("dp")
    packed = jnp.take(packed, jnp.arange(shards) ^ me, axis=0)
    bit = 1
    while packed.shape[0] > 1:
        pairs = packed.reshape(packed.shape[0] // 2, 2, packed.shape[1])
        arrived = lax.ppermute(pairs[:, 1], "dp", [(i, i ^ bit) for i in range(shards)])
        packed = (pairs[:, 0].astype(jnp.float32) + arrived.astype(jnp.float32)).astype(
            jnp.bfloat16
        )
        bit *= 2
    arrived = lax.ppermute(packed, "section", [(0, 1), (1, 0)])
    total = (packed.astype(jnp.float32) + arrived.astype(jnp.float32))[0]
    outs = []
    at = 0
    for place, gradient in enumerate(gradients):
        size = gradient.size // shards
        piece = total[at : at + size]
        at += size
        if place == 0:
            outs.append(piece.reshape(-1, gradient.shape[0]).T)
        else:
            outs.append(piece.reshape((gradient.shape[0] // shards,) + gradient.shape[1:]))
    return tuple(outs)


def local(
    chars,
    counts,
    languages,
    language_table,
    char_gain_attn,
    char_project,
    char_output,
    char_gain_mlp,
    char_expand,
    char_shrink,
    word_input,
    word_gain_attn,
    word_project,
    word_output,
    word_gain_mlp,
    word_expand,
    word_shrink,
    cotangent,
):
    char_weights = (
        char_gain_attn,
        char_project,
        char_output,
        char_gain_mlp,
        char_expand,
        char_shrink,
    )
    word_weights = (
        word_gain_attn,
        word_project,
        word_output,
        word_gain_mlp,
        word_expand,
        word_shrink,
    )
    if lax.axis_size("dp") == 16:
        return local_grouped(
            chars,
            counts,
            languages,
            language_table,
            char_weights,
            word_input,
            word_weights,
            cotangent,
        )
    section_index = lax.axis_index("section")
    char_text = chars[section_index, 0]
    char_count = counts[section_index, 0]
    language = languages[section_index, 0]
    cot_rows = cotangent[section_index, 0]
    pooled, stored, present, onehot = char_front(
        char_text, char_count, language, language_table, char_weights
    )
    result, dpooled, word_grads = word_full(pooled, cot_rows, word_input, word_weights)
    text_grad, char_grads = char_back(stored, present, onehot, char_count, dpooled, char_weights)
    totals = reduce_rows(char_grads + word_grads)
    return (result[None, None], text_grad[None, None]) + totals


def solution(mesh):
    placed = (
        P(None, "dp", None, None, None),
        P(None, "dp", None),
        P(None, "dp"),
        P(),
        P(),
        P(),
        P(),
        P(),
        P(),
        P(),
        P(),
        P(),
        P(),
        P(),
        P(),
        P(),
        P(),
        P(None, "dp", None, None),
    )
    return jax.shard_map(
        local,
        mesh=mesh,
        in_specs=placed,
        out_specs=(
            P("section", "dp", None, None),
            P("section", "dp", None, None, None),
            P(None, "dp"),
            P("dp"),
            P("dp", None),
            P("dp", None),
            P("dp"),
            P("dp", None),
            P("dp", None),
            P("dp", None),
            P("dp"),
            P("dp", None),
            P("dp", None),
            P("dp"),
            P("dp", None),
            P("dp", None),
        ),
        check_vma=False,
    )
```

```python
import functools

import jax
import jax.numpy as jnp
from jax import lax
from jax.experimental import pallas as pl
from jax.experimental.pallas import tpu as pltpu
from jax.sharding import PartitionSpec as P

CH = 4
H = 8
HEAD = 64
SLAB = 256
HEADS = SLAB // HEAD
BLOCK = 128
PART = 128
MIB = 1024 * 1024

eps = 1e-05

f32 = jnp.float32
bf16 = jnp.bfloat16


def dot(a, b):
    return jnp.dot(a, b, preferred_element_type=f32)


def dot_nt(a, b):
    return lax.dot_general(a, b, (((1,), (1,)), ((), ())), preferred_element_type=f32)


def position():
    return (lax.axis_index("section"), lax.axis_index("dp"))


def lanes(shape):
    return lax.broadcasted_iota(jnp.int32, shape, 1)


def rows_of(shape):
    return lax.broadcasted_iota(jnp.int32, shape, 0)


def stack_heads(a):
    head = lanes((1, SLAB)) // HEAD
    masks = [jnp.where(head == place, 1.0, 0.0).astype(bf16) for place in range(HEADS)]
    return jnp.concatenate([a * mask for mask in masks], axis=0)


def compact(scores, length):
    group = lanes((length, BLOCK)) // length
    total = scores[:length]
    for place in range(1, BLOCK // length):
        total = jnp.where(group == place, scores[place * length : (place + 1) * length], total)
    return total


def compact_heads(scores, length):
    return [
        compact(scores[:, head * BLOCK : (head + 1) * BLOCK], length) for head in range(HEADS)
    ]


def expand(values, length):
    group = lanes((length, BLOCK)) // length
    return jnp.concatenate(
        [jnp.where(group == place, values, 0.0) for place in range(BLOCK // length)], axis=0
    ).astype(bf16)


def expand_heads(values, tile, length):
    first = tile * HEADS * BLOCK
    return [
        expand(values[:, first + head * BLOCK : first + (head + 1) * BLOCK], length)
        for head in range(HEADS)
    ]


def head_rows(a, head):
    return a[head * HEAD : (head + 1) * HEAD]


def attend(load, tiles, key_mask, length):
    scores = []
    for tile in tiles:
        scores += compact_heads(dot_nt(load(tile, 1), stack_heads(load(tile, 0))), length)
    scores = jnp.concatenate(scores, axis=1) * HEAD**-0.5
    scores = jnp.where(key_mask, scores, -1e30)
    weights = jnp.exp(scores - jnp.max(scores, axis=0, keepdims=True))
    probs = weights / jnp.sum(weights, axis=0, keepdims=True)
    mixed = []
    for number, tile in enumerate(tiles):
        values = load(tile, 2).T
        parts = expand_heads(probs, number, length)
        mixed.append(
            jnp.concatenate(
                [dot(head_rows(values, head), parts[head]) for head in range(HEADS)], axis=0
            ).astype(bf16)
        )
    return (probs, mixed)


def attend_back(load, load_dmixed, tiles, probs, store, length):
    dprobs = []
    for number, tile in enumerate(tiles):
        grads = load_dmixed(tile)
        stacked = stack_heads(grads)
        scores = dot_nt(stack_heads(load(tile, 2)), grads)
        dprobs += [compact(scores[head * BLOCK : (head + 1) * BLOCK], length) for head in range(HEADS)]
        parts = jnp.concatenate(expand_heads(probs, number, length), axis=1)
        store(tile, 2, dot(parts, stacked).astype(bf16))
    dprobs = jnp.concatenate(dprobs, axis=1)
    dscores = probs * (dprobs - jnp.sum(probs * dprobs, axis=0, keepdims=True))
    scaling = HEAD**-0.5
    for number, tile in enumerate(tiles):
        parts = expand_heads(dscores, number, length)
        keys = load(tile, 1).T
        dq = jnp.concatenate(
            [dot(head_rows(keys, head), parts[head]) for head in range(HEADS)], axis=0
        )
        store(tile, 0, (dq * scaling).astype(bf16).T)
        dk = dot(jnp.concatenate(parts, axis=1), stack_heads(load(tile, 0)))
        store(tile, 1, (dk * scaling).astype(bf16))


def unit(x):
    scale = lax.rsqrt(jnp.mean(x * x, axis=-1, keepdims=True) + eps)
    return (x * scale, scale)


def unit_back(dnormed, gain, normal, scale):
    weighted = dnormed * gain
    return scale * (weighted - normal * jnp.mean(normal * weighted, axis=-1, keepdims=True))


def gelu_parts(before):
    c = 0.7978845608028654
    before = before.astype(bf16)
    square = before * before
    half = bf16(0.5) * jnp.tanh(before * (bf16(c) + bf16(c * 0.044715) * square)) + bf16(0.5)
    value = before * half
    slope = half + value * (bf16(1.0) - half) * (bf16(2.0 * c) + bf16(6.0 * c * 0.044715) * square)
    return (value, slope)


def pick(row, place):
    return jnp.sum(jnp.where(lanes(row.shape) == place, row, 0), axis=1, keepdims=True)


def char_rows(chars, table_ref, language):
    table = table_ref[...].astype(f32)
    row = jnp.sum(jnp.where(rows_of(table.shape) == language, table, 0.0), axis=0, keepdims=True)
    return chars.astype(f32) + row


def counts_by_row(counts, rows, slots):
    words = counts.shape[-1]
    counts = jnp.broadcast_to(counts.astype(f32), (8, words)).astype(bf16)
    shape = (words, rows)
    member = lanes(shape) // slots == rows_of(shape)
    return dot(counts, jnp.where(member, 1.0, 0.0).astype(bf16))[:1]


def counts_column(counts):
    words = counts.shape[-1]
    shape = (words, words)
    spread = jnp.broadcast_to(counts.astype(f32), shape)
    return jnp.sum(
        jnp.where(rows_of(shape) == lanes(shape), spread, 0.0), axis=1, keepdims=True
    )


def fetch_all(sources, targets, sems):
    fetches = [
        pltpu.make_async_copy(source, target, sems.at[place])
        for place, (source, target) in enumerate(zip(sources, targets))
    ]
    for fetch in fetches:
        fetch.start()
    return fetches


def in_hbm(array):
    return pltpu.with_memory_space_constraint(array, pltpu.HBM)


def char_forward_kernel(
    slots,
    chars_hbm,
    languages_hbm,
    counts_hbm,
    table_hbm,
    gain_attn_hbm,
    project_hbm,
    output_hbm,
    gain_mlp_hbm,
    expand_hbm,
    shrink_hbm,
    pooled_ref,
    hidden_sum_ref,
    counts_ref,
    qkv_ref,
    probs_ref,
    mixed_ref,
    middle_ref,
    slope_ref,
    chars_ref,
    languages_ref,
    table_ref,
    gain_attn_ref,
    project_ref,
    output_ref,
    gain_mlp_ref,
    expand_ref,
    shrink_ref,
    normed_ref,
    sems,
):
    section, _ = position()
    fetches = fetch_all(
        (
            languages_hbm,
            counts_hbm,
            table_hbm,
            gain_attn_hbm,
            chars_hbm.at[section],
            project_hbm,
            output_hbm,
            gain_mlp_hbm,
            expand_hbm,
            shrink_hbm,
        ),
        (
            languages_ref,
            counts_ref,
            table_ref,
            gain_attn_ref,
            chars_ref,
            project_ref,
            output_ref,
            gain_mlp_ref,
            expand_ref,
            shrink_ref,
        ),
        sems,
    )
    for fetch in fetches[:2]:
        fetch.wait()
    counts = counts_ref[section]
    rows = chars_ref.shape[0]
    words = counts.shape[-1]
    row_counts = counts_by_row(counts, rows, slots)
    for fetch in fetches[2:5]:
        fetch.wait()
    language = pick(languages_ref[...], section)
    parts = [slice(at, at + PART) for at in range(0, rows, PART)]
    for number, part in enumerate(parts):
        x = char_rows(chars_ref[part], table_ref, language)
        middle_ref[part] = x
        normal, _ = unit(x)
        normed = (normal * gain_attn_ref[...]).astype(bf16)
        if number == 0:
            fetches[5].wait()
        qkv_ref[part] = dot(normed, project_ref[...]).astype(bf16)
    blocks = range(rows // BLOCK)

    def load(block, which):
        return qkv_ref[block * BLOCK : (block + 1) * BLOCK, which * SLAB : (which + 1) * SLAB]

    by_head = jnp.concatenate(
        [row_counts[:, block * BLOCK : (block + 1) * BLOCK] for block in blocks for _ in range(HEADS)],
        axis=1,
    )
    key_mask = rows_of((slots, rows * HEADS)).astype(f32) < by_head
    probs, mixed = attend(load, blocks, key_mask, slots)
    probs_ref[...] = probs
    for block in blocks:
        mixed_ref[:, block * BLOCK : (block + 1) * BLOCK] = mixed[block]
    fetches[6].wait()
    fetches[7].wait()
    for part in parts:
        middle = middle_ref[part] + dot(mixed_ref[:, part].T, output_ref[...])
        middle_ref[part] = middle
        normal, _ = unit(middle)
        normed_ref[part] = (normal * gain_mlp_ref[...]).astype(bf16)
    word_shape = (words, rows)
    lane = lanes(word_shape)
    member = (lane // slots == rows_of(word_shape)) & ((lane % slots).astype(f32) < row_counts)
    member = jnp.where(member, 1.0, 0.0).astype(bf16)
    fetches[8].wait()
    parts = [slice(at, at + 256) for at in range(0, expand_ref.shape[1], 256)]
    normed = normed_ref[...]
    before = dot(normed, expand_ref[:, parts[0]])
    for number, part in enumerate(parts):
        value, slope = gelu_parts(before)
        if number + 1 < len(parts):
            before = dot(normed, expand_ref[:, parts[number + 1]])
        slope_ref[:, part] = slope
        hidden_sum_ref[:, part] = dot(member, value).astype(bf16)
    high = middle_ref[...].astype(bf16)
    fetches[9].wait()
    total = dot(member, high) + dot(hidden_sum_ref[...], shrink_ref[...])
    pooled_ref[...] = (total / counts_column(counts)).astype(bf16)


def char_forward(languages, chars, counts, table, weights, slots):
    rows, width = chars.shape[1:]
    words = rows // slots
    hidden = weights[4].shape[1]
    vmem = pl.BlockSpec(memory_space=pltpu.VMEM)
    hbm = pl.BlockSpec(memory_space=pltpu.HBM)
    fetched = (languages, counts, table) + tuple(weights)
    return pl.pallas_call(
        functools.partial(char_forward_kernel, slots),
        in_specs=[hbm] * 10,
        out_specs=[vmem] * 8,
        out_shape=[
            jax.ShapeDtypeStruct((words, width), bf16),
            jax.ShapeDtypeStruct((words, hidden), bf16),
            jax.ShapeDtypeStruct(counts.shape, counts.dtype),
            jax.ShapeDtypeStruct((rows, 3 * width), bf16),
            jax.ShapeDtypeStruct((slots, rows * HEADS), f32),
            jax.ShapeDtypeStruct((width, rows), bf16),
            jax.ShapeDtypeStruct((rows, width), f32),
            jax.ShapeDtypeStruct((rows, hidden), bf16),
        ],
        scratch_shapes=[pltpu.VMEM(chars.shape[1:], bf16)]
        + [pltpu.VMEM(array.shape, array.dtype) for array in fetched if array is not counts]
        + [pltpu.VMEM(chars.shape[1:], bf16), pltpu.SemaphoreType.DMA((10,))],
        compiler_params=pltpu.CompilerParams(vmem_limit_bytes=16 * MIB),
        cost_estimate=pl.CostEstimate(
            flops=64 * rows * width * width, bytes_accessed=8 * MIB, transcendentals=0
        ),
        name="char_forward",
    )(*[in_hbm(array) for array in (chars,) + fetched])


CHAR_FIRST_SLOT = 144
CHAR_SECTION_SLOT = 80
CHAR_CORE_SLOT = 112
CHAR_LAST_SLOT = 48


def char_shard(slot, me):
    return me ^ ((slot >> 3) | (((slot >> 1) & 3) << 1) | ((slot & 1) << 3))


def put_shards(gradient, slots, shard_of, at):
    width = SLAB
    columns = gradient.shape[1] // width
    size = gradient.shape[0] // len(slots)
    for number, slot in enumerate(slots):
        first = pl.multiple_of(shard_of(number) * size, size)
        for column in range(columns):
            start = at + column * size
            slot[start : start + size] = gradient[
                pl.ds(first, size), column * width : (column + 1) * width
            ].astype(bf16)
    return at + size * columns


def slot_refs(*refs):
    return [ref.at[place] for ref in refs for place in range(ref.shape[0])]


def char_mlp_back_kernel(
    slots,
    shards,
    counts_ref,
    gain_mlp_ref,
    expand_ref,
    shrink_ref,
    dpooled_ref,
    hidden_sum_ref,
    other_sum_ref,
    mixed_ref,
    middle_ref,
    slope_ref,
    dmiddle_ref,
    gain_ref,
    keep_ref,
    send_ref,
    counts_wide,
    spread,
    dhidden_words,
    dz,
    dbefore,
    expand_grad,
    shrink_grad,
    output_grad,
):
    section, me = position()
    counts = counts_ref[section]
    rows, width = middle_ref.shape
    words = counts.shape[-1]
    column = counts_column(counts)
    counts_wide[...] = jnp.broadcast_to(column, counts_wide.shape)
    spread_value = dpooled_ref[:words].astype(f32) / column
    spread[...] = spread_value
    spread_high = spread_value.astype(bf16)
    dhidden_words[...] = dot_nt(spread_high, shrink_ref[...]).astype(bf16).astype(f32)
    dz[:words] = spread_high
    other = dpooled_ref[words:].astype(f32) / counts_column(counts_ref[1 - section])
    dz[words:] = other.astype(bf16)
    slot = rows_of((slots, 128)).astype(f32)
    for word in range(words):
        at_word = slice(word * slots, (word + 1) * slots)
        present = slot < counts_wide[word : word + 1, :]
        for at in range(0, expand_ref.shape[1], 128):
            part = slice(at, at + 128)
            piece = jnp.where(present, dhidden_words[word : word + 1, part], 0.0).astype(bf16)
            dbefore[at_word, part] = piece * slope_ref[at_word, part]
        for at in range(0, width, 128):
            part = slice(at, at + 128)
            dmiddle_ref[at_word, part] = jnp.where(present, spread[word : word + 1, part], 0.0)
    normal, scale = unit(middle_ref[...])
    normed_t = (normal * gain_mlp_ref[...]).astype(bf16).T
    hidden_sums = jnp.concatenate([hidden_sum_ref[...], other_sum_ref[...]], axis=0)
    hidden_sums_t = hidden_sums.T

    dnormed = dot_nt(dbefore[...], expand_ref[...])
    expand_grad[...] = dot(normed_t, dbefore[...])
    half = width // 2
    own_half = dz[:, pl.ds(pl.multiple_of(section * half, half), half)]
    shrink_grad[...] = dot(hidden_sums_t, own_half)
    dmiddle = dmiddle_ref[...] + unit_back(dnormed, gain_mlp_ref[...], normal, scale)
    dmiddle_ref[...] = dmiddle
    output_grad[...] = dot(mixed_ref[...], dmiddle.astype(bf16))
    gain_ref[...] = jnp.broadcast_to(
        jnp.sum(dnormed * normal, axis=0, keepdims=True), gain_ref.shape
    )
    targets = slot_refs(keep_ref, send_ref)
    at = 0
    for gradient in (expand_grad, output_grad):
        at = put_shards(gradient, targets, lambda slot: char_shard(slot, me), at)
    size = shrink_grad.shape[0] // shards
    for number, target in enumerate(targets):
        first = pl.multiple_of(char_shard(number, me) * size, size)
        piece = shrink_grad[pl.ds(first, size), :].astype(bf16)
        target[at:, :half] = piece[: size // 2]
        target[at:, half:] = piece[size // 2 :]


def char_mlp_back(counts, weights, dpooled, stored, other_sum, slots, shards):
    _, _, output, gain_mlp, expand_w, shrink = weights
    hidden_sum, _, _, mixed, middle, slope = stored
    rows, width = middle.shape
    words = rows // slots
    hidden = expand_w.shape[1]
    half = (shards // 2, CHAR_CORE_SLOT, width)
    vmem = pl.BlockSpec(memory_space=pltpu.VMEM)
    return pl.pallas_call(
        functools.partial(char_mlp_back_kernel, slots, shards),
        in_specs=[vmem] * 10,
        out_specs=[vmem] * 4,
        out_shape=[
            jax.ShapeDtypeStruct((rows, width), f32),
            jax.ShapeDtypeStruct((8, width), f32),
            jax.ShapeDtypeStruct(half, bf16),
            jax.ShapeDtypeStruct(half, bf16),
        ],
        scratch_shapes=[
            pltpu.VMEM((words, 128), f32),
            pltpu.VMEM((words, width), f32),
            pltpu.VMEM((words, hidden), f32),
            pltpu.VMEM((2 * words, width), bf16),
            pltpu.VMEM((rows, hidden), bf16),
            pltpu.VMEM(expand_w.shape, f32),
            pltpu.VMEM((hidden, width // 2), f32),
            pltpu.VMEM(output.shape, f32),
        ],
        compiler_params=pltpu.CompilerParams(vmem_limit_bytes=16 * MIB),
        cost_estimate=pl.CostEstimate(
            flops=64 * rows * width * width, bytes_accessed=8 * MIB, transcendentals=0
        ),
        name="char_mlp_back",
    )(
        counts,
        gain_mlp,
        expand_w,
        shrink,
        dpooled,
        hidden_sum,
        other_sum,
        mixed,
        middle,
        slope,
    )


def char_attn_back_kernel(
    slots,
    shards,
    _,
    chars_hbm,
    languages_hbm,
    table_ref,
    gain_attn_ref,
    project_ref,
    output_ref,
    dmiddle_ref,
    gain_mlp_grad_ref,
    word_gains_ref,
    qkv_ref,
    probs_ref,
    grad_ref,
    keep_ref,
    send_ref,
    extra_ref,
    chars_ref,
    languages_ref,
    dmixed,
    dqkv,
    project_grad,
    sems,
):
    section, me = position()
    fetches = fetch_all(
        (chars_hbm.at[section], languages_hbm), (chars_ref, languages_ref), sems
    )
    rows, width = dmiddle_ref.shape
    dmixed[...] = dot_nt(dmiddle_ref[...].astype(bf16), output_ref[...]).astype(bf16)

    def load(block, which):
        return qkv_ref[block * BLOCK : (block + 1) * BLOCK, which * SLAB : (which + 1) * SLAB]

    def load_dmixed(block):
        return dmixed[block * BLOCK : (block + 1) * BLOCK]

    def store(block, which, value):
        dqkv[block * BLOCK : (block + 1) * BLOCK, which * SLAB : (which + 1) * SLAB] = value

    attend_back(load, load_dmixed, range(rows // BLOCK), probs_ref[...], store, slots)
    for fetch in fetches:
        fetch.wait()
    language = pick(languages_ref[...], section)
    normal, scale = unit(char_rows(chars_ref[...], table_ref, language))
    normed_t = (normal * gain_attn_ref[...]).astype(bf16).T
    dnormed = dot_nt(dqkv[...], project_ref[...])
    project_grad[...] = dot(normed_t, dqkv[...])
    gain_attn_grad = jnp.sum(dnormed * normal, axis=0, keepdims=True)
    dx = dmiddle_ref[...] + unit_back(dnormed, gain_attn_ref[...], normal, scale)
    grad_ref[...] = dx
    row_sum = jnp.sum(dx, axis=0, keepdims=True)
    targets = [
        ref.at[pl.ds(place * CHAR_LAST_SLOT, CHAR_LAST_SLOT)]
        for ref in (keep_ref, send_ref)
        for place in range(shards // 2)
    ]
    put_shards(project_grad, targets, lambda slot: char_shard(slot, me), 0)
    extra = jnp.concatenate(
        [
            gain_attn_grad,
            gain_mlp_grad_ref[:1],
            word_gains_ref[:6],
            jnp.where(rows_of((8, 1)) == language, row_sum, 0.0),
        ],
        axis=0,
    ).astype(bf16)
    extra_ref[...] = extra


def char_attn_back(
    languages,
    chars,
    table,
    weights,
    dmiddle,
    gain_mlp_grad,
    word_gains,
    stored,
    slots,
    shards,
    after,
):
    gain_attn, project, output, _, _, _ = weights
    _, qkv, probs, _, _, _ = stored
    rows, width = dmiddle.shape
    half = (shards // 2 * CHAR_LAST_SLOT, width)
    vmem = pl.BlockSpec(memory_space=pltpu.VMEM)
    hbm = pl.BlockSpec(memory_space=pltpu.HBM)
    return pl.pallas_call(
        functools.partial(char_attn_back_kernel, slots, shards),
        in_specs=[pl.BlockSpec(memory_space=pl.ANY), hbm, hbm] + [vmem] * 9,
        out_specs=[vmem] * 4,
        out_shape=[
            jax.ShapeDtypeStruct((rows, width), f32),
            jax.ShapeDtypeStruct(half, bf16),
            jax.ShapeDtypeStruct(half, bf16),
            jax.ShapeDtypeStruct((16, width), bf16),
        ],
        scratch_shapes=[
            pltpu.VMEM((rows, width), bf16),
            pltpu.VMEM(languages.shape, languages.dtype),
            pltpu.VMEM((rows, width), bf16),
            pltpu.VMEM((rows, 3 * width), bf16),
            pltpu.VMEM(project.shape, f32),
            pltpu.SemaphoreType.DMA((2,)),
        ],
        compiler_params=pltpu.CompilerParams(vmem_limit_bytes=16 * MIB),
        cost_estimate=pl.CostEstimate(
            flops=0, bytes_accessed=0, transcendentals=0
        ),
        name="char_attn_back",
    )(
        after,
        in_hbm(chars),
        in_hbm(languages),
        table,
        gain_attn,
        project,
        output,
        dmiddle,
        gain_mlp_grad,
        word_gains,
        qkv,
        probs,
    )


LONG = pl.CostEstimate(flops=20_000_000_000, bytes_accessed=8 * MIB, transcendentals=0)

WORD_SLOT = 400

SHORT_FLOPS = 400_000_000


def word_kernel(
    length,
    shards,
    own_ref,
    both_ref,
    section_ref,
    far_ref,
    cot_ref,
    cot_far_ref,
    input_ref,
    gain_attn_ref,
    project_ref,
    output_ref,
    gain_mlp_ref,
    expand_ref,
    shrink_ref,
    result_hbm,
    dpooled_ref,
    gains_ref,
    keep_ref,
    send_ref,
    pooled,
    pooled_t,
    dz,
    start,
    normed_t,
    qkv,
    kept,
    mixed_t,
    middle,
    normed_mlp_t,
    hidden,
    dbefore,
    dmixed,
    dqkv,
    dy,
    dstart,
    result,
    input_grad,
    project_grad,
    output_grad,
    expand_grad,
    shrink_grad,
    sem,
):
    total = pooled.shape[0]
    width = output_ref.shape[0]
    section, me = position()
    slabs = width // SLAB
    for place, ref in enumerate((own_ref, section_ref, far_ref, both_ref)):
        pooled[place * length : (place + 1) * length] = ref[...]
    for place, (ref, other) in enumerate(
        ((cot_ref, section), (cot_ref, 1 - section), (cot_far_ref, section), (cot_far_ref, 1 - section))
    ):
        dz[place * length : (place + 1) * length] = ref[other]

    x = dot(pooled[...], input_ref[...])
    start[...] = x
    normal, _ = unit(x)
    low = (normal * gain_attn_ref[...]).astype(bf16)
    normed_t[...] = low.T
    qkv[...] = dot(low, project_ref[...]).astype(bf16)
    tiles = [(block, slab) for block in range(total // BLOCK) for slab in range(slabs)]

    def load(tile, which):
        block, slab = tile
        at = which * width + slab * SLAB
        return qkv[block * BLOCK : (block + 1) * BLOCK, at : at + SLAB]

    mask_shape = (length, len(tiles) * HEADS * BLOCK)
    causal = rows_of(mask_shape) <= lanes(mask_shape) % length
    probs, mixed = attend(load, tiles, causal, length)
    kept[...] = probs
    for (block, slab), piece in zip(tiles, mixed):
        mixed_t[slab * SLAB : (slab + 1) * SLAB, block * BLOCK : (block + 1) * BLOCK] = piece
    x = x + dot(mixed_t[...].T, output_ref[...])
    middle[...] = x
    normal, _ = unit(x)
    low = (normal * gain_mlp_ref[...]).astype(bf16)
    normed_mlp_t[...] = low.T
    dz_all = dz[...]
    for at in range(0, expand_ref.shape[1], 256):
        part = slice(at, at + 256)
        value, bend = gelu_parts(dot(low, expand_ref[:, part]))
        hidden[:, part] = value
        dhidden = dot_nt(dz_all, shrink_ref[part, :]).astype(bf16)
        dbefore[:, part] = dhidden * bend

    def shard_of(slot):
        return (me & 7) ^ ((slot >> 2) | ((slot & 3) << 1))

    def own_rows(flipped):
        many = flipped.shape[0] // 2
        return flipped[pl.ds(pl.multiple_of((me >> 3) * many, many), many), :]

    def half_columns(ref, place):
        many = ref.shape[1] // 2
        return ref[:, pl.ds(pl.multiple_of(place * many, many), many)]

    def own_columns(ref):
        return half_columns(ref, section)

    targets = slot_refs(keep_ref, send_ref)
    hidden_t = half_columns(hidden, me >> 3).T
    pooled_t[...] = pooled[...].T
    normal, scale = unit(middle[...])
    dnormed = dot_nt(dbefore[...], expand_ref[...])
    expand_grad[...] = dot(own_rows(normed_mlp_t), own_columns(dbefore))
    shrink_grad[...] = dot(hidden_t, own_columns(dz))
    dmiddle = dz_all.astype(f32) + unit_back(dnormed, gain_mlp_ref[...], normal, scale)
    dy_low = dmiddle.astype(bf16)
    dy[...] = dy_low
    dmixed[...] = dot_nt(dy_low, output_ref[...]).astype(bf16)
    gain_mlp_grad = jnp.sum(dnormed * normal, axis=0, keepdims=True)
    result[...] = middle[:length] + dot(hidden[:length], shrink_ref[...])
    leave = pltpu.make_async_copy(result, result_hbm, sem)
    leave.start()
    output_grad[...] = dot(own_rows(mixed_t), own_columns(dy))

    def load_dmixed(tile):
        block, slab = tile
        return dmixed[block * BLOCK : (block + 1) * BLOCK, slab * SLAB : (slab + 1) * SLAB]

    def store(tile, which, value):
        block, slab = tile
        at = which * width + slab * SLAB
        dqkv[block * BLOCK : (block + 1) * BLOCK, at : at + SLAB] = value

    attend_back(load, load_dmixed, tiles, kept[...], store, length)
    normal, scale = unit(start[...])
    dnormed = dot_nt(dqkv[...], project_ref[...])
    project_grad[...] = dot(own_rows(normed_t), own_columns(dqkv))
    dword = (dmiddle + unit_back(dnormed, gain_attn_ref[...], normal, scale)).astype(bf16)
    dpooled_ref[...] = dot_nt(dword[: 2 * length], input_ref[...]).astype(bf16)
    dstart[...] = dword
    gain_attn_grad = jnp.sum(dnormed * normal, axis=0, keepdims=True)
    input_grad[...] = dot(own_rows(pooled_t), own_columns(dstart))
    at = 0
    for ref in (input_grad, project_grad, output_grad, expand_grad, shrink_grad):
        at = put_shards(ref, targets, shard_of, at)
    gains_ref[...] = 0.25 * jnp.concatenate(
        [gain_attn_grad[:, :SLAB], gain_attn_grad[:, SLAB:]]
        + [gain_mlp_grad[:, :SLAB], gain_mlp_grad[:, SLAB:]]
        + [jnp.zeros((4, SLAB), f32)],
        axis=0,
    )
    leave.wait()


def word_group(pooled, cotangents, word_input, weights, shards):
    gain_attn, project, output, gain_mlp, expand_w, shrink = weights
    length, channels = pooled[0].shape
    width = output.shape[0]
    hidden = expand_w.shape[1]
    total = 4 * length
    half = (4, WORD_SLOT, SLAB)
    vmem = pl.BlockSpec(memory_space=pltpu.VMEM)
    hbm = pl.BlockSpec(memory_space=pltpu.HBM)
    return pl.pallas_call(
        functools.partial(word_kernel, length, shards),
        in_specs=[vmem] * 13,
        out_specs=[hbm, vmem, vmem, vmem, vmem],
        out_shape=[
            jax.ShapeDtypeStruct((length, width), f32),
            jax.ShapeDtypeStruct((2 * length, channels), bf16),
            jax.ShapeDtypeStruct((8, SLAB), f32),
            jax.ShapeDtypeStruct(half, bf16),
            jax.ShapeDtypeStruct(half, bf16),
        ],
        scratch_shapes=[
            pltpu.VMEM((total, channels), bf16),
            pltpu.VMEM((channels, total), bf16),
            pltpu.VMEM((total, width), bf16),
            pltpu.VMEM((total, width), f32),
            pltpu.VMEM((width, total), bf16),
            pltpu.VMEM((total, 3 * width), bf16),
            pltpu.VMEM((length, total * (width // HEAD)), f32),
            pltpu.VMEM((width, total), bf16),
            pltpu.VMEM((total, width), f32),
            pltpu.VMEM((width, total), bf16),
            pltpu.VMEM((total, hidden), bf16),
            pltpu.VMEM((total, hidden), bf16),
            pltpu.VMEM((total, width), bf16),
            pltpu.VMEM((total, 3 * width), bf16),
            pltpu.VMEM((total, width), bf16),
            pltpu.VMEM((total, width), bf16),
            pltpu.VMEM((length, width), f32),
            pltpu.VMEM((channels // 2, width // 2), f32),
            pltpu.VMEM((width // 2, 3 * width // 2), f32),
            pltpu.VMEM((width // 2, width // 2), f32),
            pltpu.VMEM((width // 2, hidden // 2), f32),
            pltpu.VMEM((hidden // 2, width // 2), f32),
            pltpu.SemaphoreType.DMA,
        ],
        compiler_params=pltpu.CompilerParams(vmem_limit_bytes=20 * MIB),
        cost_estimate=pl.CostEstimate(
            flops=total * width * width * 25 * 4, bytes_accessed=8 * MIB, transcendentals=0
        ),
        name="word_group",
    )(*pooled, *cotangents, word_input, gain_attn, project, output, gain_mlp, expand_w, shrink)


def summed(*parts):
    return functools.reduce(lambda a, b: a + b, [part.astype(f32) for part in parts])


def added(*parts):
    return summed(*parts).astype(bf16)


def by_section(section, low, high):
    return (jnp.where(section == 0, low, high), jnp.where(section == 0, high, low))


def word_sum_kernel(keep, arrived, *outs):
    for place, ref in enumerate(outs):
        ref[...] = added(keep[place], arrived[place])


def word_sum(keep, arrived):
    return pl.pallas_call(
        word_sum_kernel,
        out_shape=[jax.ShapeDtypeStruct((WORD_SLOT, SLAB), bf16)] * 4,
        compiler_params=pltpu.CompilerParams(vmem_limit_bytes=12 * MIB),
        name="word_sum",
    )(keep, arrived)


def first_sum_kernel(keep, arrived, stay_ref, go_ref, shrink_ref):
    section, _ = position()
    half = SLAB // 2
    for place in range(keep.shape[0]):
        total = added(keep[place], arrived[place])
        rows = total[:CHAR_SECTION_SLOT]
        stay_ref[place], go_ref[place] = by_section(section, rows[:, :half], rows[:, half:])
        rows = total[CHAR_SECTION_SLOT:]
        shrink_ref[place] = jnp.concatenate([rows[:, :half], rows[:, half:]], axis=0)


def first_sum(keep, arrived):
    half = jax.ShapeDtypeStruct((keep.shape[0], CHAR_SECTION_SLOT, SLAB // 2), bf16)
    shrink = jax.ShapeDtypeStruct(
        (keep.shape[0], CHAR_FIRST_SLOT - CHAR_SECTION_SLOT, SLAB // 2), bf16
    )
    return pl.pallas_call(
        first_sum_kernel,
        out_shape=[half, half, shrink],
        compiler_params=pltpu.CompilerParams(vmem_limit_bytes=12 * MIB),
        name="first_sum",
    )(keep, arrived)


def section_sum_kernel(stay, arrived, out):
    out[...] = added(stay[...], arrived[...])


def section_sum(stay, arrived):
    return pl.pallas_call(
        section_sum_kernel,
        out_shape=jax.ShapeDtypeStruct(stay.shape, bf16),
        compiler_params=pltpu.CompilerParams(vmem_limit_bytes=12 * MIB),
        cost_estimate=pl.CostEstimate(flops=SHORT_FLOPS, bytes_accessed=0, transcendentals=0),
        name="section_sum",
    )(stay, arrived)


def second_sum_kernel(first, shrink, keep, core_arrived, own_extra, core_extra, *outs):
    _, me = position()
    half = SLAB // 2
    extra = summed(own_extra[...], core_extra[...])
    for place, out in enumerate(outs):
        at = CHAR_FIRST_SLOT
        for far in range(2):
            entry = 2 * place + far
            columns = slice(far * half, (far + 1) * half)
            total = first[entry]
            middle = CHAR_SECTION_SLOT - 16
            out[:middle, columns] = total[:middle]
            out[middle : CHAR_FIRST_SLOT - 16, columns] = shrink[entry]
            out[CHAR_FIRST_SLOT - 16 : CHAR_FIRST_SLOT, columns] = total[middle:]
            rows = slice(entry * CHAR_LAST_SLOT, (entry + 1) * CHAR_LAST_SLOT)
            out[at : at + CHAR_LAST_SLOT] = added(keep[rows], core_arrived[rows])
            at += CHAR_LAST_SLOT
            shard = char_shard(entry, me)
            turned = pltpu.roll(extra, lax.rem(SLAB - shard * 16, SLAB), 1)
            word = pltpu.roll(extra, lax.rem(2 * SLAB - shard * 32, SLAB), 1)
            upper = shard * 32 >= SLAB
            block = jnp.concatenate(
                [
                    turned[:2],
                    jnp.where(upper, word[3:4], word[2:3]),
                    jnp.where(upper, word[5:6], word[4:5]),
                    turned[4:],
                ],
                axis=0,
            )
            out[-16:, columns] = block[:, :half].astype(bf16)


def total_kernel(*refs):
    *pieces, chars_ref, out, chars_hbm, sem = refs
    leave = pltpu.make_async_copy(chars_ref, chars_hbm, sem)
    leave.start()
    out[...] = added(*[ref[...] for ref in pieces])
    leave.wait()


def total_of(*pieces, chars_grad):
    vmem = pl.BlockSpec(memory_space=pltpu.VMEM)
    return pl.pallas_call(
        total_kernel,
        in_specs=[vmem] * (len(pieces) + 1),
        out_specs=[vmem, pl.BlockSpec(memory_space=pltpu.HBM)],
        out_shape=[
            jax.ShapeDtypeStruct(pieces[0].shape, bf16),
            jax.ShapeDtypeStruct(chars_grad.shape, f32),
        ],
        scratch_shapes=[pltpu.SemaphoreType.DMA],
        compiler_params=pltpu.CompilerParams(vmem_limit_bytes=12 * MIB),
        cost_estimate=LONG,
        name="total",
    )(*pieces, chars_grad)


def second_sum(first, last):
    rows = CHAR_FIRST_SLOT + 2 * CHAR_LAST_SLOT + 16
    return pl.pallas_call(
        second_sum_kernel,
        out_shape=[jax.ShapeDtypeStruct((rows, SLAB), bf16)] * 4,
        compiler_params=pltpu.CompilerParams(vmem_limit_bytes=12 * MIB),
        name="second_sum",
    )(*first, *last)


FOLD = 80


def plane_sum_kernel(*refs):
    half = SLAB // 2
    pieces = refs[:4]
    for far, out in enumerate(refs[5:]):
        columns = slice(far * half, (far + 1) * half)
        total = added(*[ref[:CHAR_FIRST_SLOT, columns] for ref in pieces])
        out[:FOLD, :half] = total[:FOLD]
        out[:FOLD, half:] = total[CHAR_FIRST_SLOT - FOLD :]
        out[:16, half:] = added(*[ref[-16:, columns] for ref in pieces])
        first = CHAR_FIRST_SLOT + far * CHAR_LAST_SLOT
        out[FOLD:] = added(*[ref[first : first + CHAR_LAST_SLOT] for ref in pieces])


def plane_sum(pieces, after):
    return pl.pallas_call(
        plane_sum_kernel,
        in_specs=[pl.BlockSpec(memory_space=pltpu.VMEM)] * 4 + [pl.BlockSpec(memory_space=pl.ANY)],
        out_shape=[jax.ShapeDtypeStruct((FOLD + CHAR_LAST_SLOT, SLAB), bf16)] * 2,
        compiler_params=pltpu.CompilerParams(vmem_limit_bytes=12 * MIB),
        cost_estimate=LONG,
        name="plane_sum",
    )(*pieces, after)


def char_last_kernel(near_ref, both_ref, far_ref, section_ref, _, *outs):
    section, _ = position()
    half = SLAB // 2
    mine = summed(near_ref[:FOLD], far_ref[:FOLD])
    theirs = summed(section_ref[:FOLD], both_ref[:FOLD])

    def unfold(total):
        return jnp.concatenate(
            [total[:, :half], total[2 * FOLD - CHAR_FIRST_SLOT :, half:]], axis=0
        )

    first = jnp.concatenate(by_section(section, unfold(mine), unfold(theirs)), axis=1)
    extra = mine[:16, half:] + theirs[:16, half:]
    last = summed(near_ref[FOLD:], section_ref[FOLD:], far_ref[FOLD:], both_ref[FOLD:])
    (
        table_ref,
        gain_attn_ref,
        project_ref,
        output_ref,
        gain_mlp_ref,
        expand_ref,
        shrink_ref,
        word_gain_attn_ref,
        word_gain_mlp_ref,
    ) = outs
    for total, refs in ((first, (expand_ref, shrink_ref, output_ref)), (last, (project_ref,))):
        at = 0
        for ref in refs:
            size = ref.shape[0]
            for column in range(ref.shape[1] // SLAB):
                ref[:, column * SLAB : (column + 1) * SLAB] = total[at : at + size]
                at += size
    size = gain_attn_ref.shape[1]
    gain_attn_ref[...] = extra[0:1, :size]
    gain_mlp_ref[...] = extra[1:2, :size]
    table_ref[...] = extra[8:16, :size]
    size = word_gain_attn_ref.shape[1]
    word_gain_attn_ref[...] = extra[2:3, :size]
    word_gain_mlp_ref[...] = extra[3:4, :size]


def char_last(near, arrived, shapes, after):
    return pl.pallas_call(
        char_last_kernel,
        in_specs=[pl.BlockSpec(memory_space=pltpu.VMEM)] * 4 + [pl.BlockSpec(memory_space=pltpu.HBM)],
        out_shape=[jax.ShapeDtypeStruct(shape, f32) for shape in shapes],
        compiler_params=pltpu.CompilerParams(vmem_limit_bytes=12 * MIB),
        name="char_last",
    )(near, *arrived, in_hbm(after))


def word_last_kernel(own_ref, other_ref, *outs):
    section, _ = position()
    own = own_ref[...].astype(f32)
    halves = by_section(section, own, other_ref[...].astype(f32))
    at = 0
    for ref in outs:
        size = ref.shape[0]
        columns = ref.shape[1] // (2 * SLAB)
        for column in range(columns):
            for half in range(2):
                first = (half * columns + column) * SLAB
                ref[:, first : first + SLAB] = halves[half][at : at + size]
            at += size


def word_last(own, other, shapes):
    return pl.pallas_call(
        word_last_kernel,
        out_shape=[jax.ShapeDtypeStruct(shape, f32) for shape in shapes],
        compiler_params=pltpu.CompilerParams(vmem_limit_bytes=12 * MIB),
        name="word_last",
    )(own, other)


def exchange(value, section_bit, dp_bits):
    shards = lax.axis_size("dp")
    pairs = [
        (s * shards + d, (s ^ section_bit) * shards + (d ^ dp_bits))
        for s in range(lax.axis_size("section"))
        for d in range(shards)
    ]
    return lax.ppermute(value, ("section", "dp"), pairs)


CORE, SIDE, NEAR, FAR = (1, 2, 4, 8)


def plane_exchange(pieces):
    return tuple(
        exchange(piece, 0, bits) for piece, bits in zip(pieces[:0:-1], (SIDE | NEAR, NEAR, SIDE))
    ) + (pieces[0],)


def local_grouped(
    chars, counts, languages, language_table, char_weights, word_input, word_weights, cotangent
):
    shards = lax.axis_size("dp")
    micros, _, words, slots, width = chars.shape
    rows = words * slots
    cot = cotangent[:, 0]
    cot_far = exchange(cot, 0, FAR)
    char_weights = tuple(w[None] if w.ndim == 1 else w for w in char_weights)
    word_weights = tuple(w[None] if w.ndim == 1 else w for w in word_weights)
    chars = chars.reshape(micros, rows, width)
    counts = counts.reshape(micros, 1, words)
    languages = languages.reshape(1, micros)
    pooled, hidden_sum, own_counts, *stored = char_forward(
        languages, chars, counts, language_table, char_weights, slots
    )
    stored = (hidden_sum, *stored)
    other_sum = exchange(hidden_sum, 1, 0)
    others = (exchange(pooled, 1, FAR), exchange(pooled, 1, 0), exchange(pooled, 0, FAR))
    result, dpooled, word_gains, keep, send = word_group(
        (pooled,) + others, (cot, cot_far), word_input, word_weights, shards
    )
    word = plane_exchange(word_sum(keep, exchange(send, 0, CORE)))
    dmiddle, gain_mlp_grad, keep, send = char_mlp_back(
        own_counts, char_weights, dpooled, stored, other_sum, slots, shards
    )
    stay, go, shrink = first_sum(keep, exchange(send, 0, CORE))
    first = (section_sum(stay, exchange(go, 1, 0)), shrink)
    chars_grad, keep, send, extra = char_attn_back(
        languages,
        chars,
        language_table,
        char_weights,
        dmiddle,
        gain_mlp_grad,
        word_gains,
        stored,
        slots,
        shards,
        stay,
    )
    last = (keep, exchange(send, 0, CORE), extra, exchange(extra, 0, CORE))
    char = plane_exchange(second_sum(first, last))
    word, chars_grad = total_of(*word, chars_grad=chars_grad)
    near, far = plane_sum(char, word)
    arrived = (exchange(far, 1, FAR), exchange(far, 0, FAR), exchange(near, 1, 0))

    def shard_shapes(weights):
        for weight in weights:
            if weight.shape[0] == 1:
                yield (1, weight.shape[1] // shards)
            else:
                yield (weight.shape[0] // shards, weight.shape[1])

    table_shape = (language_table.shape[0], language_table.shape[1] // shards)
    input_shape, attn_shape, project_shape, output_shape, mlp_shape, expand_shape, shrink_shape = (
        shard_shapes((word_input,) + word_weights)
    )
    word_shapes = [input_shape, project_shape, output_shape, expand_shape, shrink_shape]
    word_totals = word_last(word, exchange(word, 1, 0), word_shapes)
    char_shapes = [table_shape, *shard_shapes(char_weights), attn_shape, mlp_shape]
    *char_totals, attn, mlp = char_last(near, arrived, char_shapes, word_totals[0])
    totals = [*char_totals, word_totals[0], attn, *word_totals[1:3], mlp, *word_totals[3:]]
    totals = [total[0] if total.shape[0] == 1 else total for total in totals]
    return (result[None, None], chars_grad.reshape((1, 1, words, slots, width))) + tuple(totals)


def norm_forward(inputs, gain):
    return inputs * lax.rsqrt(jnp.mean(inputs * inputs, axis=-1, keepdims=True) + eps) * gain


def attend_forward(normed, project, head_count, key_mask):
    row_count, length, channels = normed.shape
    head_size = channels // head_count
    qkv = jnp.einsum("blc,cf->blf", normed, project, preferred_element_type=jnp.float32).astype(
        jnp.bfloat16
    )
    pieces = qkv.reshape(row_count, length, 3, head_count, head_size)
    scores = jnp.einsum(
        "bqhd,bkhd->bhqk", pieces[:, :, 0], pieces[:, :, 1], preferred_element_type=jnp.float32
    ) * head_size ** (-0.5)
    scores = jnp.where(key_mask, scores, -1e30)
    row_max = jnp.max(scores, axis=-1, keepdims=True)
    weights_exp = jnp.exp(scores - row_max)
    row_total = jnp.sum(weights_exp, axis=-1, keepdims=True)
    attn_probs = (weights_exp / row_total).astype(jnp.bfloat16)
    mixed_heads = jnp.einsum(
        "bhqk,bkhd->bqhd", attn_probs, pieces[:, :, 2], preferred_element_type=jnp.float32
    )
    mixed_heads = mixed_heads.reshape(row_count, length, channels).astype(jnp.bfloat16)
    return (qkv, row_max + jnp.log(row_total), mixed_heads)


def attend_backward(
    normed, project, output, qkv, logsum, mixed_heads, dmiddle_low, head_count, key_mask
):
    row_count, length, channels = normed.shape
    head_size = channels // head_count
    scaling = head_size ** (-0.5)
    output_grad = jnp.einsum(
        "blc,bld->cd", mixed_heads, dmiddle_low, preferred_element_type=jnp.float32
    )
    dmixed = jnp.einsum(
        "bld,cd->blc", dmiddle_low, output, preferred_element_type=jnp.float32
    ).astype(jnp.bfloat16)
    dmixed = dmixed.reshape(row_count, length, head_count, head_size)
    pieces = qkv.reshape(row_count, length, 3, head_count, head_size)
    scores = (
        jnp.einsum(
            "bqhd,bkhd->bhqk", pieces[:, :, 0], pieces[:, :, 1], preferred_element_type=jnp.float32
        )
        * scaling
    )
    scores = jnp.where(key_mask, scores, -1e30)
    attn_probs = jnp.exp(scores - logsum)
    dprobs = jnp.einsum(
        "bqhd,bkhd->bhqk", dmixed, pieces[:, :, 2], preferred_element_type=jnp.float32
    )
    row_delta = jnp.sum(attn_probs * dprobs, axis=-1, keepdims=True)
    dscores = (attn_probs * (dprobs - row_delta)).astype(jnp.bfloat16)
    dquery = (
        jnp.einsum("bhqk,bkhd->bqhd", dscores, pieces[:, :, 1], preferred_element_type=jnp.float32)
        * scaling
    )
    dkeys = (
        jnp.einsum("bhqk,bqhd->bkhd", dscores, pieces[:, :, 0], preferred_element_type=jnp.float32)
        * scaling
    )
    dvalues = jnp.einsum(
        "bhqk,bqhd->bkhd",
        attn_probs.astype(jnp.bfloat16),
        dmixed,
        preferred_element_type=jnp.float32,
    )
    dqkv = (
        jnp.stack([dquery, dkeys, dvalues], axis=2)
        .reshape(row_count, length, 3 * channels)
        .astype(jnp.bfloat16)
    )
    project_grad = jnp.einsum("blc,blf->cf", normed, dqkv, preferred_element_type=jnp.float32)
    dnormed = jnp.einsum("blf,cf->blc", dqkv, project, preferred_element_type=jnp.float32)
    return (dnormed, project_grad, output_grad)


def block_forward(inputs, weights, head_count, key_mask):
    gain_attn, project, output, gain_mlp, expand, shrink = weights
    normed = norm_forward(inputs, gain_attn).astype(jnp.bfloat16)
    qkv, logsum, mixed_heads = attend_forward(normed, project, head_count, key_mask)
    middle = inputs + jnp.einsum(
        "blc,cd->bld", mixed_heads, output, preferred_element_type=jnp.float32
    )
    normed_mlp = norm_forward(middle, gain_mlp).astype(jnp.bfloat16)
    before = jnp.einsum("blc,cf->blf", normed_mlp, expand, preferred_element_type=jnp.float32)
    hidden = jax.nn.gelu(before).astype(jnp.bfloat16)
    result = middle + jnp.einsum("blf,fc->blc", hidden, shrink, preferred_element_type=jnp.float32)
    return (result, (inputs, normed, qkv, logsum, mixed_heads, middle, normed_mlp, before, hidden))


def block_backward(dresult, stored, weights, head_count, key_mask):
    gain_attn, project, output, gain_mlp, expand, shrink = weights
    inputs, normed, qkv, logsum, mixed_heads, middle, normed_mlp, before, hidden = stored
    grad_low = dresult.astype(jnp.bfloat16)
    shrink_grad = jnp.einsum("blf,blc->fc", hidden, grad_low, preferred_element_type=jnp.float32)
    dhidden = jnp.einsum(
        "blc,fc->blf", grad_low, shrink, preferred_element_type=jnp.float32
    ).astype(jnp.bfloat16)
    gelu_pull = jax.vjp(jax.nn.gelu, before)[1]
    dbefore = gelu_pull(dhidden.astype(jnp.float32))[0].astype(jnp.bfloat16)
    expand_grad = jnp.einsum("blc,blf->cf", normed_mlp, dbefore, preferred_element_type=jnp.float32)
    dnormed_mlp = jnp.einsum("blf,cf->blc", dbefore, expand, preferred_element_type=jnp.float32)
    norm_pull = jax.vjp(norm_forward, middle, gain_mlp)[1]
    dmiddle_norm, gain_mlp_grad = norm_pull(dnormed_mlp)
    dmiddle = dresult + dmiddle_norm
    dnormed, project_grad, output_grad = attend_backward(
        normed,
        project,
        output,
        qkv,
        logsum,
        mixed_heads,
        dmiddle.astype(jnp.bfloat16),
        head_count,
        key_mask,
    )
    first_pull = jax.vjp(norm_forward, inputs, gain_attn)[1]
    dinputs_norm, gain_attn_grad = first_pull(dnormed)
    return (
        dmiddle + dinputs_norm,
        (gain_attn_grad, project_grad, output_grad, gain_mlp_grad, expand_grad, shrink_grad),
    )


def char_front(char_text, char_count, language, lang_table, weights):
    present = lax.broadcasted_iota(jnp.int32, char_text.shape[:2], 1) < char_count[:, None]
    onehot = (lax.broadcasted_iota(jnp.int32, (lang_table.shape[0],), 0) == language).astype(
        jnp.bfloat16
    )
    lang_row = jnp.dot(onehot, lang_table, preferred_element_type=jnp.float32)
    inputs = char_text.astype(jnp.float32) + lang_row
    result, stored = block_forward(inputs, weights, CH, present[:, None, None, :])
    summed = jnp.sum(jnp.where(present[:, :, None], result, 0.0), axis=1)
    pooled = (summed / char_count[:, None].astype(jnp.float32)).astype(jnp.bfloat16)
    return (pooled, stored, present, onehot)


def char_back(stored, present, onehot, char_count, dpooled, weights):
    spread = dpooled.astype(jnp.float32) / char_count[:, None].astype(jnp.float32)
    dresult = jnp.where(present[:, :, None], spread[:, None, :], 0.0)
    dinputs, gradients = block_backward(dresult, stored, weights, CH, present[:, None, None, :])
    table_grad = onehot.astype(jnp.float32)[:, None] * jnp.sum(dinputs, axis=(0, 1))[None, :]
    return (dinputs, (table_grad,) + gradients)


def word_full(pooled, cot_rows, word_input, weights):
    length = pooled.shape[0]
    word_start = jnp.dot(pooled, word_input, preferred_element_type=jnp.float32)[None]
    causal = (
        lax.broadcasted_iota(jnp.int32, (length, length), 0)
        >= lax.broadcasted_iota(jnp.int32, (length, length), 1)
    )[None, None]
    result, stored = block_forward(word_start, weights, H, causal)
    dstart, gradients = block_backward(
        cot_rows.astype(jnp.float32)[None], stored, weights, H, causal
    )
    grad_low = dstart[0].astype(jnp.bfloat16)
    input_grad = jnp.einsum("wc,wd->cd", pooled, grad_low, preferred_element_type=jnp.float32)
    dpooled = jnp.einsum(
        "wd,cd->wc", grad_low, word_input, preferred_element_type=jnp.float32
    ).astype(jnp.bfloat16)
    return (result[0], dpooled, (input_grad,) + gradients)


def reduce_rows(gradients):
    shards = lax.axis_size("dp")
    flat = []
    for place, gradient in enumerate(gradients):
        if place == 0:
            gradient = gradient.T
        flat.append(gradient.astype(jnp.bfloat16).reshape(shards, -1))
    packed = jnp.concatenate(flat, axis=1)
    me = lax.axis_index("dp")
    packed = jnp.take(packed, jnp.arange(shards) ^ me, axis=0)
    bit = 1
    while packed.shape[0] > 1:
        pairs = packed.reshape(packed.shape[0] // 2, 2, packed.shape[1])
        arrived = lax.ppermute(pairs[:, 1], "dp", [(i, i ^ bit) for i in range(shards)])
        packed = (pairs[:, 0].astype(jnp.float32) + arrived.astype(jnp.float32)).astype(
            jnp.bfloat16
        )
        bit *= 2
    arrived = lax.ppermute(packed, "section", [(0, 1), (1, 0)])
    total = (packed.astype(jnp.float32) + arrived.astype(jnp.float32))[0]
    outs = []
    at = 0
    for place, gradient in enumerate(gradients):
        size = gradient.size // shards
        piece = total[at : at + size]
        at += size
        if place == 0:
            outs.append(piece.reshape(-1, gradient.shape[0]).T)
        else:
            outs.append(piece.reshape((gradient.shape[0] // shards,) + gradient.shape[1:]))
    return tuple(outs)


def local(
    chars,
    counts,
    languages,
    language_table,
    char_gain_attn,
    char_project,
    char_output,
    char_gain_mlp,
    char_expand,
    char_shrink,
    word_input,
    word_gain_attn,
    word_project,
    word_output,
    word_gain_mlp,
    word_expand,
    word_shrink,
    cotangent,
):
    char_weights = (
        char_gain_attn,
        char_project,
        char_output,
        char_gain_mlp,
        char_expand,
        char_shrink,
    )
    word_weights = (
        word_gain_attn,
        word_project,
        word_output,
        word_gain_mlp,
        word_expand,
        word_shrink,
    )
    if lax.axis_size("dp") == 16:
        return local_grouped(
            chars,
            counts,
            languages,
            language_table,
            char_weights,
            word_input,
            word_weights,
            cotangent,
        )
    section_index = lax.axis_index("section")
    char_text = chars[section_index, 0]
    char_count = counts[section_index, 0]
    language = languages[section_index, 0]
    cot_rows = cotangent[section_index, 0]
    pooled, stored, present, onehot = char_front(
        char_text, char_count, language, language_table, char_weights
    )
    result, dpooled, word_grads = word_full(pooled, cot_rows, word_input, word_weights)
    text_grad, char_grads = char_back(stored, present, onehot, char_count, dpooled, char_weights)
    totals = reduce_rows(char_grads + word_grads)
    return (result[None, None], text_grad[None, None]) + totals


def solution(mesh):
    placed = (
        P(None, "dp", None, None, None),
        P(None, "dp", None),
        P(None, "dp"),
        P(),
        P(),
        P(),
        P(),
        P(),
        P(),
        P(),
        P(),
        P(),
        P(),
        P(),
        P(),
        P(),
        P(),
        P(None, "dp", None, None),
    )
    return jax.shard_map(
        local,
        mesh=mesh,
        in_specs=placed,
        out_specs=(
            P("section", "dp", None, None),
            P("section", "dp", None, None, None),
            P(None, "dp"),
            P("dp"),
            P("dp", None),
            P("dp", None),
            P("dp"),
            P("dp", None),
            P("dp", None),
            P("dp", None),
            P("dp"),
            P("dp", None),
            P("dp", None),
            P("dp"),
            P("dp", None),
            P("dp", None),
        ),
        check_vma=False,
    )
```

```python
import functools

import jax
import jax.numpy as jnp
from jax import lax
from jax.experimental import pallas as pl
from jax.experimental.pallas import tpu as pltpu
from jax.sharding import PartitionSpec as P

CH = 4
H = 8
HEAD = 64
SLAB = 256
HEADS = SLAB // HEAD
BLOCK = 128
PART = 128
MIB = 1024 * 1024

eps = 1e-05

f32 = jnp.float32
bf16 = jnp.bfloat16


def dot(a, b):
    return jnp.dot(a, b, preferred_element_type=f32)


def dot_nt(a, b):
    return lax.dot_general(a, b, (((1,), (1,)), ((), ())), preferred_element_type=f32)


def position():
    return (lax.axis_index("section"), lax.axis_index("dp"))


def lanes(shape):
    return lax.broadcasted_iota(jnp.int32, shape, 1)


def rows_of(shape):
    return lax.broadcasted_iota(jnp.int32, shape, 0)


def stack_heads(a):
    head = lanes((1, SLAB)) // HEAD
    masks = [jnp.where(head == place, 1.0, 0.0).astype(bf16) for place in range(HEADS)]
    return jnp.concatenate([a * mask for mask in masks], axis=0)


def compact(scores, length):
    group = lanes((length, BLOCK)) // length
    total = scores[:length]
    for place in range(1, BLOCK // length):
        total = jnp.where(group == place, scores[place * length : (place + 1) * length], total)
    return total


def compact_heads(scores, length):
    return [
        compact(scores[:, head * BLOCK : (head + 1) * BLOCK], length) for head in range(HEADS)
    ]


def expand(values, length):
    group = lanes((length, BLOCK)) // length
    return jnp.concatenate(
        [jnp.where(group == place, values, 0.0) for place in range(BLOCK // length)], axis=0
    ).astype(bf16)


def expand_heads(values, tile, length):
    first = tile * HEADS * BLOCK
    return [
        expand(values[:, first + head * BLOCK : first + (head + 1) * BLOCK], length)
        for head in range(HEADS)
    ]


def head_rows(a, head):
    return a[head * HEAD : (head + 1) * HEAD]


def attend(load, tiles, key_mask, length):
    scores = []
    for tile in tiles:
        scores += compact_heads(dot_nt(load(tile, 1), stack_heads(load(tile, 0))), length)
    scores = jnp.concatenate(scores, axis=1) * HEAD**-0.5
    scores = jnp.where(key_mask, scores, -1e30)
    weights = jnp.exp(scores - jnp.max(scores, axis=0, keepdims=True))
    probs = weights / jnp.sum(weights, axis=0, keepdims=True)
    mixed = []
    for number, tile in enumerate(tiles):
        values = load(tile, 2).T
        parts = expand_heads(probs, number, length)
        mixed.append(
            jnp.concatenate(
                [dot(head_rows(values, head), parts[head]) for head in range(HEADS)], axis=0
            ).astype(bf16)
        )
    return (probs, mixed)


def attend_back(load, load_dmixed, tiles, probs, store, length, between=None):
    dprobs = []
    for number, tile in enumerate(tiles):
        grads = load_dmixed(tile)
        stacked = stack_heads(grads)
        scores = dot_nt(stack_heads(load(tile, 2)), grads)
        dprobs += [compact(scores[head * BLOCK : (head + 1) * BLOCK], length) for head in range(HEADS)]
        parts = jnp.concatenate(expand_heads(probs, number, length), axis=1)
        store(tile, 2, dot(parts, stacked).astype(bf16))
    dprobs = jnp.concatenate(dprobs, axis=1)
    dscores = probs * (dprobs - jnp.sum(probs * dprobs, axis=0, keepdims=True))
    if between is not None:
        between()
    scaling = HEAD**-0.5
    for number, tile in enumerate(tiles):
        parts = expand_heads(dscores, number, length)
        keys = load(tile, 1).T
        dq = jnp.concatenate(
            [dot(head_rows(keys, head), parts[head]) for head in range(HEADS)], axis=0
        )
        store(tile, 0, (dq * scaling).astype(bf16).T)
        dk = dot(jnp.concatenate(parts, axis=1), stack_heads(load(tile, 0)))
        store(tile, 1, (dk * scaling).astype(bf16))


def unit(x):
    scale = lax.rsqrt(jnp.mean(x * x, axis=-1, keepdims=True) + eps)
    return (x * scale, scale)


def unit_back(dnormed, gain, normal, scale):
    weighted = dnormed * gain
    return scale * (weighted - normal * jnp.mean(normal * weighted, axis=-1, keepdims=True))


def gelu_parts(before):
    c = 0.7978845608028654
    before = before.astype(bf16)
    square = before * before
    half = bf16(0.5) * jnp.tanh(before * (bf16(c) + bf16(c * 0.044715) * square)) + bf16(0.5)
    value = before * half
    slope = half + value * (bf16(1.0) - half) * (bf16(2.0 * c) + bf16(6.0 * c * 0.044715) * square)
    return (value, slope)


def pick(row, place):
    return jnp.sum(jnp.where(lanes(row.shape) == place, row, 0), axis=1, keepdims=True)


def char_rows(chars, table_ref, language):
    table = table_ref[...].astype(f32)
    row = jnp.sum(jnp.where(rows_of(table.shape) == language, table, 0.0), axis=0, keepdims=True)
    return chars.astype(f32) + row


def counts_by_row(counts, rows, slots):
    words = counts.shape[-1]
    counts = jnp.broadcast_to(counts.astype(f32), (8, words)).astype(bf16)
    shape = (words, rows)
    member = lanes(shape) // slots == rows_of(shape)
    return dot(counts, jnp.where(member, 1.0, 0.0).astype(bf16))[:1]


def counts_column(counts):
    words = counts.shape[-1]
    shape = (words, words)
    spread = jnp.broadcast_to(counts.astype(f32), shape)
    return jnp.sum(
        jnp.where(rows_of(shape) == lanes(shape), spread, 0.0), axis=1, keepdims=True
    )


def fetch_all(sources, targets, sems):
    fetches = [
        pltpu.make_async_copy(source, target, sems.at[place])
        for place, (source, target) in enumerate(zip(sources, targets))
    ]
    for fetch in fetches:
        fetch.start()
    return fetches


def in_hbm(array):
    return pltpu.with_memory_space_constraint(array, pltpu.HBM)


def char_forward_kernel(
    slots,
    chars_hbm,
    languages_hbm,
    counts_hbm,
    table_hbm,
    gain_attn_hbm,
    project_hbm,
    output_hbm,
    gain_mlp_hbm,
    expand_hbm,
    shrink_hbm,
    pooled_ref,
    hidden_sum_ref,
    counts_ref,
    qkv_ref,
    probs_ref,
    mixed_ref,
    middle_ref,
    slope_ref,
    chars_ref,
    languages_ref,
    table_ref,
    gain_attn_ref,
    project_ref,
    output_ref,
    gain_mlp_ref,
    expand_ref,
    shrink_ref,
    normed_ref,
    sems,
):
    section, _ = position()
    fetches = fetch_all(
        (
            languages_hbm,
            counts_hbm,
            table_hbm,
            gain_attn_hbm,
            chars_hbm.at[section],
            project_hbm,
            output_hbm,
            gain_mlp_hbm,
            expand_hbm,
            shrink_hbm,
        ),
        (
            languages_ref,
            counts_ref,
            table_ref,
            gain_attn_ref,
            chars_ref,
            project_ref,
            output_ref,
            gain_mlp_ref,
            expand_ref,
            shrink_ref,
        ),
        sems,
    )
    for fetch in fetches[:2]:
        fetch.wait()
    counts = counts_ref[section]
    rows = chars_ref.shape[0]
    words = counts.shape[-1]
    row_counts = counts_by_row(counts, rows, slots)
    for fetch in fetches[2:5]:
        fetch.wait()
    language = pick(languages_ref[...], section)
    parts = [slice(at, at + PART) for at in range(0, rows, PART)]
    for number, part in enumerate(parts):
        x = char_rows(chars_ref[part], table_ref, language)
        middle_ref[part] = x
        normal, _ = unit(x)
        normed = (normal * gain_attn_ref[...]).astype(bf16)
        if number == 0:
            fetches[5].wait()
        qkv_ref[part] = dot(normed, project_ref[...]).astype(bf16)
    blocks = range(rows // BLOCK)

    def load(block, which):
        return qkv_ref[block * BLOCK : (block + 1) * BLOCK, which * SLAB : (which + 1) * SLAB]

    by_head = jnp.concatenate(
        [row_counts[:, block * BLOCK : (block + 1) * BLOCK] for block in blocks for _ in range(HEADS)],
        axis=1,
    )
    key_mask = rows_of((slots, rows * HEADS)).astype(f32) < by_head
    probs, mixed = attend(load, blocks, key_mask, slots)
    probs_ref[...] = probs
    for block in blocks:
        mixed_ref[:, block * BLOCK : (block + 1) * BLOCK] = mixed[block]
    fetches[6].wait()
    fetches[7].wait()
    for part in parts:
        middle = middle_ref[part] + dot(mixed_ref[:, part].T, output_ref[...])
        middle_ref[part] = middle
        normal, _ = unit(middle)
        normed_ref[part] = (normal * gain_mlp_ref[...]).astype(bf16)
    word_shape = (words, rows)
    lane = lanes(word_shape)
    member = (lane // slots == rows_of(word_shape)) & ((lane % slots).astype(f32) < row_counts)
    member = jnp.where(member, 1.0, 0.0).astype(bf16)
    fetches[8].wait()
    parts = [slice(at, at + 256) for at in range(0, expand_ref.shape[1], 256)]
    normed = normed_ref[...]
    before = dot(normed, expand_ref[:, parts[0]])
    for number, part in enumerate(parts):
        value, slope = gelu_parts(before)
        if number + 1 < len(parts):
            before = dot(normed, expand_ref[:, parts[number + 1]])
        slope_ref[:, part] = slope
        hidden_sum_ref[:, part] = dot(member, value).astype(bf16)
    high = middle_ref[...].astype(bf16)
    fetches[9].wait()
    total = dot(member, high) + dot(hidden_sum_ref[...], shrink_ref[...])
    pooled_ref[...] = (total / counts_column(counts)).astype(bf16)


def char_forward(languages, chars, counts, table, weights, slots):
    rows, width = chars.shape[1:]
    words = rows // slots
    hidden = weights[4].shape[1]
    vmem = pl.BlockSpec(memory_space=pltpu.VMEM)
    hbm = pl.BlockSpec(memory_space=pltpu.HBM)
    fetched = (languages, counts, table) + tuple(weights)
    return pl.pallas_call(
        functools.partial(char_forward_kernel, slots),
        in_specs=[hbm] * 10,
        out_specs=[vmem] * 8,
        out_shape=[
            jax.ShapeDtypeStruct((words, width), bf16),
            jax.ShapeDtypeStruct((words, hidden), bf16),
            jax.ShapeDtypeStruct(counts.shape, counts.dtype),
            jax.ShapeDtypeStruct((rows, 3 * width), bf16),
            jax.ShapeDtypeStruct((slots, rows * HEADS), f32),
            jax.ShapeDtypeStruct((width, rows), bf16),
            jax.ShapeDtypeStruct((rows, width), f32),
            jax.ShapeDtypeStruct((rows, hidden), bf16),
        ],
        scratch_shapes=[pltpu.VMEM(chars.shape[1:], bf16)]
        + [pltpu.VMEM(array.shape, array.dtype) for array in fetched if array is not counts]
        + [pltpu.VMEM(chars.shape[1:], bf16), pltpu.SemaphoreType.DMA((10,))],
        compiler_params=pltpu.CompilerParams(vmem_limit_bytes=16 * MIB),
        cost_estimate=pl.CostEstimate(
            flops=64 * rows * width * width, bytes_accessed=8 * MIB, transcendentals=0
        ),
        name="char_forward",
    )(*[in_hbm(array) for array in (chars,) + fetched])


CHAR_FIRST_SLOT = 144
CHAR_SECTION_SLOT = 80
CHAR_CORE_SLOT = 112
CHAR_LAST_SLOT = 48


def char_shard(slot, me):
    return me ^ ((slot >> 3) | (((slot >> 1) & 3) << 1) | ((slot & 1) << 3))


def put_shards(gradient, slots, shard_of, at):
    width = SLAB
    columns = gradient.shape[1] // width
    size = gradient.shape[0] // len(slots)
    for number, slot in enumerate(slots):
        first = pl.multiple_of(shard_of(number) * size, size)
        for column in range(columns):
            start = at + column * size
            slot[start : start + size] = gradient[
                pl.ds(first, size), column * width : (column + 1) * width
            ].astype(bf16)
    return at + size * columns


def slot_refs(*refs):
    return [ref.at[place] for ref in refs for place in range(ref.shape[0])]


def char_mlp_back_kernel(
    slots,
    shards,
    counts_ref,
    gain_mlp_ref,
    expand_ref,
    shrink_ref,
    dpooled_ref,
    hidden_sum_ref,
    other_sum_ref,
    mixed_ref,
    middle_ref,
    slope_ref,
    dmiddle_ref,
    gain_ref,
    keep_ref,
    send_ref,
    counts_wide,
    spread,
    dhidden_words,
    dz,
    dbefore,
    expand_grad,
    shrink_grad,
    output_grad,
):
    section, me = position()
    counts = counts_ref[section]
    rows, width = middle_ref.shape
    words = counts.shape[-1]
    column = counts_column(counts)
    counts_wide[...] = jnp.broadcast_to(column, counts_wide.shape)
    spread_value = dpooled_ref[:words].astype(f32) / column
    spread[...] = spread_value
    spread_high = spread_value.astype(bf16)
    dhidden_words[...] = dot_nt(spread_high, shrink_ref[...]).astype(bf16).astype(f32)
    dz[:words] = spread_high
    other = dpooled_ref[words:].astype(f32) / counts_column(counts_ref[1 - section])
    dz[words:] = other.astype(bf16)
    slot = rows_of((slots, 128)).astype(f32)
    for word in range(words):
        at_word = slice(word * slots, (word + 1) * slots)
        present = slot < counts_wide[word : word + 1, :]
        for at in range(0, expand_ref.shape[1], 128):
            part = slice(at, at + 128)
            piece = jnp.where(present, dhidden_words[word : word + 1, part], 0.0).astype(bf16)
            dbefore[at_word, part] = piece * slope_ref[at_word, part]
        for at in range(0, width, 128):
            part = slice(at, at + 128)
            dmiddle_ref[at_word, part] = jnp.where(present, spread[word : word + 1, part], 0.0)
    normal, scale = unit(middle_ref[...])
    normed_t = (normal * gain_mlp_ref[...]).astype(bf16).T
    hidden_sums = jnp.concatenate([hidden_sum_ref[...], other_sum_ref[...]], axis=0)
    hidden_sums_t = hidden_sums.T

    dnormed = dot_nt(dbefore[...], expand_ref[...])
    expand_grad[...] = dot(normed_t, dbefore[...])
    half = width // 2
    own_half = dz[:, pl.ds(pl.multiple_of(section * half, half), half)]
    shrink_grad[...] = dot(hidden_sums_t, own_half)
    dmiddle = dmiddle_ref[...] + unit_back(dnormed, gain_mlp_ref[...], normal, scale)
    dmiddle_ref[...] = dmiddle
    output_grad[...] = dot(mixed_ref[...], dmiddle.astype(bf16))
    gain_ref[...] = jnp.broadcast_to(
        jnp.sum(dnormed * normal, axis=0, keepdims=True), gain_ref.shape
    )
    targets = slot_refs(keep_ref, send_ref)
    at = 0
    for gradient in (expand_grad, output_grad):
        at = put_shards(gradient, targets, lambda slot: char_shard(slot, me), at)
    size = shrink_grad.shape[0] // shards
    for number, target in enumerate(targets):
        first = pl.multiple_of(char_shard(number, me) * size, size)
        piece = shrink_grad[pl.ds(first, size), :].astype(bf16)
        target[at:, :half] = piece[: size // 2]
        target[at:, half:] = piece[size // 2 :]


def char_mlp_back(counts, weights, dpooled, stored, other_sum, slots, shards):
    _, _, output, gain_mlp, expand_w, shrink = weights
    hidden_sum, _, _, mixed, middle, slope = stored
    rows, width = middle.shape
    words = rows // slots
    hidden = expand_w.shape[1]
    half = (shards // 2, CHAR_CORE_SLOT, width)
    vmem = pl.BlockSpec(memory_space=pltpu.VMEM)
    return pl.pallas_call(
        functools.partial(char_mlp_back_kernel, slots, shards),
        in_specs=[vmem] * 10,
        out_specs=[vmem] * 4,
        out_shape=[
            jax.ShapeDtypeStruct((rows, width), f32),
            jax.ShapeDtypeStruct((8, width), f32),
            jax.ShapeDtypeStruct(half, bf16),
            jax.ShapeDtypeStruct(half, bf16),
        ],
        scratch_shapes=[
            pltpu.VMEM((words, 128), f32),
            pltpu.VMEM((words, width), f32),
            pltpu.VMEM((words, hidden), f32),
            pltpu.VMEM((2 * words, width), bf16),
            pltpu.VMEM((rows, hidden), bf16),
            pltpu.VMEM(expand_w.shape, f32),
            pltpu.VMEM((hidden, width // 2), f32),
            pltpu.VMEM(output.shape, f32),
        ],
        compiler_params=pltpu.CompilerParams(vmem_limit_bytes=16 * MIB),
        cost_estimate=pl.CostEstimate(
            flops=64 * rows * width * width, bytes_accessed=8 * MIB, transcendentals=0
        ),
        name="char_mlp_back",
    )(
        counts,
        gain_mlp,
        expand_w,
        shrink,
        dpooled,
        hidden_sum,
        other_sum,
        mixed,
        middle,
        slope,
    )


def char_attn_back_kernel(
    slots,
    shards,
    _,
    chars_hbm,
    languages_hbm,
    table_ref,
    gain_attn_ref,
    project_ref,
    output_ref,
    dmiddle_ref,
    gain_mlp_grad_ref,
    word_gains_ref,
    qkv_ref,
    probs_ref,
    grad_ref,
    keep_ref,
    send_ref,
    extra_ref,
    chars_ref,
    languages_ref,
    dmixed,
    dqkv,
    project_grad,
    sems,
):
    section, me = position()
    fetches = fetch_all(
        (chars_hbm.at[section], languages_hbm), (chars_ref, languages_ref), sems
    )
    rows, width = dmiddle_ref.shape
    dmixed[...] = dot_nt(dmiddle_ref[...].astype(bf16), output_ref[...]).astype(bf16)

    def load(block, which):
        return qkv_ref[block * BLOCK : (block + 1) * BLOCK, which * SLAB : (which + 1) * SLAB]

    def load_dmixed(block):
        return dmixed[block * BLOCK : (block + 1) * BLOCK]

    def store(block, which, value):
        dqkv[block * BLOCK : (block + 1) * BLOCK, which * SLAB : (which + 1) * SLAB] = value

    kept = []

    def norms():
        for fetch in fetches:
            fetch.wait()
        language = pick(languages_ref[...], section)
        normal, scale = unit(char_rows(chars_ref[...], table_ref, language))
        kept.extend((language, normal, scale, (normal * gain_attn_ref[...]).astype(bf16).T))

    blocks = range(rows // BLOCK)
    attend_back(load, load_dmixed, blocks, probs_ref[...], store, slots, norms)
    language, normal, scale, normed_t = kept
    dnormed = dot_nt(dqkv[...], project_ref[...])
    project_grad[...] = dot(normed_t, dqkv[...])
    gain_attn_grad = jnp.sum(dnormed * normal, axis=0, keepdims=True)
    dx = dmiddle_ref[...] + unit_back(dnormed, gain_attn_ref[...], normal, scale)
    grad_ref[...] = dx
    row_sum = jnp.sum(dx, axis=0, keepdims=True)
    targets = [
        ref.at[pl.ds(place * CHAR_LAST_SLOT, CHAR_LAST_SLOT)]
        for ref in (keep_ref, send_ref)
        for place in range(shards // 2)
    ]
    put_shards(project_grad, targets, lambda slot: char_shard(slot, me), 0)
    extra = jnp.concatenate(
        [
            gain_attn_grad,
            gain_mlp_grad_ref[:1],
            word_gains_ref[:6],
            jnp.where(rows_of((8, 1)) == language, row_sum, 0.0),
        ],
        axis=0,
    ).astype(bf16)
    extra_ref[...] = extra


def char_attn_back(
    languages,
    chars,
    table,
    weights,
    dmiddle,
    gain_mlp_grad,
    word_gains,
    stored,
    slots,
    shards,
    after,
):
    gain_attn, project, output, _, _, _ = weights
    _, qkv, probs, _, _, _ = stored
    rows, width = dmiddle.shape
    half = (shards // 2 * CHAR_LAST_SLOT, width)
    vmem = pl.BlockSpec(memory_space=pltpu.VMEM)
    hbm = pl.BlockSpec(memory_space=pltpu.HBM)
    return pl.pallas_call(
        functools.partial(char_attn_back_kernel, slots, shards),
        in_specs=[pl.BlockSpec(memory_space=pl.ANY), hbm, hbm] + [vmem] * 9,
        out_specs=[vmem] * 4,
        out_shape=[
            jax.ShapeDtypeStruct((rows, width), f32),
            jax.ShapeDtypeStruct(half, bf16),
            jax.ShapeDtypeStruct(half, bf16),
            jax.ShapeDtypeStruct((16, width), bf16),
        ],
        scratch_shapes=[
            pltpu.VMEM((rows, width), bf16),
            pltpu.VMEM(languages.shape, languages.dtype),
            pltpu.VMEM((rows, width), bf16),
            pltpu.VMEM((rows, 3 * width), bf16),
            pltpu.VMEM(project.shape, f32),
            pltpu.SemaphoreType.DMA((2,)),
        ],
        compiler_params=pltpu.CompilerParams(vmem_limit_bytes=16 * MIB),
        cost_estimate=pl.CostEstimate(
            flops=0, bytes_accessed=0, transcendentals=0
        ),
        name="char_attn_back",
    )(
        after,
        in_hbm(chars),
        in_hbm(languages),
        table,
        gain_attn,
        project,
        output,
        dmiddle,
        gain_mlp_grad,
        word_gains,
        qkv,
        probs,
    )


LONG = pl.CostEstimate(flops=20_000_000_000, bytes_accessed=8 * MIB, transcendentals=0)

WORD_SLOT = 400

SHORT_FLOPS = 400_000_000


def word_kernel(
    length,
    shards,
    own_ref,
    both_ref,
    section_ref,
    far_ref,
    cot_ref,
    cot_far_ref,
    input_ref,
    gain_attn_ref,
    project_ref,
    output_ref,
    gain_mlp_ref,
    expand_ref,
    shrink_ref,
    result_hbm,
    dpooled_ref,
    gains_ref,
    keep_ref,
    send_ref,
    pooled,
    pooled_t,
    dz,
    start,
    normed_t,
    qkv,
    kept,
    mixed_t,
    middle,
    normed_mlp_t,
    hidden,
    dbefore,
    dmixed,
    dqkv,
    dy,
    dstart,
    result,
    input_grad,
    project_grad,
    output_grad,
    expand_grad,
    shrink_grad,
    sem,
):
    total = pooled.shape[0]
    width = output_ref.shape[0]
    section, me = position()
    slabs = width // SLAB
    for place, ref in enumerate((own_ref, section_ref, far_ref, both_ref)):
        pooled[place * length : (place + 1) * length] = ref[...]
    for place, (ref, other) in enumerate(
        ((cot_ref, section), (cot_ref, 1 - section), (cot_far_ref, section), (cot_far_ref, 1 - section))
    ):
        dz[place * length : (place + 1) * length] = ref[other]

    x = dot(pooled[...], input_ref[...])
    start[...] = x
    normal, _ = unit(x)
    low = (normal * gain_attn_ref[...]).astype(bf16)
    normed_t[...] = low.T
    qkv[...] = dot(low, project_ref[...]).astype(bf16)
    tiles = [(block, slab) for block in range(total // BLOCK) for slab in range(slabs)]

    def load(tile, which):
        block, slab = tile
        at = which * width + slab * SLAB
        return qkv[block * BLOCK : (block + 1) * BLOCK, at : at + SLAB]

    mask_shape = (length, len(tiles) * HEADS * BLOCK)
    causal = rows_of(mask_shape) <= lanes(mask_shape) % length
    probs, mixed = attend(load, tiles, causal, length)
    kept[...] = probs
    for (block, slab), piece in zip(tiles, mixed):
        mixed_t[slab * SLAB : (slab + 1) * SLAB, block * BLOCK : (block + 1) * BLOCK] = piece
    x = x + dot(mixed_t[...].T, output_ref[...])
    middle[...] = x
    normal, _ = unit(x)
    low = (normal * gain_mlp_ref[...]).astype(bf16)
    normed_mlp_t[...] = low.T
    dz_all = dz[...]
    for at in range(0, expand_ref.shape[1], 256):
        part = slice(at, at + 256)
        value, bend = gelu_parts(dot(low, expand_ref[:, part]))
        hidden[:, part] = value
        dhidden = dot_nt(dz_all, shrink_ref[part, :]).astype(bf16)
        dbefore[:, part] = dhidden * bend

    def shard_of(slot):
        return (me & 7) ^ ((slot >> 2) | ((slot & 3) << 1))

    def own_rows(flipped):
        many = flipped.shape[0] // 2
        return flipped[pl.ds(pl.multiple_of((me >> 3) * many, many), many), :]

    def half_columns(ref, place):
        many = ref.shape[1] // 2
        return ref[:, pl.ds(pl.multiple_of(place * many, many), many)]

    def own_columns(ref):
        return half_columns(ref, section)

    targets = slot_refs(keep_ref, send_ref)
    hidden_t = half_columns(hidden, me >> 3).T
    pooled_t[...] = pooled[...].T
    normal, scale = unit(middle[...])
    dnormed = dot_nt(dbefore[...], expand_ref[...])
    expand_grad[...] = dot(own_rows(normed_mlp_t), own_columns(dbefore))
    shrink_grad[...] = dot(hidden_t, own_columns(dz))
    dmiddle = dz_all.astype(f32) + unit_back(dnormed, gain_mlp_ref[...], normal, scale)
    dy_low = dmiddle.astype(bf16)
    dy[...] = dy_low
    dmixed[...] = dot_nt(dy_low, output_ref[...]).astype(bf16)
    gain_mlp_grad = jnp.sum(dnormed * normal, axis=0, keepdims=True)
    result[...] = middle[:length] + dot(hidden[:length], shrink_ref[...])
    leave = pltpu.make_async_copy(result, result_hbm, sem)
    leave.start()
    output_grad[...] = dot(own_rows(mixed_t), own_columns(dy))

    def load_dmixed(tile):
        block, slab = tile
        return dmixed[block * BLOCK : (block + 1) * BLOCK, slab * SLAB : (slab + 1) * SLAB]

    def store(tile, which, value):
        block, slab = tile
        at = which * width + slab * SLAB
        dqkv[block * BLOCK : (block + 1) * BLOCK, at : at + SLAB] = value

    attend_back(load, load_dmixed, tiles, kept[...], store, length)
    normal, scale = unit(start[...])
    dnormed = dot_nt(dqkv[...], project_ref[...])
    project_grad[...] = dot(own_rows(normed_t), own_columns(dqkv))
    dword = (dmiddle + unit_back(dnormed, gain_attn_ref[...], normal, scale)).astype(bf16)
    dpooled_ref[...] = dot_nt(dword[: 2 * length], input_ref[...]).astype(bf16)
    dstart[...] = dword
    gain_attn_grad = jnp.sum(dnormed * normal, axis=0, keepdims=True)
    input_grad[...] = dot(own_rows(pooled_t), own_columns(dstart))
    at = 0
    for ref in (input_grad, project_grad, output_grad, expand_grad, shrink_grad):
        at = put_shards(ref, targets, shard_of, at)
    gains_ref[...] = 0.25 * jnp.concatenate(
        [gain_attn_grad[:, :SLAB], gain_attn_grad[:, SLAB:]]
        + [gain_mlp_grad[:, :SLAB], gain_mlp_grad[:, SLAB:]]
        + [jnp.zeros((4, SLAB), f32)],
        axis=0,
    )
    leave.wait()


def word_group(pooled, cotangents, word_input, weights, shards):
    gain_attn, project, output, gain_mlp, expand_w, shrink = weights
    length, channels = pooled[0].shape
    width = output.shape[0]
    hidden = expand_w.shape[1]
    total = 4 * length
    half = (4, WORD_SLOT, SLAB)
    vmem = pl.BlockSpec(memory_space=pltpu.VMEM)
    hbm = pl.BlockSpec(memory_space=pltpu.HBM)
    return pl.pallas_call(
        functools.partial(word_kernel, length, shards),
        in_specs=[vmem] * 13,
        out_specs=[hbm, vmem, vmem, vmem, vmem],
        out_shape=[
            jax.ShapeDtypeStruct((length, width), f32),
            jax.ShapeDtypeStruct((2 * length, channels), bf16),
            jax.ShapeDtypeStruct((8, SLAB), f32),
            jax.ShapeDtypeStruct(half, bf16),
            jax.ShapeDtypeStruct(half, bf16),
        ],
        scratch_shapes=[
            pltpu.VMEM((total, channels), bf16),
            pltpu.VMEM((channels, total), bf16),
            pltpu.VMEM((total, width), bf16),
            pltpu.VMEM((total, width), f32),
            pltpu.VMEM((width, total), bf16),
            pltpu.VMEM((total, 3 * width), bf16),
            pltpu.VMEM((length, total * (width // HEAD)), f32),
            pltpu.VMEM((width, total), bf16),
            pltpu.VMEM((total, width), f32),
            pltpu.VMEM((width, total), bf16),
            pltpu.VMEM((total, hidden), bf16),
            pltpu.VMEM((total, hidden), bf16),
            pltpu.VMEM((total, width), bf16),
            pltpu.VMEM((total, 3 * width), bf16),
            pltpu.VMEM((total, width), bf16),
            pltpu.VMEM((total, width), bf16),
            pltpu.VMEM((length, width), f32),
            pltpu.VMEM((channels // 2, width // 2), f32),
            pltpu.VMEM((width // 2, 3 * width // 2), f32),
            pltpu.VMEM((width // 2, width // 2), f32),
            pltpu.VMEM((width // 2, hidden // 2), f32),
            pltpu.VMEM((hidden // 2, width // 2), f32),
            pltpu.SemaphoreType.DMA,
        ],
        compiler_params=pltpu.CompilerParams(vmem_limit_bytes=20 * MIB),
        cost_estimate=pl.CostEstimate(
            flops=total * width * width * 25 * 4, bytes_accessed=8 * MIB, transcendentals=0
        ),
        name="word_group",
    )(*pooled, *cotangents, word_input, gain_attn, project, output, gain_mlp, expand_w, shrink)


def summed(*parts):
    return functools.reduce(lambda a, b: a + b, [part.astype(f32) for part in parts])


def added(*parts):
    return summed(*parts).astype(bf16)


def by_section(section, low, high):
    return (jnp.where(section == 0, low, high), jnp.where(section == 0, high, low))


def word_sum_kernel(keep, arrived, *outs):
    for place, ref in enumerate(outs):
        ref[...] = added(keep[place], arrived[place])


def word_sum(keep, arrived):
    return pl.pallas_call(
        word_sum_kernel,
        out_shape=[jax.ShapeDtypeStruct((WORD_SLOT, SLAB), bf16)] * 4,
        compiler_params=pltpu.CompilerParams(vmem_limit_bytes=12 * MIB),
        name="word_sum",
    )(keep, arrived)


def first_sum_kernel(keep, arrived, stay_ref, go_ref, shrink_ref):
    section, _ = position()
    half = SLAB // 2
    for place in range(keep.shape[0]):
        total = added(keep[place], arrived[place])
        rows = total[:CHAR_SECTION_SLOT]
        stay_ref[place], go_ref[place] = by_section(section, rows[:, :half], rows[:, half:])
        rows = total[CHAR_SECTION_SLOT:]
        shrink_ref[place] = jnp.concatenate([rows[:, :half], rows[:, half:]], axis=0)


def first_sum(keep, arrived):
    half = jax.ShapeDtypeStruct((keep.shape[0], CHAR_SECTION_SLOT, SLAB // 2), bf16)
    shrink = jax.ShapeDtypeStruct(
        (keep.shape[0], CHAR_FIRST_SLOT - CHAR_SECTION_SLOT, SLAB // 2), bf16
    )
    return pl.pallas_call(
        first_sum_kernel,
        out_shape=[half, half, shrink],
        compiler_params=pltpu.CompilerParams(vmem_limit_bytes=12 * MIB),
        name="first_sum",
    )(keep, arrived)


def section_sum_kernel(stay, arrived, out):
    out[...] = added(stay[...], arrived[...])


def section_sum(stay, arrived):
    return pl.pallas_call(
        section_sum_kernel,
        out_shape=jax.ShapeDtypeStruct(stay.shape, bf16),
        compiler_params=pltpu.CompilerParams(vmem_limit_bytes=12 * MIB),
        cost_estimate=pl.CostEstimate(flops=SHORT_FLOPS, bytes_accessed=0, transcendentals=0),
        name="section_sum",
    )(stay, arrived)


def second_sum_kernel(first, shrink, keep, core_arrived, own_extra, core_extra, *outs):
    _, me = position()
    half = SLAB // 2
    extra = summed(own_extra[...], core_extra[...])
    for place, out in enumerate(outs):
        at = CHAR_FIRST_SLOT
        for far in range(2):
            entry = 2 * place + far
            columns = slice(far * half, (far + 1) * half)
            total = first[entry]
            middle = CHAR_SECTION_SLOT - 16
            out[:middle, columns] = total[:middle]
            out[middle : CHAR_FIRST_SLOT - 16, columns] = shrink[entry]
            out[CHAR_FIRST_SLOT - 16 : CHAR_FIRST_SLOT, columns] = total[middle:]
            rows = slice(entry * CHAR_LAST_SLOT, (entry + 1) * CHAR_LAST_SLOT)
            out[at : at + CHAR_LAST_SLOT] = added(keep[rows], core_arrived[rows])
            at += CHAR_LAST_SLOT
            shard = char_shard(entry, me)
            turned = pltpu.roll(extra, lax.rem(SLAB - shard * 16, SLAB), 1)
            word = pltpu.roll(extra, lax.rem(2 * SLAB - shard * 32, SLAB), 1)
            upper = shard * 32 >= SLAB
            block = jnp.concatenate(
                [
                    turned[:2],
                    jnp.where(upper, word[3:4], word[2:3]),
                    jnp.where(upper, word[5:6], word[4:5]),
                    turned[4:],
                ],
                axis=0,
            )
            out[-16:, columns] = block[:, :half].astype(bf16)


def total_kernel(*refs):
    *pieces, chars_ref, out, chars_hbm, sem = refs
    leave = pltpu.make_async_copy(chars_ref, chars_hbm, sem)
    leave.start()
    out[...] = added(*[ref[...] for ref in pieces])
    leave.wait()


def total_of(*pieces, chars_grad):
    vmem = pl.BlockSpec(memory_space=pltpu.VMEM)
    return pl.pallas_call(
        total_kernel,
        in_specs=[vmem] * (len(pieces) + 1),
        out_specs=[vmem, pl.BlockSpec(memory_space=pltpu.HBM)],
        out_shape=[
            jax.ShapeDtypeStruct(pieces[0].shape, bf16),
            jax.ShapeDtypeStruct(chars_grad.shape, f32),
        ],
        scratch_shapes=[pltpu.SemaphoreType.DMA],
        compiler_params=pltpu.CompilerParams(vmem_limit_bytes=12 * MIB),
        cost_estimate=LONG,
        name="total",
    )(*pieces, chars_grad)


def second_sum(first, last):
    rows = CHAR_FIRST_SLOT + 2 * CHAR_LAST_SLOT + 16
    return pl.pallas_call(
        second_sum_kernel,
        out_shape=[jax.ShapeDtypeStruct((rows, SLAB), bf16)] * 4,
        compiler_params=pltpu.CompilerParams(vmem_limit_bytes=12 * MIB),
        name="second_sum",
    )(*first, *last)


FOLD = 80


def plane_sum_kernel(*refs):
    half = SLAB // 2
    pieces = refs[:4]
    for far, out in enumerate(refs[5:]):
        columns = slice(far * half, (far + 1) * half)
        total = added(*[ref[:CHAR_FIRST_SLOT, columns] for ref in pieces])
        out[:FOLD, :half] = total[:FOLD]
        out[:FOLD, half:] = total[CHAR_FIRST_SLOT - FOLD :]
        out[:16, half:] = added(*[ref[-16:, columns] for ref in pieces])
        first = CHAR_FIRST_SLOT + far * CHAR_LAST_SLOT
        out[FOLD:] = added(*[ref[first : first + CHAR_LAST_SLOT] for ref in pieces])


def plane_sum(pieces, after):
    return pl.pallas_call(
        plane_sum_kernel,
        in_specs=[pl.BlockSpec(memory_space=pltpu.VMEM)] * 4 + [pl.BlockSpec(memory_space=pl.ANY)],
        out_shape=[jax.ShapeDtypeStruct((FOLD + CHAR_LAST_SLOT, SLAB), bf16)] * 2,
        compiler_params=pltpu.CompilerParams(vmem_limit_bytes=12 * MIB),
        cost_estimate=LONG,
        name="plane_sum",
    )(*pieces, after)


def char_last_kernel(near_ref, both_ref, far_ref, section_ref, _, *outs):
    section, _ = position()
    half = SLAB // 2
    mine = summed(near_ref[:FOLD], far_ref[:FOLD])
    theirs = summed(section_ref[:FOLD], both_ref[:FOLD])

    def unfold(total):
        return jnp.concatenate(
            [total[:, :half], total[2 * FOLD - CHAR_FIRST_SLOT :, half:]], axis=0
        )

    first = jnp.concatenate(by_section(section, unfold(mine), unfold(theirs)), axis=1)
    extra = mine[:16, half:] + theirs[:16, half:]
    last = summed(near_ref[FOLD:], section_ref[FOLD:], far_ref[FOLD:], both_ref[FOLD:])
    (
        table_ref,
        gain_attn_ref,
        project_ref,
        output_ref,
        gain_mlp_ref,
        expand_ref,
        shrink_ref,
        word_gain_attn_ref,
        word_gain_mlp_ref,
    ) = outs
    for total, refs in ((first, (expand_ref, shrink_ref, output_ref)), (last, (project_ref,))):
        at = 0
        for ref in refs:
            size = ref.shape[0]
            for column in range(ref.shape[1] // SLAB):
                ref[:, column * SLAB : (column + 1) * SLAB] = total[at : at + size]
                at += size
    size = gain_attn_ref.shape[1]
    gain_attn_ref[...] = extra[0:1, :size]
    gain_mlp_ref[...] = extra[1:2, :size]
    table_ref[...] = extra[8:16, :size]
    size = word_gain_attn_ref.shape[1]
    word_gain_attn_ref[...] = extra[2:3, :size]
    word_gain_mlp_ref[...] = extra[3:4, :size]


def char_last(near, arrived, shapes, after):
    return pl.pallas_call(
        char_last_kernel,
        in_specs=[pl.BlockSpec(memory_space=pltpu.VMEM)] * 4 + [pl.BlockSpec(memory_space=pltpu.HBM)],
        out_shape=[jax.ShapeDtypeStruct(shape, f32) for shape in shapes],
        compiler_params=pltpu.CompilerParams(vmem_limit_bytes=12 * MIB),
        name="char_last",
    )(near, *arrived, in_hbm(after))


def word_last_kernel(own_ref, other_ref, *outs):
    section, _ = position()
    own = own_ref[...].astype(f32)
    halves = by_section(section, own, other_ref[...].astype(f32))
    at = 0
    for ref in outs:
        size = ref.shape[0]
        columns = ref.shape[1] // (2 * SLAB)
        for column in range(columns):
            for half in range(2):
                first = (half * columns + column) * SLAB
                ref[:, first : first + SLAB] = halves[half][at : at + size]
            at += size


def word_last(own, other, shapes):
    return pl.pallas_call(
        word_last_kernel,
        out_shape=[jax.ShapeDtypeStruct(shape, f32) for shape in shapes],
        compiler_params=pltpu.CompilerParams(vmem_limit_bytes=12 * MIB),
        name="word_last",
    )(own, other)


def exchange(value, section_bit, dp_bits):
    shards = lax.axis_size("dp")
    pairs = [
        (s * shards + d, (s ^ section_bit) * shards + (d ^ dp_bits))
        for s in range(lax.axis_size("section"))
        for d in range(shards)
    ]
    return lax.ppermute(value, ("section", "dp"), pairs)


CORE, SIDE, NEAR, FAR = (1, 2, 4, 8)


def plane_exchange(pieces):
    return tuple(
        exchange(piece, 0, bits) for piece, bits in zip(pieces[:0:-1], (SIDE | NEAR, NEAR, SIDE))
    ) + (pieces[0],)


def local_grouped(
    chars, counts, languages, language_table, char_weights, word_input, word_weights, cotangent
):
    shards = lax.axis_size("dp")
    micros, _, words, slots, width = chars.shape
    rows = words * slots
    cot = cotangent[:, 0]
    cot_far = exchange(cot, 0, FAR)
    char_weights = tuple(w[None] if w.ndim == 1 else w for w in char_weights)
    word_weights = tuple(w[None] if w.ndim == 1 else w for w in word_weights)
    chars = chars.reshape(micros, rows, width)
    counts = counts.reshape(micros, 1, words)
    languages = languages.reshape(1, micros)
    pooled, hidden_sum, own_counts, *stored = char_forward(
        languages, chars, counts, language_table, char_weights, slots
    )
    stored = (hidden_sum, *stored)
    other_sum = exchange(hidden_sum, 1, 0)
    others = (exchange(pooled, 1, FAR), exchange(pooled, 1, 0), exchange(pooled, 0, FAR))
    result, dpooled, word_gains, keep, send = word_group(
        (pooled,) + others, (cot, cot_far), word_input, word_weights, shards
    )
    word = plane_exchange(word_sum(keep, exchange(send, 0, CORE)))
    dmiddle, gain_mlp_grad, keep, send = char_mlp_back(
        own_counts, char_weights, dpooled, stored, other_sum, slots, shards
    )
    stay, go, shrink = first_sum(keep, exchange(send, 0, CORE))
    first = (section_sum(stay, exchange(go, 1, 0)), shrink)
    chars_grad, keep, send, extra = char_attn_back(
        languages,
        chars,
        language_table,
        char_weights,
        dmiddle,
        gain_mlp_grad,
        word_gains,
        stored,
        slots,
        shards,
        stay,
    )
    last = (keep, exchange(send, 0, CORE), extra, exchange(extra, 0, CORE))
    char = plane_exchange(second_sum(first, last))
    word, chars_grad = total_of(*word, chars_grad=chars_grad)
    near, far = plane_sum(char, word)
    arrived = (exchange(far, 1, FAR), exchange(far, 0, FAR), exchange(near, 1, 0))

    def shard_shapes(weights):
        for weight in weights:
            if weight.shape[0] == 1:
                yield (1, weight.shape[1] // shards)
            else:
                yield (weight.shape[0] // shards, weight.shape[1])

    table_shape = (language_table.shape[0], language_table.shape[1] // shards)
    input_shape, attn_shape, project_shape, output_shape, mlp_shape, expand_shape, shrink_shape = (
        shard_shapes((word_input,) + word_weights)
    )
    word_shapes = [input_shape, project_shape, output_shape, expand_shape, shrink_shape]
    word_totals = word_last(word, exchange(word, 1, 0), word_shapes)
    char_shapes = [table_shape, *shard_shapes(char_weights), attn_shape, mlp_shape]
    *char_totals, attn, mlp = char_last(near, arrived, char_shapes, word_totals[0])
    totals = [*char_totals, word_totals[0], attn, *word_totals[1:3], mlp, *word_totals[3:]]
    totals = [total[0] if total.shape[0] == 1 else total for total in totals]
    return (result[None, None], chars_grad.reshape((1, 1, words, slots, width))) + tuple(totals)


def norm_forward(inputs, gain):
    return inputs * lax.rsqrt(jnp.mean(inputs * inputs, axis=-1, keepdims=True) + eps) * gain


def attend_forward(normed, project, head_count, key_mask):
    row_count, length, channels = normed.shape
    head_size = channels // head_count
    qkv = jnp.einsum("blc,cf->blf", normed, project, preferred_element_type=jnp.float32).astype(
        jnp.bfloat16
    )
    pieces = qkv.reshape(row_count, length, 3, head_count, head_size)
    scores = jnp.einsum(
        "bqhd,bkhd->bhqk", pieces[:, :, 0], pieces[:, :, 1], preferred_element_type=jnp.float32
    ) * head_size ** (-0.5)
    scores = jnp.where(key_mask, scores, -1e30)
    row_max = jnp.max(scores, axis=-1, keepdims=True)
    weights_exp = jnp.exp(scores - row_max)
    row_total = jnp.sum(weights_exp, axis=-1, keepdims=True)
    attn_probs = (weights_exp / row_total).astype(jnp.bfloat16)
    mixed_heads = jnp.einsum(
        "bhqk,bkhd->bqhd", attn_probs, pieces[:, :, 2], preferred_element_type=jnp.float32
    )
    mixed_heads = mixed_heads.reshape(row_count, length, channels).astype(jnp.bfloat16)
    return (qkv, row_max + jnp.log(row_total), mixed_heads)


def attend_backward(
    normed, project, output, qkv, logsum, mixed_heads, dmiddle_low, head_count, key_mask
):
    row_count, length, channels = normed.shape
    head_size = channels // head_count
    scaling = head_size ** (-0.5)
    output_grad = jnp.einsum(
        "blc,bld->cd", mixed_heads, dmiddle_low, preferred_element_type=jnp.float32
    )
    dmixed = jnp.einsum(
        "bld,cd->blc", dmiddle_low, output, preferred_element_type=jnp.float32
    ).astype(jnp.bfloat16)
    dmixed = dmixed.reshape(row_count, length, head_count, head_size)
    pieces = qkv.reshape(row_count, length, 3, head_count, head_size)
    scores = (
        jnp.einsum(
            "bqhd,bkhd->bhqk", pieces[:, :, 0], pieces[:, :, 1], preferred_element_type=jnp.float32
        )
        * scaling
    )
    scores = jnp.where(key_mask, scores, -1e30)
    attn_probs = jnp.exp(scores - logsum)
    dprobs = jnp.einsum(
        "bqhd,bkhd->bhqk", dmixed, pieces[:, :, 2], preferred_element_type=jnp.float32
    )
    row_delta = jnp.sum(attn_probs * dprobs, axis=-1, keepdims=True)
    dscores = (attn_probs * (dprobs - row_delta)).astype(jnp.bfloat16)
    dquery = (
        jnp.einsum("bhqk,bkhd->bqhd", dscores, pieces[:, :, 1], preferred_element_type=jnp.float32)
        * scaling
    )
    dkeys = (
        jnp.einsum("bhqk,bqhd->bkhd", dscores, pieces[:, :, 0], preferred_element_type=jnp.float32)
        * scaling
    )
    dvalues = jnp.einsum(
        "bhqk,bqhd->bkhd",
        attn_probs.astype(jnp.bfloat16),
        dmixed,
        preferred_element_type=jnp.float32,
    )
    dqkv = (
        jnp.stack([dquery, dkeys, dvalues], axis=2)
        .reshape(row_count, length, 3 * channels)
        .astype(jnp.bfloat16)
    )
    project_grad = jnp.einsum("blc,blf->cf", normed, dqkv, preferred_element_type=jnp.float32)
    dnormed = jnp.einsum("blf,cf->blc", dqkv, project, preferred_element_type=jnp.float32)
    return (dnormed, project_grad, output_grad)


def block_forward(inputs, weights, head_count, key_mask):
    gain_attn, project, output, gain_mlp, expand, shrink = weights
    normed = norm_forward(inputs, gain_attn).astype(jnp.bfloat16)
    qkv, logsum, mixed_heads = attend_forward(normed, project, head_count, key_mask)
    middle = inputs + jnp.einsum(
        "blc,cd->bld", mixed_heads, output, preferred_element_type=jnp.float32
    )
    normed_mlp = norm_forward(middle, gain_mlp).astype(jnp.bfloat16)
    before = jnp.einsum("blc,cf->blf", normed_mlp, expand, preferred_element_type=jnp.float32)
    hidden = jax.nn.gelu(before).astype(jnp.bfloat16)
    result = middle + jnp.einsum("blf,fc->blc", hidden, shrink, preferred_element_type=jnp.float32)
    return (result, (inputs, normed, qkv, logsum, mixed_heads, middle, normed_mlp, before, hidden))


def block_backward(dresult, stored, weights, head_count, key_mask):
    gain_attn, project, output, gain_mlp, expand, shrink = weights
    inputs, normed, qkv, logsum, mixed_heads, middle, normed_mlp, before, hidden = stored
    grad_low = dresult.astype(jnp.bfloat16)
    shrink_grad = jnp.einsum("blf,blc->fc", hidden, grad_low, preferred_element_type=jnp.float32)
    dhidden = jnp.einsum(
        "blc,fc->blf", grad_low, shrink, preferred_element_type=jnp.float32
    ).astype(jnp.bfloat16)
    gelu_pull = jax.vjp(jax.nn.gelu, before)[1]
    dbefore = gelu_pull(dhidden.astype(jnp.float32))[0].astype(jnp.bfloat16)
    expand_grad = jnp.einsum("blc,blf->cf", normed_mlp, dbefore, preferred_element_type=jnp.float32)
    dnormed_mlp = jnp.einsum("blf,cf->blc", dbefore, expand, preferred_element_type=jnp.float32)
    norm_pull = jax.vjp(norm_forward, middle, gain_mlp)[1]
    dmiddle_norm, gain_mlp_grad = norm_pull(dnormed_mlp)
    dmiddle = dresult + dmiddle_norm
    dnormed, project_grad, output_grad = attend_backward(
        normed,
        project,
        output,
        qkv,
        logsum,
        mixed_heads,
        dmiddle.astype(jnp.bfloat16),
        head_count,
        key_mask,
    )
    first_pull = jax.vjp(norm_forward, inputs, gain_attn)[1]
    dinputs_norm, gain_attn_grad = first_pull(dnormed)
    return (
        dmiddle + dinputs_norm,
        (gain_attn_grad, project_grad, output_grad, gain_mlp_grad, expand_grad, shrink_grad),
    )


def char_front(char_text, char_count, language, lang_table, weights):
    present = lax.broadcasted_iota(jnp.int32, char_text.shape[:2], 1) < char_count[:, None]
    onehot = (lax.broadcasted_iota(jnp.int32, (lang_table.shape[0],), 0) == language).astype(
        jnp.bfloat16
    )
    lang_row = jnp.dot(onehot, lang_table, preferred_element_type=jnp.float32)
    inputs = char_text.astype(jnp.float32) + lang_row
    result, stored = block_forward(inputs, weights, CH, present[:, None, None, :])
    summed = jnp.sum(jnp.where(present[:, :, None], result, 0.0), axis=1)
    pooled = (summed / char_count[:, None].astype(jnp.float32)).astype(jnp.bfloat16)
    return (pooled, stored, present, onehot)


def char_back(stored, present, onehot, char_count, dpooled, weights):
    spread = dpooled.astype(jnp.float32) / char_count[:, None].astype(jnp.float32)
    dresult = jnp.where(present[:, :, None], spread[:, None, :], 0.0)
    dinputs, gradients = block_backward(dresult, stored, weights, CH, present[:, None, None, :])
    table_grad = onehot.astype(jnp.float32)[:, None] * jnp.sum(dinputs, axis=(0, 1))[None, :]
    return (dinputs, (table_grad,) + gradients)


def word_full(pooled, cot_rows, word_input, weights):
    length = pooled.shape[0]
    word_start = jnp.dot(pooled, word_input, preferred_element_type=jnp.float32)[None]
    causal = (
        lax.broadcasted_iota(jnp.int32, (length, length), 0)
        >= lax.broadcasted_iota(jnp.int32, (length, length), 1)
    )[None, None]
    result, stored = block_forward(word_start, weights, H, causal)
    dstart, gradients = block_backward(
        cot_rows.astype(jnp.float32)[None], stored, weights, H, causal
    )
    grad_low = dstart[0].astype(jnp.bfloat16)
    input_grad = jnp.einsum("wc,wd->cd", pooled, grad_low, preferred_element_type=jnp.float32)
    dpooled = jnp.einsum(
        "wd,cd->wc", grad_low, word_input, preferred_element_type=jnp.float32
    ).astype(jnp.bfloat16)
    return (result[0], dpooled, (input_grad,) + gradients)


def reduce_rows(gradients):
    shards = lax.axis_size("dp")
    flat = []
    for place, gradient in enumerate(gradients):
        if place == 0:
            gradient = gradient.T
        flat.append(gradient.astype(jnp.bfloat16).reshape(shards, -1))
    packed = jnp.concatenate(flat, axis=1)
    me = lax.axis_index("dp")
    packed = jnp.take(packed, jnp.arange(shards) ^ me, axis=0)
    bit = 1
    while packed.shape[0] > 1:
        pairs = packed.reshape(packed.shape[0] // 2, 2, packed.shape[1])
        arrived = lax.ppermute(pairs[:, 1], "dp", [(i, i ^ bit) for i in range(shards)])
        packed = (pairs[:, 0].astype(jnp.float32) + arrived.astype(jnp.float32)).astype(
            jnp.bfloat16
        )
        bit *= 2
    arrived = lax.ppermute(packed, "section", [(0, 1), (1, 0)])
    total = (packed.astype(jnp.float32) + arrived.astype(jnp.float32))[0]
    outs = []
    at = 0
    for place, gradient in enumerate(gradients):
        size = gradient.size // shards
        piece = total[at : at + size]
        at += size
        if place == 0:
            outs.append(piece.reshape(-1, gradient.shape[0]).T)
        else:
            outs.append(piece.reshape((gradient.shape[0] // shards,) + gradient.shape[1:]))
    return tuple(outs)


def local(
    chars,
    counts,
    languages,
    language_table,
    char_gain_attn,
    char_project,
    char_output,
    char_gain_mlp,
    char_expand,
    char_shrink,
    word_input,
    word_gain_attn,
    word_project,
    word_output,
    word_gain_mlp,
    word_expand,
    word_shrink,
    cotangent,
):
    char_weights = (
        char_gain_attn,
        char_project,
        char_output,
        char_gain_mlp,
        char_expand,
        char_shrink,
    )
    word_weights = (
        word_gain_attn,
        word_project,
        word_output,
        word_gain_mlp,
        word_expand,
        word_shrink,
    )
    if lax.axis_size("dp") == 16:
        return local_grouped(
            chars,
            counts,
            languages,
            language_table,
            char_weights,
            word_input,
            word_weights,
            cotangent,
        )
    section_index = lax.axis_index("section")
    char_text = chars[section_index, 0]
    char_count = counts[section_index, 0]
    language = languages[section_index, 0]
    cot_rows = cotangent[section_index, 0]
    pooled, stored, present, onehot = char_front(
        char_text, char_count, language, language_table, char_weights
    )
    result, dpooled, word_grads = word_full(pooled, cot_rows, word_input, word_weights)
    text_grad, char_grads = char_back(stored, present, onehot, char_count, dpooled, char_weights)
    totals = reduce_rows(char_grads + word_grads)
    return (result[None, None], text_grad[None, None]) + totals


def solution(mesh):
    placed = (
        P(None, "dp", None, None, None),
        P(None, "dp", None),
        P(None, "dp"),
        P(),
        P(),
        P(),
        P(),
        P(),
        P(),
        P(),
        P(),
        P(),
        P(),
        P(),
        P(),
        P(),
        P(),
        P(None, "dp", None, None),
    )
    return jax.shard_map(
        local,
        mesh=mesh,
        in_specs=placed,
        out_specs=(
            P("section", "dp", None, None),
            P("section", "dp", None, None, None),
            P(None, "dp"),
            P("dp"),
            P("dp", None),
            P("dp", None),
            P("dp"),
            P("dp", None),
            P("dp", None),
            P("dp", None),
            P("dp"),
            P("dp", None),
            P("dp", None),
            P("dp"),
            P("dp", None),
            P("dp", None),
        ),
        check_vma=False,
    )
```
